32 devices in a mesh: section: 2 (over y), ctx: 8 (over z, core), wsh: 2 (over x).
Axes of the slice: x: 2, y: 2, z: 4, core: 2. Of those that a mesh axis runs over, the one named last changes fastest.
Arguments:
- tokens: bfloat16 [2, 2, 1024, 768], P(None, 'wsh', 'ctx'), may hold values from -6 to 6
- out_cotangent: bfloat16 [2, 2, 1024, 768], P(None, 'wsh', 'ctx'), may hold values from -6 to 6
- attn_weights: bfloat16 [2, 4, 768, 768], P('section', None, 'wsh')
- up_weights: bfloat16 [2, 768, 3072], P('section', 'wsh'), may hold values from -0.21875 to 0.21875
- down_weights: bfloat16 [2, 3072, 768], P('section', 'wsh'), may hold values from -0.109375 to 0.109375
- norm_gains: bfloat16 [2, 2, 768], P('section', None, 'wsh'), may hold values from 0.25 to 1.75
- bias_rows: bfloat16 [2, 5, 768], P('section', None, 'wsh'), may hold values from -2 to 2
- up_bias: bfloat16 [2, 3072], P('section', 'wsh'), may hold values from -2 to 2
- seq_lengths: int32 [2, 2], P(None, 'wsh'), may hold values from 128 to 1024, as said below
- rand_owner: int32 [2, 2, 16, 12, 3], P(None, 'wsh'), may hold values from 0 to 7, all different within a row; in each aligned block of 24 rows (0 to 23, 24 to 47, ..., all dimensions but the last counted through in order) at most 18 rows name the same one
- rand_local: int32 [2, 2, 16, 12, 3], P(None, 'wsh'), may hold values from 0 to 1
- global_raw: int32 [2, 2, 2], P(None, 'wsh'), may hold values from 0 to 15
Outputs:
- layer_outputs: bfloat16 [2, 2, 2, 1024, 768], P('section', None, 'wsh', 'ctx')
- input_grads: bfloat16 [2, 2, 2, 1024, 768], P('section', None, 'wsh', 'ctx')
- grad_attn: float32 [2, 4, 768, 768], P('section', None, 'wsh')
- grad_up: float32 [2, 768, 3072], P('section', 'wsh')
- grad_down: float32 [2, 3072, 768], P('section', 'wsh')
- grad_gains: float32 [2, 2, 768], P('section', None, 'wsh')
- grad_biases: float32 [2, 5, 768], P('section', None, 'wsh')
- grad_up_bias: float32 [2, 3072], P('section', 'wsh')
- clipped_qk: bfloat16 [2, 2, 768, 768], P('section', None, 'wsh')
The draws below stay inside these ranges and needn't reach their ends.
Inputs may be any that keep to these rules, and one draw needn't show every extreme that they name: `seq_lengths`: in every shard the sequence of one micro-batch, drawn from the seed, has 1024 tokens. `rand_owner`: within the 24 rows (a query block and head each) of one device's query blocks (aligned blocks) the 3 owners of a row differ and no owner is named by more than 18 of those rows; some device's rows name one owner exactly 18 times.
All inputs are finite; a program needn't handle non-finite values.
Results may differ from the reference program's by a relative error of at most 0.03.
Values may be sent and summed in bfloat16 or wider, within the bound.
A program may use at most 320 MiB of HBM per device.

```python
import math
import jax
import jax.numpy as jnp
import numpy as np
from jax import lax

D = 768
H = 12
HD = 64
FF = 3072
BLK = 64
RND = 3
MB = 2
SECTIONS = 2
SEQUENCE_SHARDS = 2
GROUP_TOK = 1024
GROUP_BLK = 16
BLK_DEV = 2
LEN_MIN = 128
CAP = 18
N_CTX = 8


def draw_attn_weights(key, part):
    key = jax.random.fold_in(key, 11)
    base_key, head_key = jax.random.split(key)
    full_shape = (SECTIONS, 4, D, D)
    base = jax.random.normal(base_key, full_shape, jnp.float32)
    head_scale = jnp.exp(jax.random.uniform(head_key, (SECTIONS, 2, 1, H, 1), jnp.float32, math.log(0.6), math.log(1.7)))
    leading = (base[:, :2].reshape(SECTIONS, 2, D, H, HD) * head_scale).reshape(SECTIONS, 2, D, D)
    trailing = base[:, 2:] * jnp.array([1.0, 6.0], jnp.float32)[None, :, None, None]
    return (jnp.concatenate([leading, trailing], 1) * D ** (-0.5)).astype(jnp.bfloat16)


def draw_seq_lengths(key, part):
    key = jax.random.fold_in(key, 12)
    drawn_key, pick_key = jax.random.split(key)
    drawn = jax.random.randint(drawn_key, (MB, SEQUENCE_SHARDS), LEN_MIN, GROUP_TOK + 1)
    longest = jax.random.randint(pick_key, (SEQUENCE_SHARDS,), 0, MB)
    chosen = jnp.arange(MB)[:, None] == longest[None, :]
    return jnp.where(chosen, GROUP_TOK, drawn).astype(jnp.int32)


def touch_ends(result, stream_key, low, high):
    longest = result.shape.index(max(result.shape))
    spots = []
    for shift in (0, 1):
        where = [jax.random.randint(jax.random.fold_in(stream_key, axis), (), 0, length) for axis, length in enumerate(result.shape)]
        where[longest] = (where[longest] + shift) % result.shape[longest]
        spots.append(tuple(where))
    return result.at[spots[0]].set(low).at[spots[1]].set(high)


def block_levels(key, dims, cuts, low, top_value):
    loudness, own = 1.0, jax.random.fold_in(key, 6)
    for dim, blocks in cuts:
        heights = jnp.exp(jax.random.uniform(jax.random.fold_in(own, dim), (blocks,), jnp.float32, low / len(cuts), top_value / len(cuts)))
        loudness = loudness * jnp.repeat(heights, dims[dim] // blocks).reshape([-1 if axis == dim else 1 for axis in range(len(dims))])
    return loudness


def deal_out(own_key, own, number, rows, amount, top, limit, skew):
    sequence = jax.random.permutation(own_key, amount)
    heavy_load, common = load_shares(amount, rows * top, limit, skew, True), load_shares(amount, rows * top, limit, skew, False)
    places = jnp.arange(amount)

    def named(sizes, rotation):
        used = int((sizes > 0).sum())
        fixed = max(1, used // 4)
        passed = fixed + (places - fixed + rotation * (used - fixed)) % max(1, amount - fixed)
        return jnp.zeros((amount,), jnp.int32).at[sequence[jnp.where(places < fixed, places, passed)]].set(jnp.asarray(sizes, jnp.int32))

    sizes = jnp.where(number % 4 == 0, named(heavy_load, number // 4), named(common, number - number // 4 - 1))
    mixed = jax.random.permutation(jax.random.fold_in(own, 3), amount)
    donor, sink = mixed[0:amount // 2 * 2:2], mixed[1:amount // 2 * 2:2]
    margin = jnp.minimum(sizes[donor] - 1, limit - sizes[sink]) // 2
    margin = jnp.where((donor == sequence[0]) | (sink == sequence[0]) | (sizes[sink] == 0), 0, jnp.maximum(margin, 0))
    passed = jax.random.randint(jax.random.fold_in(own, 4), (amount // 2,), 0, 1 << 20) % (margin + 1)
    sizes = sizes.at[donor].add(-passed).at[sink].add(passed)
    labels = jnp.searchsorted(jnp.cumsum(sizes), jnp.arange(rows * top), side="right").astype(jnp.int32)
    listing = labels.reshape(top, rows).T
    listing = listing[jax.random.permutation(jax.random.fold_in(own, 1), rows)]
    rotation = jax.random.randint(jax.random.fold_in(own, 2), (rows, 1), 0, top)
    return jnp.take_along_axis(listing, (jnp.arange(top)[None, :] + rotation) % top, axis=1)


def load_shares(count, total, most, lean, full):
    loads = [(1 << 20) // math.isqrt(grade ** lean) + 1 for grade in range(1, count + 1)]
    largest = most if full else min(most, max(-(-total // count), total * loads[0] // sum(loads)))
    least = 1 if total - largest >= count - 1 else 0
    given, rest = [largest] + [least] * (count - 1), total - largest - least * (count - 1)
    while rest > 0:
        movable = [i for i in range(1, count) if given[i] < largest] or [i for i in range(1, count) if given[i] < most]
        mass, budget = sum([loads[i] for i in movable]), rest
        for i in movable:
            extra = min(most - given[i], max(1, budget * loads[i] // mass), rest)
            given[i] = given[i] + extra
            rest = rest - extra
    return np.array(given)


def scatter_about(stream_key, dims, scale, bound, shards=(), kind=jnp.bfloat16):
    entries = scale * jax.random.normal(stream_key, dims, jnp.float32)
    if shards:
        entries = entries * block_levels(stream_key, dims, shards, -0.22, 0.18)
    return jnp.clip(entries, -bound, bound).astype(kind)


def setup_inputs(seed: int = 0) -> dict:
    key_list = jax.random.split(jax.random.key(seed), 13)
    tokens = scatter_about(key_list[0], (MB, SEQUENCE_SHARDS, GROUP_TOK, D), 1.0, 6.0, ((1, 2), (2, 8)))
    out_cotangent = scatter_about(key_list[1], (MB, SEQUENCE_SHARDS, GROUP_TOK, D), 1.0, 6.0, ((1, 2), (2, 8)))
    attn_weights = draw_attn_weights(jax.random.fold_in(key_list[12], 71), 0)
    up_weights = scatter_about(key_list[3], (SECTIONS, D, FF), D ** -0.5, 0.21875, ((0, 2), (1, 2)))
    down_weights = scatter_about(key_list[4], (SECTIONS, FF, D), FF ** -0.5, 0.109375, ((0, 2), (1, 2)))
    norm_gains = jnp.clip(1.0 + 0.15 * jax.random.normal(key_list[5], (SECTIONS, 2, D), jnp.float32), 0.25, 1.75).astype(jnp.bfloat16)
    bias_rows = scatter_about(key_list[6], (SECTIONS, 5, D), 0.3, 2.0, ((0, 2), (2, 2)))
    up_bias = scatter_about(key_list[7], (SECTIONS, FF), 0.3, 2.0, ((0, 2), (1, 2)))
    seq_lengths = draw_seq_lengths(jax.random.fold_in(key_list[12], 71), 0)
    rand_owner_keys = jax.random.split(jax.random.fold_in(key_list[9], 1), MB * SEQUENCE_SHARDS * GROUP_BLK * H // (BLK_DEV * H))
    rand_owner_turns = jax.random.permutation(jax.random.fold_in(key_list[9], 3), MB * SEQUENCE_SHARDS * GROUP_BLK * H // (BLK_DEV * H))
    rand_owner = jax.vmap(lambda own, number: deal_out(jax.random.fold_in(key_list[9], 2), own, number, BLK_DEV * H, N_CTX, RND, CAP, 1))(rand_owner_keys, rand_owner_turns).reshape((MB, SEQUENCE_SHARDS, GROUP_BLK, H, RND))
    rand_local = touch_ends(jax.random.randint(key_list[10], (MB, SEQUENCE_SHARDS, GROUP_BLK, H, RND), 0, BLK_DEV), jax.random.fold_in(key_list[10], 1), 0, BLK_DEV - 1).astype(jnp.int32)
    global_raw = touch_ends(jax.random.randint(key_list[11], (MB, SEQUENCE_SHARDS, 2), 0, GROUP_BLK), jax.random.fold_in(key_list[11], 1), 0, GROUP_BLK - 1).astype(jnp.int32)
    return {"tokens": tokens, "out_cotangent": out_cotangent, "attn_weights": attn_weights, "up_weights": up_weights, "down_weights": down_weights, "norm_gains": norm_gains, "bias_rows": bias_rows, "up_bias": up_bias, "seq_lengths": seq_lengths, "rand_owner": rand_owner, "rand_local": rand_local, "global_raw": global_raw}


norm_eps = 1e-05
clip_limit = 6.0
masked_score = -1e+30
peak_score = lax.Precision.HIGHEST

@jax.custom_vjp
def low(v):
    return lax.optimization_barrier(v.astype(jnp.bfloat16)).astype(jnp.float32)

@jax.custom_vjp
def low_back(v):
    return v

def low_keep(v):
    return (low(v), None)

def low_pass(kept, grad):
    return (grad,)

def back_keep(v):
    return (v, None)

def back_low(kept, grad):
    return (low(grad),)
low.defvjp(low_keep, low_pass)
low_back.defvjp(back_keep, back_low)

def both_ways(values):
    return low(low_back(values))

def matmul(left_side, right_side):
    return jnp.dot(left_side, right_side, precision=peak_score, preferred_element_type=jnp.float32)

def layer_norm(inputs, norm_gain, norm_shift):
    center = inputs - lax.optimization_barrier(jnp.mean(inputs, -1, keepdims=True))
    spread = lax.optimization_barrier(jnp.mean(center * center, -1, keepdims=True))
    return center * lax.rsqrt(spread + norm_eps) * norm_gain + norm_shift

def gelu_exact(values):
    return jax.nn.gelu(values, approximate=False)

def key_table(length, owners, local_ids, global_row):
    valid_blocks = (length + BLK - 1) // BLK
    global_ids = (global_row % valid_blocks).astype(jnp.int32)
    block_ids = jnp.arange(GROUP_BLK, dtype=jnp.int32)
    window = block_ids[:, None] + jnp.arange(3, dtype=jnp.int32)[None, :] - 1
    window_ok = (window >= 0) & (window < GROUP_BLK)
    window = jnp.clip(window, 0, GROUP_BLK - 1).astype(jnp.int32)
    random_blocks = (owners * BLK_DEV + local_ids).astype(jnp.int32)
    block_index = jnp.concatenate([jnp.broadcast_to(window[:, None, :], (GROUP_BLK, H, 3)), jnp.broadcast_to(global_ids[None, None, :], (GROUP_BLK, H, 2)), random_blocks], -1)
    block_ok = jnp.concatenate([jnp.broadcast_to(window_ok[:, None, :], (GROUP_BLK, H, 3)), jnp.ones((GROUP_BLK, H, 2 + RND), dtype=bool)], -1)
    return (block_index, block_ok, global_ids)

def attend(queries, key_rows, values, length, block_index, block_ok, global_ids):
    score_scale = HD ** (-0.5)
    groups = GROUP_BLK // 8
    slot_count = 5 + RND
    key_heads = key_rows.reshape(GROUP_BLK, BLK, H, HD).transpose(2, 0, 1, 3)
    value_heads = values.reshape(GROUP_BLK, BLK, H, HD).transpose(2, 0, 1, 3)
    head_ids = jnp.arange(H, dtype=jnp.int32)[None, :, None]
    offsets = jnp.arange(BLK, dtype=jnp.int32)

    @jax.checkpoint
    def block_rows(pieces):
        query_rows, group_index, group_ok, first_row = pieces
        picked_keys = key_heads[head_ids, group_index]
        selected_values = value_heads[head_ids, group_index]
        raw_scores = jnp.einsum('ibhd,ihjkd->ihbjk', query_rows, picked_keys, precision=peak_score) * score_scale
        scores = low_back(raw_scores)
        key_ok = (group_ok[..., None] & (group_index[..., None] * BLK + offsets < length))[:, :, None]
        masked = jnp.where(key_ok, scores, masked_score)
        largest = lax.optimization_barrier(jnp.max(masked, axis=(3, 4), keepdims=True))
        powers = jnp.where(key_ok, jnp.exp(masked - largest), 0.0)
        attn_probs = powers / lax.optimization_barrier(jnp.sum(powers, axis=(3, 4), keepdims=True))
        mixed_rows = jnp.einsum('ihbjk,ihjkd->ibhd', low(attn_probs), selected_values, precision=peak_score)
        query_ok = (first_row + jnp.arange(8 * BLK, dtype=jnp.int32) < length).reshape(8, 1, BLK, 1, 1)
        head_top = lax.optimization_barrier(jnp.max(jnp.where(key_ok & query_ok, masked, masked_score), axis=(0, 2, 3, 4)))
        return (mixed_rows.reshape(8 * BLK, D), head_top)
    starts = jnp.arange(groups, dtype=jnp.int32) * (8 * BLK)
    mixed_rows, group_tops = lax.map(block_rows, (queries.reshape(groups, 8, BLK, H, HD), block_index.reshape(groups, 8, H, slot_count), block_ok.reshape(groups, 8, H, slot_count), starts))
    global_queries = queries.reshape(GROUP_BLK, BLK, H, HD)[global_ids]
    key_all = key_rows.reshape(GROUP_TOK, H, HD)
    value_all = values.reshape(GROUP_TOK, H, HD)
    wide = low_back(jnp.einsum('gqhd,khd->ghqk', global_queries, key_all, precision=peak_score) * score_scale)
    key_live = (jnp.arange(GROUP_TOK, dtype=jnp.int32) < length)[None, None, None, :]
    wide_masked = jnp.where(key_live, wide, masked_score)
    wide_top = lax.optimization_barrier(jnp.max(wide_masked, -1, keepdims=True))
    wide_powers = jnp.where(key_live, jnp.exp(wide_masked - wide_top), 0.0)
    wide_probs = wide_powers / lax.optimization_barrier(jnp.sum(wide_powers, -1, keepdims=True))
    global_rows = jnp.einsum('ghqk,khd->gqhd', low(wide_probs), value_all, precision=peak_score).reshape(2, BLK, D)
    query_live = (global_ids[:, None] * BLK + offsets[None, :] < length)[:, None, :, None]
    wide_max = lax.optimization_barrier(jnp.max(jnp.where(key_live & query_live, wide_masked, masked_score), axis=(0, 2, 3)))
    block_ids = jnp.arange(GROUP_BLK, dtype=jnp.int32)
    blocks = mixed_rows.reshape(GROUP_BLK, BLK, D)
    blocks = jnp.where((block_ids == global_ids[0])[:, None, None], global_rows[0][None], blocks)
    blocks = jnp.where((block_ids == global_ids[1])[:, None, None], global_rows[1][None], blocks)
    return (blocks.reshape(GROUP_TOK, D), jnp.maximum(lax.optimization_barrier(jnp.max(group_tops, 0)), wide_max))

def layer(layer_in, params, length, block_index, block_ok, global_ids):
    attn_full, up_full, down_full, gains_full, biases_full, up_bias_full = params
    layer_in = low_back(layer_in)
    queries = both_ways(matmul(layer_in, attn_full[0]))
    key_rows = both_ways(matmul(layer_in, attn_full[1]))
    values = both_ways(matmul(layer_in, attn_full[2]) + biases_full[0])
    mixed_rows, head_top = attend(queries, key_rows, values, length, block_index, block_ok, global_ids)
    mixed_rows = both_ways(mixed_rows)
    branch = low_back(matmul(mixed_rows, attn_full[3]) + biases_full[1])
    normed = layer_norm(layer_in + branch, gains_full[0], biases_full[3])
    hidden_pre = low_back(matmul(low(normed), up_full) + up_bias_full)
    gated = low(gelu_exact(hidden_pre))
    feed_out = low_back(matmul(gated, down_full) + biases_full[2])
    return (low(layer_norm(normed + feed_out, gains_full[1], biases_full[4])), head_top)

def reference(tokens, out_cotangent, attn_weights, up_weights, down_weights, norm_gains, bias_rows, up_bias, seq_lengths, rand_owner, rand_local, global_raw):
    weight_args = (attn_weights, up_weights, down_weights, norm_gains, bias_rows, up_bias)
    first_params = tuple((weight_arg[0].astype(jnp.float32) for weight_arg in weight_args))
    second_params = tuple((weight_arg[1].astype(jnp.float32) for weight_arg in weight_args))
    seq_count = MB * SEQUENCE_SHARDS
    sequences = (tokens.astype(jnp.float32).reshape(seq_count, GROUP_TOK, D), out_cotangent.astype(jnp.float32).reshape(seq_count, GROUP_TOK, D), seq_lengths.reshape(seq_count).astype(jnp.int32), rand_owner.reshape(seq_count, GROUP_BLK, H, RND).astype(jnp.int32), rand_local.reshape(seq_count, GROUP_BLK, H, RND).astype(jnp.int32), global_raw.reshape(seq_count, 2).astype(jnp.int32))

    def one_sequence(scan_state, seq_item):
        first_acc, second_acc, first_top, second_top = scan_state
        seq_rows, cotangent, length, owners, local_ids, global_row = seq_item
        block_index, block_ok, global_ids = key_table(length, owners, local_ids, global_row)

        def run_layer(layer_in, params):
            return layer(layer_in, params, length, block_index, block_ok, global_ids)
        first_out, first_back, first_max = jax.vjp(run_layer, seq_rows, first_params, has_aux=True)
        second_out, second_back, second_max = jax.vjp(run_layer, first_out, second_params, has_aux=True)
        middle_grad, second_grads = second_back(cotangent)
        input_grad, first_grads = first_back(middle_grad)
        first_acc = jax.tree.map(jnp.add, first_acc, first_grads)
        second_acc = jax.tree.map(jnp.add, second_acc, second_grads)
        scan_state = (first_acc, second_acc, jnp.maximum(first_top, first_max), jnp.maximum(second_top, second_max))
        return (scan_state, (first_out, second_out, input_grad, middle_grad))
    start_top = jnp.full((H,), masked_score, jnp.float32)
    zero_first = tuple((jnp.zeros_like(piece) for piece in first_params))
    zero_second = tuple((jnp.zeros_like(piece) for piece in second_params))
    scan_state, stacked = lax.scan(one_sequence, (zero_first, zero_second, start_top, start_top), sequences)
    first_acc, second_acc, first_top, second_top = scan_state
    first_out, second_out, input_grad, middle_grad = stacked
    out_shape = (MB, SEQUENCE_SHARDS, GROUP_TOK, D)
    layer_outputs = jnp.stack([first_out.reshape(out_shape), second_out.reshape(out_shape)]).astype(jnp.bfloat16)
    input_grads = jnp.stack([input_grad.reshape(out_shape), middle_grad.reshape(out_shape)]).astype(jnp.bfloat16)
    grads = [jnp.stack([first_piece, second_piece]) for first_piece, second_piece in zip(first_acc, second_acc)]
    head_tops = jnp.stack([first_top, second_top])
    factor = jnp.sqrt(clip_limit / jnp.maximum(head_tops, clip_limit))
    clipped = attn_weights[:, :2].astype(jnp.float32).reshape(SECTIONS, 2, D, H, HD) * factor[:, None, None, :, None]
    clipped_qk = clipped.reshape(SECTIONS, 2, D, D).astype(jnp.bfloat16)
    return (layer_outputs, input_grads, grads[0], grads[1], grads[2], grads[3], grads[4], grads[5], clipped_qk)
```

```python
import functools

import jax
import jax.numpy as jnp
from jax import lax
from jax.experimental import pallas as pl
from jax.experimental.pallas import tpu as pltpu
from jax.sharding import PartitionSpec as P

D = 768
H = 12
HD = 64
FF = 3072
BLK = 64
TD = 128
BLK_DEV = 2
PAIRS = H // 2
CHUNK = 768
NCH = FF // CHUNK
STEP = 1024

MESH = pl.DeviceIdType.MESH
norm_eps = 1e-05
clip_limit = 6.0
masked_score = -1e30
exact_dot = lax.Precision.HIGHEST
f32 = jnp.float32
bf16 = jnp.bfloat16


def dot(a, b):
    return jnp.dot(a, b, preferred_element_type=f32)


def dot_t(a, b):
    return lax.dot_general(a, b, (((1,), (1,)), ((), ())), preferred_element_type=f32)


def dot_0(a, b):
    return lax.dot_general(a, b, (((0,), (0,)), ((), ())), preferred_element_type=f32)


def column_sum(v):
    return jnp.sum(v, 0, keepdims=True)


def norm_parts(v):
    center = v - jnp.mean(v, -1, keepdims=True)
    rstd = lax.rsqrt(jnp.mean(center * center, -1, keepdims=True) + norm_eps)
    return center * rstd, rstd


def norm_back(grad, hat, rstd, gain):
    scaled = grad * gain
    return rstd * (
        scaled
        - jnp.mean(scaled, -1, keepdims=True)
        - hat * jnp.mean(scaled * hat, -1, keepdims=True)
    )


def gelu(v):
    return 0.5 * v * (1.0 + lax.erf(v * (0.5**0.5)))


def gelu_both(v):
    phi = 0.5 * (1.0 + lax.erf(v * (0.5**0.5)))
    return v * phi, phi + v * jnp.exp(-0.5 * v * v) * 0.3989422804014327


def place():
    return lax.axis_index("section"), lax.axis_index("ctx"), lax.axis_index("wsh")


def greet(peers):
    barrier = pltpu.get_barrier_semaphore()
    for peer in peers:
        pl.semaphore_signal(barrier, inc=1, device_id=peer, device_id_type=MESH)
    pl.semaphore_wait(barrier, len(peers))


def push(src, dst, send, recv, peer):
    return pltpu.make_async_remote_copy(
        src_ref=src, dst_ref=dst, send_sem=send, recv_sem=recv, device_id=peer, device_id_type=MESH
    )


def halves(rows):
    low = lax.broadcasted_iota(jnp.int32, rows.shape, 1) < HD
    zero = jnp.zeros_like(rows)
    return jnp.concatenate([jnp.where(low, rows, zero), jnp.where(low, zero, rows)], 0)


def joined(rows):
    low = lax.broadcasted_iota(jnp.int32, (TD, 2 * HD), 1) < HD
    return jnp.where(low, rows[:TD], rows[TD:])


def spread4(rows, width):
    return jnp.concatenate(
        [jnp.broadcast_to(rows[r : r + 1], (BLK, width)) for r in range(4)], 0
    )


def block_lanes(blocks, width):
    lane = lax.broadcasted_iota(jnp.int32, (blocks, width), 1)
    row = lax.broadcasted_iota(jnp.int32, (blocks, width), 0)
    return jnp.where(lax.shift_right_logical(lane, 6) == row, 1.0, 0.0).astype(bf16)


def head_column(columns, head):
    lane = lax.broadcasted_iota(jnp.int32, columns.shape, 1)
    return jnp.sum(jnp.where(lane == head, columns, 0.0), 1, keepdims=True)


def pair_lanes(g):
    return pl.ds(pl.multiple_of(g * (2 * HD), 2 * HD), 2 * HD)


def forward_kernel(
    nz, W, MB, T,
    lens, tokens, attn_w, up_w, down_w, small_in, counts,
    out_o, xall_o, kv_o, q_o, att_o, mix_o, lse_o, first_o, second_o, hidden_o, top_o,
    attn_o, up_o, down_o, small_o,
    attn, up, down, small_all, small, xall, kv, q, att, mix, lse, top, first, second, hidden, out,
    wide,
    load_sem, w_send, w_recv, wf_send, wf_recv, s_send, s_recv,
    b_send, b_recv, f_send, f_recv, o_send, save_sem,
):
    s, c, w = place()
    z, core = c // 2, lax.rem(c, 2)
    part = D // W
    half = part // 2
    ffp = FF // W
    ffh = ffp // 2
    partner = {"ctx": c + 1 - 2 * core}
    xs = [{"wsh": lax.rem(w + k, W)} for k in range(1, W)]
    zs = [{"ctx": lax.rem(z + k, nz) * 2 + core} for k in range(1, nz)]
    over = [{"section": 1 - s, "ctx": lax.rem(z + k, nz) * 2 + core} for k in range(nz)]
    greet(xs + zs + over + [partner])

    def rows_of(zz, cc):
        return pl.ds(pl.multiple_of((zz * 2 + cc) * TD, TD), TD)

    mine = rows_of(z, core)

    def token_push(m, k):
        return push(
            tokens.at[m, 0], xall.at[m, mine], b_send.at[m, k], b_recv.at[m, k], zs[k - 1]
        )

    def block_arrival(m, k):
        zz = lax.rem(z + nz - k, nz)
        return push(
            xall.at[m, mine],
            xall.at[m, rows_of(zz, core)],
            b_send.at[m, k],
            b_recv.at[m, k],
            over[0],
        )

    def forward_push(m, k):
        zz = lax.rem(z + nz - k, nz)
        block = xall.at[m, rows_of(zz, core)]
        return push(block, block, f_send.at[m, k], f_recv.at[m, k], partner)

    def out_push(m, k):
        return push(out.at[m], xall.at[m, mine], o_send.at[m, k], b_recv.at[m, k], over[k])

    def own_tokens(m):
        return pltpu.make_async_copy(tokens.at[m, 0], xall.at[m, mine], b_recv.at[m, 0])

    def pieces(cc, ww):
        r = pl.ds(pl.multiple_of(ww * part + cc * half, 16), half)
        f = pl.ds(pl.multiple_of(ww * ffp + cc * ffh, 16), ffh)
        return [attn.at[0:3, r], attn.at[3:4, r], up.at[r], down.at[f]]

    sr = pl.ds(pl.multiple_of(core * half, 16), half)
    sf = pl.ds(pl.multiple_of(core * ffh, 16), ffh)
    sources = [attn_w.at[0, 0:3, sr], attn_w.at[0, 3:4, sr], up_w.at[0, sr], down_w.at[0, sf]]

    def weight_push(k, p):
        return push(
            sources[p], pieces(core, w)[p], w_send.at[k - 1, p], w_recv.at[k - 1, p], xs[k - 1]
        )

    def weight_forward(k, p):
        spot = pieces(core, lax.rem(w + W - k, W))[p]
        return push(spot, spot, wf_send.at[k - 1, p], wf_recv.at[k - 1, p], partner)

    def small_push(k):
        return push(small_in, small_all.at[k], s_send.at[k - 1], s_recv.at[k - 1], xs[k - 1])

    own_r = pl.ds(pl.multiple_of(w * part, 16), part)
    own_f = pl.ds(pl.multiple_of(w * ffp, 16), ffp)
    own_loads = [
        pltpu.make_async_copy(attn_w.at[0, 0:3], attn.at[0:3, own_r], load_sem.at[0]),
        pltpu.make_async_copy(attn_w.at[0, 3:4], attn.at[3:4, own_r], load_sem.at[1]),
        pltpu.make_async_copy(up_w.at[0], up.at[own_r], load_sem.at[2]),
        pltpu.make_async_copy(down_w.at[0], down.at[own_f], load_sem.at[3]),
    ]

    @pl.when(s == 0)
    def _():
        own_tokens(0).start()
        for k in range(1, nz):
            token_push(0, k).start()

    for p in range(4):
        own_loads[p].start()
    for k in range(1, W):
        small_push(k).start()
    for p in range(4):
        for k in range(1, W):
            weight_push(k, p).start()

    @pl.when(s == 0)
    def _():
        for m in range(1, MB):
            own_tokens(m).start()
            for k in range(1, nz):
                token_push(m, k).start()

    def weights_ready(p):
        for k in range(1, W):
            weight_push(k, p).wait_recv()
            weight_forward(k, p).start()
        own_loads[p].wait()
        for k in range(1, W):
            weight_forward(k, p).wait_recv()

    def rows_ready(m):
        @pl.when(s == 0)
        def _():
            own_tokens(m).wait()

        @pl.when(s == 1)
        def _():
            block_arrival(m, 0).wait_recv()

        forward_push(m, 0).start()
        for k in range(1, nz):
            block_arrival(m, k).wait_recv()
            forward_push(m, k).start()
        for k in range(nz):
            forward_push(m, k).wait_recv()

    saves = []

    def save(src, dst):
        copy = pltpu.make_async_copy(src, dst, save_sem.at[next(numbers)])
        copy.start()
        saves.append(copy)

    numbers = iter(range(100))
    lane = lax.broadcasted_iota(jnp.int32, (TD, 128), 1)
    row = lax.broadcasted_iota(jnp.int32, (TD, 128), 0)
    spots = lax.broadcasted_iota(jnp.int32, (1, T), 1)
    tops = jnp.full((1, 128), masked_score, f32)

    slots = kv.shape[0]

    for m in range(MB):
        rows_ready(m)
        if m == 0:
            weights_ready(0)
            for k in range(1, W):
                small_push(k).wait_recv()
            total = small_in[...]
            for k in range(1, W):
                total = total + small_all[k]
            small[...] = total
            save(small, small_o)
        save(xall.at[m], xall_o.at[m])
        bias_v = small[0:1, :]

        def project(i, _):
            r = pl.ds(pl.multiple_of(i * 256, 256), 256)
            x = xall[m, r, :]
            kv[m % slots, r, 0:D] = dot(x, attn[1]).astype(bf16)
            kv[m % slots, r, D : 2 * D] = (dot(x, attn[2]) + bias_v).astype(bf16)
            return 0

        lax.fori_loop(0, T // 256, project, 0)
        save(kv.at[m % slots], kv_o.at[m])
        kept_kv = saves[-1]
        x_own = xall[m, mine, :]
        q[m] = (dot(x_own, attn[0]).astype(bf16).astype(f32) * (HD**-0.5)).astype(bf16)
        save(q.at[m], q_o.at[m])
        length = lens[m]
        live = spots < length
        weights = dot(counts[m].astype(bf16), block_lanes(T // BLK, T))
        weights = jnp.where(live, weights, 0.0)
        wide[...] = weights.reshape(PAIRS, 8, T)

        def attend(g, kept):
            lse_c, top_c = kept
            keys = kv[m % slots, :, pair_lanes(g)]
            values = kv[m % slots, :, pl.ds(pl.multiple_of(D + g * 128, 128), 128)]
            scores = dot_t(halves(q[m, :, pair_lanes(g)]), keys)
            count = spread4(wide[g], T)
            scores = jnp.where(count > 0, scores, masked_score)
            largest = jnp.max(scores, 1, keepdims=True)
            powers = jnp.exp(scores - largest) * count
            total = jnp.sum(powers, 1, keepdims=True)
            mixed = dot(powers.astype(bf16), values) / total
            mix[m, :, pair_lanes(g)] = joined(mixed)
            log_total = largest + jnp.log(total)
            for e in range(2):
                lse_c = jnp.where(lane == 2 * g + e, log_total[e * TD : (e + 1) * TD], lse_c)
                top_c = jnp.where(lane == 2 * g + e, largest[e * TD : (e + 1) * TD], top_c)
            return lse_c, top_c

        zeros = jnp.zeros((TD, 128), f32)
        lse_c, top_c = lax.fori_loop(0, PAIRS, attend, (zeros, zeros))
        lse[m] = lse_c
        if slots < MB:
            saves[:] = [x for x in saves if x is not kept_kv]
            kept_kv.wait()
        top_c = jnp.where(c * TD + row < length, top_c, masked_score)
        tops = jnp.maximum(tops, jnp.max(top_c, 0, keepdims=True))
        att[m] = mix[m].astype(bf16)
        save(lse.at[m], lse_o.at[m])
        save(mix.at[m], mix_o.at[m])
        save(att.at[m], att_o.at[m])

    top[...] = jnp.broadcast_to(tops, (8, 128))
    save(top, top_o)
    for p in range(1, 4):
        weights_ready(p)
    save(attn, attn_o)
    save(up, up_o)
    save(down, down_o)

    for m in range(MB):
        branch = dot(att[m], attn[3]) + small[1:2, :]
        first_sum = xall[m, mine, :].astype(f32) + branch
        first[m] = first_sum
        save(first.at[m], first_o.at[m])
        hat, _ = norm_parts(first_sum)
        normed = hat * small[5:6, :] + small[3:4, :]
        low = normed.astype(bf16)
        second[m] = normed + small[2:3, :]
        for j in range(NCH):
            cols = slice(j * CHUNK, (j + 1) * CHUNK)
            pre = dot(low, up[:, cols]) + small[7 + j : 8 + j, :]
            hidden[m, :, cols] = pre
            second[m] += dot(gelu(pre).astype(bf16), down[cols, :])
        save(hidden.at[m], hidden_o.at[m])
        save(second.at[m], second_o.at[m])
        hat, _ = norm_parts(second[m])
        out[m] = (hat * small[6:7, :] + small[4:5, :]).astype(bf16)

        @pl.when(s == 0)
        def _():
            for k in range(nz):
                out_push(m, k).start()

        save(out.at[m], out_o.at[0, m, 0])

    for k in range(1, W):
        small_push(k).wait_send()
        for p in range(4):
            weight_push(k, p).wait_send()
            weight_forward(k, p).wait_send()
    for m in range(MB):
        for k in range(nz):
            forward_push(m, k).wait_send()

        @pl.when(s == 0)
        def _():
            for k in range(1, nz):
                token_push(m, k).wait_send()
            for k in range(nz):
                out_push(m, k).wait_send()

    for copy in saves:
        copy.wait()


def backward_kernel(
    nz, W, MB, T,
    lens, cot, counts_q, counts_k, xall_h, kv_h, q_h, mix_h, lse_h, first_h, second_h, hidden_h, top,
    attn_h, up_h, down_h, small,
    grad_in_o, rows_qkv, rows_branch, rows_normed, rows_hidden, rows_gated, rows_down, small_o, top_o,
    attn, up, down, xall, kv, q, mix, lse, first, second, hidden, dout,
    gfirst, gbranch, gall, aux, kvp, wide_q, wide_k, lse_all, del_all, del_c, dqkv, gnorm, ghid, gated,
    gdown, small_g, gin, top_x,
    load_sem, y_send, y_recv, b_send, b_recv, f_send, f_recv, a_send, a_recv, af_send, af_recv,
    t_send, t_recv, kvp_sem, save_sem,
):
    s, c, w = place()
    z, core = c // 2, lax.rem(c, 2)
    partner = {"ctx": c + 1 - 2 * core}
    xs = [{"wsh": lax.rem(w + k, W)} for k in range(1, W)]
    zs = [{"ctx": lax.rem(z + k, nz) * 2 + core} for k in range(1, nz)]
    across = {"section": 1 - s}
    greet(xs + zs + [across, partner])

    def rows_of(zz, cc):
        return pl.ds(pl.multiple_of((zz * 2 + cc) * TD, TD), TD)

    mine = rows_of(z, core)
    loads = []

    def load(src, dst):
        copy = pltpu.make_async_copy(src, dst, load_sem.at[len(loads)])
        copy.start()
        loads.append(copy)
        return copy

    saves = []

    def save(src, dst):
        copy = pltpu.make_async_copy(src, dst, save_sem.at[next(numbers)])
        copy.start()
        saves.append(copy)

    numbers = iter(range(100))

    def cot_load(m):
        return pltpu.make_async_copy(cot.at[m, 0], dout.at[m], y_recv.at[m])

    def grad_push(m):
        return push(gin.at[m], dout.at[m], y_send.at[m], y_recv.at[m], across)

    @pl.when(s == 1)
    def _():
        for m in range(MB):
            cot_load(m).start()

    load_second = [load(second_h.at[m], second.at[m]) for m in range(MB)]
    load_down = load(down_h, down)
    slots = xall.shape[0]
    load_hidden = [load(hidden_h.at[m], hidden.at[m]) for m in range(slots)]
    load_up = load(up_h, up)
    load_first = [load(first_h.at[m], first.at[m]) for m in range(MB)]
    load_mix = [load(mix_h.at[m], mix.at[m]) for m in range(MB)]
    load_attn = load(attn_h, attn)
    load_lse = [load(lse_h.at[m], lse.at[m]) for m in range(MB)]
    load_x = [load(xall_h.at[m], xall.at[m]) for m in range(slots)]
    load_kv = [load(kv_h.at[m, mine], kv.at[m]) for m in range(MB)]
    load_q = [load(q_h.at[m], q.at[m]) for m in range(MB)]

    def rows_push(m, k):
        block = gall.at[m, mine]
        peer = partner if k == 0 else zs[k - 1]
        send, recv = (f_send, f_recv) if k == 0 else (b_send, b_recv)
        return push(block, block, send.at[m, k], recv.at[m, k], peer)

    def rows_arrival(m, k):
        block = gall.at[m, rows_of(lax.rem(z + nz - k, nz), core)]
        return push(block, block, b_send.at[m, k], b_recv.at[m, k], partner)

    def rows_forward(m, k):
        block = gall.at[m, rows_of(lax.rem(z + nz - k, nz), core)]
        return push(block, block, f_send.at[m, k], f_recv.at[m, k], partner)

    def aux_push(m, k):
        block = aux.at[m, c]
        peer = partner if k == 0 else zs[k - 1]
        send, recv = (af_send, af_recv) if k == 0 else (a_send, a_recv)
        return push(block, block, send.at[m, k], recv.at[m, k], peer)

    def aux_arrival(m, k):
        block = aux.at[m, lax.rem(z + nz - k, nz) * 2 + core]
        return push(block, block, a_send.at[m, k], a_recv.at[m, k], partner)

    def aux_forward(m, k):
        block = aux.at[m, lax.rem(z + nz - k, nz) * 2 + core]
        return push(block, block, af_send.at[m, k], af_recv.at[m, k], partner)

    def top_push(k):
        return push(top_x.at[0], top_x.at[k], t_send.at[k - 1], t_recv.at[k - 1], xs[k - 1])

    heads = lax.broadcasted_iota(jnp.int32, (D, 128), 0)
    heads = lax.shift_right_logical(heads, 6) == lax.broadcasted_iota(jnp.int32, (D, 128), 1)
    heads = jnp.where(heads, 1.0, 0.0).astype(f32)
    small_g[...] = jnp.zeros_like(small_g)

    for m in range(MB):
        load_second[m].wait()
        if m == 0:
            load_down.wait()

        @pl.when(s == 1)
        def _():
            cot_load(m).wait()

        @pl.when(s == 0)
        def _():
            grad_push(m).wait_recv()

        grad_out = dout[m].astype(f32)
        hat, rstd = norm_parts(second[m])
        small_g[1:2, :] += column_sum(grad_out * hat)
        small_g[6:7, :] += column_sum(grad_out)
        grad_second = norm_back(grad_out, hat, rstd, small[6:7, :])
        low_second = grad_second.astype(bf16)
        gdown[m] = low_second
        save(gdown.at[m], rows_down.at[m])
        small_g[4:5, :] += column_sum(low_second.astype(f32))
        if m >= slots:
            load_hidden.append(load(hidden_h.at[m], hidden.at[m % slots]))
            for copy in hidden_saves:
                saves[:] = [x for x in saves if x is not copy]
                copy.wait()
        load_hidden[m].wait()
        if m == 0:
            load_up.wait()
        gfirst[m] = grad_second
        for j in range(NCH):
            cols = slice(j * CHUNK, (j + 1) * CHUNK)
            value, slope = gelu_both(hidden[m % slots, :, cols])
            gated[m % slots, :, cols] = value.astype(bf16)
            grad_hidden = (slope * dot_t(low_second, down[cols, :])).astype(bf16)
            ghid[m % slots, :, cols] = grad_hidden
            small_g[7 + j : 8 + j, :] += column_sum(grad_hidden.astype(f32))
            gfirst[m] += dot_t(grad_hidden, up[:, cols])
        save(gated.at[m % slots], rows_gated.at[m])
        save(ghid.at[m % slots], rows_hidden.at[m])
        hidden_saves = saves[-2:]
        grad_normed = gfirst[m]
        load_first[m].wait()
        hat, rstd = norm_parts(first[m])
        gnorm[m] = (hat * small[5:6, :] + small[3:4, :]).astype(bf16)
        save(gnorm.at[m], rows_normed.at[m])
        small_g[0:1, :] += column_sum(grad_normed * hat)
        small_g[5:6, :] += column_sum(grad_normed)
        grad_first = norm_back(grad_normed, hat, rstd, small[5:6, :])
        gfirst[m] = grad_first
        low_first = grad_first.astype(bf16)
        gbranch[m] = low_first
        save(gbranch.at[m], rows_branch.at[m])
        small_g[3:4, :] += column_sum(low_first.astype(f32))
        load_mix[m].wait()
        load_lse[m].wait()
        if m == 0:
            load_attn.wait()
        grad_att = dot_t(low_first, attn[3]).astype(bf16)
        gall[m, mine, :] = grad_att
        for k in range(nz):
            rows_push(m, k).start()
        weighed = grad_att.astype(f32) * mix[m]
        delta = jnp.dot(weighed, heads, preferred_element_type=f32, precision=exact_dot)
        del_c[m] = delta
        aux[m, c, 0:16] = lse[m].T[0:16]
        aux[m, c, 16:32] = delta.T[0:16]
        aux[m, c, 32:40] = top[...]
        for k in range(nz):
            aux_push(m, k).start()

    spots = lax.broadcasted_iota(jnp.int32, (1, T), 1)
    rows_here = lax.broadcasted_iota(jnp.int32, (TD, 128), 0)
    for m in range(MB):
        if m >= slots:
            load_x.append(load(xall_h.at[m], xall.at[m % slots]))
        load_x[m].wait()
        load_kv[m].wait()
        load_q[m].wait()

        def stream(g):
            slot = lax.rem(g, 2)
            return [
                pltpu.make_async_copy(
                    kv_h.at[m, :, pl.ds(pl.multiple_of(e * D + g * 128, 128), 128)],
                    kvp.at[slot, e],
                    kvp_sem.at[slot, e],
                )
                for e in range(2)
            ]

        for copy in stream(0):
            copy.start()
        length = lens[m]
        lanes = block_lanes(T // BLK, T)
        counted = jnp.where(spots < length, dot(counts_q[m].astype(bf16), lanes), 0.0)
        counted = jnp.where(counted > 0, jnp.log(jnp.maximum(counted, 1.0)), masked_score)
        wide_q[...] = counted.reshape(PAIRS, 8, T)

        def own_rows(g, _):
            @pl.when(g + 1 < PAIRS)
            def _():
                for copy in stream(g + 1):
                    copy.start()

            for copy in stream(g):
                copy.wait()
            slot = lax.rem(g, 2)
            lse_c = jnp.concatenate([head_column(lse[m], 2 * g + e) for e in range(2)], 0)
            delta = jnp.concatenate([head_column(del_c[m], 2 * g + e) for e in range(2)], 0)
            queries = halves(q[m, :, pair_lanes(g)])
            grads = halves(gall[m, mine, pair_lanes(g)])
            grad_q = jnp.zeros((2 * TD, 2 * HD), f32)
            for t in range(0, T, STEP):
                keys = kvp[slot, 0, t : t + STEP]
                values = kvp[slot, 1, t : t + STEP]
                shift = wide_q[g, :, t : t + STEP]
                probs = jnp.exp(dot_t(queries, keys) + spread4(shift, STEP) - lse_c)
                grad_probs = dot_t(grads, values)
                grad_scores = (probs * (grad_probs - delta)).astype(bf16)
                grad_q = grad_q + dot(grad_scores, keys)
            dqkv[m, :, pair_lanes(g)] = (joined(grad_q) * (HD**-0.5)).astype(bf16)
            return 0

        lax.fori_loop(0, PAIRS, own_rows, 0)

        def project(i, _):
            r = pl.ds(pl.multiple_of(i * 256, 256), 256)
            rows = dot(xall[m % slots, r, :], attn[0]).astype(bf16).astype(f32)
            xall[m % slots, r, :] = (rows * (HD**-0.5)).astype(bf16)
            return 0

        lax.fori_loop(0, T // 256, project, 0)
        for k in range(1, nz):
            rows_arrival(m, k).wait_recv()
            rows_forward(m, k).start()
            aux_arrival(m, k).wait_recv()
            aux_forward(m, k).start()
        for k in range(nz):
            rows_forward(m, k).wait_recv()
            aux_forward(m, k).wait_recv()
        for cc in range(2 * nz):
            lse_all[:, cc * TD : (cc + 1) * TD] = aux[m, cc, 0:16]
            del_all[:, cc * TD : (cc + 1) * TD] = aux[m, cc, 16:32]
        if m == 0:
            most = aux[0, 0, 32:40]
            for cc in range(1, 2 * nz):
                most = jnp.maximum(most, aux[0, cc, 32:40])
            top_x[0] = most
            for k in range(1, W):
                top_push(k).start()
        counted = dot(counts_k[m].astype(bf16), lanes)
        counted = jnp.where(counted > 0, jnp.log(jnp.maximum(counted, 1.0)), masked_score)
        wide_k[...] = counted.reshape(PAIRS, 8, T)
        live = c * TD + rows_here < length

        def own_keys(g, _):
            keys = halves(kv[m, :, pair_lanes(g)])
            values = halves(kv[m, :, pl.ds(pl.multiple_of(D + g * 128, 128), 128)])
            lse_r = [lse_all[pl.ds(2 * g + e, 1), :] for e in range(2)]
            delta = [del_all[pl.ds(2 * g + e, 1), :] for e in range(2)]
            shift = wide_k[g]
            shift = jnp.concatenate([shift[0:2] - lse_r[0], shift[2:4] - lse_r[1]], 0)
            grad_k = jnp.zeros((2 * TD, 2 * HD), f32)
            grad_v = jnp.zeros((2 * TD, 2 * HD), f32)
            for t in range(0, T, STEP):
                queries = xall[m % slots, t : t + STEP, pair_lanes(g)]
                grads = gall[m, t : t + STEP, pair_lanes(g)]
                probs = jnp.exp(dot_t(keys, queries) + spread4(shift[:, t : t + STEP], STEP))
                grad_v = grad_v + dot(probs.astype(bf16), grads)
                centre = jnp.concatenate(
                    [jnp.broadcast_to(d[:, t : t + STEP], (TD, STEP)) for d in delta], 0
                )
                grad_scores = (probs * (dot_t(values, grads) - centre)).astype(bf16)
                grad_k = grad_k + dot(grad_scores, queries)
            grad_k, grad_v = joined(grad_k), joined(grad_v)
            lanes_k = pl.ds(pl.multiple_of(D + g * 128, 128), 128)
            lanes_v = pl.ds(pl.multiple_of(2 * D + g * 128, 128), 128)
            dqkv[m, :, lanes_k] = jnp.where(live, grad_k, 0.0).astype(bf16)
            dqkv[m, :, lanes_v] = jnp.where(live, grad_v, 0.0).astype(bf16)
            return 0

        lax.fori_loop(0, PAIRS, own_keys, 0)
        save(dqkv.at[m], rows_qkv.at[m])
        small_g[2:3, :] += column_sum(dqkv[m, :, 2 * D :].astype(f32))
        total = gfirst[m]
        for p in range(3):
            total = total + dot_t(dqkv[m, :, p * D : (p + 1) * D], attn[p])
        gin[m] = total.astype(bf16)

        @pl.when(s == 1)
        def _():
            grad_push(m).start()

        save(gin.at[m], grad_in_o.at[0, m, 0])

    save(small_g, small_o)
    for k in range(1, W):
        top_push(k).wait()
    most = top_x[0]
    for k in range(1, W):
        most = jnp.maximum(most, top_x[k])
    top_o[...] = most
    for m in range(MB):
        for k in range(nz):
            rows_forward(m, k).wait_send()
            aux_forward(m, k).wait_send()
        for k in range(1, nz):
            rows_push(m, k).wait_send()
            aux_push(m, k).wait_send()

        @pl.when(s == 1)
        def _():
            grad_push(m).wait_send()

    for copy in saves:
        copy.wait()


def counts_of(seq_lengths, rand_owner, rand_local, global_raw, c, n_ctx):
    blocks = BLK_DEV * n_ctx
    length = seq_lengths[:, 0]
    valid = (length + BLK - 1) // BLK
    chosen = global_raw[:, 0] % valid[:, None]
    random = rand_owner[:, 0] * BLK_DEV + rand_local[:, 0]
    ids = jnp.arange(blocks)
    near = (jnp.abs(ids[:, None] - ids[None, :]) <= 1).astype(jnp.int32)
    named = jnp.sum((random[..., None] == ids).astype(jnp.int32), 3)
    is_global = chosen[..., None] == ids
    glob = jnp.sum(is_global.astype(jnp.int32), 1)
    wide_row = jnp.any(is_global, 1)
    table = named + near[None, :, None, :] + glob[:, None, None, :]
    table = jnp.where(wide_row[:, :, None, None], 1, table).astype(f32)
    mb = table.shape[0]
    by_q = lax.dynamic_slice_in_dim(table, c * BLK_DEV, BLK_DEV, 1)
    by_k = lax.dynamic_slice_in_dim(table, c * BLK_DEV, BLK_DEV, 3)
    by_q = by_q.transpose(0, 2, 1, 3).reshape(mb, PAIRS, 4, blocks)
    by_k = by_k.transpose(0, 2, 3, 1).reshape(mb, PAIRS, 4, blocks)
    both = jnp.pad(jnp.stack([by_q, by_k]), ((0, 0), (0, 0), (0, 0), (0, 4), (0, 0)))
    both = both.reshape(2, mb, PAIRS * 8, blocks)
    return both[0], both[1]


VMEM = pl.BlockSpec(memory_space=pltpu.VMEM)
SMEM = pl.BlockSpec(memory_space=pltpu.SMEM)
ANY = pl.BlockSpec(memory_space=pl.ANY)
DMA = pltpu.SemaphoreType.DMA


def slots_of(T, MB):
    return MB if T <= 2048 else 1


def run_forward(nz, W, MB, lens, tokens, attn_w, up_w, down_w, small_in, counts):
    T = 2 * nz * TD
    shape = jax.ShapeDtypeStruct
    outs = [
        shape((1, MB, 1, TD, D), bf16),
        shape((MB, T, D), bf16),
        shape((MB, T, 2 * D), bf16),
        shape((MB, TD, D), bf16),
        shape((MB, TD, D), bf16),
        shape((MB, TD, D), f32),
        shape((MB, TD, 128), f32),
        shape((MB, TD, D), f32),
        shape((MB, TD, D), f32),
        shape((MB, TD, FF), f32),
        shape((8, 128), f32),
        shape((4, D, D), bf16),
        shape((D, FF), bf16),
        shape((FF, D), bf16),
        shape((16, D), f32),
    ]
    scratch = [
        pltpu.VMEM((4, D, D), bf16),
        pltpu.VMEM((D, FF), bf16),
        pltpu.VMEM((FF, D), bf16),
        pltpu.VMEM((W, 16, D), f32),
        pltpu.VMEM((16, D), f32),
        pltpu.VMEM((MB, T, D), bf16),
        pltpu.VMEM((slots_of(T, MB), T, 2 * D), bf16),
        pltpu.VMEM((MB, TD, D), bf16),
        pltpu.VMEM((MB, TD, D), bf16),
        pltpu.VMEM((MB, TD, D), f32),
        pltpu.VMEM((MB, TD, 128), f32),
        pltpu.VMEM((8, 128), f32),
        pltpu.VMEM((MB, TD, D), f32),
        pltpu.VMEM((MB, TD, D), f32),
        pltpu.VMEM((MB, TD, FF), f32),
        pltpu.VMEM((MB, TD, D), bf16),
        pltpu.VMEM((PAIRS, 8, T), f32),
        DMA((4,)),
        DMA((W - 1, 4)),
        DMA((W - 1, 4)),
        DMA((W - 1, 4)),
        DMA((W - 1, 4)),
        DMA((W - 1,)),
        DMA((W - 1,)),
        DMA((MB, nz)),
        DMA((MB, nz)),
        DMA((MB, nz)),
        DMA((MB, nz)),
        DMA((MB, nz)),
        DMA((5 + 10 * MB,)),
    ]
    return pl.pallas_call(
        functools.partial(forward_kernel, nz, W, MB, T),
        out_shape=outs,
        in_specs=[SMEM, ANY, ANY, ANY, ANY, VMEM, VMEM],
        out_specs=[ANY] * len(outs),
        scratch_shapes=scratch,
        compiler_params=pltpu.CompilerParams(
            collective_id=0, has_side_effects=True, vmem_limit_bytes=60 << 20
        ),
        name="forward",
    )(lens, tokens, attn_w, up_w, down_w, small_in, counts)


def run_backward(nz, W, MB, lens, cot, counts_q, counts_k, saved):
    T = 2 * nz * TD
    slots = slots_of(T, MB)
    shape = jax.ShapeDtypeStruct
    (xall, kv, q, mix, lse, first, second, hidden, top, attn, up, down, small) = saved
    outs = [
        shape((1, MB, 1, TD, D), bf16),
        shape((MB, TD, 3 * D), bf16),
        shape((MB, TD, D), bf16),
        shape((MB, TD, D), bf16),
        shape((MB, TD, FF), bf16),
        shape((MB, TD, FF), bf16),
        shape((MB, TD, D), bf16),
        shape((16, D), f32),
        shape((8, 128), f32),
    ]
    scratch = [
        pltpu.VMEM((4, D, D), bf16),
        pltpu.VMEM((D, FF), bf16),
        pltpu.VMEM((FF, D), bf16),
        pltpu.VMEM((slots, T, D), bf16),
        pltpu.VMEM((MB, TD, 2 * D), bf16),
        pltpu.VMEM((MB, TD, D), bf16),
        pltpu.VMEM((MB, TD, D), f32),
        pltpu.VMEM((MB, TD, 128), f32),
        pltpu.VMEM((MB, TD, D), f32),
        pltpu.VMEM((MB, TD, D), f32),
        pltpu.VMEM((slots, TD, FF), f32),
        pltpu.VMEM((MB, TD, D), bf16),
        pltpu.VMEM((MB, TD, D), f32),
        pltpu.VMEM((MB, TD, D), bf16),
        pltpu.VMEM((MB, T, D), bf16),
        pltpu.VMEM((MB, 2 * nz, 40, 128), f32),
        pltpu.VMEM((2, 2, T, 2 * HD), bf16),
        pltpu.VMEM((PAIRS, 8, T), f32),
        pltpu.VMEM((PAIRS, 8, T), f32),
        pltpu.VMEM((16, T), f32),
        pltpu.VMEM((16, T), f32),
        pltpu.VMEM((MB, TD, 128), f32),
        pltpu.VMEM((MB, TD, 3 * D), bf16),
        pltpu.VMEM((MB, TD, D), bf16),
        pltpu.VMEM((slots, TD, FF), bf16),
        pltpu.VMEM((slots, TD, FF), bf16),
        pltpu.VMEM((MB, TD, D), bf16),
        pltpu.VMEM((16, D), f32),
        pltpu.VMEM((MB, TD, D), bf16),
        pltpu.VMEM((W, 8, 128), f32),
        DMA((3 + 8 * MB,)),
        DMA((MB,)),
        DMA((MB,)),
        DMA((MB, nz)),
        DMA((MB, nz)),
        DMA((MB, nz)),
        DMA((MB, nz)),
        DMA((MB, nz)),
        DMA((MB, nz)),
        DMA((MB, nz)),
        DMA((MB, nz)),
        DMA((W - 1,)),
        DMA((W - 1,)),
        DMA((2, 2)),
        DMA((1 + 7 * MB,)),
    ]
    return pl.pallas_call(
        functools.partial(backward_kernel, nz, W, MB, T),
        out_shape=outs,
        in_specs=[SMEM, ANY, VMEM, VMEM] + [ANY] * 8 + [VMEM] + [ANY] * 3 + [VMEM],
        out_specs=[ANY] * 8 + [VMEM],
        scratch_shapes=scratch,
        compiler_params=pltpu.CompilerParams(
            collective_id=1, has_side_effects=True, vmem_limit_bytes=60 << 20
        ),
        name="backward",
    )(
        lens, cot, counts_q, counts_k, xall, kv, q, mix, lse, first, second, hidden, top,
        attn, up, down, small,
    )


def contract_rows(left_side, right_side):
    return lax.dot_general(
        left_side, right_side, (((0,), (0,)), ((), ())), preferred_element_type=f32
    )


def per_device(
    tokens, out_cotangent, attn_weights, up_weights, down_weights, norm_gains, bias_rows, up_bias,
    seq_lengths, rand_owner, rand_local, global_raw,
):
    n_ctx, W = lax.axis_size("ctx"), lax.axis_size("wsh")
    nz = n_ctx // 2
    c, w = lax.axis_index("ctx"), lax.axis_index("wsh")
    MB = tokens.shape[0]
    part, ffp = D // W, FF // W
    rows = jnp.concatenate([bias_rows[0], norm_gains[0]], 0).astype(f32)
    rows = lax.dynamic_update_slice(jnp.zeros((7, D), f32), rows, (0, w * part))
    wide = lax.dynamic_update_slice(jnp.zeros((FF,), f32), up_bias[0].astype(f32), (w * ffp,))
    small_in = jnp.concatenate([rows, wide.reshape(NCH, CHUNK), jnp.zeros((5, D), f32)], 0)
    counts_q, counts_k = counts_of(seq_lengths, rand_owner, rand_local, global_raw, c, n_ctx)
    lens = seq_lengths[:, 0]
    (
        out, xall, kv, q, att, mix, lse, first, second, hidden, top, attn, up, down, small,
    ) = run_forward(nz, W, MB, lens, tokens, attn_weights, up_weights, down_weights, small_in, counts_q)
    (
        grad_in, rows_qkv, rows_branch, rows_normed, rows_hidden, rows_gated, rows_down, small_g, tops,
    ) = run_backward(
        nz, W, MB, lens, out_cotangent, counts_q, counts_k,
        (xall, kv, q, mix, lse, first, second, hidden, top, attn, up, down, small),
    )
    head_tops = tops[0, :H]
    factor = jnp.sqrt(clip_limit / jnp.maximum(head_tops, clip_limit))
    clipped = (
        attn_weights[0, :2].astype(f32).reshape(2, -1, H, HD) * factor[None, None, :, None]
    )
    clipped_qk = clipped.reshape(1, 2, -1, D).astype(bf16)

    def flat(v):
        return v.reshape(-1, v.shape[-1])

    x_own = flat(lax.dynamic_slice_in_dim(xall, c * TD, TD, 1))
    qkv = flat(rows_qkv)
    grads = (
        jnp.stack(
            [contract_rows(x_own, qkv[:, p * D : (p + 1) * D]) for p in range(3)]
            + [contract_rows(flat(att), flat(rows_branch))]
        ),
        contract_rows(flat(rows_normed), flat(rows_hidden)),
        contract_rows(flat(rows_gated), flat(rows_down)),
    )
    dims = (1, 0, 0)
    shards = tuple(
        lax.psum_scatter(g.astype(bf16), "wsh", scatter_dimension=d, tiled=True)
        for g, d in zip(grads, dims)
    )
    total = tuple(lax.psum(g, "ctx").astype(f32) for g in shards)
    small_g = lax.psum(small_g, ("ctx", "wsh"))
    gains = lax.dynamic_slice(small_g[0:2], (0, w * part), (2, part))
    biases = lax.dynamic_slice(small_g[2:7], (0, w * part), (5, part))
    up_grad = lax.dynamic_slice(small_g[7:11].reshape(-1), (w * ffp,), (ffp,))
    return (
        out, grad_in, total[0][None], total[1][None], total[2][None], gains[None], biases[None],
        up_grad[None], clipped_qk,
    )


def solution(mesh):
    placed = (
        P(None, "wsh", "ctx", None),
        P(None, "wsh", "ctx", None),
        P("section", None, "wsh", None),
        P("section", "wsh", None),
        P("section", "wsh", None),
        P("section", None, "wsh"),
        P("section", None, "wsh"),
        P("section", "wsh"),
        P(None, "wsh"),
        P(None, "wsh", None, None, None),
        P(None, "wsh", None, None, None),
        P(None, "wsh", None),
    )
    return jax.shard_map(
        per_device,
        mesh=mesh,
        in_specs=placed,
        out_specs=(
            P("section", None, "wsh", "ctx", None),
            P("section", None, "wsh", "ctx", None),
            P("section", None, "wsh", None),
            P("section", "wsh", None),
            P("section", "wsh", None),
            P("section", None, "wsh"),
            P("section", None, "wsh"),
            P("section", "wsh"),
            P("section", None, "wsh", None),
        ),
        check_vma=False,
    )
```

```python
import functools

import jax
import jax.numpy as jnp
from jax import lax
from jax.experimental import pallas as pl
from jax.experimental.pallas import tpu as pltpu
from jax.sharding import PartitionSpec as P

D = 768
H = 12
HD = 64
FF = 3072
BLK = 64
TD = 128
BLK_DEV = 2
PAIRS = H // 2
CHUNK = 768
NCH = FF // CHUNK
STEP = 1024
ROWS = 48
FLIGHT = 4
LAG = 4

MESH = pl.DeviceIdType.MESH
norm_eps = 1e-05
clip_limit = 6.0
masked_score = -1e30
exact_dot = lax.Precision.HIGHEST
f32 = jnp.float32
bf16 = jnp.bfloat16


def dot(a, b):
    return jnp.dot(a, b, preferred_element_type=f32)


def dot_t(a, b):
    return lax.dot_general(a, b, (((1,), (1,)), ((), ())), preferred_element_type=f32)


def dot_0(a, b):
    return lax.dot_general(a, b, (((0,), (0,)), ((), ())), preferred_element_type=f32)


def column_sum(v):
    return jnp.sum(v, 0, keepdims=True)


def norm_parts(v):
    center = v - jnp.mean(v, -1, keepdims=True)
    rstd = lax.rsqrt(jnp.mean(center * center, -1, keepdims=True) + norm_eps)
    return center * rstd, rstd


def norm_back(grad, hat, rstd, gain):
    scaled = grad * gain
    return rstd * (
        scaled
        - jnp.mean(scaled, -1, keepdims=True)
        - hat * jnp.mean(scaled * hat, -1, keepdims=True)
    )


def gelu(v):
    return 0.5 * v * (1.0 + lax.erf(v * (0.5**0.5)))


def gelu_both(v):
    phi = 0.5 * (1.0 + lax.erf(v * (0.5**0.5)))
    return v * phi, phi + v * jnp.exp(-0.5 * v * v) * 0.3989422804014327


def place():
    return lax.axis_index("section"), lax.axis_index("ctx"), lax.axis_index("wsh")


def greet(peers):
    barrier = pltpu.get_barrier_semaphore()
    for peer in peers:
        pl.semaphore_signal(barrier, inc=1, device_id=peer, device_id_type=MESH)
    pl.semaphore_wait(barrier, len(peers))


def push(src, dst, send, recv, peer):
    return pltpu.make_async_remote_copy(
        src_ref=src, dst_ref=dst, send_sem=send, recv_sem=recv, device_id=peer, device_id_type=MESH
    )


def halves(rows):
    low = lax.broadcasted_iota(jnp.int32, rows.shape, 1) < HD
    zero = jnp.zeros_like(rows)
    return jnp.concatenate([jnp.where(low, rows, zero), jnp.where(low, zero, rows)], 0)


def joined(rows):
    low = lax.broadcasted_iota(jnp.int32, (TD, 2 * HD), 1) < HD
    return jnp.where(low, rows[:TD], rows[TD:])


def spread4(rows, width):
    return jnp.concatenate(
        [jnp.broadcast_to(rows[r : r + 1], (BLK, width)) for r in range(4)], 0
    )


def block_lanes(blocks, width):
    lane = lax.broadcasted_iota(jnp.int32, (blocks, width), 1)
    row = lax.broadcasted_iota(jnp.int32, (blocks, width), 0)
    return jnp.where(lax.shift_right_logical(lane, 6) == row, 1.0, 0.0).astype(bf16)


def head_column(columns, head):
    lane = lax.broadcasted_iota(jnp.int32, columns.shape, 1)
    return jnp.sum(jnp.where(lane == head, columns, 0.0), 1, keepdims=True)


def pair_lanes(g):
    return pl.ds(pl.multiple_of(g * (2 * HD), 2 * HD), 2 * HD)


def forward_kernel(
    nz, W, MB, T,
    lens, tokens, attn_w, up_w, down_w, small_in, counts,
    out_o, xall_o, kv_o, q_o, att_o, mix_o, lse_o, first_o, second_o, hidden_o, top_o,
    attn_o, up_o, down_o, small_o,
    attn, up, down, small_all, small, xall, kv, q, att, mix, lse, top, first, second, hidden, out,
    wide,
    load_sem, w_send, w_recv, wf_send, wf_recv, s_send, s_recv,
    b_send, b_recv, f_send, f_recv, o_send, save_sem,
):
    s, c, w = place()
    z, core = c // 2, lax.rem(c, 2)
    part = D // W
    half = part // 2
    ffp = FF // W
    ffh = ffp // 2
    partner = {"ctx": c + 1 - 2 * core}
    xs = [{"wsh": lax.rem(w + k, W)} for k in range(1, W)]
    zs = [{"ctx": lax.rem(z + k, nz) * 2 + core} for k in range(1, nz)]
    over = [{"section": 1 - s, "ctx": lax.rem(z + k, nz) * 2 + core} for k in range(nz)]
    greet(xs + zs + over + [partner])

    def rows_of(zz, cc):
        return pl.ds(pl.multiple_of((zz * 2 + cc) * TD, TD), TD)

    mine = rows_of(z, core)

    def token_push(m, k):
        return push(
            tokens.at[m, 0], xall.at[m, mine], b_send.at[m, k], b_recv.at[m, k], zs[k - 1]
        )

    def block_arrival(m, k):
        zz = lax.rem(z + nz - k, nz)
        return push(
            xall.at[m, mine],
            xall.at[m, rows_of(zz, core)],
            b_send.at[m, k],
            b_recv.at[m, k],
            over[0],
        )

    def forward_push(m, k):
        zz = lax.rem(z + nz - k, nz)
        block = xall.at[m, rows_of(zz, core)]
        return push(block, block, f_send.at[m, k], f_recv.at[m, k], partner)

    def out_push(m, k):
        return push(out.at[m], xall.at[m, mine], o_send.at[m, k], b_recv.at[m, k], over[k])

    def own_tokens(m):
        return pltpu.make_async_copy(tokens.at[m, 0], xall.at[m, mine], b_recv.at[m, 0])

    def pieces(cc, ww):
        r = pl.ds(pl.multiple_of(ww * part + cc * half, 16), half)
        f = pl.ds(pl.multiple_of(ww * ffp + cc * ffh, 16), ffh)
        return [attn.at[0:3, r], attn.at[3:4, r], up.at[r], down.at[f]]

    sr = pl.ds(pl.multiple_of(core * half, 16), half)
    sf = pl.ds(pl.multiple_of(core * ffh, 16), ffh)
    sources = [attn_w.at[0, 0:3, sr], attn_w.at[0, 3:4, sr], up_w.at[0, sr], down_w.at[0, sf]]

    def weight_push(k, p):
        return push(
            sources[p], pieces(core, w)[p], w_send.at[k - 1, p], w_recv.at[k - 1, p], xs[k - 1]
        )

    def weight_forward(k, p):
        spot = pieces(core, lax.rem(w + W - k, W))[p]
        return push(spot, spot, wf_send.at[k - 1, p], wf_recv.at[k - 1, p], partner)

    def small_push(k):
        return push(small_in, small_all.at[k], s_send.at[k - 1], s_recv.at[k - 1], xs[k - 1])

    own_r = pl.ds(pl.multiple_of(w * part, 16), part)
    own_f = pl.ds(pl.multiple_of(w * ffp, 16), ffp)
    own_loads = [
        pltpu.make_async_copy(attn_w.at[0, 0:3], attn.at[0:3, own_r], load_sem.at[0]),
        pltpu.make_async_copy(attn_w.at[0, 3:4], attn.at[3:4, own_r], load_sem.at[1]),
        pltpu.make_async_copy(up_w.at[0], up.at[own_r], load_sem.at[2]),
        pltpu.make_async_copy(down_w.at[0], down.at[own_f], load_sem.at[3]),
    ]

    @pl.when(s == 0)
    def _():
        own_tokens(0).start()
        for k in range(1, nz):
            token_push(0, k).start()

    for p in range(4):
        own_loads[p].start()
    for k in range(1, W):
        small_push(k).start()
    for p in range(4):
        for k in range(1, W):
            weight_push(k, p).start()

    @pl.when(s == 0)
    def _():
        for m in range(1, MB):
            own_tokens(m).start()
            for k in range(1, nz):
                token_push(m, k).start()

    def weights_ready(p):
        for k in range(1, W):
            weight_push(k, p).wait_recv()
            weight_forward(k, p).start()
        own_loads[p].wait()
        for k in range(1, W):
            weight_forward(k, p).wait_recv()

    def rows_ready(m):
        @pl.when(s == 0)
        def _():
            own_tokens(m).wait()

        @pl.when(s == 1)
        def _():
            block_arrival(m, 0).wait_recv()

        forward_push(m, 0).start()
        for k in range(1, nz):
            block_arrival(m, k).wait_recv()
            forward_push(m, k).start()
        for k in range(nz):
            forward_push(m, k).wait_recv()

    saves = []

    def save(src, dst):
        copy = pltpu.make_async_copy(src, dst, save_sem.at[next(numbers)])
        copy.start()
        saves.append(copy)

    numbers = iter(range(100))
    lane = lax.broadcasted_iota(jnp.int32, (TD, 128), 1)
    row = lax.broadcasted_iota(jnp.int32, (TD, 128), 0)
    spots = lax.broadcasted_iota(jnp.int32, (1, T), 1)
    tops = jnp.full((1, 128), masked_score, f32)

    slots = kv.shape[0]

    for m in range(MB):
        rows_ready(m)
        if m == 0:
            weights_ready(0)
            for k in range(1, W):
                small_push(k).wait_recv()
            total = small_in[...]
            for k in range(1, W):
                total = total + small_all[k]
            small[...] = total
            save(small, small_o)
        save(xall.at[m], xall_o.at[m])
        bias_v = small[0:1, :]

        def project(i, _):
            r = pl.ds(pl.multiple_of(i * 256, 256), 256)
            x = xall[m, r, :]
            kv[m % slots, r, 0:D] = dot(x, attn[1]).astype(bf16)
            kv[m % slots, r, D : 2 * D] = (dot(x, attn[2]) + bias_v).astype(bf16)
            return 0

        lax.fori_loop(0, T // 256, project, 0)
        save(kv.at[m % slots], kv_o.at[m])
        kept_kv = saves[-1]
        x_own = xall[m, mine, :]
        q[m] = (dot(x_own, attn[0]).astype(bf16).astype(f32) * (HD**-0.5)).astype(bf16)
        save(q.at[m], q_o.at[m])
        length = lens[m]
        live = spots < length
        weights = dot(counts[m].astype(bf16), block_lanes(T // BLK, T))
        weights = jnp.where(live, weights, 0.0)
        wide[...] = weights.reshape(PAIRS, 8, T)

        def attend(g, kept):
            lse_c, top_c = kept
            keys = kv[m % slots, :, pair_lanes(g)]
            values = kv[m % slots, :, pl.ds(pl.multiple_of(D + g * 128, 128), 128)]
            scores = dot_t(halves(q[m, :, pair_lanes(g)]), keys)
            count = spread4(wide[g], T)
            scores = jnp.where(count > 0, scores, masked_score)
            largest = jnp.max(scores, 1, keepdims=True)
            powers = jnp.exp(scores - largest) * count
            total = jnp.sum(powers, 1, keepdims=True)
            mixed = dot(powers.astype(bf16), values) / total
            mix[m, :, pair_lanes(g)] = joined(mixed)
            log_total = largest + jnp.log(total)
            for e in range(2):
                lse_c = jnp.where(lane == 2 * g + e, log_total[e * TD : (e + 1) * TD], lse_c)
                top_c = jnp.where(lane == 2 * g + e, largest[e * TD : (e + 1) * TD], top_c)
            return lse_c, top_c

        zeros = jnp.zeros((TD, 128), f32)
        lse_c, top_c = lax.fori_loop(0, PAIRS, attend, (zeros, zeros))
        lse[m] = lse_c
        if slots < MB:
            saves[:] = [x for x in saves if x is not kept_kv]
            kept_kv.wait()
        top_c = jnp.where(c * TD + row < length, top_c, masked_score)
        tops = jnp.maximum(tops, jnp.max(top_c, 0, keepdims=True))
        att[m] = mix[m].astype(bf16)
        save(lse.at[m], lse_o.at[m])
        save(mix.at[m], mix_o.at[m])
        save(att.at[m], att_o.at[m])

    top[...] = jnp.broadcast_to(tops, (8, 128))
    save(top, top_o)
    for p in range(1, 4):
        weights_ready(p)
    save(attn, attn_o)
    save(up, up_o)
    save(down, down_o)

    for m in range(MB):
        branch = dot(att[m], attn[3]) + small[1:2, :]
        first_sum = xall[m, mine, :].astype(f32) + branch
        first[m] = first_sum
        save(first.at[m], first_o.at[m])
        hat, _ = norm_parts(first_sum)
        normed = hat * small[5:6, :] + small[3:4, :]
        low = normed.astype(bf16)
        second[m] = normed + small[2:3, :]
        for j in range(NCH):
            cols = slice(j * CHUNK, (j + 1) * CHUNK)
            pre = dot(low, up[:, cols]) + small[7 + j : 8 + j, :]
            hidden[m, :, cols] = pre
            second[m] += dot(gelu(pre).astype(bf16), down[cols, :])
        save(hidden.at[m], hidden_o.at[m])
        save(second.at[m], second_o.at[m])
        hat, _ = norm_parts(second[m])
        out[m] = (hat * small[6:7, :] + small[4:5, :]).astype(bf16)

        @pl.when(s == 0)
        def _():
            for k in range(nz):
                out_push(m, k).start()

        save(out.at[m], out_o.at[0, m, 0])

    for k in range(1, W):
        small_push(k).wait_send()
        for p in range(4):
            weight_push(k, p).wait_send()
            weight_forward(k, p).wait_send()
    for m in range(MB):
        for k in range(nz):
            forward_push(m, k).wait_send()

        @pl.when(s == 0)
        def _():
            for k in range(1, nz):
                token_push(m, k).wait_send()
            for k in range(nz):
                out_push(m, k).wait_send()

    for copy in saves:
        copy.wait()


def backward_kernel(
    nz, W, MB, T,
    lens, cot, counts_q, counts_k, xall_h, kv_h, q_h, mix_h, lse_h, first_h, second_h, hidden_h, top,
    attn_h, up_h, down_h, small,
    grad_in_o, rows_qkv, rows_branch, rows_normed, rows_hidden, rows_gated, rows_down, small_o, top_o,
    attn, up, down, xall, kv, q, mix, lse, first, second, hidden, dout,
    gfirst, gbranch, gall, aux, kvp, wide_q, wide_k, lse_all, del_all, del_c, dqkv, gnorm, ghid, gated,
    gdown, small_g, gin, top_x,
    load_sem, y_send, y_recv, b_send, b_recv, f_send, f_recv, a_send, a_recv, af_send, af_recv,
    t_send, t_recv, kvp_sem, save_sem,
):
    s, c, w = place()
    z, core = c // 2, lax.rem(c, 2)
    partner = {"ctx": c + 1 - 2 * core}
    xs = [{"wsh": lax.rem(w + k, W)} for k in range(1, W)]
    zs = [{"ctx": lax.rem(z + k, nz) * 2 + core} for k in range(1, nz)]
    across = {"section": 1 - s}
    greet(xs + zs + [across, partner])

    def rows_of(zz, cc):
        return pl.ds(pl.multiple_of((zz * 2 + cc) * TD, TD), TD)

    mine = rows_of(z, core)
    loads = []

    def load(src, dst):
        copy = pltpu.make_async_copy(src, dst, load_sem.at[len(loads)])
        copy.start()
        loads.append(copy)
        return copy

    saves = []

    def save(src, dst):
        copy = pltpu.make_async_copy(src, dst, save_sem.at[next(numbers)])
        copy.start()
        saves.append(copy)

    numbers = iter(range(100))

    def cot_load(m):
        return pltpu.make_async_copy(cot.at[m, 0], dout.at[m], y_recv.at[m])

    def grad_push(m):
        return push(gin.at[m], dout.at[m], y_send.at[m], y_recv.at[m], across)

    @pl.when(s == 1)
    def _():
        for m in range(MB):
            cot_load(m).start()

    load_second = [load(second_h.at[m], second.at[m]) for m in range(MB)]
    load_down = load(down_h, down)
    slots = xall.shape[0]
    load_hidden = [load(hidden_h.at[m], hidden.at[m]) for m in range(slots)]
    load_up = load(up_h, up)
    load_first = [load(first_h.at[m], first.at[m]) for m in range(MB)]
    load_mix = [load(mix_h.at[m], mix.at[m]) for m in range(MB)]
    load_attn = load(attn_h, attn)
    load_lse = [load(lse_h.at[m], lse.at[m]) for m in range(MB)]
    load_x = [load(xall_h.at[m], xall.at[m]) for m in range(slots)]
    load_kv = [load(kv_h.at[m, mine], kv.at[m]) for m in range(MB)]
    load_q = [load(q_h.at[m], q.at[m]) for m in range(MB)]

    def rows_push(m, k):
        block = gall.at[m, mine]
        peer = partner if k == 0 else zs[k - 1]
        send, recv = (f_send, f_recv) if k == 0 else (b_send, b_recv)
        return push(block, block, send.at[m, k], recv.at[m, k], peer)

    def rows_arrival(m, k):
        block = gall.at[m, rows_of(lax.rem(z + nz - k, nz), core)]
        return push(block, block, b_send.at[m, k], b_recv.at[m, k], partner)

    def rows_forward(m, k):
        block = gall.at[m, rows_of(lax.rem(z + nz - k, nz), core)]
        return push(block, block, f_send.at[m, k], f_recv.at[m, k], partner)

    def aux_push(m, k):
        block = aux.at[m, c]
        peer = partner if k == 0 else zs[k - 1]
        send, recv = (af_send, af_recv) if k == 0 else (a_send, a_recv)
        return push(block, block, send.at[m, k], recv.at[m, k], peer)

    def aux_arrival(m, k):
        block = aux.at[m, lax.rem(z + nz - k, nz) * 2 + core]
        return push(block, block, a_send.at[m, k], a_recv.at[m, k], partner)

    def aux_forward(m, k):
        block = aux.at[m, lax.rem(z + nz - k, nz) * 2 + core]
        return push(block, block, af_send.at[m, k], af_recv.at[m, k], partner)

    def top_push(k):
        return push(top_x.at[0], top_x.at[k], t_send.at[k - 1], t_recv.at[k - 1], xs[k - 1])

    heads = lax.broadcasted_iota(jnp.int32, (D, 128), 0)
    heads = lax.shift_right_logical(heads, 6) == lax.broadcasted_iota(jnp.int32, (D, 128), 1)
    heads = jnp.where(heads, 1.0, 0.0).astype(f32)
    small_g[...] = jnp.zeros_like(small_g)

    for m in range(MB):
        load_second[m].wait()
        if m == 0:
            load_down.wait()

        @pl.when(s == 1)
        def _():
            cot_load(m).wait()

        @pl.when(s == 0)
        def _():
            grad_push(m).wait_recv()

        grad_out = dout[m].astype(f32)
        hat, rstd = norm_parts(second[m])
        small_g[1:2, :] += column_sum(grad_out * hat)
        small_g[6:7, :] += column_sum(grad_out)
        grad_second = norm_back(grad_out, hat, rstd, small[6:7, :])
        low_second = grad_second.astype(bf16)
        gdown[m] = low_second
        save(gdown.at[m], rows_down.at[m])
        small_g[4:5, :] += column_sum(low_second.astype(f32))
        if m >= slots:
            load_hidden.append(load(hidden_h.at[m], hidden.at[m % slots]))
            for copy in hidden_saves:
                saves[:] = [x for x in saves if x is not copy]
                copy.wait()
        load_hidden[m].wait()
        if m == 0:
            load_up.wait()
        gfirst[m] = grad_second
        for j in range(NCH):
            cols = slice(j * CHUNK, (j + 1) * CHUNK)
            value, slope = gelu_both(hidden[m % slots, :, cols])
            gated[m % slots, :, cols] = value.astype(bf16)
            grad_hidden = (slope * dot_t(low_second, down[cols, :])).astype(bf16)
            ghid[m % slots, :, cols] = grad_hidden
            small_g[7 + j : 8 + j, :] += column_sum(grad_hidden.astype(f32))
            gfirst[m] += dot_t(grad_hidden, up[:, cols])
        save(gated.at[m % slots], rows_gated.at[m])
        save(ghid.at[m % slots], rows_hidden.at[m])
        hidden_saves = saves[-2:]
        grad_normed = gfirst[m]
        load_first[m].wait()
        hat, rstd = norm_parts(first[m])
        gnorm[m] = (hat * small[5:6, :] + small[3:4, :]).astype(bf16)
        save(gnorm.at[m], rows_normed.at[m])
        small_g[0:1, :] += column_sum(grad_normed * hat)
        small_g[5:6, :] += column_sum(grad_normed)
        grad_first = norm_back(grad_normed, hat, rstd, small[5:6, :])
        gfirst[m] = grad_first
        low_first = grad_first.astype(bf16)
        gbranch[m] = low_first
        save(gbranch.at[m], rows_branch.at[m])
        small_g[3:4, :] += column_sum(low_first.astype(f32))
        load_mix[m].wait()
        load_lse[m].wait()
        if m == 0:
            load_attn.wait()
        grad_att = dot_t(low_first, attn[3]).astype(bf16)
        gall[m, mine, :] = grad_att
        for k in range(nz):
            rows_push(m, k).start()
        weighed = grad_att.astype(f32) * mix[m]
        delta = jnp.dot(weighed, heads, preferred_element_type=f32, precision=exact_dot)
        del_c[m] = delta
        aux[m, c, 0:16] = lse[m].T[0:16]
        aux[m, c, 16:32] = delta.T[0:16]
        aux[m, c, 32:40] = top[...]
        for k in range(nz):
            aux_push(m, k).start()

    spots = lax.broadcasted_iota(jnp.int32, (1, T), 1)
    rows_here = lax.broadcasted_iota(jnp.int32, (TD, 128), 0)
    for m in range(MB):
        if m >= slots:
            load_x.append(load(xall_h.at[m], xall.at[m % slots]))
        load_x[m].wait()
        load_kv[m].wait()
        load_q[m].wait()

        def stream(g):
            slot = lax.rem(g, 2)
            return [
                pltpu.make_async_copy(
                    kv_h.at[m, :, pl.ds(pl.multiple_of(e * D + g * 128, 128), 128)],
                    kvp.at[slot, e],
                    kvp_sem.at[slot, e],
                )
                for e in range(2)
            ]

        for copy in stream(0):
            copy.start()
        length = lens[m]
        lanes = block_lanes(T // BLK, T)
        counted = jnp.where(spots < length, dot(counts_q[m].astype(bf16), lanes), 0.0)
        counted = jnp.where(counted > 0, jnp.log(jnp.maximum(counted, 1.0)), masked_score)
        wide_q[...] = counted.reshape(PAIRS, 8, T)

        def own_rows(g, _):
            @pl.when(g + 1 < PAIRS)
            def _():
                for copy in stream(g + 1):
                    copy.start()

            for copy in stream(g):
                copy.wait()
            slot = lax.rem(g, 2)
            lse_c = jnp.concatenate([head_column(lse[m], 2 * g + e) for e in range(2)], 0)
            delta = jnp.concatenate([head_column(del_c[m], 2 * g + e) for e in range(2)], 0)
            queries = halves(q[m, :, pair_lanes(g)])
            grads = halves(gall[m, mine, pair_lanes(g)])
            grad_q = jnp.zeros((2 * TD, 2 * HD), f32)
            for t in range(0, T, STEP):
                keys = kvp[slot, 0, t : t + STEP]
                values = kvp[slot, 1, t : t + STEP]
                shift = wide_q[g, :, t : t + STEP]
                probs = jnp.exp(dot_t(queries, keys) + spread4(shift, STEP) - lse_c)
                grad_probs = dot_t(grads, values)
                grad_scores = (probs * (grad_probs - delta)).astype(bf16)
                grad_q = grad_q + dot(grad_scores, keys)
            dqkv[m, :, pair_lanes(g)] = (joined(grad_q) * (HD**-0.5)).astype(bf16)
            return 0

        lax.fori_loop(0, PAIRS, own_rows, 0)

        def project(i, _):
            r = pl.ds(pl.multiple_of(i * 256, 256), 256)
            rows = dot(xall[m % slots, r, :], attn[0]).astype(bf16).astype(f32)
            xall[m % slots, r, :] = (rows * (HD**-0.5)).astype(bf16)
            return 0

        lax.fori_loop(0, T // 256, project, 0)
        for k in range(1, nz):
            rows_arrival(m, k).wait_recv()
            rows_forward(m, k).start()
            aux_arrival(m, k).wait_recv()
            aux_forward(m, k).start()
        for k in range(nz):
            rows_forward(m, k).wait_recv()
            aux_forward(m, k).wait_recv()
        for cc in range(2 * nz):
            lse_all[:, cc * TD : (cc + 1) * TD] = aux[m, cc, 0:16]
            del_all[:, cc * TD : (cc + 1) * TD] = aux[m, cc, 16:32]
        if m == 0:
            most = aux[0, 0, 32:40]
            for cc in range(1, 2 * nz):
                most = jnp.maximum(most, aux[0, cc, 32:40])
            top_x[0] = most
            for k in range(1, W):
                top_push(k).start()
        counted = dot(counts_k[m].astype(bf16), lanes)
        counted = jnp.where(counted > 0, jnp.log(jnp.maximum(counted, 1.0)), masked_score)
        wide_k[...] = counted.reshape(PAIRS, 8, T)
        live = c * TD + rows_here < length

        def own_keys(g, _):
            keys = halves(kv[m, :, pair_lanes(g)])
            values = halves(kv[m, :, pl.ds(pl.multiple_of(D + g * 128, 128), 128)])
            lse_r = [lse_all[pl.ds(2 * g + e, 1), :] for e in range(2)]
            delta = [del_all[pl.ds(2 * g + e, 1), :] for e in range(2)]
            shift = wide_k[g]
            shift = jnp.concatenate([shift[0:2] - lse_r[0], shift[2:4] - lse_r[1]], 0)
            grad_k = jnp.zeros((2 * TD, 2 * HD), f32)
            grad_v = jnp.zeros((2 * TD, 2 * HD), f32)
            for t in range(0, T, STEP):
                queries = xall[m % slots, t : t + STEP, pair_lanes(g)]
                grads = gall[m, t : t + STEP, pair_lanes(g)]
                probs = jnp.exp(dot_t(keys, queries) + spread4(shift[:, t : t + STEP], STEP))
                grad_v = grad_v + dot(probs.astype(bf16), grads)
                centre = jnp.concatenate(
                    [jnp.broadcast_to(d[:, t : t + STEP], (TD, STEP)) for d in delta], 0
                )
                grad_scores = (probs * (dot_t(values, grads) - centre)).astype(bf16)
                grad_k = grad_k + dot(grad_scores, queries)
            grad_k, grad_v = joined(grad_k), joined(grad_v)
            lanes_k = pl.ds(pl.multiple_of(D + g * 128, 128), 128)
            lanes_v = pl.ds(pl.multiple_of(2 * D + g * 128, 128), 128)
            dqkv[m, :, lanes_k] = jnp.where(live, grad_k, 0.0).astype(bf16)
            dqkv[m, :, lanes_v] = jnp.where(live, grad_v, 0.0).astype(bf16)
            return 0

        lax.fori_loop(0, PAIRS, own_keys, 0)
        save(dqkv.at[m], rows_qkv.at[m])
        small_g[2:3, :] += column_sum(dqkv[m, :, 2 * D :].astype(f32))
        total = gfirst[m]
        for p in range(3):
            total = total + dot_t(dqkv[m, :, p * D : (p + 1) * D], attn[p])
        gin[m] = total.astype(bf16)

        @pl.when(s == 1)
        def _():
            grad_push(m).start()

        save(gin.at[m], grad_in_o.at[0, m, 0])

    save(small_g, small_o)
    for k in range(1, W):
        top_push(k).wait()
    most = top_x[0]
    for k in range(1, W):
        most = jnp.maximum(most, top_x[k])
    top_o[...] = most
    for m in range(MB):
        for k in range(nz):
            rows_forward(m, k).wait_send()
            aux_forward(m, k).wait_send()
        for k in range(1, nz):
            rows_push(m, k).wait_send()
            aux_push(m, k).wait_send()

        @pl.when(s == 1)
        def _():
            grad_push(m).wait_send()

    for copy in saves:
        copy.wait()


def reduce_kernel(
    nz, W, MB,
    gated_h, down_h, normed_h, hidden_h, x_h, qkv_h, att_h, branch_h, small_g, tops, attn_w,
    attn_o, up_o, down_o, small_o, clip_o,
    lg, rd, ln, rh, la, ra, lb, rb, grads, from_x, chain, totals, theirs, own_w, core_s, wsh_s, z_s,
    load_sem, c_send, c_recv, x_send, x_recv, ch_send, ch_recv, b_send, b_recv, p_send, p_recv,
    o_sem, s_send, s_recv, sx_send, sx_recv, sz_send, sz_recv,
):
    s, c, w = place()
    z, core = c // 2, lax.rem(c, 2)
    part, ffp = D // W, FF // W
    R = MB * TD
    per = part // ROWS
    count = 6 * per
    root = (nz - 1) // 2
    partner = {"ctx": c + 1 - 2 * core}
    xs = [{"wsh": lax.rem(w + k, W)} for k in range(1, W)]
    zs = [{"ctx": lax.rem(z + k, nz) * 2 + core} for k in range(1, nz)]
    greet(xs + zs + [partner])

    def operands(cc):
        gate = [
            (
                gated_h.at[:, pl.ds(pl.multiple_of(e * ffp + cc * (ffp // 2), 128), ffp // 2)],
                lg,
                e * (ffp // 2),
                ffp // 2,
            )
            for e in range(W)
        ]
        hid = hidden_h.at[:, pl.ds(pl.multiple_of(cc * (FF // 2), 128), FF // 2)]
        return gate + [(down_h, rd, 0, D), (normed_h, ln, 0, D), (hid, rh, 0, FF // 2)]

    def rows_of_x(buffer):
        mine = pl.ds(pl.multiple_of(c * TD, TD), TD)
        return [(x_h.at[m, mine], buffer, m) for m in range(MB)]

    def heads_operands(cc):
        if cc == 0:
            return [(qkv_h.at[:, 0:D], ra), (qkv_h.at[:, D : 2 * D], rb)]
        return [(qkv_h.at[:, 2 * D : 3 * D], ra), (att_h, lb), (branch_h, rb)]

    first = operands(core)
    second = operands(1 - core)
    n1 = len(first)
    base = [0, R]

    def local(n, src, dst):
        return pltpu.make_async_copy(src, dst, load_sem.at[n])

    def to_core(n, src, dst):
        return push(src, dst, c_send.at[n], c_recv.at[n], partner)

    def window(dst, at, width, side):
        return dst.at[side * R : side * R + R, at : at + width]

    fast = [local(n, a, window(b, at, wd, 0)) for n, (a, b, at, wd) in enumerate(first)]
    fast_x = [to_core(n, a, window(b, at, wd, 1)) for n, (a, b, at, wd) in enumerate(second)]
    for one, two in zip(fast, fast_x):
        two.start()
        one.start()

    def attn_copies(cc, make, side):
        found = []
        for n, (a, b) in enumerate(heads_operands(cc)):
            found.append(make(n1 + n, a, b.at[side * R : side * R + R]))
        n = n1 + 3
        for buffer in (la, lb) if cc == 0 else (la,):
            for a, b, m in rows_of_x(buffer):
                lo = side * R + m * TD
                found.append(make(n, a, b.at[lo : lo + TD]))
                n += 1
        return found

    for cc in range(2):

        @pl.when(core == cc)
        def _():
            for copy in attn_copies(1 - cc, to_core, 1) + attn_copies(cc, local, 0):
                copy.start()

    small_push = push(small_g, core_s.at[core], s_send, s_recv, partner)
    small_push.start()
    core_s[core] = small_g[...]
    weights_in = local(n1 + 3 + 2 * MB, attn_w.at[0, 0:2], own_w)
    weights_in.start()

    def spot(i, ww):
        at = (i // per) * D + ww * part + lax.rem(i, per) * ROWS
        return pl.ds(pl.multiple_of(at, 16), ROWS)

    def lines(i):
        return pl.ds(pl.multiple_of(i * ROWS, 16), ROWS)

    def x_push(i, k):
        return push(
            grads.at[spot(i, lax.rem(w + k, W))],
            from_x.at[k - 1, lines(i)],
            x_send.at[k - 1, i],
            x_recv.at[k - 1, i],
            xs[k - 1],
        )

    for n in range(W + 1):
        fast[n].wait()
        fast_x[n].wait_recv()
    gate_half = ffp // 2
    for e in range(W):
        block = dot_0(lg[:, e * gate_half : (e + 1) * gate_half], rd[...]).astype(bf16)
        for j in range(2):
            grads[j * D + e * part : j * D + (e + 1) * part] = block[j * part : (j + 1) * part]
    for i in range(FLIGHT):
        for k in range(1, W):
            x_push(i, k).start()
    for n in range(W + 1, n1):
        fast[n].wait()
        fast_x[n].wait_recv()
    for j in range(2):
        block = dot_0(ln[...], rh[:, j * D : (j + 1) * D])
        grads[(2 + j) * D : (3 + j) * D] = block.astype(bf16)
    for cc in range(2):

        @pl.when(core == cc)
        def _():
            for copy in attn_copies(cc, local, 0):
                copy.wait()
            for copy in attn_copies(cc, to_core, 1):
                copy.wait_recv()

    for j, (left, right) in enumerate(((la, ra), (lb, rb))):
        grads[(4 + j) * D : (5 + j) * D] = dot_0(left[...], right[...]).astype(bf16)

    small_push.wait_recv()
    pair = core_s[0] + core_s[1]
    wsh_s[w] = pair
    small_x = [push(wsh_s.at[w], wsh_s.at[w], sx_send.at[k - 1], sx_recv.at[k - 1], xs[k - 1]) for k in range(1, W)]
    for copy in small_x:
        copy.start()
    weights_in.wait()
    factor = jnp.sqrt(clip_limit / jnp.maximum(tops[...], clip_limit))
    lane = lax.broadcasted_iota(jnp.int32, (128, D), 1)
    head = lax.broadcasted_iota(jnp.int32, (128, D), 0)
    heads = jnp.where(lax.shift_right_logical(lane, 6) == head, 1.0, 0.0).astype(f32)
    wide = jnp.dot(factor, heads, preferred_element_type=f32, precision=exact_dot)[0:1]
    for p in range(2):
        clip_o[0, p] = (own_w[p].astype(f32) * wide).astype(bf16)
    for k in range(1, W):
        e = lax.rem(w + W - k, W)
        push(wsh_s.at[w], wsh_s.at[e], sx_send.at[k - 1], sx_recv.at[k - 1], xs[k - 1]).wait_recv()
    total = wsh_s[0]
    for e in range(1, W):
        total = total + wsh_s[e]
    z_s[z] = total
    small_z = [push(z_s.at[z], z_s.at[z], sz_send.at[k - 1], sz_recv.at[k - 1], zs[k - 1]) for k in range(1, nz)]
    for copy in small_z:
        copy.start()

    is_left = z < root
    to_left = {"ctx": jnp.maximum(z - 1, 0) * 2 + core}
    to_right = {"ctx": jnp.minimum(z + 1, nz - 1) * 2 + core}
    far = max(root, nz - 1 - root)
    depth = jnp.where(z == root, far, jnp.where(is_left, z, nz - 1 - z))
    away = jnp.where(is_left, root - z, z - root)

    def chain_push(i, side, peer):
        block = grads.at[spot(i, w)]
        return push(block, chain.at[side, lines(i)], ch_send.at[i], ch_recv.at[side, i], peer)

    def total_push(i, side, peer):
        block = totals.at[lines(i)]
        return push(block, block, b_send.at[side, i], b_recv.at[i], peer)

    def partner_push(i):
        return push(totals.at[lines(i)], theirs.at[lines(i)], p_send.at[i], p_recv.at[i], partner)

    def deliver(i, cc, source, side, go):
        j, r = i // per, lax.rem(i, per)
        places = [
            (j < 2, lambda: down_o.at[pl.ds(pl.multiple_of(cc * gate_half + i * ROWS, 16), ROWS)]),
            (
                (j >= 2) & (j < 4),
                lambda: up_o.at[
                    pl.ds(pl.multiple_of(r * ROWS, 16), ROWS),
                    pl.ds(pl.multiple_of((cc * 2 + j - 2) * D, 128), D),
                ],
            ),
            (
                j >= 4,
                lambda: attn_o.at[cc * 2 + j - 4, pl.ds(pl.multiple_of(r * ROWS, 16), ROWS)],
            ),
        ]
        for when, spot_of in places:

            @pl.when(when)
            def _():
                go(pltpu.make_async_copy(source.at[lines(i)], spot_of(), o_sem.at[side, i]))

    def start(copy):
        copy.start()

    def finish(copy):
        copy.wait()

    def step(t, _):
        @pl.when(t + FLIGHT < count)
        def _():
            for k in range(1, W):
                x_push(t, k).wait_send()
                x_push(t + FLIGHT, k).start()

        i = t - LAG * depth

        @pl.when((i >= 0) & (i < count))
        def _():
            acc = grads[spot(i, w), :].astype(f32)
            for k in range(1, W):
                x_push(i, k).wait_recv()
                acc = acc + from_x[k - 1, lines(i), :].astype(f32)
            grads[spot(i, w), :] = acc.astype(bf16)

            @pl.when((z > 0) & (z <= root))
            def _():
                chain_push(i, 0, to_right).wait_recv()
                both = grads[spot(i, w), :].astype(f32) + chain[0, lines(i), :].astype(f32)
                grads[spot(i, w), :] = both.astype(bf16)

            @pl.when((z < nz - 1) & (z >= root))
            def _():
                chain_push(i, 1, to_left).wait_recv()
                both = grads[spot(i, w), :].astype(f32) + chain[1, lines(i), :].astype(f32)
                grads[spot(i, w), :] = both.astype(bf16)

            @pl.when(z < root)
            def _():
                chain_push(i, 0, to_right).start()

            @pl.when(z > root)
            def _():
                chain_push(i, 1, to_left).start()

            @pl.when(z == root)
            def _():
                totals[lines(i), :] = grads[spot(i, w), :]

        b = t - LAG * (far + away)

        @pl.when((b >= 0) & (b < count))
        def _():
            @pl.when(z != root)
            def _():
                total_push(b, 0, to_left).wait_recv()

            @pl.when((z <= root) & (z > 0))
            def _():
                total_push(b, 0, to_left).start()

            @pl.when((z >= root) & (z < nz - 1))
            def _():
                total_push(b, 1, to_right).start()

            partner_push(b).start()
            deliver(b, core, totals, 0, start)

        p = b - LAG

        @pl.when((p >= 0) & (p < count))
        def _():
            partner_push(p).wait_recv()
            deliver(p, 1 - core, theirs, 1, start)

        return 0

    lax.fori_loop(0, count + LAG * (2 * far + 1), step, 0)

    for k in range(1, nz):
        e = lax.rem(z + nz - k, nz)
        push(z_s.at[z], z_s.at[e], sz_send.at[k - 1], sz_recv.at[k - 1], zs[k - 1]).wait_recv()
    total = z_s[0]
    for e in range(1, nz):
        total = total + z_s[e]
    small_o[...] = total

    small_push.wait_send()
    for copy in small_x + small_z:
        copy.wait_send()
    for copy in fast_x:
        copy.wait_send()
    for cc in range(2):

        @pl.when(core == cc)
        def _():
            for copy in attn_copies(1 - cc, to_core, 1):
                copy.wait_send()

    def drain(i, _):
        @pl.when(i + FLIGHT >= count)
        def _():
            for k in range(1, W):
                x_push(i, k).wait_send()

        partner_push(i).wait_send()
        deliver(i, core, totals, 0, finish)
        deliver(i, 1 - core, theirs, 1, finish)

        @pl.when(z != root)
        def _():
            chain_push(i, 0, to_right).wait_send()

        @pl.when((z <= root) & (z > 0))
        def _():
            total_push(i, 0, to_left).wait_send()

        @pl.when((z >= root) & (z < nz - 1))
        def _():
            total_push(i, 1, to_right).wait_send()

        return 0

    lax.fori_loop(0, count, drain, 0)


def counts_of(seq_lengths, rand_owner, rand_local, global_raw, c, n_ctx):
    blocks = BLK_DEV * n_ctx
    length = seq_lengths[:, 0]
    valid = (length + BLK - 1) // BLK
    chosen = global_raw[:, 0] % valid[:, None]
    random = rand_owner[:, 0] * BLK_DEV + rand_local[:, 0]
    ids = jnp.arange(blocks)
    near = (jnp.abs(ids[:, None] - ids[None, :]) <= 1).astype(jnp.int32)
    named = jnp.sum((random[..., None] == ids).astype(jnp.int32), 3)
    is_global = chosen[..., None] == ids
    glob = jnp.sum(is_global.astype(jnp.int32), 1)
    wide_row = jnp.any(is_global, 1)
    table = named + near[None, :, None, :] + glob[:, None, None, :]
    table = jnp.where(wide_row[:, :, None, None], 1, table).astype(f32)
    mb = table.shape[0]
    by_q = lax.dynamic_slice_in_dim(table, c * BLK_DEV, BLK_DEV, 1)
    by_k = lax.dynamic_slice_in_dim(table, c * BLK_DEV, BLK_DEV, 3)
    by_q = by_q.transpose(0, 2, 1, 3).reshape(mb, PAIRS, 4, blocks)
    by_k = by_k.transpose(0, 2, 3, 1).reshape(mb, PAIRS, 4, blocks)
    both = jnp.pad(jnp.stack([by_q, by_k]), ((0, 0), (0, 0), (0, 0), (0, 4), (0, 0)))
    both = both.reshape(2, mb, PAIRS * 8, blocks)
    return both[0], both[1]


VMEM = pl.BlockSpec(memory_space=pltpu.VMEM)
SMEM = pl.BlockSpec(memory_space=pltpu.SMEM)
ANY = pl.BlockSpec(memory_space=pl.ANY)
DMA = pltpu.SemaphoreType.DMA


def slots_of(T, MB):
    return MB if T <= 2048 else 1


def run_forward(nz, W, MB, lens, tokens, attn_w, up_w, down_w, small_in, counts):
    T = 2 * nz * TD
    shape = jax.ShapeDtypeStruct
    outs = [
        shape((1, MB, 1, TD, D), bf16),
        shape((MB, T, D), bf16),
        shape((MB, T, 2 * D), bf16),
        shape((MB, TD, D), bf16),
        shape((MB, TD, D), bf16),
        shape((MB, TD, D), f32),
        shape((MB, TD, 128), f32),
        shape((MB, TD, D), f32),
        shape((MB, TD, D), f32),
        shape((MB, TD, FF), f32),
        shape((8, 128), f32),
        shape((4, D, D), bf16),
        shape((D, FF), bf16),
        shape((FF, D), bf16),
        shape((16, D), f32),
    ]
    scratch = [
        pltpu.VMEM((4, D, D), bf16),
        pltpu.VMEM((D, FF), bf16),
        pltpu.VMEM((FF, D), bf16),
        pltpu.VMEM((W, 16, D), f32),
        pltpu.VMEM((16, D), f32),
        pltpu.VMEM((MB, T, D), bf16),
        pltpu.VMEM((slots_of(T, MB), T, 2 * D), bf16),
        pltpu.VMEM((MB, TD, D), bf16),
        pltpu.VMEM((MB, TD, D), bf16),
        pltpu.VMEM((MB, TD, D), f32),
        pltpu.VMEM((MB, TD, 128), f32),
        pltpu.VMEM((8, 128), f32),
        pltpu.VMEM((MB, TD, D), f32),
        pltpu.VMEM((MB, TD, D), f32),
        pltpu.VMEM((MB, TD, FF), f32),
        pltpu.VMEM((MB, TD, D), bf16),
        pltpu.VMEM((PAIRS, 8, T), f32),
        DMA((4,)),
        DMA((W - 1, 4)),
        DMA((W - 1, 4)),
        DMA((W - 1, 4)),
        DMA((W - 1, 4)),
        DMA((W - 1,)),
        DMA((W - 1,)),
        DMA((MB, nz)),
        DMA((MB, nz)),
        DMA((MB, nz)),
        DMA((MB, nz)),
        DMA((MB, nz)),
        DMA((5 + 10 * MB,)),
    ]
    return pl.pallas_call(
        functools.partial(forward_kernel, nz, W, MB, T),
        out_shape=outs,
        in_specs=[SMEM, ANY, ANY, ANY, ANY, VMEM, VMEM],
        out_specs=[ANY] * len(outs),
        scratch_shapes=scratch,
        compiler_params=pltpu.CompilerParams(
            collective_id=0, has_side_effects=True, vmem_limit_bytes=60 << 20
        ),
        name="forward",
    )(lens, tokens, attn_w, up_w, down_w, small_in, counts)


def run_backward(nz, W, MB, lens, cot, counts_q, counts_k, saved):
    T = 2 * nz * TD
    slots = slots_of(T, MB)
    shape = jax.ShapeDtypeStruct
    (xall, kv, q, mix, lse, first, second, hidden, top, attn, up, down, small) = saved
    outs = [
        shape((1, MB, 1, TD, D), bf16),
        shape((MB, TD, 3 * D), bf16),
        shape((MB, TD, D), bf16),
        shape((MB, TD, D), bf16),
        shape((MB, TD, FF), bf16),
        shape((MB, TD, FF), bf16),
        shape((MB, TD, D), bf16),
        shape((16, D), f32),
        shape((8, 128), f32),
    ]
    scratch = [
        pltpu.VMEM((4, D, D), bf16),
        pltpu.VMEM((D, FF), bf16),
        pltpu.VMEM((FF, D), bf16),
        pltpu.VMEM((slots, T, D), bf16),
        pltpu.VMEM((MB, TD, 2 * D), bf16),
        pltpu.VMEM((MB, TD, D), bf16),
        pltpu.VMEM((MB, TD, D), f32),
        pltpu.VMEM((MB, TD, 128), f32),
        pltpu.VMEM((MB, TD, D), f32),
        pltpu.VMEM((MB, TD, D), f32),
        pltpu.VMEM((slots, TD, FF), f32),
        pltpu.VMEM((MB, TD, D), bf16),
        pltpu.VMEM((MB, TD, D), f32),
        pltpu.VMEM((MB, TD, D), bf16),
        pltpu.VMEM((MB, T, D), bf16),
        pltpu.VMEM((MB, 2 * nz, 40, 128), f32),
        pltpu.VMEM((2, 2, T, 2 * HD), bf16),
        pltpu.VMEM((PAIRS, 8, T), f32),
        pltpu.VMEM((PAIRS, 8, T), f32),
        pltpu.VMEM((16, T), f32),
        pltpu.VMEM((16, T), f32),
        pltpu.VMEM((MB, TD, 128), f32),
        pltpu.VMEM((MB, TD, 3 * D), bf16),
        pltpu.VMEM((MB, TD, D), bf16),
        pltpu.VMEM((slots, TD, FF), bf16),
        pltpu.VMEM((slots, TD, FF), bf16),
        pltpu.VMEM((MB, TD, D), bf16),
        pltpu.VMEM((16, D), f32),
        pltpu.VMEM((MB, TD, D), bf16),
        pltpu.VMEM((W, 8, 128), f32),
        DMA((3 + 8 * MB,)),
        DMA((MB,)),
        DMA((MB,)),
        DMA((MB, nz)),
        DMA((MB, nz)),
        DMA((MB, nz)),
        DMA((MB, nz)),
        DMA((MB, nz)),
        DMA((MB, nz)),
        DMA((MB, nz)),
        DMA((MB, nz)),
        DMA((W - 1,)),
        DMA((W - 1,)),
        DMA((2, 2)),
        DMA((1 + 7 * MB,)),
    ]
    return pl.pallas_call(
        functools.partial(backward_kernel, nz, W, MB, T),
        out_shape=outs,
        in_specs=[SMEM, ANY, VMEM, VMEM] + [ANY] * 8 + [VMEM] + [ANY] * 3 + [VMEM],
        out_specs=[ANY] * 8 + [VMEM],
        scratch_shapes=scratch,
        compiler_params=pltpu.CompilerParams(
            collective_id=1, has_side_effects=True, vmem_limit_bytes=60 << 20
        ),
        name="backward",
    )(
        lens, cot, counts_q, counts_k, xall, kv, q, mix, lse, first, second, hidden, top,
        attn, up, down, small,
    )


def run_reduce(nz, W, MB, rows, small_g, tops, attn_w):
    part, ffp, R = D // W, FF // W, MB * TD
    per = part // ROWS
    count = 6 * per
    shape = jax.ShapeDtypeStruct
    outs = [
        shape((4, part, D), bf16),
        shape((part, FF), bf16),
        shape((ffp, D), bf16),
        shape((16, D), f32),
        shape((1, 2, part, D), bf16),
    ]
    scratch = [
        pltpu.VMEM((2 * R, FF // 2), bf16),
        pltpu.VMEM((2 * R, D), bf16),
        pltpu.VMEM((2 * R, D), bf16),
        pltpu.VMEM((2 * R, FF // 2), bf16),
        pltpu.VMEM((2 * R, D), bf16),
        pltpu.VMEM((2 * R, D), bf16),
        pltpu.VMEM((2 * R, D), bf16),
        pltpu.VMEM((2 * R, D), bf16),
        pltpu.VMEM((6 * D, D), bf16),
        pltpu.VMEM((W - 1, 6 * part, D), bf16),
        pltpu.VMEM((2, 6 * part, D), bf16),
        pltpu.VMEM((6 * part, D), bf16),
        pltpu.VMEM((6 * part, D), bf16),
        pltpu.VMEM((2, part, D), bf16),
        pltpu.VMEM((2, 16, D), f32),
        pltpu.VMEM((W, 16, D), f32),
        pltpu.VMEM((nz, 16, D), f32),
        DMA((W + 7 + 2 * MB,)),
        DMA((W + 6 + 2 * MB,)),
        DMA((W + 6 + 2 * MB,)),
        DMA((W - 1, count)),
        DMA((W - 1, count)),
        DMA((count,)),
        DMA((2, count)),
        DMA((2, count)),
        DMA((count,)),
        DMA((count,)),
        DMA((count,)),
        DMA((2, count)),
        DMA,
        DMA,
        DMA((W - 1,)),
        DMA((W - 1,)),
        DMA((nz - 1,)),
        DMA((nz - 1,)),
    ]
    return pl.pallas_call(
        functools.partial(reduce_kernel, nz, W, MB),
        out_shape=outs,
        in_specs=[ANY] * 8 + [VMEM, VMEM, ANY],
        out_specs=[ANY] * 3 + [VMEM] * 2,
        scratch_shapes=scratch,
        compiler_params=pltpu.CompilerParams(
            collective_id=2, has_side_effects=True, vmem_limit_bytes=60 << 20
        ),
        name="reduce",
    )(*rows, small_g, tops, attn_w)


def per_device(
    tokens, out_cotangent, attn_weights, up_weights, down_weights, norm_gains, bias_rows, up_bias,
    seq_lengths, rand_owner, rand_local, global_raw,
):
    n_ctx, W = lax.axis_size("ctx"), lax.axis_size("wsh")
    nz = n_ctx // 2
    c, w = lax.axis_index("ctx"), lax.axis_index("wsh")
    MB = tokens.shape[0]
    part, ffp = D // W, FF // W
    rows = jnp.concatenate([bias_rows[0], norm_gains[0]], 0).astype(f32)
    rows = lax.dynamic_update_slice(jnp.zeros((7, D), f32), rows, (0, w * part))
    wide = lax.dynamic_update_slice(jnp.zeros((FF,), f32), up_bias[0].astype(f32), (w * ffp,))
    small_in = jnp.concatenate([rows, wide.reshape(NCH, CHUNK), jnp.zeros((5, D), f32)], 0)
    counts_q, counts_k = counts_of(seq_lengths, rand_owner, rand_local, global_raw, c, n_ctx)
    lens = seq_lengths[:, 0]
    (
        out, xall, kv, q, att, mix, lse, first, second, hidden, top, attn, up, down, small,
    ) = run_forward(nz, W, MB, lens, tokens, attn_weights, up_weights, down_weights, small_in, counts_q)
    (
        grad_in, rows_qkv, rows_branch, rows_normed, rows_hidden, rows_gated, rows_down, small_g, tops,
    ) = run_backward(
        nz, W, MB, lens, out_cotangent, counts_q, counts_k,
        (xall, kv, q, mix, lse, first, second, hidden, top, attn, up, down, small),
    )

    def flat(v):
        return v.reshape(-1, v.shape[-1])

    rows = (
        flat(rows_gated), flat(rows_down), flat(rows_normed), flat(rows_hidden), xall,
        flat(rows_qkv), flat(att), flat(rows_branch),
    )
    grad_attn, grad_up, grad_down, small_g, clipped_qk = run_reduce(
        nz, W, MB, rows, small_g, tops, attn_weights
    )
    total = (grad_attn.astype(f32), grad_up.astype(f32), grad_down.astype(f32))
    gains = lax.dynamic_slice(small_g[0:2], (0, w * part), (2, part))
    biases = lax.dynamic_slice(small_g[2:7], (0, w * part), (5, part))
    up_grad = lax.dynamic_slice(small_g[7:11].reshape(-1), (w * ffp,), (ffp,))
    return (
        out, grad_in, total[0][None], total[1][None], total[2][None], gains[None], biases[None],
        up_grad[None], clipped_qk,
    )


def solution(mesh):
    placed = (
        P(None, "wsh", "ctx", None),
        P(None, "wsh", "ctx", None),
        P("section", None, "wsh", None),
        P("section", "wsh", None),
        P("section", "wsh", None),
        P("section", None, "wsh"),
        P("section", None, "wsh"),
        P("section", "wsh"),
        P(None, "wsh"),
        P(None, "wsh", None, None, None),
        P(None, "wsh", None, None, None),
        P(None, "wsh", None),
    )
    return jax.shard_map(
        per_device,
        mesh=mesh,
        in_specs=placed,
        out_specs=(
            P("section", None, "wsh", "ctx", None),
            P("section", None, "wsh", "ctx", None),
            P("section", None, "wsh", None),
            P("section", "wsh", None),
            P("section", "wsh", None),
            P("section", None, "wsh"),
            P("section", None, "wsh"),
            P("section", "wsh"),
            P("section", None, "wsh", None),
        ),
        check_vma=False,
    )
```

```python
import functools

import jax
import jax.numpy as jnp
from jax import lax
from jax.experimental import pallas as pl
from jax.experimental.pallas import tpu as pltpu
from jax.sharding import PartitionSpec as P

D = 768
H = 12
HD = 64
FF = 3072
BLK = 64
TD = 128
BLK_DEV = 2
PAIRS = H // 2
CHUNK = 768
NCH = FF // CHUNK
STEP = 1024
ROWS = 48
FLIGHT = 4
LAG = 4

MESH = pl.DeviceIdType.MESH
norm_eps = 1e-05
clip_limit = 6.0
masked_score = -1e30
exact_dot = lax.Precision.HIGHEST
f32 = jnp.float32
bf16 = jnp.bfloat16


def dot(a, b):
    return jnp.dot(a, b, preferred_element_type=f32)


def dot_t(a, b):
    return lax.dot_general(a, b, (((1,), (1,)), ((), ())), preferred_element_type=f32)


def dot_0(a, b):
    return lax.dot_general(a, b, (((0,), (0,)), ((), ())), preferred_element_type=f32)


def column_sum(v):
    return jnp.sum(v, 0, keepdims=True)


def norm_parts(v):
    center = v - jnp.mean(v, -1, keepdims=True)
    rstd = lax.rsqrt(jnp.mean(center * center, -1, keepdims=True) + norm_eps)
    return center * rstd, rstd


def norm_back(grad, hat, rstd, gain):
    scaled = grad * gain
    return rstd * (
        scaled
        - jnp.mean(scaled, -1, keepdims=True)
        - hat * jnp.mean(scaled * hat, -1, keepdims=True)
    )


def gelu(v):
    return 0.5 * v * (1.0 + lax.erf(v * (0.5**0.5)))


def gelu_both(v):
    phi = 0.5 * (1.0 + lax.erf(v * (0.5**0.5)))
    return v * phi, phi + v * jnp.exp(-0.5 * v * v) * 0.3989422804014327


def place():
    return lax.axis_index("section"), lax.axis_index("ctx"), lax.axis_index("wsh")


def greet(peers):
    barrier = pltpu.get_barrier_semaphore()
    for peer in peers:
        pl.semaphore_signal(barrier, inc=1, device_id=peer, device_id_type=MESH)
    pl.semaphore_wait(barrier, len(peers))


def push(src, dst, send, recv, peer):
    return pltpu.make_async_remote_copy(
        src_ref=src, dst_ref=dst, send_sem=send, recv_sem=recv, device_id=peer, device_id_type=MESH
    )


def halves(rows):
    low = lax.broadcasted_iota(jnp.int32, rows.shape, 1) < HD
    zero = jnp.zeros_like(rows)
    return jnp.concatenate([jnp.where(low, rows, zero), jnp.where(low, zero, rows)], 0)


def joined(rows):
    low = lax.broadcasted_iota(jnp.int32, (TD, 2 * HD), 1) < HD
    return jnp.where(low, rows[:TD], rows[TD:])


def spread4(rows, width):
    return jnp.concatenate(
        [jnp.broadcast_to(rows[r : r + 1], (BLK, width)) for r in range(4)], 0
    )


def block_lanes(blocks, width):
    lane = lax.broadcasted_iota(jnp.int32, (blocks, width), 1)
    row = lax.broadcasted_iota(jnp.int32, (blocks, width), 0)
    return jnp.where(lax.shift_right_logical(lane, 6) == row, 1.0, 0.0).astype(bf16)


def head_column(columns, head):
    lane = lax.broadcasted_iota(jnp.int32, columns.shape, 1)
    return jnp.sum(jnp.where(lane == head, columns, 0.0), 1, keepdims=True)


def pair_lanes(g):
    return pl.ds(pl.multiple_of(g * (2 * HD), 2 * HD), 2 * HD)


def forward_kernel(
    nz, W, MB, T,
    lens, tokens, attn_w, up_w, down_w, small_in, counts,
    out_o, xall_o, kv_o, q_o, att_o, mix_o, lse_o, first_o, second_o, hidden_o, top_o,
    attn_o, up_o, down_o, small_o,
    attn, up, down, small_all, small, xall, kv, q, att, mix, lse, top, first, second, hidden, out,
    wide,
    load_sem, w_send, w_recv, wf_send, wf_recv, s_send, s_recv,
    b_send, b_recv, f_send, f_recv, o_send, r_send, r_recv, save_sem,
):
    s, c, w = place()
    z, core = c // 2, lax.rem(c, 2)
    par = lax.rem(z, 2)
    part = D // W
    ffp = FF // W
    partner = {"ctx": c + 1 - 2 * core}
    buddy = {"ctx": (z + 1 - 2 * par) * 2 + core}
    xs = [{"wsh": lax.rem(w + k, W)} for k in range(1, W)]
    zs = [{"ctx": lax.rem(z + k, nz) * 2 + core} for k in range(1, nz)]
    over = [{"section": 1 - s, "ctx": lax.rem(z + k, nz) * 2 + core} for k in range(nz)]
    greet(xs + zs + over + [partner])

    def rows_of(zz, cc):
        return pl.ds(pl.multiple_of((zz * 2 + cc) * TD, TD), TD)

    def direct_rows(zz, cc):
        return pl.ds(pl.multiple_of((zz * 2 + cc) * TD, TD), BLK)

    def relay_rows(zz, cc):
        return pl.ds(pl.multiple_of((zz * 2 + cc) * TD + BLK, BLK), BLK)

    mine = rows_of(z, core)

    def token_push(m, k):
        peer = zs[k - 1] if m == 0 else over[k]
        return push(tokens.at[m, 0], xall.at[m, mine], b_send.at[m, k], b_recv.at[m, k], peer)

    def token_arrival(m, k):
        block = xall.at[m, rows_of(lax.rem(z + nz - k, nz), core)]
        return push(block, block, b_send.at[m, k], b_recv.at[m, k], partner)

    def own_tokens(m):
        return pltpu.make_async_copy(tokens.at[m, 0], xall.at[m, mine], b_recv.at[m, 0])

    def out_push(m, k):
        return push(
            out.at[m, 0:BLK],
            xall.at[m, direct_rows(z, core)],
            o_send.at[m, k],
            b_recv.at[m, k],
            over[k],
        )

    def out_arrival(m, k):
        block = xall.at[m, direct_rows(lax.rem(z + nz - k, nz), core)]
        return push(block, block, o_send.at[m, k], b_recv.at[m, k], partner)

    def out_relay(m):
        return push(
            out.at[m, BLK:TD],
            xall.at[m, relay_rows(z, core)],
            r_send.at[m, 0],
            r_recv.at[m, 0],
            over[0],
        )

    def relay_push(m, k):
        block = xall.at[m, relay_rows(z, core)]
        return push(block, block, r_send.at[m, k], r_recv.at[m, k], zs[k - 1])

    def relay_arrival(m, k):
        block = xall.at[m, relay_rows(lax.rem(z + nz - k, nz), core)]
        return push(block, block, r_send.at[m, k], r_recv.at[m, k], partner)

    def forward_push(m, k):
        zz = lax.rem(z + nz - k, nz)
        block = xall.at[m, rows_of(zz, core)]
        return push(block, block, f_send.at[m, k], f_recv.at[m, k], partner)

    def cut(base, ww, stride, rows, cc, zp, shared):
        share = rows // 4 if shared else rows // 2
        at = base + ww * stride + ((cc * 2 + zp) if shared else cc) * share
        return pl.ds(pl.multiple_of(at, 16), share)

    def piece(p, ww, cc, zp, local):
        stride = 0 if local else 1
        if p < 4:
            r = cut(0, ww, part * stride, part, cc, zp, False)
            matrix = (1, 2, 0, 3)[p]
            return attn_w.at[0, matrix, r] if local else attn.at[matrix, r]
        if p < 6:
            r = cut(0, ww, part * stride, part, cc, zp, True)
            cols = pl.ds((p - 4) * (FF // 2), FF // 2)
            return up_w.at[0, r, cols] if local else up.at[r, cols]
        base = (p - 6) * (ffp // 2)
        r = cut(base, ww, ffp * stride, ffp // 2, cc, zp, p == 6)
        return down_w.at[0, r] if local else down.at[r]

    shared = [p in (4, 5, 6) for p in range(8)]

    def weight_push(k, p):
        return push(
            piece(p, w, core, par, True),
            piece(p, w, core, par, False),
            w_send.at[k - 1, p],
            w_recv.at[k - 1, p],
            xs[k - 1],
        )

    def weight_forward(k, p, way):
        zp = 1 - par if way == 2 else par
        spot = piece(p, lax.rem(w + W - k, W), core, zp, False)
        peer = buddy if way == 1 else partner
        return push(spot, spot, wf_send.at[k - 1, p, way], wf_recv.at[k - 1, p, way], peer)

    def x_start(p):
        for k in range(1, W):
            weight_push(k, p).start()

    def x_arrive(p):
        for k in range(1, W):
            weight_push(k, p).wait_recv()
            weight_forward(k, p, 0).start()
            if shared[p]:
                weight_forward(k, p, 1).start()

    def z_arrive(p):
        for k in range(1, W):
            weight_forward(k, p, 1).wait_recv()
            weight_forward(k, p, 2).start()

    def core_arrive(p):
        for k in range(1, W):
            weight_forward(k, p, 0).wait_recv()
            if shared[p]:
                weight_forward(k, p, 2).wait_recv()

    def small_push(k):
        return push(small_in, small_all.at[k], s_send.at[k - 1], s_recv.at[k - 1], xs[k - 1])

    own_r = pl.ds(pl.multiple_of(w * part, 16), part)
    own_f = pl.ds(pl.multiple_of(w * ffp, 16), ffp)
    own_loads = [
        pltpu.make_async_copy(attn_w.at[0], attn.at[:, own_r], load_sem.at[0]),
        pltpu.make_async_copy(up_w.at[0], up.at[own_r], load_sem.at[1]),
        pltpu.make_async_copy(down_w.at[0], down.at[own_f], load_sem.at[2]),
    ]

    @pl.when(s == 0)
    def _():
        for k in range(1, nz):
            token_push(0, k).start()
        for m in range(MB):
            own_tokens(m).start()

    @pl.when(s == 1)
    def _():
        for m in range(1, MB):
            for k in range(1, nz):
                token_push(m, k).start()

    x_start(0)
    x_start(1)
    for k in range(1, W):
        small_push(k).start()
    for copy in own_loads:
        copy.start()

    def relay_start(m):
        out_relay(m).wait_recv()
        for k in range(1, nz):
            relay_push(m, k).start()

    def rows_ready(m):
        @pl.when(s == 0)
        def _():
            own_tokens(m).wait()

        @pl.when(s == 1)
        def _():
            out_arrival(m, 0).wait_recv()

        forward_push(m, 0).start()
        for k in range(1, nz):

            @pl.when(s == 0)
            def _():
                token_arrival(m, k).wait_recv()

            @pl.when(s == 1)
            def _():
                out_arrival(m, k).wait_recv()
                relay_arrival(m, k).wait_recv()

            forward_push(m, k).start()
        for k in range(nz):
            forward_push(m, k).wait_recv()

    saves = []

    def save(src, dst):
        copy = pltpu.make_async_copy(src, dst, save_sem.at[next(numbers)])
        copy.start()
        saves.append(copy)

    numbers = iter(range(100))
    lane = lax.broadcasted_iota(jnp.int32, (TD, 128), 1)
    row = lax.broadcasted_iota(jnp.int32, (TD, 128), 0)
    spots = lax.broadcasted_iota(jnp.int32, (1, T), 1)
    tops = jnp.full((1, 128), masked_score, f32)

    slots = kv.shape[0]

    @pl.when(s == 1)
    def _():
        for p in range(8):
            x_arrive(p)
            if p + 2 < 8:
                x_start(p + 2)
            if p and shared[p - 1]:
                z_arrive(p - 1)
        for p in range(8):
            core_arrive(p)
        relay_start(0)

    @pl.when(s == 0)
    def _():
        for p in range(3):
            x_arrive(p)
            x_start(p + 2)
        x_start(5)

    for k in range(1, W):
        small_push(k).wait_recv()
    total = small_in[...]
    for k in range(1, W):
        total = total + small_all[k]
    small[...] = total
    save(small, small_o)
    own_loads[0].wait()
    bias_v = small[0:1, :]

    for m in range(MB):
        rows_ready(m)
        if m + 1 < MB:

            @pl.when(s == 1)
            def _():
                relay_start(m + 1)

        if m == 0:

            @pl.when(s == 0)
            def _():
                for p in range(3):
                    core_arrive(p)

        save(xall.at[m], xall_o.at[m])

        def project(i, _):
            r = pl.ds(pl.multiple_of(i * 256, 256), 256)
            x = xall[m, r, :]
            kv[m % slots, r, 0:D] = dot(x, attn[1]).astype(bf16)
            kv[m % slots, r, D : 2 * D] = (dot(x, attn[2]) + bias_v).astype(bf16)
            return 0

        lax.fori_loop(0, T // 256, project, 0)
        save(kv.at[m % slots], kv_o.at[m])
        kept_kv = saves[-1]
        x_own = xall[m, mine, :]
        q[m] = (dot(x_own, attn[0]).astype(bf16).astype(f32) * (HD**-0.5)).astype(bf16)
        save(q.at[m], q_o.at[m])
        length = lens[m]
        live = spots < length
        weights = dot(counts[m].astype(bf16), block_lanes(T // BLK, T))
        weights = jnp.where(live, weights, 0.0)
        wide[...] = weights.reshape(PAIRS, 8, T)

        def attend(g, kept):
            lse_c, top_c = kept
            keys = kv[m % slots, :, pair_lanes(g)]
            values = kv[m % slots, :, pl.ds(pl.multiple_of(D + g * 128, 128), 128)]
            scores = dot_t(halves(q[m, :, pair_lanes(g)]), keys)
            count = spread4(wide[g], T)
            scores = jnp.where(count > 0, scores, masked_score)
            largest = jnp.max(scores, 1, keepdims=True)
            powers = jnp.exp(scores - largest) * count
            total = jnp.sum(powers, 1, keepdims=True)
            mixed = dot(powers.astype(bf16), values) / total
            mix[m, :, pair_lanes(g)] = joined(mixed)
            log_total = largest + jnp.log(total)
            for e in range(2):
                lse_c = jnp.where(lane == 2 * g + e, log_total[e * TD : (e + 1) * TD], lse_c)
                top_c = jnp.where(lane == 2 * g + e, largest[e * TD : (e + 1) * TD], top_c)
            return lse_c, top_c

        zeros = jnp.zeros((TD, 128), f32)
        lse_c, top_c = lax.fori_loop(0, PAIRS, attend, (zeros, zeros))
        lse[m] = lse_c
        if slots < MB:
            saves[:] = [x for x in saves if x is not kept_kv]
            kept_kv.wait()
        top_c = jnp.where(c * TD + row < length, top_c, masked_score)
        tops = jnp.maximum(tops, jnp.max(top_c, 0, keepdims=True))
        att[m] = mix[m].astype(bf16)
        save(lse.at[m], lse_o.at[m])
        save(mix.at[m], mix_o.at[m])
        save(att.at[m], att_o.at[m])
        if m < 2:

            @pl.when(s == 0)
            def _():
                if m == 0:
                    x_arrive(3)
                x_start(6 + m)

    if MB == 1:

        @pl.when(s == 0)
        def _():
            x_start(7)

    top[...] = jnp.broadcast_to(tops, (8, 128))
    save(top, top_o)

    @pl.when(s == 0)
    def _():
        core_arrive(3)

    for m in range(MB):
        branch = dot(att[m], attn[3]) + small[1:2, :]
        first[m] = xall[m, mine, :].astype(f32) + branch
        save(first.at[m], first_o.at[m])
    save(attn, attn_o)

    @pl.when(s == 0)
    def _():
        x_arrive(4)
        x_arrive(5)
        z_arrive(4)
        x_arrive(6)
        z_arrive(5)
        x_arrive(7)
        z_arrive(6)
        for p in range(4, 8):
            core_arrive(p)

    for copy in own_loads[1:]:
        copy.wait()
    save(up, up_o)
    save(down, down_o)

    for m in range(MB):
        hat, _ = norm_parts(first[m])
        normed = hat * small[5:6, :] + small[3:4, :]
        low = normed.astype(bf16)
        second[m] = normed + small[2:3, :]
        for j in range(NCH):
            cols = slice(j * CHUNK, (j + 1) * CHUNK)
            pre = dot(low, up[:, cols]) + small[7 + j : 8 + j, :]
            hidden[m, :, cols] = pre
            second[m] += dot(gelu(pre).astype(bf16), down[cols, :])
        hat, _ = norm_parts(second[m])
        out[m] = (hat * small[6:7, :] + small[4:5, :]).astype(bf16)

        save(hidden.at[m], hidden_o.at[m])
        save(second.at[m], second_o.at[m])
        save(out.at[m], out_o.at[0, m, 0])

        @pl.when(s == 0)
        def _():
            if m:
                for k in range(nz):
                    out_push(m - 1, k).wait_send()
            out_relay(m).start()
            out_relay(m).wait_send()
            for k in range(nz):
                out_push(m, k).start()


    for k in range(1, W):
        small_push(k).wait_send()
        for p in range(8):
            weight_push(k, p).wait_send()
            for way in range(3 if shared[p] else 1):
                weight_forward(k, p, way).wait_send()
    for m in range(MB):
        for k in range(nz):
            forward_push(m, k).wait_send()

        if m == MB - 1:

            @pl.when(s == 0)
            def _():
                for k in range(nz):
                    out_push(m, k).wait_send()

        @pl.when(s == 1)
        def _():
            for k in range(1, nz):
                relay_push(m, k).wait_send()

        @pl.when(s == (0 if m == 0 else 1))
        def _():
            for k in range(1, nz):
                token_push(m, k).wait_send()

    for copy in saves:
        copy.wait()


def backward_kernel(
    nz, W, MB, T,
    lens, cot, counts_q, counts_k, xall_h, kv_h, q_h, mix_h, lse_h, first_h, second_h, hidden_h, top,
    attn_h, up_h, down_h, small,
    grad_in_o, rows_qkv, rows_branch, rows_normed, rows_hidden, rows_gated, rows_down, small_o, top_o,
    attn, up, down, xall, kv, q, mix, lse, first, second, hidden, dout,
    gfirst, gbranch, gall, relay, aux, kvp, wide_q, wide_k, lse_all, del_all, del_c, dqkv, gnorm, ghid, gated,
    gdown, small_g, gin, top_x,
    load_sem, y_send, y_recv, b_send, b_recv, f_send, f_recv, a_send, a_recv, af_send, af_recv,
    t_send, t_recv, r_send, r_recv, kvp_sem, save_sem,
):
    s, c, w = place()
    z, core = c // 2, lax.rem(c, 2)
    partner = {"ctx": c + 1 - 2 * core}
    xs = [{"wsh": lax.rem(w + k, W)} for k in range(1, W)]
    zs = [{"ctx": lax.rem(z + k, nz) * 2 + core} for k in range(1, nz)]
    across = {"section": 1 - s}
    over = [{"section": 1 - s, "ctx": lax.rem(z + k, nz) * 2 + core} for k in range(1, nz)]
    greet(xs + zs + over + [across, partner])

    def rows_of(zz, cc):
        return pl.ds(pl.multiple_of((zz * 2 + cc) * TD, TD), TD)

    mine = rows_of(z, core)
    loads = []

    def load(src, dst):
        copy = pltpu.make_async_copy(src, dst, load_sem.at[len(loads)])
        copy.start()
        loads.append(copy)
        return copy

    saves = []

    def save(src, dst):
        copy = pltpu.make_async_copy(src, dst, save_sem.at[next(numbers)])
        copy.start()
        saves.append(copy)

    numbers = iter(range(100))

    def cot_load(m):
        return pltpu.make_async_copy(cot.at[m, 0], dout.at[m], y_recv.at[m])

    def grad_push(m):
        return push(gin.at[m], dout.at[m], y_send.at[m], y_recv.at[m], across)

    @pl.when(s == 1)
    def _():
        for m in range(MB):
            cot_load(m).start()

    load_second = [load(second_h.at[m], second.at[m]) for m in range(MB)]
    load_down = load(down_h, down)
    slots = xall.shape[0]
    load_hidden = [load(hidden_h.at[m], hidden.at[m]) for m in range(slots)]
    load_up = load(up_h, up)
    load_first = [load(first_h.at[m], first.at[m]) for m in range(MB)]
    load_mix = [load(mix_h.at[m], mix.at[m]) for m in range(MB)]
    load_attn = load(attn_h, attn)
    load_lse = [load(lse_h.at[m], lse.at[m]) for m in range(MB)]
    load_x = [load(xall_h.at[m], xall.at[m]) for m in range(slots)]
    load_kv = [load(kv_h.at[m, mine], kv.at[m]) for m in range(MB)]
    load_q = [load(q_h.at[m], q.at[m]) for m in range(MB)]

    def cut_rows(zz, cc, side):
        return pl.ds(pl.multiple_of((zz * 2 + cc) * TD + side * BLK, BLK), BLK)

    def rows_push(m, k):
        if k == 0:
            block = gall.at[m, mine]
            return push(block, block, f_send.at[m, 0], f_recv.at[m, 0], partner)
        block = gall.at[m, cut_rows(z, core, 0)]
        return push(block, block, b_send.at[m, k], b_recv.at[m, k], zs[k - 1])

    def rows_arrival(m, k):
        block = gall.at[m, cut_rows(lax.rem(z + nz - k, nz), core, 0)]
        return push(block, block, b_send.at[m, k], b_recv.at[m, k], partner)

    def relay_out(m):
        block = gall.at[m, cut_rows(z, core, 1)]
        return push(block, relay.at[m], r_send.at[m, 0], r_recv.at[m, 0], across)

    def relay_push(m, k):
        block = gall.at[m, cut_rows(z, core, 1)]
        return push(relay.at[m], block, r_send.at[m, k], r_recv.at[m, k], over[k - 1])

    def relay_arrival(m, k):
        block = gall.at[m, cut_rows(lax.rem(z + nz - k, nz), core, 1)]
        return push(block, block, r_send.at[m, k], r_recv.at[m, k], partner)

    def rows_forward(m, k):
        block = gall.at[m, rows_of(lax.rem(z + nz - k, nz), core)]
        return push(block, block, f_send.at[m, k], f_recv.at[m, k], partner)

    def spread_start(m):
        relay_out(m).start()
        for k in range(nz):
            aux_push(m, k).start()
            rows_push(m, k).start()

    def spread_sent(m):
        relay_out(m).wait_send()
        for k in range(1, nz):
            rows_push(m, k).wait_send()

    def relay_all():
        for m in range(MB):
            relay_out(m).wait_recv()
            for k in range(1, nz):
                relay_push(m, k).start()

    def aux_push(m, k):
        block = aux.at[m, c]
        peer = partner if k == 0 else zs[k - 1]
        send, recv = (af_send, af_recv) if k == 0 else (a_send, a_recv)
        return push(block, block, send.at[m, k], recv.at[m, k], peer)

    def aux_arrival(m, k):
        block = aux.at[m, lax.rem(z + nz - k, nz) * 2 + core]
        return push(block, block, a_send.at[m, k], a_recv.at[m, k], partner)

    def aux_forward(m, k):
        block = aux.at[m, lax.rem(z + nz - k, nz) * 2 + core]
        return push(block, block, af_send.at[m, k], af_recv.at[m, k], partner)

    def top_push(k):
        return push(top_x.at[0], top_x.at[k], t_send.at[k - 1], t_recv.at[k - 1], xs[k - 1])

    @pl.when(s == 0)
    def _():
        relay_all()

    heads = lax.broadcasted_iota(jnp.int32, (D, 128), 0)
    heads = lax.shift_right_logical(heads, 6) == lax.broadcasted_iota(jnp.int32, (D, 128), 1)
    heads = jnp.where(heads, 1.0, 0.0).astype(f32)
    small_g[...] = jnp.zeros_like(small_g)

    for m in range(MB):
        load_second[m].wait()
        if m == 0:
            load_down.wait()

        @pl.when(s == 1)
        def _():
            cot_load(m).wait()

        @pl.when(s == 0)
        def _():
            grad_push(m).wait_recv()

        grad_out = dout[m].astype(f32)
        hat, rstd = norm_parts(second[m])
        small_g[1:2, :] += column_sum(grad_out * hat)
        small_g[6:7, :] += column_sum(grad_out)
        grad_second = norm_back(grad_out, hat, rstd, small[6:7, :])
        low_second = grad_second.astype(bf16)
        gdown[m] = low_second
        save(gdown.at[m], rows_down.at[m])
        small_g[4:5, :] += column_sum(low_second.astype(f32))
        if m >= slots:
            load_hidden.append(load(hidden_h.at[m], hidden.at[m % slots]))
            for copy in hidden_saves:
                saves[:] = [x for x in saves if x is not copy]
                copy.wait()
        load_hidden[m].wait()
        if m == 0:
            load_up.wait()
        gfirst[m] = grad_second
        for j in range(NCH):
            cols = slice(j * CHUNK, (j + 1) * CHUNK)
            value, slope = gelu_both(hidden[m % slots, :, cols])
            gated[m % slots, :, cols] = value.astype(bf16)
            grad_hidden = (slope * dot_t(low_second, down[cols, :])).astype(bf16)
            ghid[m % slots, :, cols] = grad_hidden
            small_g[7 + j : 8 + j, :] += column_sum(grad_hidden.astype(f32))
            gfirst[m] += dot_t(grad_hidden, up[:, cols])
        save(gated.at[m % slots], rows_gated.at[m])
        save(ghid.at[m % slots], rows_hidden.at[m])
        hidden_saves = saves[-2:]
        grad_normed = gfirst[m]
        load_first[m].wait()
        hat, rstd = norm_parts(first[m])
        gnorm[m] = (hat * small[5:6, :] + small[3:4, :]).astype(bf16)
        save(gnorm.at[m], rows_normed.at[m])
        small_g[0:1, :] += column_sum(grad_normed * hat)
        small_g[5:6, :] += column_sum(grad_normed)
        grad_first = norm_back(grad_normed, hat, rstd, small[5:6, :])
        gfirst[m] = grad_first
        low_first = grad_first.astype(bf16)
        gbranch[m] = low_first
        save(gbranch.at[m], rows_branch.at[m])
        small_g[3:4, :] += column_sum(low_first.astype(f32))
        load_mix[m].wait()
        load_lse[m].wait()
        if m == 0:
            load_attn.wait()
        grad_att = dot_t(low_first, attn[3]).astype(bf16)
        gall[m, mine, :] = grad_att
        weighed = grad_att.astype(f32) * mix[m]
        delta = jnp.dot(weighed, heads, preferred_element_type=f32, precision=exact_dot)
        del_c[m] = delta
        aux[m, c, 0:16] = lse[m].T[0:16]
        aux[m, c, 16:32] = delta.T[0:16]
        aux[m, c, 32:40] = top[...]
        if m == 0:
            spread_start(0)

    spots = lax.broadcasted_iota(jnp.int32, (1, T), 1)
    rows_here = lax.broadcasted_iota(jnp.int32, (TD, 128), 0)
    for m in range(MB):
        if m >= slots:
            load_x.append(load(xall_h.at[m], xall.at[m % slots]))
        load_x[m].wait()
        load_kv[m].wait()
        load_q[m].wait()

        def stream(g):
            slot = lax.rem(g, 2)
            return [
                pltpu.make_async_copy(
                    kv_h.at[m, :, pl.ds(pl.multiple_of(e * D + g * 128, 128), 128)],
                    kvp.at[slot, e],
                    kvp_sem.at[slot, e],
                )
                for e in range(2)
            ]

        for copy in stream(0):
            copy.start()
        length = lens[m]
        lanes = block_lanes(T // BLK, T)
        counted = jnp.where(spots < length, dot(counts_q[m].astype(bf16), lanes), 0.0)
        counted = jnp.where(counted > 0, jnp.log(jnp.maximum(counted, 1.0)), masked_score)
        wide_q[...] = counted.reshape(PAIRS, 8, T)

        def own_rows(g, _):
            @pl.when(g + 1 < PAIRS)
            def _():
                for copy in stream(g + 1):
                    copy.start()

            for copy in stream(g):
                copy.wait()
            slot = lax.rem(g, 2)
            lse_c = jnp.concatenate([head_column(lse[m], 2 * g + e) for e in range(2)], 0)
            delta = jnp.concatenate([head_column(del_c[m], 2 * g + e) for e in range(2)], 0)
            queries = halves(q[m, :, pair_lanes(g)])
            grads = halves(gall[m, mine, pair_lanes(g)])
            grad_q = jnp.zeros((2 * TD, 2 * HD), f32)
            for t in range(0, T, STEP):
                keys = kvp[slot, 0, t : t + STEP]
                values = kvp[slot, 1, t : t + STEP]
                shift = wide_q[g, :, t : t + STEP]
                probs = jnp.exp(dot_t(queries, keys) + spread4(shift, STEP) - lse_c)
                grad_probs = dot_t(grads, values)
                grad_scores = (probs * (grad_probs - delta)).astype(bf16)
                grad_q = grad_q + dot(grad_scores, keys)
            dqkv[m, :, pair_lanes(g)] = (joined(grad_q) * (HD**-0.5)).astype(bf16)
            return 0

        lax.fori_loop(0, PAIRS, own_rows, 0)
        if m + 1 < MB:
            spread_sent(m)
            spread_start(m + 1)

        def project(i, _):
            r = pl.ds(pl.multiple_of(i * 256, 256), 256)
            rows = dot(xall[m % slots, r, :], attn[0]).astype(bf16).astype(f32)
            xall[m % slots, r, :] = (rows * (HD**-0.5)).astype(bf16)
            return 0

        lax.fori_loop(0, T // 256, project, 0)
        for k in range(1, nz):
            rows_arrival(m, k).wait_recv()
            relay_arrival(m, k).wait_recv()
            rows_forward(m, k).start()
            aux_arrival(m, k).wait_recv()
            aux_forward(m, k).start()
        for k in range(nz):
            rows_forward(m, k).wait_recv()
            aux_forward(m, k).wait_recv()
        for cc in range(2 * nz):
            lse_all[:, cc * TD : (cc + 1) * TD] = aux[m, cc, 0:16]
            del_all[:, cc * TD : (cc + 1) * TD] = aux[m, cc, 16:32]
        if m == 0:
            most = aux[0, 0, 32:40]
            for cc in range(1, 2 * nz):
                most = jnp.maximum(most, aux[0, cc, 32:40])
            top_x[0] = most
            for k in range(1, W):
                top_push(k).start()
        counted = dot(counts_k[m].astype(bf16), lanes)
        counted = jnp.where(counted > 0, jnp.log(jnp.maximum(counted, 1.0)), masked_score)
        wide_k[...] = counted.reshape(PAIRS, 8, T)
        live = c * TD + rows_here < length

        def own_keys(g, _):
            keys = halves(kv[m, :, pair_lanes(g)])
            values = halves(kv[m, :, pl.ds(pl.multiple_of(D + g * 128, 128), 128)])
            lse_r = [lse_all[pl.ds(2 * g + e, 1), :] for e in range(2)]
            delta = [del_all[pl.ds(2 * g + e, 1), :] for e in range(2)]
            shift = wide_k[g]
            shift = jnp.concatenate([shift[0:2] - lse_r[0], shift[2:4] - lse_r[1]], 0)
            grad_k = jnp.zeros((2 * TD, 2 * HD), f32)
            grad_v = jnp.zeros((2 * TD, 2 * HD), f32)
            for t in range(0, T, STEP):
                queries = xall[m % slots, t : t + STEP, pair_lanes(g)]
                grads = gall[m, t : t + STEP, pair_lanes(g)]
                probs = jnp.exp(dot_t(keys, queries) + spread4(shift[:, t : t + STEP], STEP))
                grad_v = grad_v + dot(probs.astype(bf16), grads)
                centre = jnp.concatenate(
                    [jnp.broadcast_to(d[:, t : t + STEP], (TD, STEP)) for d in delta], 0
                )
                grad_scores = (probs * (dot_t(values, grads) - centre)).astype(bf16)
                grad_k = grad_k + dot(grad_scores, queries)
            grad_k, grad_v = joined(grad_k), joined(grad_v)
            lanes_k = pl.ds(pl.multiple_of(D + g * 128, 128), 128)
            lanes_v = pl.ds(pl.multiple_of(2 * D + g * 128, 128), 128)
            dqkv[m, :, lanes_k] = jnp.where(live, grad_k, 0.0).astype(bf16)
            dqkv[m, :, lanes_v] = jnp.where(live, grad_v, 0.0).astype(bf16)
            return 0

        lax.fori_loop(0, PAIRS, own_keys, 0)
        save(dqkv.at[m], rows_qkv.at[m])
        small_g[2:3, :] += column_sum(dqkv[m, :, 2 * D :].astype(f32))
        total = gfirst[m]
        for p in range(3):
            total = total + dot_t(dqkv[m, :, p * D : (p + 1) * D], attn[p])
        gin[m] = total.astype(bf16)

        @pl.when(s == 1)
        def _():
            grad_push(m).start()

        save(gin.at[m], grad_in_o.at[0, m, 0])

    @pl.when(s == 1)
    def _():
        relay_all()

    save(small_g, small_o)
    for k in range(1, W):
        top_push(k).wait()
    most = top_x[0]
    for k in range(1, W):
        most = jnp.maximum(most, top_x[k])
    top_o[...] = most
    for m in range(MB):
        for k in range(nz):
            rows_forward(m, k).wait_send()
            aux_forward(m, k).wait_send()
        for k in range(1, nz):
            aux_push(m, k).wait_send()
            relay_push(m, k).wait_send()
        if m == MB - 1:
            spread_sent(m)

        @pl.when(s == 1)
        def _():
            grad_push(m).wait_send()

    for copy in saves:
        copy.wait()


def reduce_kernel(
    nz, W, MB,
    gated_h, down_h, normed_h, hidden_h, x_h, qkv_h, att_h, branch_h, small_g, tops, attn_w,
    attn_o, up_o, down_o, small_o, clip_o,
    lg, rd, ln, rh, la, ra, lb, rb, grads, from_x, chain, totals, theirs, own_w, core_s, wsh_s, z_s,
    load_sem, c_send, c_recv, x_send, x_recv, ch_send, ch_recv, b_send, b_recv, p_send, p_recv,
    o_sem, s_send, s_recv, sx_send, sx_recv, sz_send, sz_recv,
):
    s, c, w = place()
    z, core = c // 2, lax.rem(c, 2)
    part, ffp = D // W, FF // W
    R = MB * TD
    per = part // ROWS
    count = 6 * per
    root = (nz - 1) // 2
    partner = {"ctx": c + 1 - 2 * core}
    xs = [{"wsh": lax.rem(w + k, W)} for k in range(1, W)]
    zs = [{"ctx": lax.rem(z + k, nz) * 2 + core} for k in range(1, nz)]
    greet(xs + zs + [partner])

    def operands(cc):
        gate = [
            (
                gated_h.at[:, pl.ds(pl.multiple_of(e * ffp + cc * (ffp // 2), 128), ffp // 2)],
                lg,
                e * (ffp // 2),
                ffp // 2,
            )
            for e in range(W)
        ]
        hid = hidden_h.at[:, pl.ds(pl.multiple_of(cc * (FF // 2), 128), FF // 2)]
        return gate + [(down_h, rd, 0, D), (normed_h, ln, 0, D), (hid, rh, 0, FF // 2)]

    def rows_of_x(buffer):
        mine = pl.ds(pl.multiple_of(c * TD, TD), TD)
        return [(x_h.at[m, mine], buffer, m) for m in range(MB)]

    def heads_operands(cc):
        if cc == 0:
            return [(qkv_h.at[:, 0:D], ra), (qkv_h.at[:, D : 2 * D], rb)]
        return [(qkv_h.at[:, 2 * D : 3 * D], ra), (att_h, lb), (branch_h, rb)]

    first = operands(core)
    second = operands(1 - core)
    n1 = len(first)
    base = [0, R]

    def local(n, src, dst):
        return pltpu.make_async_copy(src, dst, load_sem.at[n])

    def to_core(n, src, dst):
        return push(src, dst, c_send.at[n], c_recv.at[n], partner)

    def window(dst, at, width, side):
        return dst.at[side * R : side * R + R, at : at + width]

    fast = [local(n, a, window(b, at, wd, 0)) for n, (a, b, at, wd) in enumerate(first)]
    fast_x = [to_core(n, a, window(b, at, wd, 1)) for n, (a, b, at, wd) in enumerate(second)]
    for one, two in zip(fast, fast_x):
        two.start()
        one.start()

    def attn_copies(cc, make, side):
        found = []
        for n, (a, b) in enumerate(heads_operands(cc)):
            found.append(make(n1 + n, a, b.at[side * R : side * R + R]))
        n = n1 + 3
        for buffer in (la, lb) if cc == 0 else (la,):
            for a, b, m in rows_of_x(buffer):
                lo = side * R + m * TD
                found.append(make(n, a, b.at[lo : lo + TD]))
                n += 1
        return found

    for cc in range(2):

        @pl.when(core == cc)
        def _():
            for copy in attn_copies(1 - cc, to_core, 1) + attn_copies(cc, local, 0):
                copy.start()

    small_push = push(small_g, core_s.at[core], s_send, s_recv, partner)
    small_push.start()
    core_s[core] = small_g[...]
    weights_in = local(n1 + 3 + 2 * MB, attn_w.at[0, 0:2], own_w)
    weights_in.start()

    def spot(i, ww):
        at = (i // per) * D + ww * part + lax.rem(i, per) * ROWS
        return pl.ds(pl.multiple_of(at, 16), ROWS)

    def lines(i):
        return pl.ds(pl.multiple_of(i * ROWS, 16), ROWS)

    def x_push(i, k):
        return push(
            grads.at[spot(i, lax.rem(w + k, W))],
            from_x.at[k - 1, lines(i)],
            x_send.at[k - 1, i],
            x_recv.at[k - 1, i],
            xs[k - 1],
        )

    for n in range(W + 1):
        fast[n].wait()
        fast_x[n].wait_recv()
    gate_half = ffp // 2
    for e in range(W):
        block = dot_0(lg[:, e * gate_half : (e + 1) * gate_half], rd[...]).astype(bf16)
        for j in range(2):
            grads[j * D + e * part : j * D + (e + 1) * part] = block[j * part : (j + 1) * part]
    for i in range(FLIGHT):
        for k in range(1, W):
            x_push(i, k).start()
    for n in range(W + 1, n1):
        fast[n].wait()
        fast_x[n].wait_recv()
    for j in range(2):
        block = dot_0(ln[...], rh[:, j * D : (j + 1) * D])
        grads[(2 + j) * D : (3 + j) * D] = block.astype(bf16)
    for cc in range(2):

        @pl.when(core == cc)
        def _():
            for copy in attn_copies(cc, local, 0):
                copy.wait()
            for copy in attn_copies(cc, to_core, 1):
                copy.wait_recv()

    for j, (left, right) in enumerate(((la, ra), (lb, rb))):
        grads[(4 + j) * D : (5 + j) * D] = dot_0(left[...], right[...]).astype(bf16)

    small_push.wait_recv()
    pair = core_s[0] + core_s[1]
    wsh_s[w] = pair
    small_x = [push(wsh_s.at[w], wsh_s.at[w], sx_send.at[k - 1], sx_recv.at[k - 1], xs[k - 1]) for k in range(1, W)]
    for copy in small_x:
        copy.start()
    weights_in.wait()
    factor = jnp.sqrt(clip_limit / jnp.maximum(tops[...], clip_limit))
    lane = lax.broadcasted_iota(jnp.int32, (128, D), 1)
    head = lax.broadcasted_iota(jnp.int32, (128, D), 0)
    heads = jnp.where(lax.shift_right_logical(lane, 6) == head, 1.0, 0.0).astype(f32)
    wide = jnp.dot(factor, heads, preferred_element_type=f32, precision=exact_dot)[0:1]
    for p in range(2):
        clip_o[0, p] = (own_w[p].astype(f32) * wide).astype(bf16)
    for k in range(1, W):
        e = lax.rem(w + W - k, W)
        push(wsh_s.at[w], wsh_s.at[e], sx_send.at[k - 1], sx_recv.at[k - 1], xs[k - 1]).wait_recv()
    total = wsh_s[0]
    for e in range(1, W):
        total = total + wsh_s[e]
    z_s[z] = total
    small_z = [push(z_s.at[z], z_s.at[z], sz_send.at[k - 1], sz_recv.at[k - 1], zs[k - 1]) for k in range(1, nz)]
    for copy in small_z:
        copy.start()

    is_left = z < root
    to_left = {"ctx": jnp.maximum(z - 1, 0) * 2 + core}
    to_right = {"ctx": jnp.minimum(z + 1, nz - 1) * 2 + core}
    far = max(root, nz - 1 - root)
    depth = jnp.where(z == root, far, jnp.where(is_left, z, nz - 1 - z))
    away = jnp.where(is_left, root - z, z - root)

    def chain_push(i, side, peer):
        block = grads.at[spot(i, w)]
        return push(block, chain.at[side, lines(i)], ch_send.at[i], ch_recv.at[side, i], peer)

    def total_push(i, side, peer):
        block = totals.at[lines(i)]
        return push(block, block, b_send.at[side, i], b_recv.at[i], peer)

    def partner_push(i):
        return push(totals.at[lines(i)], theirs.at[lines(i)], p_send.at[i], p_recv.at[i], partner)

    def deliver(i, cc, source, side, go):
        j, r = i // per, lax.rem(i, per)
        places = [
            (j < 2, lambda: down_o.at[pl.ds(pl.multiple_of(cc * gate_half + i * ROWS, 16), ROWS)]),
            (
                (j >= 2) & (j < 4),
                lambda: up_o.at[
                    pl.ds(pl.multiple_of(r * ROWS, 16), ROWS),
                    pl.ds(pl.multiple_of((cc * 2 + j - 2) * D, 128), D),
                ],
            ),
            (
                j >= 4,
                lambda: attn_o.at[cc * 2 + j - 4, pl.ds(pl.multiple_of(r * ROWS, 16), ROWS)],
            ),
        ]
        for when, spot_of in places:

            @pl.when(when)
            def _():
                go(pltpu.make_async_copy(source.at[lines(i)], spot_of(), o_sem.at[side, i]))

    def start(copy):
        copy.start()

    def finish(copy):
        copy.wait()

    def step(t, _):
        @pl.when(t + FLIGHT < count)
        def _():
            for k in range(1, W):
                x_push(t, k).wait_send()
                x_push(t + FLIGHT, k).start()

        i = t - LAG * depth

        @pl.when((i >= 0) & (i < count))
        def _():
            acc = grads[spot(i, w), :].astype(f32)
            for k in range(1, W):
                x_push(i, k).wait_recv()
                acc = acc + from_x[k - 1, lines(i), :].astype(f32)
            grads[spot(i, w), :] = acc.astype(bf16)

            @pl.when((z > 0) & (z <= root))
            def _():
                chain_push(i, 0, to_right).wait_recv()
                both = grads[spot(i, w), :].astype(f32) + chain[0, lines(i), :].astype(f32)
                grads[spot(i, w), :] = both.astype(bf16)

            @pl.when((z < nz - 1) & (z >= root))
            def _():
                chain_push(i, 1, to_left).wait_recv()
                both = grads[spot(i, w), :].astype(f32) + chain[1, lines(i), :].astype(f32)
                grads[spot(i, w), :] = both.astype(bf16)

            @pl.when(z < root)
            def _():
                chain_push(i, 0, to_right).start()

            @pl.when(z > root)
            def _():
                chain_push(i, 1, to_left).start()

            @pl.when(z == root)
            def _():
                totals[lines(i), :] = grads[spot(i, w), :]

        b = t - LAG * (far + away)

        @pl.when((b >= 0) & (b < count))
        def _():
            @pl.when(z != root)
            def _():
                total_push(b, 0, to_left).wait_recv()

            @pl.when((z <= root) & (z > 0))
            def _():
                total_push(b, 0, to_left).start()

            @pl.when((z >= root) & (z < nz - 1))
            def _():
                total_push(b, 1, to_right).start()

            partner_push(b).start()
            deliver(b, core, totals, 0, start)

        p = b - LAG

        @pl.when((p >= 0) & (p < count))
        def _():
            partner_push(p).wait_recv()
            deliver(p, 1 - core, theirs, 1, start)

        return 0

    lax.fori_loop(0, count + LAG * (2 * far + 1), step, 0)

    for k in range(1, nz):
        e = lax.rem(z + nz - k, nz)
        push(z_s.at[z], z_s.at[e], sz_send.at[k - 1], sz_recv.at[k - 1], zs[k - 1]).wait_recv()
    total = z_s[0]
    for e in range(1, nz):
        total = total + z_s[e]
    small_o[...] = total

    small_push.wait_send()
    for copy in small_x + small_z:
        copy.wait_send()
    for copy in fast_x:
        copy.wait_send()
    for cc in range(2):

        @pl.when(core == cc)
        def _():
            for copy in attn_copies(1 - cc, to_core, 1):
                copy.wait_send()

    def drain(i, _):
        @pl.when(i + FLIGHT >= count)
        def _():
            for k in range(1, W):
                x_push(i, k).wait_send()

        partner_push(i).wait_send()
        deliver(i, core, totals, 0, finish)
        deliver(i, 1 - core, theirs, 1, finish)

        @pl.when(z != root)
        def _():
            chain_push(i, 0, to_right).wait_send()

        @pl.when((z <= root) & (z > 0))
        def _():
            total_push(i, 0, to_left).wait_send()

        @pl.when((z >= root) & (z < nz - 1))
        def _():
            total_push(i, 1, to_right).wait_send()

        return 0

    lax.fori_loop(0, count, drain, 0)


def counts_of(seq_lengths, rand_owner, rand_local, global_raw, c, n_ctx):
    blocks = BLK_DEV * n_ctx
    length = seq_lengths[:, 0]
    valid = (length + BLK - 1) // BLK
    chosen = global_raw[:, 0] % valid[:, None]
    random = rand_owner[:, 0] * BLK_DEV + rand_local[:, 0]
    ids = jnp.arange(blocks)
    near = (jnp.abs(ids[:, None] - ids[None, :]) <= 1).astype(jnp.int32)
    named = jnp.sum((random[..., None] == ids).astype(jnp.int32), 3)
    is_global = chosen[..., None] == ids
    glob = jnp.sum(is_global.astype(jnp.int32), 1)
    wide_row = jnp.any(is_global, 1)
    table = named + near[None, :, None, :] + glob[:, None, None, :]
    table = jnp.where(wide_row[:, :, None, None], 1, table).astype(f32)
    mb = table.shape[0]
    by_q = lax.dynamic_slice_in_dim(table, c * BLK_DEV, BLK_DEV, 1)
    by_k = lax.dynamic_slice_in_dim(table, c * BLK_DEV, BLK_DEV, 3)
    by_q = by_q.transpose(0, 2, 1, 3).reshape(mb, PAIRS, 4, blocks)
    by_k = by_k.transpose(0, 2, 3, 1).reshape(mb, PAIRS, 4, blocks)
    both = jnp.pad(jnp.stack([by_q, by_k]), ((0, 0), (0, 0), (0, 0), (0, 4), (0, 0)))
    both = both.reshape(2, mb, PAIRS * 8, blocks)
    return both[0], both[1]


VMEM = pl.BlockSpec(memory_space=pltpu.VMEM)
SMEM = pl.BlockSpec(memory_space=pltpu.SMEM)
ANY = pl.BlockSpec(memory_space=pl.ANY)
DMA = pltpu.SemaphoreType.DMA


def slots_of(T, MB):
    return MB if T <= 2048 else 1


def run_forward(nz, W, MB, lens, tokens, attn_w, up_w, down_w, small_in, counts):
    T = 2 * nz * TD
    shape = jax.ShapeDtypeStruct
    outs = [
        shape((1, MB, 1, TD, D), bf16),
        shape((MB, T, D), bf16),
        shape((MB, T, 2 * D), bf16),
        shape((MB, TD, D), bf16),
        shape((MB, TD, D), bf16),
        shape((MB, TD, D), f32),
        shape((MB, TD, 128), f32),
        shape((MB, TD, D), f32),
        shape((MB, TD, D), f32),
        shape((MB, TD, FF), f32),
        shape((8, 128), f32),
        shape((4, D, D), bf16),
        shape((D, FF), bf16),
        shape((FF, D), bf16),
        shape((16, D), f32),
    ]
    scratch = [
        pltpu.VMEM((4, D, D), bf16),
        pltpu.VMEM((D, FF), bf16),
        pltpu.VMEM((FF, D), bf16),
        pltpu.VMEM((W, 16, D), f32),
        pltpu.VMEM((16, D), f32),
        pltpu.VMEM((MB, T, D), bf16),
        pltpu.VMEM((slots_of(T, MB), T, 2 * D), bf16),
        pltpu.VMEM((MB, TD, D), bf16),
        pltpu.VMEM((MB, TD, D), bf16),
        pltpu.VMEM((MB, TD, D), f32),
        pltpu.VMEM((MB, TD, 128), f32),
        pltpu.VMEM((8, 128), f32),
        pltpu.VMEM((MB, TD, D), f32),
        pltpu.VMEM((MB, TD, D), f32),
        pltpu.VMEM((MB, TD, FF), f32),
        pltpu.VMEM((MB, TD, D), bf16),
        pltpu.VMEM((PAIRS, 8, T), f32),
        DMA((3,)),
        DMA((W - 1, 8)),
        DMA((W - 1, 8)),
        DMA((W - 1, 8, 3)),
        DMA((W - 1, 8, 3)),
        DMA((W - 1,)),
        DMA((W - 1,)),
        DMA((MB, nz)),
        DMA((MB, nz)),
        DMA((MB, nz)),
        DMA((MB, nz)),
        DMA((MB, nz)),
        DMA((MB, nz)),
        DMA((MB, nz)),
        DMA((5 + 10 * MB,)),
    ]
    return pl.pallas_call(
        functools.partial(forward_kernel, nz, W, MB, T),
        out_shape=outs,
        in_specs=[SMEM, ANY, ANY, ANY, ANY, VMEM, VMEM],
        out_specs=[ANY] * len(outs),
        scratch_shapes=scratch,
        compiler_params=pltpu.CompilerParams(
            collective_id=0, has_side_effects=True, vmem_limit_bytes=60 << 20
        ),
        name="forward",
    )(lens, tokens, attn_w, up_w, down_w, small_in, counts)


def run_backward(nz, W, MB, lens, cot, counts_q, counts_k, saved):
    T = 2 * nz * TD
    slots = slots_of(T, MB)
    shape = jax.ShapeDtypeStruct
    (xall, kv, q, mix, lse, first, second, hidden, top, attn, up, down, small) = saved
    outs = [
        shape((1, MB, 1, TD, D), bf16),
        shape((MB, TD, 3 * D), bf16),
        shape((MB, TD, D), bf16),
        shape((MB, TD, D), bf16),
        shape((MB, TD, FF), bf16),
        shape((MB, TD, FF), bf16),
        shape((MB, TD, D), bf16),
        shape((16, D), f32),
        shape((8, 128), f32),
    ]
    scratch = [
        pltpu.VMEM((4, D, D), bf16),
        pltpu.VMEM((D, FF), bf16),
        pltpu.VMEM((FF, D), bf16),
        pltpu.VMEM((slots, T, D), bf16),
        pltpu.VMEM((MB, TD, 2 * D), bf16),
        pltpu.VMEM((MB, TD, D), bf16),
        pltpu.VMEM((MB, TD, D), f32),
        pltpu.VMEM((MB, TD, 128), f32),
        pltpu.VMEM((MB, TD, D), f32),
        pltpu.VMEM((MB, TD, D), f32),
        pltpu.VMEM((slots, TD, FF), f32),
        pltpu.VMEM((MB, TD, D), bf16),
        pltpu.VMEM((MB, TD, D), f32),
        pltpu.VMEM((MB, TD, D), bf16),
        pltpu.VMEM((MB, T, D), bf16),
        pltpu.VMEM((MB, BLK, D), bf16),
        pltpu.VMEM((MB, 2 * nz, 40, 128), f32),
        pltpu.VMEM((2, 2, T, 2 * HD), bf16),
        pltpu.VMEM((PAIRS, 8, T), f32),
        pltpu.VMEM((PAIRS, 8, T), f32),
        pltpu.VMEM((16, T), f32),
        pltpu.VMEM((16, T), f32),
        pltpu.VMEM((MB, TD, 128), f32),
        pltpu.VMEM((MB, TD, 3 * D), bf16),
        pltpu.VMEM((MB, TD, D), bf16),
        pltpu.VMEM((slots, TD, FF), bf16),
        pltpu.VMEM((slots, TD, FF), bf16),
        pltpu.VMEM((MB, TD, D), bf16),
        pltpu.VMEM((16, D), f32),
        pltpu.VMEM((MB, TD, D), bf16),
        pltpu.VMEM((W, 8, 128), f32),
        DMA((3 + 8 * MB,)),
        DMA((MB,)),
        DMA((MB,)),
        DMA((MB, nz)),
        DMA((MB, nz)),
        DMA((MB, nz)),
        DMA((MB, nz)),
        DMA((MB, nz)),
        DMA((MB, nz)),
        DMA((MB, nz)),
        DMA((MB, nz)),
        DMA((W - 1,)),
        DMA((W - 1,)),
        DMA((MB, nz)),
        DMA((MB, nz)),
        DMA((2, 2)),
        DMA((1 + 7 * MB,)),
    ]
    return pl.pallas_call(
        functools.partial(backward_kernel, nz, W, MB, T),
        out_shape=outs,
        in_specs=[SMEM, ANY, VMEM, VMEM] + [ANY] * 8 + [VMEM] + [ANY] * 3 + [VMEM],
        out_specs=[ANY] * 8 + [VMEM],
        scratch_shapes=scratch,
        compiler_params=pltpu.CompilerParams(
            collective_id=1, has_side_effects=True, vmem_limit_bytes=60 << 20
        ),
        name="backward",
    )(
        lens, cot, counts_q, counts_k, xall, kv, q, mix, lse, first, second, hidden, top,
        attn, up, down, small,
    )


def run_reduce(nz, W, MB, rows, small_g, tops, attn_w):
    part, ffp, R = D // W, FF // W, MB * TD
    per = part // ROWS
    count = 6 * per
    shape = jax.ShapeDtypeStruct
    outs = [
        shape((4, part, D), bf16),
        shape((part, FF), bf16),
        shape((ffp, D), bf16),
        shape((16, D), f32),
        shape((1, 2, part, D), bf16),
    ]
    scratch = [
        pltpu.VMEM((2 * R, FF // 2), bf16),
        pltpu.VMEM((2 * R, D), bf16),
        pltpu.VMEM((2 * R, D), bf16),
        pltpu.VMEM((2 * R, FF // 2), bf16),
        pltpu.VMEM((2 * R, D), bf16),
        pltpu.VMEM((2 * R, D), bf16),
        pltpu.VMEM((2 * R, D), bf16),
        pltpu.VMEM((2 * R, D), bf16),
        pltpu.VMEM((6 * D, D), bf16),
        pltpu.VMEM((W - 1, 6 * part, D), bf16),
        pltpu.VMEM((2, 6 * part, D), bf16),
        pltpu.VMEM((6 * part, D), bf16),
        pltpu.VMEM((6 * part, D), bf16),
        pltpu.VMEM((2, part, D), bf16),
        pltpu.VMEM((2, 16, D), f32),
        pltpu.VMEM((W, 16, D), f32),
        pltpu.VMEM((nz, 16, D), f32),
        DMA((W + 7 + 2 * MB,)),
        DMA((W + 6 + 2 * MB,)),
        DMA((W + 6 + 2 * MB,)),
        DMA((W - 1, count)),
        DMA((W - 1, count)),
        DMA((count,)),
        DMA((2, count)),
        DMA((2, count)),
        DMA((count,)),
        DMA((count,)),
        DMA((count,)),
        DMA((2, count)),
        DMA,
        DMA,
        DMA((W - 1,)),
        DMA((W - 1,)),
        DMA((nz - 1,)),
        DMA((nz - 1,)),
    ]
    return pl.pallas_call(
        functools.partial(reduce_kernel, nz, W, MB),
        out_shape=outs,
        in_specs=[ANY] * 8 + [VMEM, VMEM, ANY],
        out_specs=[ANY] * 3 + [VMEM] * 2,
        scratch_shapes=scratch,
        compiler_params=pltpu.CompilerParams(
            collective_id=2, has_side_effects=True, vmem_limit_bytes=60 << 20
        ),
        name="reduce",
    )(*rows, small_g, tops, attn_w)


def per_device(
    tokens, out_cotangent, attn_weights, up_weights, down_weights, norm_gains, bias_rows, up_bias,
    seq_lengths, rand_owner, rand_local, global_raw,
):
    n_ctx, W = lax.axis_size("ctx"), lax.axis_size("wsh")
    nz = n_ctx // 2
    c, w = lax.axis_index("ctx"), lax.axis_index("wsh")
    MB = tokens.shape[0]
    part, ffp = D // W, FF // W
    rows = jnp.concatenate([bias_rows[0], norm_gains[0]], 0).astype(f32)
    rows = lax.dynamic_update_slice(jnp.zeros((7, D), f32), rows, (0, w * part))
    wide = lax.dynamic_update_slice(jnp.zeros((FF,), f32), up_bias[0].astype(f32), (w * ffp,))
    small_in = jnp.concatenate([rows, wide.reshape(NCH, CHUNK), jnp.zeros((5, D), f32)], 0)
    counts_q, counts_k = counts_of(seq_lengths, rand_owner, rand_local, global_raw, c, n_ctx)
    lens = seq_lengths[:, 0]
    (
        out, xall, kv, q, att, mix, lse, first, second, hidden, top, attn, up, down, small,
    ) = run_forward(nz, W, MB, lens, tokens, attn_weights, up_weights, down_weights, small_in, counts_q)
    (
        grad_in, rows_qkv, rows_branch, rows_normed, rows_hidden, rows_gated, rows_down, small_g, tops,
    ) = run_backward(
        nz, W, MB, lens, out_cotangent, counts_q, counts_k,
        (xall, kv, q, mix, lse, first, second, hidden, top, attn, up, down, small),
    )

    def flat(v):
        return v.reshape(-1, v.shape[-1])

    rows = (
        flat(rows_gated), flat(rows_down), flat(rows_normed), flat(rows_hidden), xall,
        flat(rows_qkv), flat(att), flat(rows_branch),
    )
    grad_attn, grad_up, grad_down, small_g, clipped_qk = run_reduce(
        nz, W, MB, rows, small_g, tops, attn_weights
    )
    total = (grad_attn.astype(f32), grad_up.astype(f32), grad_down.astype(f32))
    gains = lax.dynamic_slice(small_g[0:2], (0, w * part), (2, part))
    biases = lax.dynamic_slice(small_g[2:7], (0, w * part), (5, part))
    up_grad = lax.dynamic_slice(small_g[7:11].reshape(-1), (w * ffp,), (ffp,))
    return (
        out, grad_in, total[0][None], total[1][None], total[2][None], gains[None], biases[None],
        up_grad[None], clipped_qk,
    )


def solution(mesh):
    placed = (
        P(None, "wsh", "ctx", None),
        P(None, "wsh", "ctx", None),
        P("section", None, "wsh", None),
        P("section", "wsh", None),
        P("section", "wsh", None),
        P("section", None, "wsh"),
        P("section", None, "wsh"),
        P("section", "wsh"),
        P(None, "wsh"),
        P(None, "wsh", None, None, None),
        P(None, "wsh", None, None, None),
        P(None, "wsh", None),
    )
    return jax.shard_map(
        per_device,
        mesh=mesh,
        in_specs=placed,
        out_specs=(
            P("section", None, "wsh", "ctx", None),
            P("section", None, "wsh", "ctx", None),
            P("section", None, "wsh", None),
            P("section", "wsh", None),
            P("section", "wsh", None),
            P("section", None, "wsh"),
            P("section", None, "wsh"),
            P("section", "wsh"),
            P("section", None, "wsh", None),
        ),
        check_vma=False,
    )
```

```python
import functools
import types

import jax
import jax.numpy as jnp
from jax import lax
from jax.experimental import pallas as pl
from jax.experimental.pallas import tpu as pltpu
from jax.sharding import PartitionSpec as P

D = 768
H = 12
HD = 64
FF = 3072
BLK = 64
TD = 128
BLK_DEV = 2
PAIRS = H // 2
CHUNK = 768
NCH = FF // CHUNK
STEP = 1024
ROWS = 48
FLIGHT = 4
LAG = 3
PACE = 1
EARLY = 4
RINGS = [a + b for a in ("b", "f", "a", "af", "r") for b in ("_send", "_recv")]

MESH = pl.DeviceIdType.MESH
norm_eps = 1e-05
clip_limit = 6.0
masked_score = -1e30
exact_dot = lax.Precision.HIGHEST
f32 = jnp.float32
bf16 = jnp.bfloat16


def dot(a, b):
    return jnp.dot(a, b, preferred_element_type=f32)


def dot_t(a, b):
    return lax.dot_general(a, b, (((1,), (1,)), ((), ())), preferred_element_type=f32)


def dot_0(a, b):
    return lax.dot_general(a, b, (((0,), (0,)), ((), ())), preferred_element_type=f32)


def column_sum(v):
    return jnp.sum(v, 0, keepdims=True)


def norm_parts(v):
    center = v - jnp.mean(v, -1, keepdims=True)
    rstd = lax.rsqrt(jnp.mean(center * center, -1, keepdims=True) + norm_eps)
    return center * rstd, rstd


def norm_back(grad, hat, rstd, gain):
    scaled = grad * gain
    return rstd * (
        scaled
        - jnp.mean(scaled, -1, keepdims=True)
        - hat * jnp.mean(scaled * hat, -1, keepdims=True)
    )


def gelu(v):
    return 0.5 * v * (1.0 + lax.erf(v * (0.5**0.5)))


def gelu_both(v):
    phi = 0.5 * (1.0 + lax.erf(v * (0.5**0.5)))
    return v * phi, phi + v * jnp.exp(-0.5 * v * v) * 0.3989422804014327


def place():
    return lax.axis_index("section"), lax.axis_index("ctx"), lax.axis_index("wsh")


def greet(peers):
    barrier = pltpu.get_barrier_semaphore()
    for peer in peers:
        pl.semaphore_signal(barrier, inc=1, device_id=peer, device_id_type=MESH)
    pl.semaphore_wait(barrier, len(peers))


def push(src, dst, send, recv, peer):
    return pltpu.make_async_remote_copy(
        src_ref=src, dst_ref=dst, send_sem=send, recv_sem=recv, device_id=peer, device_id_type=MESH
    )


def halves(rows):
    low = lax.broadcasted_iota(jnp.int32, rows.shape, 1) < HD
    zero = jnp.zeros_like(rows)
    return jnp.concatenate([jnp.where(low, rows, zero), jnp.where(low, zero, rows)], 0)


def joined(rows):
    low = lax.broadcasted_iota(jnp.int32, (TD, 2 * HD), 1) < HD
    return jnp.where(low, rows[:TD], rows[TD:])


def spread4(rows, width):
    return jnp.concatenate(
        [jnp.broadcast_to(rows[r : r + 1], (BLK, width)) for r in range(4)], 0
    )


def block_lanes(blocks, width):
    lane = lax.broadcasted_iota(jnp.int32, (blocks, width), 1)
    row = lax.broadcasted_iota(jnp.int32, (blocks, width), 0)
    return jnp.where(lax.shift_right_logical(lane, 6) == row, 1.0, 0.0).astype(bf16)


def head_column(columns, head):
    lane = lax.broadcasted_iota(jnp.int32, columns.shape, 1)
    return jnp.sum(jnp.where(lane == head, columns, 0.0), 1, keepdims=True)


def pair_lanes(g):
    return pl.ds(pl.multiple_of(g * (2 * HD), 2 * HD), 2 * HD)


def forward_kernel(
    nz, W, MB, T,
    lens, tokens, attn_w, up_w, down_w, small_in, counts,
    out_o, xall_o, kv_o, q_o, att_o, mix_o, lse_o, first_o, second_o, hidden_o, top_o,
    attn_o, up_o, down_o, small_o,
    attn, up, down, small_all, small, xall, kv, q, att, mix, lse, top, first, second, hidden, out,
    wide,
    load_sem, w_send, w_recv, wf_send, wf_recv, s_send, s_recv,
    b_send, b_recv, f_send, f_recv, o_send, r_send, r_recv, save_sem,
):
    s, c, w = place()
    z, core = c // 2, lax.rem(c, 2)
    par = lax.rem(z, 2)
    part = D // W
    ffp = FF // W
    partner = {"ctx": c + 1 - 2 * core}
    buddy = {"ctx": (z + 1 - 2 * par) * 2 + core}
    xs = [{"wsh": lax.rem(w + k, W)} for k in range(1, W)]
    zs = [{"ctx": lax.rem(z + k, nz) * 2 + core} for k in range(1, nz)]
    over = [{"section": 1 - s, "ctx": lax.rem(z + k, nz) * 2 + core} for k in range(nz)]
    greet(xs + zs + over + [partner])

    def rows_of(zz, cc):
        return pl.ds(pl.multiple_of((zz * 2 + cc) * TD, TD), TD)

    def direct_rows(zz, cc):
        return pl.ds(pl.multiple_of((zz * 2 + cc) * TD, TD), BLK)

    def relay_rows(zz, cc):
        return pl.ds(pl.multiple_of((zz * 2 + cc) * TD + BLK, BLK), BLK)

    mine = rows_of(z, core)

    def token_push(m, k):
        peer = zs[k - 1] if m == 0 else over[k]
        return push(tokens.at[m, 0], xall.at[m, mine], b_send.at[m, k], b_recv.at[m, k], peer)

    def token_arrival(m, k):
        block = xall.at[m, rows_of(lax.rem(z + nz - k, nz), core)]
        return push(block, block, b_send.at[m, k], b_recv.at[m, k], partner)

    def own_tokens(m):
        return pltpu.make_async_copy(tokens.at[m, 0], xall.at[m, mine], b_recv.at[m, 0])

    def out_push(m, k):
        return push(
            out.at[m, 0:BLK],
            xall.at[m, direct_rows(z, core)],
            o_send.at[m, k],
            b_recv.at[m, k],
            over[k],
        )

    def out_arrival(m, k):
        block = xall.at[m, direct_rows(lax.rem(z + nz - k, nz), core)]
        return push(block, block, o_send.at[m, k], b_recv.at[m, k], partner)

    def out_relay(m):
        return push(
            out.at[m, BLK:TD],
            xall.at[m, relay_rows(z, core)],
            r_send.at[m, 0],
            r_recv.at[m, 0],
            over[0],
        )

    def relay_push(m, k):
        block = xall.at[m, relay_rows(z, core)]
        return push(block, block, r_send.at[m, k], r_recv.at[m, k], zs[k - 1])

    def relay_arrival(m, k):
        block = xall.at[m, relay_rows(lax.rem(z + nz - k, nz), core)]
        return push(block, block, r_send.at[m, k], r_recv.at[m, k], partner)

    def forward_push(m, k):
        zz = lax.rem(z + nz - k, nz)
        block = xall.at[m, rows_of(zz, core)]
        return push(block, block, f_send.at[m, k], f_recv.at[m, k], partner)

    def cut(base, ww, stride, rows, cc, zp, shared):
        share = rows // 4 if shared else rows // 2
        at = base + ww * stride + ((cc * 2 + zp) if shared else cc) * share
        return pl.ds(pl.multiple_of(at, 16), share)

    def piece(p, ww, cc, zp, local):
        stride = 0 if local else 1
        if p < 4:
            r = cut(0, ww, part * stride, part, cc, zp, False)
            matrix = (1, 2, 0, 3)[p]
            return attn_w.at[0, matrix, r] if local else attn.at[matrix, r]
        if p < 6:
            r = cut(0, ww, part * stride, part, cc, zp, True)
            cols = pl.ds((p - 4) * (FF // 2), FF // 2)
            return up_w.at[0, r, cols] if local else up.at[r, cols]
        base = (p - 6) * (ffp // 2)
        r = cut(base, ww, ffp * stride, ffp // 2, cc, zp, p == 6)
        return down_w.at[0, r] if local else down.at[r]

    shared = [p in (4, 5, 6) for p in range(8)]

    def weight_push(k, p):
        return push(
            piece(p, w, core, par, True),
            piece(p, w, core, par, False),
            w_send.at[k - 1, p],
            w_recv.at[k - 1, p],
            xs[k - 1],
        )

    def weight_forward(k, p, way):
        zp = 1 - par if way == 2 else par
        spot = piece(p, lax.rem(w + W - k, W), core, zp, False)
        peer = buddy if way == 1 else partner
        return push(spot, spot, wf_send.at[k - 1, p, way], wf_recv.at[k - 1, p, way], peer)

    def x_start(p):
        for k in range(1, W):
            weight_push(k, p).start()

    def x_arrive(p):
        for k in range(1, W):
            weight_push(k, p).wait_recv()
            weight_forward(k, p, 0).start()
            if shared[p]:
                weight_forward(k, p, 1).start()

    def z_arrive(p):
        for k in range(1, W):
            weight_forward(k, p, 1).wait_recv()
            weight_forward(k, p, 2).start()

    def core_arrive(p):
        for k in range(1, W):
            weight_forward(k, p, 0).wait_recv()
            if shared[p]:
                weight_forward(k, p, 2).wait_recv()

    def small_push(k):
        return push(small_in, small_all.at[k], s_send.at[k - 1], s_recv.at[k - 1], xs[k - 1])

    own_r = pl.ds(pl.multiple_of(w * part, 16), part)
    own_f = pl.ds(pl.multiple_of(w * ffp, 16), ffp)
    own_loads = [
        pltpu.make_async_copy(attn_w.at[0], attn.at[:, own_r], load_sem.at[0]),
        pltpu.make_async_copy(up_w.at[0], up.at[own_r], load_sem.at[1]),
        pltpu.make_async_copy(down_w.at[0], down.at[own_f], load_sem.at[2]),
    ]

    @pl.when(s == 0)
    def _():
        for k in range(1, nz):
            token_push(0, k).start()
        for m in range(MB):
            own_tokens(m).start()

    @pl.when(s == 1)
    def _():
        for m in range(1, MB):
            for k in range(1, nz):
                token_push(m, k).start()

    x_start(0)
    x_start(1)
    for k in range(1, W):
        small_push(k).start()
    for copy in own_loads:
        copy.start()

    def relay_start(m):
        out_relay(m).wait_recv()
        for k in range(1, nz):
            relay_push(m, k).start()

    def rows_ready(m):
        @pl.when(s == 0)
        def _():
            own_tokens(m).wait()

        @pl.when(s == 1)
        def _():
            out_arrival(m, 0).wait_recv()

        forward_push(m, 0).start()
        for k in range(1, nz):

            @pl.when(s == 0)
            def _():
                token_arrival(m, k).wait_recv()

            @pl.when(s == 1)
            def _():
                out_arrival(m, k).wait_recv()
                relay_arrival(m, k).wait_recv()

            forward_push(m, k).start()
        for k in range(nz):
            forward_push(m, k).wait_recv()

    saves = []

    def save(src, dst):
        copy = pltpu.make_async_copy(src, dst, save_sem.at[next(numbers)])
        copy.start()
        saves.append(copy)

    numbers = iter(range(100))
    lane = lax.broadcasted_iota(jnp.int32, (TD, 128), 1)
    row = lax.broadcasted_iota(jnp.int32, (TD, 128), 0)
    spots = lax.broadcasted_iota(jnp.int32, (1, T), 1)
    tops = jnp.full((1, 128), masked_score, f32)

    slots = kv.shape[0]

    @pl.when(s == 1)
    def _():
        for p in range(8):
            x_arrive(p)
            if p + 2 < 8:
                x_start(p + 2)
            if p and shared[p - 1]:
                z_arrive(p - 1)
        for p in range(8):
            core_arrive(p)
        relay_start(0)

    @pl.when(s == 0)
    def _():
        for p in range(3):
            x_arrive(p)
            x_start(p + 2)
        x_start(5)

    for k in range(1, W):
        small_push(k).wait_recv()
    total = small_in[...]
    for k in range(1, W):
        total = total + small_all[k]
    small[...] = total
    save(small, small_o)
    own_loads[0].wait()
    bias_v = small[0:1, :]

    for m in range(MB):
        rows_ready(m)
        if m + 1 < MB:

            @pl.when(s == 1)
            def _():
                relay_start(m + 1)

        if m == 0:

            @pl.when(s == 0)
            def _():
                for p in range(3):
                    core_arrive(p)

        save(xall.at[m], xall_o.at[m])

        def project(i, _):
            r = pl.ds(pl.multiple_of(i * 256, 256), 256)
            x = xall[m, r, :]
            kv[m % slots, r, 0:D] = dot(x, attn[1]).astype(bf16)
            kv[m % slots, r, D : 2 * D] = (dot(x, attn[2]) + bias_v).astype(bf16)
            return 0

        lax.fori_loop(0, T // 256, project, 0)
        save(kv.at[m % slots], kv_o.at[m])
        kept_kv = saves[-1]
        x_own = xall[m, mine, :]
        q[m] = (dot(x_own, attn[0]).astype(bf16).astype(f32) * (HD**-0.5)).astype(bf16)
        save(q.at[m], q_o.at[m])
        length = lens[m]
        live = spots < length
        weights = dot(counts[m].astype(bf16), block_lanes(T // BLK, T))
        weights = jnp.where(live, weights, 0.0)
        wide[...] = weights.reshape(PAIRS, 8, T)

        def attend(g, kept):
            lse_c, top_c = kept
            keys = kv[m % slots, :, pair_lanes(g)]
            values = kv[m % slots, :, pl.ds(pl.multiple_of(D + g * 128, 128), 128)]
            scores = dot_t(halves(q[m, :, pair_lanes(g)]), keys)
            count = spread4(wide[g], T)
            scores = jnp.where(count > 0, scores, masked_score)
            largest = jnp.max(scores, 1, keepdims=True)
            powers = jnp.exp(scores - largest) * count
            total = jnp.sum(powers, 1, keepdims=True)
            mixed = dot(powers.astype(bf16), values) / total
            mix[m, :, pair_lanes(g)] = joined(mixed)
            log_total = largest + jnp.log(total)
            for e in range(2):
                lse_c = jnp.where(lane == 2 * g + e, log_total[e * TD : (e + 1) * TD], lse_c)
                top_c = jnp.where(lane == 2 * g + e, largest[e * TD : (e + 1) * TD], top_c)
            return lse_c, top_c

        zeros = jnp.zeros((TD, 128), f32)
        lse_c, top_c = lax.fori_loop(0, PAIRS, attend, (zeros, zeros))
        lse[m] = lse_c
        if slots < MB:
            saves[:] = [x for x in saves if x is not kept_kv]
            kept_kv.wait()
        top_c = jnp.where(c * TD + row < length, top_c, masked_score)
        tops = jnp.maximum(tops, jnp.max(top_c, 0, keepdims=True))
        att[m] = mix[m].astype(bf16)
        save(lse.at[m], lse_o.at[m])
        save(mix.at[m], mix_o.at[m])
        save(att.at[m], att_o.at[m])
        if m < 2:

            @pl.when(s == 0)
            def _():
                if m == 0:
                    x_arrive(3)
                x_start(6 + m)

    if MB == 1:

        @pl.when(s == 0)
        def _():
            x_start(7)

    top[...] = jnp.broadcast_to(tops, (8, 128))
    save(top, top_o)

    @pl.when(s == 0)
    def _():
        core_arrive(3)

    for m in range(MB):
        branch = dot(att[m], attn[3]) + small[1:2, :]
        first[m] = xall[m, mine, :].astype(f32) + branch
        save(first.at[m], first_o.at[m])
    save(attn, attn_o)

    @pl.when(s == 0)
    def _():
        x_arrive(4)
        x_arrive(5)
        z_arrive(4)
        x_arrive(6)
        z_arrive(5)
        x_arrive(7)
        z_arrive(6)
        for p in range(4, 8):
            core_arrive(p)

    for copy in own_loads[1:]:
        copy.wait()
    save(up, up_o)
    save(down, down_o)

    for m in range(MB):
        hat, _ = norm_parts(first[m])
        normed = hat * small[5:6, :] + small[3:4, :]
        low = normed.astype(bf16)
        second[m] = normed + small[2:3, :]
        for j in range(NCH):
            cols = slice(j * CHUNK, (j + 1) * CHUNK)
            pre = dot(low, up[:, cols]) + small[7 + j : 8 + j, :]
            hidden[m, :, cols] = pre
            second[m] += dot(gelu(pre).astype(bf16), down[cols, :])
        hat, _ = norm_parts(second[m])
        out[m] = (hat * small[6:7, :] + small[4:5, :]).astype(bf16)

        save(hidden.at[m], hidden_o.at[m])
        save(second.at[m], second_o.at[m])
        save(out.at[m], out_o.at[0, m, 0])

        @pl.when(s == 0)
        def _():
            if m:
                for k in range(nz):
                    out_push(m - 1, k).wait_send()
            out_relay(m).start()
            out_relay(m).wait_send()
            for k in range(nz):
                out_push(m, k).start()


    for k in range(1, W):
        small_push(k).wait_send()
        for p in range(8):
            weight_push(k, p).wait_send()
            for way in range(3 if shared[p] else 1):
                weight_forward(k, p, way).wait_send()
    for m in range(MB):
        for k in range(nz):
            forward_push(m, k).wait_send()

        if m == MB - 1:

            @pl.when(s == 0)
            def _():
                for k in range(nz):
                    out_push(m, k).wait_send()

        @pl.when(s == 1)
        def _():
            for k in range(1, nz):
                relay_push(m, k).wait_send()

        @pl.when(s == (0 if m == 0 else 1))
        def _():
            for k in range(1, nz):
                token_push(m, k).wait_send()

    for copy in saves:
        copy.wait()


def sum_steps(r, nz, W, count, per):
    s, c, w = place()
    z, core = c // 2, lax.rem(c, 2)
    part = D // W
    root = (nz - 1) // 2
    partner = {"ctx": c + 1 - 2 * core}
    xs = [{"wsh": lax.rem(w + k, W)} for k in range(1, W)]
    grads, from_x, chain, sums = r.grads, r.from_x, r.chain, r.sums

    def spot(i, ww):
        at = (i // per) * D + ww * part + lax.rem(i, per) * ROWS
        return pl.ds(pl.multiple_of(at, 16), ROWS)

    def lines(i):
        return pl.ds(pl.multiple_of(i * ROWS, 16), ROWS)

    def x_push(i, k):
        return push(
            grads.at[spot(i, lax.rem(w + k, W))],
            from_x.at[k - 1, lines(i)],
            r.x_send.at[k - 1, i],
            r.x_recv.at[k - 1, i],
            xs[k - 1],
        )

    is_left = z < root
    to_left = {"ctx": jnp.maximum(z - 1, 0) * 2 + core}
    to_right = {"ctx": jnp.minimum(z + 1, nz - 1) * 2 + core}
    far = max(root, nz - 1 - root)
    depth = jnp.where(z == root, far, jnp.where(is_left, z, nz - 1 - z))
    away = jnp.where(is_left, root - z, z - root)

    def chain_push(i, side, peer):
        block = grads.at[spot(i, w)]
        return push(block, chain.at[side, lines(i)], r.ch_send.at[i], r.ch_recv.at[side, i], peer)

    def total_push(i, side, peer, block):
        return push(block, sums.at[core, lines(i)], r.t_send.at[side, i], r.t_recv.at[i], peer)

    def partner_push(i, block):
        return push(block, sums.at[core, lines(i)], r.p_send.at[i], r.p_recv.at[i], partner)

    def partner_arrival(i):
        block = sums.at[1 - core, lines(i)]
        return push(block, block, r.p_send.at[i], r.p_recv.at[i], partner)

    def own_copy(i):
        return pltpu.make_async_copy(grads.at[spot(i, w)], sums.at[core, lines(i)], r.o_sem.at[i])

    def begin():
        for i in range(FLIGHT):
            for k in range(1, W):
                x_push(i, k).start()

    def step(t):
        @pl.when(t + FLIGHT < count)
        def _():
            for k in range(1, W):
                x_push(t, k).wait_send()
                x_push(t + FLIGHT, k).start()

        i = t - LAG * depth

        @pl.when((i >= 0) & (i < count))
        def _():
            acc = grads[spot(i, w), :].astype(f32)
            for k in range(1, W):
                x_push(i, k).wait_recv()
                acc = acc + from_x[k - 1, lines(i), :].astype(f32)
            grads[spot(i, w), :] = acc.astype(bf16)

            @pl.when((z > 0) & (z <= root))
            def _():
                chain_push(i, 0, to_right).wait_recv()
                both = grads[spot(i, w), :].astype(f32) + chain[0, lines(i), :].astype(f32)
                grads[spot(i, w), :] = both.astype(bf16)

            @pl.when((z < nz - 1) & (z >= root))
            def _():
                chain_push(i, 1, to_left).wait_recv()
                both = grads[spot(i, w), :].astype(f32) + chain[1, lines(i), :].astype(f32)
                grads[spot(i, w), :] = both.astype(bf16)

            @pl.when(z < root)
            def _():
                chain_push(i, 0, to_right).start()

            @pl.when(z > root)
            def _():
                chain_push(i, 1, to_left).start()

            @pl.when(z == root)
            def _():
                block = grads.at[spot(i, w)]
                if root > 0:
                    total_push(i, 0, to_left, block).start()
                if root < nz - 1:
                    total_push(i, 1, to_right, block).start()
                partner_push(i, block).start()
                own_copy(i).start()

        b = t - LAG * (far + away)

        @pl.when((b >= 0) & (b < count) & (z != root))
        def _():
            block = sums.at[core, lines(b)]
            total_push(b, 0, to_left, block).wait_recv()

            @pl.when((z < root) & (z > 0))
            def _():
                total_push(b, 0, to_left, block).start()

            @pl.when((z > root) & (z < nz - 1))
            def _():
                total_push(b, 1, to_right, block).start()

            partner_push(b, block).start()

    last = count + LAG * 2 * far

    def drain():
        def one(i, _):
            block = sums.at[core, lines(i)]
            partner_arrival(i).wait_recv()
            partner_push(i, block).wait_send()

            @pl.when(i + FLIGHT >= count)
            def _():
                for k in range(1, W):
                    x_push(i, k).wait_send()

            @pl.when(z != root)
            def _():
                chain_push(i, 0, to_right).wait_send()

            @pl.when(z == root)
            def _():
                own_copy(i).wait()

            @pl.when((z <= root) & (z > 0))
            def _():
                total_push(i, 0, to_left, block).wait_send()

            @pl.when((z >= root) & (z < nz - 1))
            def _():
                total_push(i, 1, to_right, block).wait_send()

            return 0

        lax.fori_loop(0, count, one, 0)

    return begin, step, last, drain


def small_steps(r, nz, W):
    s, c, w = place()
    z, core = c // 2, lax.rem(c, 2)
    partner = {"ctx": c + 1 - 2 * core}
    xs = [{"wsh": lax.rem(w + k, W)} for k in range(1, W)]
    zs = [{"ctx": lax.rem(z + k, nz) * 2 + core} for k in range(1, nz)]

    def core_push(e):
        return push(r.core_s.at[e], r.core_s.at[e], r.sc_send, r.sc_recv, partner)

    def x_push(k, e):
        return push(
            r.wsh_s.at[e], r.wsh_s.at[e], r.sx_send.at[k - 1], r.sx_recv.at[k - 1], xs[k - 1]
        )

    def z_push(k, e):
        return push(r.z_s.at[e], r.z_s.at[e], r.sz_send.at[k - 1], r.sz_recv.at[k - 1], zs[k - 1])

    def first(value):
        r.core_s[core] = value
        core_push(core).start()

    def second():
        core_push(1 - core).wait_recv()
        r.wsh_s[w] = r.core_s[0] + r.core_s[1]
        for k in range(1, W):
            x_push(k, w).start()

    def third():
        for k in range(1, W):
            x_push(k, lax.rem(w + W - k, W)).wait_recv()
        total = r.wsh_s[0]
        for e in range(1, W):
            total = total + r.wsh_s[e]
        r.z_s[z] = total
        for k in range(1, nz):
            z_push(k, z).start()

    def finish():
        for k in range(1, nz):
            z_push(k, lax.rem(z + nz - k, nz)).wait_recv()
        total = r.z_s[0]
        for e in range(1, nz):
            total = total + r.z_s[e]
        r.small_o[...] = total
        core_push(core).wait_send()
        for k in range(1, W):
            x_push(k, w).wait_send()
        for k in range(1, nz):
            z_push(k, z).wait_send()

    return first, second, third, finish


def clip_weights(r, tops, own):
    factor = jnp.sqrt(clip_limit / jnp.maximum(tops, clip_limit))
    lane = lax.broadcasted_iota(jnp.int32, (128, D), 1)
    head = lax.broadcasted_iota(jnp.int32, (128, D), 0)
    heads = jnp.where(lax.shift_right_logical(lane, 6) == head, 1.0, 0.0).astype(f32)
    wide = jnp.dot(factor, heads, preferred_element_type=f32, precision=exact_dot)[0:1]
    for p in range(2):
        r.clip_o[0, p] = (own(p).astype(f32) * wide).astype(bf16)


def down_tiles(r, W):
    part, gate_half = D // W, FF // W // 2
    for e in range(W):
        cols = slice(e * gate_half, (e + 1) * gate_half)
        block = dot_0(r.lg[:, cols], r.rd[...]).astype(bf16)
        for j in range(2):
            at = j * D + e * part
            r.grads[at : at + part] = block[j * part : (j + 1) * part]


def up_tiles(r):
    for j in range(2):
        block = dot_0(r.ln[...], r.rh[:, j * D : (j + 1) * D])
        r.grads[(2 + j) * D : (3 + j) * D] = block.astype(bf16)


def attn_tiles(r):
    for j, (left, right) in enumerate(((r.la, r.ra), (r.lb, r.rb))):
        r.grads[(4 + j) * D : (5 + j) * D] = dot_0(left[...], right[...]).astype(bf16)


def ff_operands(W, cc, gated, down, normed, hidden, r):
    ffp = FF // W
    found = []
    for e in range(W):
        cols = pl.ds(pl.multiple_of(e * ffp + cc * (ffp // 2), 128), ffp // 2)
        found.append((gated.at[:, cols], r.lg, e * (ffp // 2), ffp // 2))
    cols = pl.ds(pl.multiple_of(cc * (FF // 2), 128), FF // 2)
    return found + [(down, r.rd, 0, D), (normed, r.ln, 0, D), (hidden.at[:, cols], r.rh, 0, FF // 2)]


def attn_operands(cc, qkv, att, branch, x, r):
    if cc == 0:
        return [(x, r.la), (qkv.at[:, 0:D], r.ra), (x, r.lb), (qkv.at[:, D : 2 * D], r.rb)]
    return [(x, r.la), (qkv.at[:, 2 * D : 3 * D], r.ra), (att, r.lb), (branch, r.rb)]


def reduce_kernel(nz, W, MB, r):
    s, c, w = place()
    z, core = c // 2, lax.rem(c, 2)
    part = D // W
    per = part // ROWS
    partner = {"ctx": c + 1 - 2 * core}
    xs = [{"wsh": lax.rem(w + k, W)} for k in range(1, W)]
    zs = [{"ctx": lax.rem(z + k, nz) * 2 + core} for k in range(1, nz)]
    greet(xs + zs + [partner])
    begin, step, last, drain = sum_steps(r, nz, W, 6 * per, per)
    small_first, small_second, small_third, small_finish = small_steps(r, nz, W)
    mine = pl.ds(pl.multiple_of(c * TD, TD), TD)

    def copies(m, cc, far):
        n = W + 3
        found = []
        rows = (r.gated_h.at[m], r.down_h.at[m], r.normed_h.at[m], r.hidden_h.at[m])
        side = (MB + m if far else m) * TD
        for e, (src, dst, at, width) in enumerate(ff_operands(W, cc, *rows, r)):
            spot = dst.at[side : side + TD, at : at + width]
            found.append((src, spot, m * (n + 4) + e))
        rows = (r.qkv_h.at[m], r.att_h.at[m], r.branch_h.at[m], r.x_h.at[m, mine])
        for e, (src, dst) in enumerate(attn_operands(cc, *rows, r)):
            found.append((src, dst.at[side : side + TD], m * (n + 4) + n + e))
        if far:
            return [push(a, b, r.c_send.at[e], r.c_recv.at[e], partner) for a, b, e in found]
        return [pltpu.make_async_copy(a, b, r.load_sem.at[e]) for a, b, e in found]

    own_load = pltpu.make_async_copy(r.attn_w.at[0, 0:2], r.own_w, r.own_sem)
    own_load.start()
    small_first(r.small_g[...])
    for cc in range(2):

        @pl.when(core == cc)
        def _():
            for m in range(MB):
                for copy in copies(m, 1 - cc, True) + copies(m, cc, False):
                    copy.start()
            for m in range(MB):
                for copy in copies(m, cc, False):
                    copy.wait()
                for copy in copies(m, cc, True):
                    copy.wait_recv()

    down_tiles(r, W)
    begin()
    up_tiles(r)
    attn_tiles(r)
    small_second()
    own_load.wait()
    clip_weights(r, r.tops[...], lambda p: r.own_w[p])
    small_third()

    def loop(t, _):
        step(t)
        return 0

    lax.fori_loop(0, last, loop, 0)
    small_finish()
    for cc in range(2):

        @pl.when(core == cc)
        def _():
            for m in range(MB):
                for copy in copies(m, 1 - cc, True):
                    copy.wait_send()

    drain()


def backward_kernel(nz, W, MB, T, fused, r):
    lens, cot, counts_q, counts_k, top, small = (
        r.lens, r.cot, r.counts_q, r.counts_k, r.top, r.small,
    )
    attn, up, down, xall, kv, q, mix, lse = r.attn, r.up, r.down, r.xall, r.kv, r.q, r.mix, r.lse
    first, second, hidden, dout, gfirst = r.first, r.second, r.hidden, r.dout, r.gfirst
    gbranch, gall, relay, aux, kvp = r.gbranch, r.gall, r.relay, r.aux, r.kvp
    wide_q, wide_k, lse_all, del_all, del_c = r.wide_q, r.wide_k, r.lse_all, r.del_all, r.del_c
    dqkv, gnorm, ghid, gated, gdown = r.dqkv, r.gnorm, r.ghid, r.gated, r.gdown
    small_g, gin, top_x = r.small_g, r.gin, r.top_x
    s, c, w = place()
    z, core = c // 2, lax.rem(c, 2)
    partner = {"ctx": c + 1 - 2 * core}
    xs = [{"wsh": lax.rem(w + k, W)} for k in range(1, W)]
    zs = [{"ctx": lax.rem(z + k, nz) * 2 + core} for k in range(1, nz)]
    across = {"section": 1 - s}
    over = [{"section": 1 - s, "ctx": lax.rem(z + k, nz) * 2 + core} for k in range(1, nz)]
    greet(xs + zs + over + [across, partner])
    part = D // W
    per = part // ROWS
    if fused:
        begin, step, last, drain = sum_steps(r, nz, W, 6 * per, per)
        small_first, small_second, small_third, small_finish = small_steps(r, nz, W)

    def rows_of(zz, cc):
        return pl.ds(pl.multiple_of((zz * 2 + cc) * TD, TD), TD)

    mine = rows_of(z, core)
    loads = []

    def load(src, dst):
        copy = pltpu.make_async_copy(src, dst, r.load_sem.at[len(loads)])
        copy.start()
        loads.append(copy)
        return copy

    saves = []
    numbers = iter(range(100))

    def save(src, dst):
        copy = pltpu.make_async_copy(src, dst, r.save_sem.at[next(numbers)])
        copy.start()
        saves.append(copy)

    def cot_load(m):
        return pltpu.make_async_copy(cot.at[m, 0], dout.at[m], r.y_recv.at[m])

    def grad_push(m):
        return push(gin.at[m], dout.at[m], r.y_send.at[m], r.y_recv.at[m], across)

    @pl.when(s == 1)
    def _():
        for m in range(MB):
            cot_load(m).start()

    slots = xall.shape[0]
    load_second = [load(r.second_h.at[m], second.at[m]) for m in range(MB)]
    cuts = [slice(j * CHUNK, (j + 1) * CHUNK) for j in range(NCH)]
    load_hidden, load_down, load_up = [[]], [], []
    for cut in cuts:
        load_hidden[0].append(load(r.hidden_h.at[0, :, cut], hidden.at[0, :, cut]))
        load_down.append(load(r.down_h.at[cut], down.at[cut]))
        load_up.append(load(r.up_h.at[:, cut], up.at[:, cut]))
    late = {}

    def load_rest():
        late["first"] = [load(r.first_h.at[m], first.at[m]) for m in range(MB)]
        late["attn"] = load(r.attn_h, attn)
        late["mix"] = [load(r.mix_h.at[m], mix.at[m]) for m in range(MB)]
        late["lse"] = [load(r.lse_h.at[m], lse.at[m]) for m in range(MB)]
        for m in range(1, slots):
            load_hidden.append([load(r.hidden_h.at[m], hidden.at[m])])
        late["x"] = [load(r.xall_h.at[m], xall.at[m]) for m in range(slots)]
        late["kv"] = [load(r.kv_h.at[m, mine], kv.at[m]) for m in range(MB)]
        late["q"] = [load(r.q_h.at[m], q.at[m]) for m in range(MB)]

    def cut_rows(zz, cc, side):
        return pl.ds(pl.multiple_of((zz * 2 + cc) * TD + side * BLK, BLK), BLK)

    def rows_push(m, k):
        if k == 0:
            block = gall.at[m, mine]
            return push(block, block, r.f_send.at[m, 0], r.f_recv.at[m, 0], partner)
        block = gall.at[m, cut_rows(z, core, 0)]
        return push(block, block, r.b_send.at[m, k], r.b_recv.at[m, k], zs[k - 1])

    def rows_arrival(m, k):
        block = gall.at[m, cut_rows(lax.rem(z + nz - k, nz), core, 0)]
        return push(block, block, r.b_send.at[m, k], r.b_recv.at[m, k], partner)

    def relay_out(m):
        block = gall.at[m, cut_rows(z, core, 1)]
        return push(block, relay.at[m], r.r_send.at[m, 0], r.r_recv.at[m, 0], across)

    def relay_push(m, k):
        block = gall.at[m, cut_rows(z, core, 1)]
        return push(relay.at[m], block, r.r_send.at[m, k], r.r_recv.at[m, k], over[k - 1])

    def relay_arrival(m, k):
        block = gall.at[m, cut_rows(lax.rem(z + nz - k, nz), core, 1)]
        return push(block, block, r.r_send.at[m, k], r.r_recv.at[m, k], partner)

    def rows_forward(m, k):
        block = gall.at[m, rows_of(lax.rem(z + nz - k, nz), core)]
        return push(block, block, r.f_send.at[m, k], r.f_recv.at[m, k], partner)

    def aux_push(m, k):
        block = aux.at[m, c]
        peer = partner if k == 0 else zs[k - 1]
        send, recv = (r.af_send, r.af_recv) if k == 0 else (r.a_send, r.a_recv)
        return push(block, block, send.at[m, k], recv.at[m, k], peer)

    def aux_arrival(m, k):
        block = aux.at[m, lax.rem(z + nz - k, nz) * 2 + core]
        return push(block, block, r.a_send.at[m, k], r.a_recv.at[m, k], partner)

    def aux_forward(m, k):
        block = aux.at[m, lax.rem(z + nz - k, nz) * 2 + core]
        return push(block, block, r.af_send.at[m, k], r.af_recv.at[m, k], partner)

    def top_push(k):
        return push(top_x.at[0], top_x.at[k], r.tp_send.at[k - 1], r.tp_recv.at[k - 1], xs[k - 1])

    def spread_start(m):
        relay_out(m).start()
        for k in range(nz):
            aux_push(m, k).start()
            rows_push(m, k).start()

    def spread_sent(m):
        relay_out(m).wait_send()
        for k in range(1, nz):
            rows_push(m, k).wait_send()

    def relay_one(m):
        relay_out(m).wait_recv()
        for k in range(1, nz):
            relay_push(m, k).start()

    def rows_copies(m, cc, far, late):
        side = (MB + m if far else m) * TD
        found = []
        if late:
            rows = (dqkv.at[m], r.att_h.at[m], gbranch.at[m], r.xall_h.at[m, mine])
            for e, (src, dst) in enumerate(attn_operands(cc, *rows, r)):
                found.append((src, dst.at[side : side + TD], m * (W + 7) + W + 3 + e))
        else:
            rows = (gated.at[m], gdown.at[m], gnorm.at[m], ghid.at[m])
            for e, (src, dst, at, width) in enumerate(ff_operands(W, cc, *rows, r)):
                found.append((src, dst.at[side : side + TD, at : at + width], m * (W + 7) + e))
        if far:
            return [push(a, b, r.c_send.at[e], r.c_recv.at[e], partner) for a, b, e in found]
        return [pltpu.make_async_copy(a, b, r.c_load.at[e]) for a, b, e in found]

    def rows_start(m, late):
        for cc in range(2):

            @pl.when(core == cc)
            def _():
                for copy in rows_copies(m, 1 - cc, True, late) + rows_copies(m, cc, False, late):
                    copy.start()

    def rows_here(late, picked):
        for cc in range(2):

            @pl.when(core == cc)
            def _():
                for m in range(MB):
                    for copy in rows_copies(m, cc, False, late)[picked]:
                        copy.wait()
                    for copy in rows_copies(m, cc, True, late)[picked]:
                        copy.wait_recv()

    def ff_gradients():
        rows_here(False, slice(0, W + 1))
        down_tiles(r, W)
        begin()
        rows_here(False, slice(W + 1, None))
        up_tiles(r)

    def rows_sent():
        for cc in range(2):

            @pl.when(core == cc)
            def _():
                for m in range(MB):
                    for late in (False, True):
                        for copy in rows_copies(m, 1 - cc, True, late):
                            copy.wait_send()

    @pl.when(s == 0)
    def _():
        for m in range(MB):
            relay_one(m)

    heads = lax.broadcasted_iota(jnp.int32, (D, 128), 0)
    heads = lax.shift_right_logical(heads, 6) == lax.broadcasted_iota(jnp.int32, (D, 128), 1)
    heads = jnp.where(heads, 1.0, 0.0).astype(f32)
    small_g[...] = jnp.zeros_like(small_g)

    for m in range(MB):
        load_second[m].wait()

        @pl.when(s == 1)
        def _():
            cot_load(m).wait()

        @pl.when(s == 0)
        def _():
            grad_push(m).wait_recv()

        grad_out = dout[m].astype(f32)
        hat, rstd = norm_parts(second[m])
        small_g[1:2, :] += column_sum(grad_out * hat)
        small_g[6:7, :] += column_sum(grad_out)
        grad_second = norm_back(grad_out, hat, rstd, small[6:7, :])
        low_second = grad_second.astype(bf16)
        gdown[m] = low_second
        if not fused:
            save(gdown.at[m], r.rows_down.at[m])
        small_g[4:5, :] += column_sum(low_second.astype(f32))
        if m >= slots:
            load_hidden.append([load(r.hidden_h.at[m], hidden.at[m % slots])])
            for copy in hidden_saves:
                saves[:] = [x for x in saves if x is not copy]
                copy.wait()
        if m:
            load_hidden[m][0].wait()
        gfirst[m] = grad_second
        for j in range(NCH):
            cols = slice(j * CHUNK, (j + 1) * CHUNK)
            if m == 0:
                load_hidden[0][j].wait()
                load_down[j].wait()
                if j == NCH - 1:
                    load_rest()
            value, slope = gelu_both(hidden[m % slots, :, cols])
            gated[m % slots, :, cols] = value.astype(bf16)
            grad_hidden = (slope * dot_t(low_second, down[cols, :])).astype(bf16)
            ghid[m % slots, :, cols] = grad_hidden
            small_g[7 + j : 8 + j, :] += column_sum(grad_hidden.astype(f32))
            if m == 0:
                load_up[j].wait()
            gfirst[m] += dot_t(grad_hidden, up[:, cols])
        if not fused:
            save(gated.at[m % slots], r.rows_gated.at[m])
            save(ghid.at[m % slots], r.rows_hidden.at[m])
            hidden_saves = saves[-2:]
        grad_normed = gfirst[m]
        late["first"][m].wait()
        hat, rstd = norm_parts(first[m])
        gnorm[m] = (hat * small[5:6, :] + small[3:4, :]).astype(bf16)
        small_g[0:1, :] += column_sum(grad_normed * hat)
        small_g[5:6, :] += column_sum(grad_normed)
        grad_first = norm_back(grad_normed, hat, rstd, small[5:6, :])
        gfirst[m] = grad_first
        low_first = grad_first.astype(bf16)
        gbranch[m] = low_first
        if not fused:
            save(gnorm.at[m], r.rows_normed.at[m])
            save(gbranch.at[m], r.rows_branch.at[m])
        small_g[3:4, :] += column_sum(low_first.astype(f32))
        late["mix"][m].wait()
        late["lse"][m].wait()
        if m == 0:
            late["attn"].wait()
        grad_att = dot_t(low_first, attn[3]).astype(bf16)
        gall[m, mine, :] = grad_att
        weighed = grad_att.astype(f32) * mix[m]
        delta = jnp.dot(weighed, heads, preferred_element_type=f32, precision=exact_dot)
        del_c[m] = delta
        aux[m, c, 0:16] = lse[m].T[0:16]
        aux[m, c, 16:32] = delta.T[0:16]
        aux[m, c, 32:40] = top[...]
        if m == 0:
            spread_start(0)
        elif m == 1:

            @pl.when(s == 0)
            def _():
                spread_sent(0)
                spread_start(1)

        if fused:
            rows_start(m, False)

    if fused:

        @pl.when(s == 0)
        def _():
            ff_gradients()

    def paced(at):
        if not fused:
            return lambda g: None

        def run(g):
            @pl.when((s == 0) & (lax.rem(g, PACE) == PACE - 1))
            def _():
                step(at * (PAIRS // PACE) + g // PACE)

        return run

    spots = lax.broadcasted_iota(jnp.int32, (1, T), 1)
    here = lax.broadcasted_iota(jnp.int32, (TD, 128), 0)
    for m in range(MB):
        if m >= slots:
            late["x"].append(load(r.xall_h.at[m], xall.at[m % slots]))
        for name in ("x", "kv", "q"):
            late[name][m].wait()

        def stream(g):
            slot = lax.rem(g, 2)
            return [
                pltpu.make_async_copy(
                    r.kv_h.at[m, :, pl.ds(pl.multiple_of(e * D + g * 128, 128), 128)],
                    kvp.at[slot, e],
                    r.kvp_sem.at[slot, e],
                )
                for e in range(2)
            ]

        for copy in stream(0):
            copy.start()
        length = lens[m]
        lanes = block_lanes(T // BLK, T)
        counted = jnp.where(spots < length, dot(counts_q[m].astype(bf16), lanes), 0.0)
        counted = jnp.where(counted > 0, jnp.log(jnp.maximum(counted, 1.0)), masked_score)
        wide_q[...] = counted.reshape(PAIRS, 8, T)
        advance = paced(2 * m)

        def own_rows(g, _):
            @pl.when(g + 1 < PAIRS)
            def _():
                for copy in stream(g + 1):
                    copy.start()

            for copy in stream(g):
                copy.wait()
            slot = lax.rem(g, 2)
            lse_c = jnp.concatenate([head_column(lse[m], 2 * g + e) for e in range(2)], 0)
            delta = jnp.concatenate([head_column(del_c[m], 2 * g + e) for e in range(2)], 0)
            queries = halves(q[m, :, pair_lanes(g)])
            grads = halves(gall[m, mine, pair_lanes(g)])
            grad_q = jnp.zeros((2 * TD, 2 * HD), f32)
            for t in range(0, T, STEP):
                keys = kvp[slot, 0, t : t + STEP]
                values = kvp[slot, 1, t : t + STEP]
                shift = wide_q[g, :, t : t + STEP]
                probs = jnp.exp(dot_t(queries, keys) + spread4(shift, STEP) - lse_c)
                grad_probs = dot_t(grads, values)
                grad_scores = (probs * (grad_probs - delta)).astype(bf16)
                grad_q = grad_q + dot(grad_scores, keys)
            dqkv[m, :, pair_lanes(g)] = (joined(grad_q) * (HD**-0.5)).astype(bf16)
            advance(g)
            return 0

        lax.fori_loop(0, PAIRS, own_rows, 0)
        if m + 1 < MB:

            @pl.when((s == 1) | (m > 0))
            def _():
                spread_sent(m)
                spread_start(m + 1)

        def project(i, _):
            rows = pl.ds(pl.multiple_of(i * 256, 256), 256)
            all_q = dot(xall[m % slots, rows, :], attn[0]).astype(bf16).astype(f32)
            xall[m % slots, rows, :] = (all_q * (HD**-0.5)).astype(bf16)
            return 0

        lax.fori_loop(0, T // 256, project, 0)
        for k in range(1, nz):
            rows_arrival(m, k).wait_recv()
            relay_arrival(m, k).wait_recv()
            rows_forward(m, k).start()
            aux_arrival(m, k).wait_recv()
            aux_forward(m, k).start()
        for k in range(nz):
            rows_forward(m, k).wait_recv()
            aux_forward(m, k).wait_recv()
        for cc in range(2 * nz):
            lse_all[:, cc * TD : (cc + 1) * TD] = aux[m, cc, 0:16]
            del_all[:, cc * TD : (cc + 1) * TD] = aux[m, cc, 16:32]
        if m == 0:
            most = aux[0, 0, 32:40]
            for cc in range(1, 2 * nz):
                most = jnp.maximum(most, aux[0, cc, 32:40])
            top_x[0] = most
            for k in range(1, W):
                top_push(k).start()
        counted = dot(counts_k[m].astype(bf16), lanes)
        counted = jnp.where(counted > 0, jnp.log(jnp.maximum(counted, 1.0)), masked_score)
        wide_k[...] = counted.reshape(PAIRS, 8, T)
        live = c * TD + here < length
        advance_keys = paced(2 * m + 1)

        def own_keys(g, _):
            keys = halves(kv[m, :, pair_lanes(g)])
            values = halves(kv[m, :, pl.ds(pl.multiple_of(D + g * 128, 128), 128)])
            lse_r = [lse_all[pl.ds(2 * g + e, 1), :] for e in range(2)]
            delta = [del_all[pl.ds(2 * g + e, 1), :] for e in range(2)]
            shift = wide_k[g]
            shift = jnp.concatenate([shift[0:2] - lse_r[0], shift[2:4] - lse_r[1]], 0)
            grad_k = jnp.zeros((2 * TD, 2 * HD), f32)
            grad_v = jnp.zeros((2 * TD, 2 * HD), f32)
            for t in range(0, T, STEP):
                queries = xall[m % slots, t : t + STEP, pair_lanes(g)]
                grads = gall[m, t : t + STEP, pair_lanes(g)]
                probs = jnp.exp(dot_t(keys, queries) + spread4(shift[:, t : t + STEP], STEP))
                grad_v = grad_v + dot(probs.astype(bf16), grads)
                centre = jnp.concatenate(
                    [jnp.broadcast_to(d[:, t : t + STEP], (TD, STEP)) for d in delta], 0
                )
                grad_scores = (probs * (dot_t(values, grads) - centre)).astype(bf16)
                grad_k = grad_k + dot(grad_scores, queries)
            grad_k, grad_v = joined(grad_k), joined(grad_v)
            lanes_k = pl.ds(pl.multiple_of(D + g * 128, 128), 128)
            lanes_v = pl.ds(pl.multiple_of(2 * D + g * 128, 128), 128)
            dqkv[m, :, lanes_k] = jnp.where(live, grad_k, 0.0).astype(bf16)
            dqkv[m, :, lanes_v] = jnp.where(live, grad_v, 0.0).astype(bf16)
            advance_keys(g)
            return 0

        lax.fori_loop(0, PAIRS, own_keys, 0)
        if fused:
            rows_start(m, True)
        else:
            save(dqkv.at[m], r.rows_qkv.at[m])
        small_g[2:3, :] += column_sum(dqkv[m, :, 2 * D :].astype(f32))
        total = gfirst[m]
        for p in range(3):
            total = total + dot_t(dqkv[m, :, p * D : (p + 1) * D], attn[p])
        gin[m] = total.astype(bf16)

        @pl.when(s == 1)
        def _():
            grad_push(m).start()

        save(gin.at[m], r.grad_in_o.at[0, m, 0])

    def loop(t, _):
        step(t)
        return 0

    if fused:
        small_first(small_g[...])
        done_1 = EARLY

        @pl.when(s == 1)
        def _():
            relay_one(0)
            ff_gradients()
            lax.fori_loop(0, EARLY, loop, 0)
            for m in range(1, MB):
                relay_one(m)

        rows_here(True, slice(None))
        attn_tiles(r)
        small_second()
        done_0 = 2 * MB * (PAIRS // PACE)
        now = jnp.where(s == 0, done_0, done_1)
        lax.fori_loop(now, now + 3, loop, 0)
        small_third()
    else:

        @pl.when(s == 1)
        def _():
            for m in range(MB):
                relay_one(m)

        save(small_g, r.small_o)
    for k in range(1, W):
        top_push(k).wait()
    most = top_x[0]
    for k in range(1, W):
        most = jnp.maximum(most, top_x[k])
    if fused:
        clip_weights(
            r, most, lambda p: attn[p, pl.ds(pl.multiple_of(w * part, 16), part), :]
        )
        lax.fori_loop(now + 3, last, loop, 0)
        small_finish()
        rows_sent()
        drain()
    else:
        r.top_o[...] = most
    for m in range(MB):
        for k in range(nz):
            rows_forward(m, k).wait_send()
            aux_forward(m, k).wait_send()
        for k in range(1, nz):
            aux_push(m, k).wait_send()
            relay_push(m, k).wait_send()
        if m == MB - 1:
            spread_sent(m)

        @pl.when(s == 1)
        def _():
            grad_push(m).wait_send()

    for copy in saves:
        copy.wait()


def widen_kernel(sums, attn_o, up_o, down_o):
    t = pl.program_id(0)
    rows = sums[0].astype(f32)

    @pl.when(t < 4)
    def _():
        down_o[...] = rows

    @pl.when((t >= 4) & (t < 8))
    def _():
        up_o[...] = rows

    @pl.when(t >= 8)
    def _():
        attn_o[0, 0] = rows


def counts_of(seq_lengths, rand_owner, rand_local, global_raw, c, n_ctx):
    blocks = BLK_DEV * n_ctx
    length = seq_lengths[:, 0]
    valid = (length + BLK - 1) // BLK
    chosen = global_raw[:, 0] % valid[:, None]
    random = rand_owner[:, 0] * BLK_DEV + rand_local[:, 0]
    ids = jnp.arange(blocks)
    near = (jnp.abs(ids[:, None] - ids[None, :]) <= 1).astype(jnp.int32)
    named = jnp.sum((random[..., None] == ids).astype(jnp.int32), 3)
    is_global = chosen[..., None] == ids
    glob = jnp.sum(is_global.astype(jnp.int32), 1)
    wide_row = jnp.any(is_global, 1)
    table = named + near[None, :, None, :] + glob[:, None, None, :]
    table = jnp.where(wide_row[:, :, None, None], 1, table).astype(f32)
    mb = table.shape[0]
    by_q = lax.dynamic_slice_in_dim(table, c * BLK_DEV, BLK_DEV, 1)
    by_k = lax.dynamic_slice_in_dim(table, c * BLK_DEV, BLK_DEV, 3)
    by_q = by_q.transpose(0, 2, 1, 3).reshape(mb, PAIRS, 4, blocks)
    by_k = by_k.transpose(0, 2, 3, 1).reshape(mb, PAIRS, 4, blocks)
    both = jnp.pad(jnp.stack([by_q, by_k]), ((0, 0), (0, 0), (0, 0), (0, 4), (0, 0)))
    both = both.reshape(2, mb, PAIRS * 8, blocks)
    return both[0], both[1]


VMEM = pl.BlockSpec(memory_space=pltpu.VMEM)
SMEM = pl.BlockSpec(memory_space=pltpu.SMEM)
ANY = pl.BlockSpec(memory_space=pl.ANY)
DMA = pltpu.SemaphoreType.DMA


def slots_of(T, MB):
    return MB if T <= 2048 else 1


def run_forward(nz, W, MB, lens, tokens, attn_w, up_w, down_w, small_in, counts):
    T = 2 * nz * TD
    shape = jax.ShapeDtypeStruct
    outs = [
        shape((1, MB, 1, TD, D), bf16),
        shape((MB, T, D), bf16),
        shape((MB, T, 2 * D), bf16),
        shape((MB, TD, D), bf16),
        shape((MB, TD, D), bf16),
        shape((MB, TD, D), f32),
        shape((MB, TD, 128), f32),
        shape((MB, TD, D), f32),
        shape((MB, TD, D), f32),
        shape((MB, TD, FF), f32),
        shape((8, 128), f32),
        shape((4, D, D), bf16),
        shape((D, FF), bf16),
        shape((FF, D), bf16),
        shape((16, D), f32),
    ]
    scratch = [
        pltpu.VMEM((4, D, D), bf16),
        pltpu.VMEM((D, FF), bf16),
        pltpu.VMEM((FF, D), bf16),
        pltpu.VMEM((W, 16, D), f32),
        pltpu.VMEM((16, D), f32),
        pltpu.VMEM((MB, T, D), bf16),
        pltpu.VMEM((slots_of(T, MB), T, 2 * D), bf16),
        pltpu.VMEM((MB, TD, D), bf16),
        pltpu.VMEM((MB, TD, D), bf16),
        pltpu.VMEM((MB, TD, D), f32),
        pltpu.VMEM((MB, TD, 128), f32),
        pltpu.VMEM((8, 128), f32),
        pltpu.VMEM((MB, TD, D), f32),
        pltpu.VMEM((MB, TD, D), f32),
        pltpu.VMEM((MB, TD, FF), f32),
        pltpu.VMEM((MB, TD, D), bf16),
        pltpu.VMEM((PAIRS, 8, T), f32),
        DMA((3,)),
        DMA((W - 1, 8)),
        DMA((W - 1, 8)),
        DMA((W - 1, 8, 3)),
        DMA((W - 1, 8, 3)),
        DMA((W - 1,)),
        DMA((W - 1,)),
        DMA((MB, nz)),
        DMA((MB, nz)),
        DMA((MB, nz)),
        DMA((MB, nz)),
        DMA((MB, nz)),
        DMA((MB, nz)),
        DMA((MB, nz)),
        DMA((5 + 10 * MB,)),
    ]
    return pl.pallas_call(
        functools.partial(forward_kernel, nz, W, MB, T),
        out_shape=outs,
        in_specs=[SMEM, ANY, ANY, ANY, ANY, VMEM, VMEM],
        out_specs=[ANY] * len(outs),
        scratch_shapes=scratch,
        compiler_params=pltpu.CompilerParams(
            collective_id=0, has_side_effects=True, vmem_limit_bytes=60 << 20
        ),
        name="forward",
    )(lens, tokens, attn_w, up_w, down_w, small_in, counts)


def call(kernel, name, number, limit, ins, outs, scratch):
    names = list(ins) + list(outs) + list(scratch)

    def body(*refs):
        kernel(types.SimpleNamespace(**dict(zip(names, refs, strict=True))))

    found = pl.pallas_call(
        body,
        out_shape=[jax.ShapeDtypeStruct(*v[:2]) for v in outs.values()],
        in_specs=[v[1] for v in ins.values()],
        out_specs=[v[2] for v in outs.values()],
        scratch_shapes=list(scratch.values()),
        compiler_params=pltpu.CompilerParams(
            collective_id=number, has_side_effects=True, vmem_limit_bytes=limit << 20
        ),
        name=name,
    )(*(v[0] for v in ins.values()))
    return dict(zip(outs, found))


def sum_scratch(nz, W, MB):
    part, R = D // W, MB * TD
    count = 6 * (part // ROWS)
    copies = MB * (W + 7)
    return dict(
        lg=pltpu.VMEM((2 * R, FF // 2), bf16),
        rd=pltpu.VMEM((2 * R, D), bf16),
        ln=pltpu.VMEM((2 * R, D), bf16),
        rh=pltpu.VMEM((2 * R, FF // 2), bf16),
        la=pltpu.VMEM((2 * R, D), bf16),
        ra=pltpu.VMEM((2 * R, D), bf16),
        lb=pltpu.VMEM((2 * R, D), bf16),
        rb=pltpu.VMEM((2 * R, D), bf16),
        from_x=pltpu.VMEM((W - 1, 6 * part, D), bf16),
        chain=pltpu.VMEM((2, 6 * part, D), bf16),
        core_s=pltpu.VMEM((2, 16, D), f32),
        wsh_s=pltpu.VMEM((W, 16, D), f32),
        z_s=pltpu.VMEM((nz, 16, D), f32),
        c_send=DMA((copies,)),
        c_recv=DMA((copies,)),
        c_load=DMA((copies,)),
        x_send=DMA((W - 1, count)),
        x_recv=DMA((W - 1, count)),
        ch_send=DMA((count,)),
        ch_recv=DMA((2, count)),
        t_send=DMA((2, count)),
        t_recv=DMA((count,)),
        p_send=DMA((count,)),
        p_recv=DMA((count,)),
        o_sem=DMA((count,)),
        sc_send=DMA,
        sc_recv=DMA,
        sx_send=DMA((W - 1,)),
        sx_recv=DMA((W - 1,)),
        sz_send=DMA((nz - 1,)),
        sz_recv=DMA((nz - 1,)),
    )


def sum_outs(W):
    part = D // W
    return dict(
        sums=((2, 6 * part, D), bf16, ANY),
        small_o=((16, D), f32, VMEM),
        clip_o=((1, 2, part, D), bf16, VMEM),
    )


def run_backward(nz, W, MB, fused, lens, cot, counts_q, counts_k, saved):
    T = 2 * nz * TD
    slots = slots_of(T, MB)
    ins = dict(
        lens=(lens, SMEM),
        cot=(cot, ANY),
        counts_q=(counts_q, VMEM),
        counts_k=(counts_k, VMEM),
        **{k: (v, VMEM if k in ("top", "small") else ANY) for k, v in saved.items()},
    )
    outs = dict(grad_in_o=((1, MB, 1, TD, D), bf16, ANY))
    if fused:
        outs.update(sum_outs(W))
    else:
        outs.update(
            rows_qkv=((MB, TD, 3 * D), bf16, ANY),
            rows_branch=((MB, TD, D), bf16, ANY),
            rows_normed=((MB, TD, D), bf16, ANY),
            rows_hidden=((MB, TD, FF), bf16, ANY),
            rows_gated=((MB, TD, FF), bf16, ANY),
            rows_down=((MB, TD, D), bf16, ANY),
            small_o=((16, D), f32, ANY),
            top_o=((8, 128), f32, VMEM),
        )
    scratch = dict(
        attn=pltpu.VMEM((4, D, D), bf16),
        up=pltpu.VMEM((D, FF), bf16),
        down=pltpu.VMEM((FF + 2 * D if fused else FF, D), bf16),
        xall=pltpu.VMEM((slots, T, D), bf16),
        kv=pltpu.VMEM((MB, TD, 2 * D), bf16),
        q=pltpu.VMEM((MB, TD, D), bf16),
        mix=pltpu.VMEM((MB, TD, D), f32),
        lse=pltpu.VMEM((MB, TD, 128), f32),
        first=pltpu.VMEM((MB, TD, D), f32),
        second=pltpu.VMEM((MB, TD, D), f32),
        hidden=pltpu.VMEM((slots, TD, FF), f32),
        dout=pltpu.VMEM((MB, TD, D), bf16),
        gfirst=pltpu.VMEM((MB, TD, D), f32),
        gbranch=pltpu.VMEM((MB, TD, D), bf16),
        gall=pltpu.VMEM((MB, T, D), bf16),
        relay=pltpu.VMEM((MB, BLK, D), bf16),
        aux=pltpu.VMEM((MB, 2 * nz, 40, 128), f32),
        kvp=pltpu.VMEM((2, 2, T, 2 * HD), bf16),
        wide_q=pltpu.VMEM((PAIRS, 8, T), f32),
        wide_k=pltpu.VMEM((PAIRS, 8, T), f32),
        lse_all=pltpu.VMEM((16, T), f32),
        del_all=pltpu.VMEM((16, T), f32),
        del_c=pltpu.VMEM((MB, TD, 128), f32),
        dqkv=pltpu.VMEM((MB, TD, 3 * D), bf16),
        gnorm=pltpu.VMEM((MB, TD, D), bf16),
        ghid=pltpu.VMEM((slots, TD, FF), bf16),
        gated=pltpu.VMEM((slots, TD, FF), bf16),
        gdown=pltpu.VMEM((MB, TD, D), bf16),
        small_g=pltpu.VMEM((16, D), f32),
        gin=pltpu.VMEM((MB, TD, D), bf16),
        top_x=pltpu.VMEM((W, 8, 128), f32),
        load_sem=DMA((1 + 3 * NCH + 8 * MB,)),
        y_send=DMA((MB,)),
        y_recv=DMA((MB,)),
        tp_send=DMA((W - 1,)),
        tp_recv=DMA((W - 1,)),
        kvp_sem=DMA((2, 2)),
        save_sem=DMA((1 + 7 * MB,)),
        **{k: DMA((MB, nz)) for k in RINGS},
    )
    if fused:
        scratch.update(sum_scratch(nz, W, MB))

    def kernel(r):
        if fused:
            r.grads = r.down
        backward_kernel(nz, W, MB, T, fused, r)

    return call(kernel, "backward", 1, 63 if fused else 60, ins, outs, scratch)


def run_reduce(nz, W, MB, ins):
    part = D // W
    scratch = sum_scratch(nz, W, MB)
    scratch.update(
        grads=pltpu.VMEM((6 * D, D), bf16),
        own_w=pltpu.VMEM((2, part, D), bf16),
        load_sem=DMA((MB * (W + 7),)),
        own_sem=DMA,
    )
    ins = {k: (v, VMEM if k in ("small_g", "tops") else ANY) for k, v in ins.items()}
    return call(
        functools.partial(reduce_kernel, nz, W, MB), "reduce", 2, 60, ins, sum_outs(W), scratch
    )


def widen(sums, W):
    part, ffp = D // W, FF // W

    def source(t):
        return (lax.rem(t, 4) // 2, (t // 4) * 2 + lax.rem(t, 2), 0)

    return pl.pallas_call(
        widen_kernel,
        grid=(12,),
        out_shape=[
            jax.ShapeDtypeStruct((1, 4, part, D), f32),
            jax.ShapeDtypeStruct((part, FF), f32),
            jax.ShapeDtypeStruct((ffp, D), f32),
        ],
        in_specs=[pl.BlockSpec((1, part, D), source)],
        out_specs=[
            pl.BlockSpec((1, 1, part, D), lambda t: (0, jnp.maximum(t - 8, 0), 0, 0)),
            pl.BlockSpec((part, D), lambda t: (0, jnp.clip(t - 4, 0, 3))),
            pl.BlockSpec((part, D), lambda t: (jnp.minimum(t, 3), 0)),
        ],
        compiler_params=pltpu.CompilerParams(vmem_limit_bytes=40 << 20),
        name="widen",
    )(sums)


def per_device(
    tokens, out_cotangent, attn_weights, up_weights, down_weights, norm_gains, bias_rows, up_bias,
    seq_lengths, rand_owner, rand_local, global_raw,
):
    n_ctx, W = lax.axis_size("ctx"), lax.axis_size("wsh")
    nz = n_ctx // 2
    c, w = lax.axis_index("ctx"), lax.axis_index("wsh")
    MB = tokens.shape[0]
    part, ffp = D // W, FF // W
    rows = jnp.concatenate([bias_rows[0], norm_gains[0]], 0).astype(f32)
    rows = lax.dynamic_update_slice(jnp.zeros((7, D), f32), rows, (0, w * part))
    wide = lax.dynamic_update_slice(jnp.zeros((FF,), f32), up_bias[0].astype(f32), (w * ffp,))
    small_in = jnp.concatenate([rows, wide.reshape(NCH, CHUNK), jnp.zeros((5, D), f32)], 0)
    counts_q, counts_k = counts_of(seq_lengths, rand_owner, rand_local, global_raw, c, n_ctx)
    lens = seq_lengths[:, 0]
    (
        out, xall, kv, q, att, mix, lse, first, second, hidden, top, attn, up, down, small,
    ) = run_forward(nz, W, MB, lens, tokens, attn_weights, up_weights, down_weights, small_in, counts_q)
    fused = W == 2 and n_ctx * TD <= 2048
    saved = dict(
        xall_h=xall, kv_h=kv, q_h=q, mix_h=mix, lse_h=lse, first_h=first, second_h=second,
        hidden_h=hidden, top=top, attn_h=attn, up_h=up, down_h=down, small=small,
    )
    if fused:
        saved["att_h"] = att
    got = run_backward(nz, W, MB, fused, lens, out_cotangent, counts_q, counts_k, saved)
    grad_in = got["grad_in_o"]
    if not fused:
        names = ("gated", "down", "normed", "hidden", "qkv", "branch")
        rows = {k + "_h": got["rows_" + k] for k in names}
        rows.update(
            att_h=att, x_h=xall, small_g=got["small_o"], tops=got["top_o"], attn_w=attn_weights
        )
        got = run_reduce(nz, W, MB, rows)
    small_g, clipped_qk = got["small_o"], got["clip_o"]
    grad_attn, grad_up, grad_down = widen(got["sums"], W)
    gains = lax.dynamic_slice(small_g[0:2], (0, w * part), (2, part))
    biases = lax.dynamic_slice(small_g[2:7], (0, w * part), (5, part))
    up_grad = lax.dynamic_slice(small_g[7:11].reshape(-1), (w * ffp,), (ffp,))
    return (
        out, grad_in, grad_attn, grad_up[None], grad_down[None], gains[None], biases[None],
        up_grad[None], clipped_qk,
    )


def solution(mesh):
    placed = (
        P(None, "wsh", "ctx", None),
        P(None, "wsh", "ctx", None),
        P("section", None, "wsh", None),
        P("section", "wsh", None),
        P("section", "wsh", None),
        P("section", None, "wsh"),
        P("section", None, "wsh"),
        P("section", "wsh"),
        P(None, "wsh"),
        P(None, "wsh", None, None, None),
        P(None, "wsh", None, None, None),
        P(None, "wsh", None),
    )
    return jax.shard_map(
        per_device,
        mesh=mesh,
        in_specs=placed,
        out_specs=(
            P("section", None, "wsh", "ctx", None),
            P("section", None, "wsh", "ctx", None),
            P("section", None, "wsh", None),
            P("section", "wsh", None),
            P("section", "wsh", None),
            P("section", None, "wsh"),
            P("section", None, "wsh"),
            P("section", "wsh"),
            P("section", None, "wsh", None),
        ),
        check_vma=False,
    )
```

```python
import functools
import types

import jax
import jax.numpy as jnp
from jax import lax
from jax.experimental import pallas as pl
from jax.experimental.pallas import tpu as pltpu
from jax.sharding import PartitionSpec as P

D = 768
H = 12
HD = 64
FF = 3072
BLK = 64
TD = 128
BLK_DEV = 2
RND = 3
PAIRS = H // 2
CHUNK = 768
NCH = FF // CHUNK
STEP = 1024
ROWS = 48
FLIGHT = 4
LAG = 3
PACE = 1
EARLY = 4
BUFFERS = 4
V_RINGS = [a + b for a in ("b", "f", "r") for b in ("_send", "_recv")] + ["o_send"]
RINGS = [a + b for a in ("b", "f", "a", "af", "r") for b in ("_send", "_recv")]

MESH = pl.DeviceIdType.MESH
norm_eps = 1e-05
clip_limit = 6.0
masked_score = -1e30
exact_dot = lax.Precision.HIGHEST
f32 = jnp.float32
bf16 = jnp.bfloat16


def dot(a, b):
    return jnp.dot(a, b, preferred_element_type=f32)


def dot_t(a, b):
    return lax.dot_general(a, b, (((1,), (1,)), ((), ())), preferred_element_type=f32)


def dot_0(a, b):
    return lax.dot_general(a, b, (((0,), (0,)), ((), ())), preferred_element_type=f32)


def column_sum(v):
    return jnp.sum(v, 0, keepdims=True)


def norm_parts(v):
    center = v - jnp.mean(v, -1, keepdims=True)
    rstd = lax.rsqrt(jnp.mean(center * center, -1, keepdims=True) + norm_eps)
    return center * rstd, rstd


def norm_back(grad, hat, rstd, gain):
    scaled = grad * gain
    return rstd * (
        scaled
        - jnp.mean(scaled, -1, keepdims=True)
        - hat * jnp.mean(scaled * hat, -1, keepdims=True)
    )


def gelu(v):
    return 0.5 * v * (1.0 + lax.erf(v * (0.5**0.5)))


def gelu_both(v):
    phi = 0.5 * (1.0 + lax.erf(v * (0.5**0.5)))
    return v * phi, phi + v * jnp.exp(-0.5 * v * v) * 0.3989422804014327


def place():
    return lax.axis_index("section"), lax.axis_index("ctx"), lax.axis_index("wsh")


def greet(peers):
    barrier = pltpu.get_barrier_semaphore()
    for peer in peers:
        pl.semaphore_signal(barrier, inc=1, device_id=peer, device_id_type=MESH)
    pl.semaphore_wait(barrier, len(peers))


def push(src, dst, send, recv, peer):
    return pltpu.make_async_remote_copy(
        src_ref=src, dst_ref=dst, send_sem=send, recv_sem=recv, device_id=peer, device_id_type=MESH
    )


def halves(rows):
    low = lax.broadcasted_iota(jnp.int32, rows.shape, 1) < HD
    zero = jnp.zeros_like(rows)
    return jnp.concatenate([jnp.where(low, rows, zero), jnp.where(low, zero, rows)], 0)


def joined(rows):
    low = lax.broadcasted_iota(jnp.int32, (TD, 2 * HD), 1) < HD
    return jnp.where(low, rows[:TD], rows[TD:])


def spread4(rows, width):
    return jnp.concatenate(
        [jnp.broadcast_to(rows[r : r + 1], (BLK, width)) for r in range(4)], 0
    )


def block_lanes(blocks, width):
    lane = lax.broadcasted_iota(jnp.int32, (blocks, width), 1)
    row = lax.broadcasted_iota(jnp.int32, (blocks, width), 0)
    return jnp.where(lax.shift_right_logical(lane, 6) == row, 1.0, 0.0).astype(bf16)


def value_lanes(g):
    return pl.ds(pl.multiple_of(D + g * (2 * HD), 2 * HD), 2 * HD)


def head_column(columns, head):
    lane = lax.broadcasted_iota(jnp.int32, columns.shape, 1)
    return jnp.sum(jnp.where(lane == head, columns, 0.0), 1, keepdims=True)


def pair_lanes(g):
    return pl.ds(pl.multiple_of(g * (2 * HD), 2 * HD), 2 * HD)


def count_tables(m, lens, chosen, random, c, blocks):
    rows, names = PAIRS * 8, H * RND
    valid = (lens[m] + BLK - 1) // BLK
    picked = [lax.rem(chosen[m, 0, k], valid) for k in range(2)]
    table = random[m]
    row = lax.broadcasted_iota(jnp.int32, (rows, blocks), 0)
    lane = lax.broadcasted_iota(jnp.int32, (rows, blocks), 1)
    here = c * BLK_DEV + lax.rem(row, BLK_DEV)
    near = jnp.where(jnp.abs(lane - here) <= 1, 1.0, 0.0)

    def is_picked(ids):
        return [jnp.where(ids == p, 1.0, 0.0) for p in picked]

    kind = lax.broadcasted_iota(jnp.int32, (rows, names), 0)
    name = lax.broadcasted_iota(jnp.int32, (rows, names), 1)
    owner = (kind // 8) * 2 + lax.rem(kind, 8) // BLK_DEV
    same = (lax.rem(kind, 8) < 4) & (name // RND == owner)
    diagonal = jnp.where(
        lax.broadcasted_iota(jnp.int32, (names, names), 0)
        == lax.broadcasted_iota(jnp.int32, (names, names), 1),
        1.0,
        0.0,
    )
    lanes = lax.broadcasted_iota(jnp.int32, (names, blocks), 1).astype(f32)
    by_q = near + sum(is_picked(lane))
    by_k = near + sum(is_picked(here))
    for side in range(BLK_DEV):
        pick = jnp.where(same & (lax.rem(kind, BLK_DEV) == side), 1.0, 0.0).astype(bf16)
        own = random[m, pl.ds(c * BLK_DEV + side, 1), :].astype(f32)
        column = dot((diagonal * own).astype(bf16), jnp.ones((names, blocks), bf16))
        by_q += dot(pick, jnp.where(column == lanes, 1.0, 0.0).astype(bf16))
        match = jnp.where(table == c * BLK_DEV + side, 1.0, 0.0).astype(bf16)
        by_k += dot_t(pick, match)
    return (
        jnp.where(sum(is_picked(here)) > 0, 1.0, by_q),
        jnp.where(sum(is_picked(lane)) > 0, 1.0, by_k),
    )


class Spare:
    def __getattr__(self, name):
        return self

    def __getitem__(self, at):
        return self


def forward_part(nz, W, MB, T, fused, r):
    lens, chosen, random, tokens = r.lens, r.chosen, r.random, r.tokens
    attn_w, up_w, down_w, bias_w, gain_w, up_b = (
        r.attn_w, r.up_w, r.down_w, r.bias_w, r.gain_w, r.up_b,
    )
    attn, up, down, small_in, small_all, small = (
        r.attn, r.up, r.down, r.small_in, r.small_all, r.small,
    )
    xall, kv, q, att, mix, lse, top = r.xall, r.kv, r.q, r.att, r.mix, r.lse, r.top
    first, second, hidden, out, wide, counts = (
        r.first, r.second, r.hidden, r.out, r.wide_q, r.counts,
    )
    s, c, w = place()
    z, core = c // 2, lax.rem(c, 2)
    par = lax.rem(z, 2)
    part = D // W
    ffp = FF // W
    partner = {"ctx": c + 1 - 2 * core}
    buddy = {"ctx": (z + 1 - 2 * par) * 2 + core}
    xs = [{"wsh": lax.rem(w + k, W)} for k in range(1, W)]
    zs = [{"ctx": lax.rem(z + k, nz) * 2 + core} for k in range(1, nz)]
    over = [{"section": 1 - s, "ctx": lax.rem(z + k, nz) * 2 + core} for k in range(nz)]
    greet(xs + zs + over + [partner])

    def rows_of(zz, cc):
        return pl.ds(pl.multiple_of((zz * 2 + cc) * TD, TD), TD)

    def direct_rows(zz, cc):
        return pl.ds(pl.multiple_of((zz * 2 + cc) * TD, TD), BLK)

    def relay_rows(zz, cc):
        return pl.ds(pl.multiple_of((zz * 2 + cc) * TD + BLK, BLK), BLK)

    mine = rows_of(z, core)

    def token_push(m, k):
        peer = zs[k - 1] if m == 0 else over[k]
        return push(tokens.at[m, 0], xall.at[m, mine], r.v_b_send.at[m, k], r.v_b_recv.at[m, k], peer)

    def token_arrival(m, k):
        block = xall.at[m, rows_of(lax.rem(z + nz - k, nz), core)]
        return push(block, block, r.v_b_send.at[m, k], r.v_b_recv.at[m, k], partner)

    def own_tokens(m):
        return pltpu.make_async_copy(tokens.at[m, 0], xall.at[m, mine], r.v_b_recv.at[m, 0])

    def out_push(m, k):
        return push(
            out.at[m, 0:BLK],
            xall.at[m, direct_rows(z, core)],
            r.v_o_send.at[m, k],
            r.v_b_recv.at[m, k],
            over[k],
        )

    def out_arrival(m, k):
        block = xall.at[m, direct_rows(lax.rem(z + nz - k, nz), core)]
        return push(block, block, r.v_o_send.at[m, k], r.v_b_recv.at[m, k], partner)

    def out_relay(m):
        return push(
            out.at[m, BLK:TD],
            xall.at[m, relay_rows(z, core)],
            r.v_r_send.at[m, 0],
            r.v_r_recv.at[m, 0],
            over[0],
        )

    def relay_push(m, k):
        block = xall.at[m, relay_rows(z, core)]
        return push(block, block, r.v_r_send.at[m, k], r.v_r_recv.at[m, k], zs[k - 1])

    def relay_arrival(m, k):
        block = xall.at[m, relay_rows(lax.rem(z + nz - k, nz), core)]
        return push(block, block, r.v_r_send.at[m, k], r.v_r_recv.at[m, k], partner)

    def forward_push(m, k):
        zz = lax.rem(z + nz - k, nz)
        block = xall.at[m, rows_of(zz, core)]
        return push(block, block, r.v_f_send.at[m, k], r.v_f_recv.at[m, k], partner)

    def cut(base, ww, stride, rows, cc, zp, shared):
        share = rows // 4 if shared else rows // 2
        at = base + ww * stride + ((cc * 2 + zp) if shared else cc) * share
        return pl.ds(pl.multiple_of(at, 16), share)

    def piece(p, ww, cc, zp, local):
        stride = 0 if local else 1
        if p < 4:
            r = cut(0, ww, part * stride, part, cc, zp, False)
            matrix = (1, 2, 0, 3)[p]
            return attn_w.at[0, matrix, r] if local else attn.at[matrix, r]
        if p < 6:
            r = cut(0, ww, part * stride, part, cc, zp, True)
            cols = pl.ds((p - 4) * (FF // 2), FF // 2)
            return up_w.at[0, r, cols] if local else up.at[r, cols]
        base = (p - 6) * (ffp // 2)
        r = cut(base, ww, ffp * stride, ffp // 2, cc, zp, p == 6)
        return down_w.at[0, r] if local else down.at[r]

    shared = [p in (4, 5, 6) for p in range(8)]

    def weight_push(k, p):
        return push(
            piece(p, w, core, par, True),
            piece(p, w, core, par, False),
            r.v_w_send.at[k - 1, p],
            r.v_w_recv.at[k - 1, p],
            xs[k - 1],
        )

    def weight_forward(k, p, way):
        zp = 1 - par if way == 2 else par
        spot = piece(p, lax.rem(w + W - k, W), core, zp, False)
        peer = buddy if way == 1 else partner
        return push(spot, spot, r.v_wf_send.at[k - 1, p, way], r.v_wf_recv.at[k - 1, p, way], peer)

    def x_start(p):
        for k in range(1, W):
            weight_push(k, p).start()

    def x_arrive(p):
        for k in range(1, W):
            weight_push(k, p).wait_recv()
            weight_forward(k, p, 0).start()
            if shared[p]:
                weight_forward(k, p, 1).start()

    def z_arrive(p):
        for k in range(1, W):
            weight_forward(k, p, 1).wait_recv()
            weight_forward(k, p, 2).start()

    def core_arrive(p):
        for k in range(1, W):
            weight_forward(k, p, 0).wait_recv()
            if shared[p]:
                weight_forward(k, p, 2).wait_recv()

    def small_push(k):
        return push(small_in, small_all.at[k], r.v_s_send.at[k - 1], r.v_s_recv.at[k - 1], xs[k - 1])

    own_r = pl.ds(pl.multiple_of(w * part, 16), part)
    own_f = pl.ds(pl.multiple_of(w * ffp, 16), ffp)
    own_loads = [
        pltpu.make_async_copy(attn_w.at[0], attn.at[:, own_r], r.v_load_sem.at[0]),
        pltpu.make_async_copy(up_w.at[0], up.at[own_r], r.v_load_sem.at[1]),
        pltpu.make_async_copy(down_w.at[0], down.at[own_f], r.v_load_sem.at[2]),
    ]

    @pl.when(s == 0)
    def _():
        for k in range(1, nz):
            token_push(0, k).start()
        for m in range(MB):
            own_tokens(m).start()

    @pl.when(s == 1)
    def _():
        for m in range(1, MB):
            for k in range(1, nz):
                token_push(m, k).start()

    x_start(0)
    x_start(1)
    for copy in own_loads:
        copy.start()
    small_in[...] = jnp.zeros_like(small_in)
    span = ffp // D
    for e in range(W):

        @pl.when(w == e)
        def _():
            cols = slice(e * part, (e + 1) * part)
            small_in[0:5, cols] = bias_w[0].astype(f32)
            small_in[5:7, cols] = gain_w[0].astype(f32)
            for j in range(span):
                at = 7 + e * span + j
                small_in[at : at + 1, :] = up_b[0:1, j * D : (j + 1) * D].astype(f32)

    for k in range(1, W):
        small_push(k).start()
    for m in range(MB):
        counts[0, m], counts[1, m] = count_tables(m, lens, chosen, random, c, T // BLK)

    def relay_start(m):
        out_relay(m).wait_recv()
        for k in range(1, nz):
            relay_push(m, k).start()

    def rows_ready(m):
        @pl.when(s == 0)
        def _():
            own_tokens(m).wait()

        @pl.when(s == 1)
        def _():
            out_arrival(m, 0).wait_recv()

        forward_push(m, 0).start()
        for k in range(1, nz):

            @pl.when(s == 0)
            def _():
                token_arrival(m, k).wait_recv()

            @pl.when(s == 1)
            def _():
                out_arrival(m, k).wait_recv()
                relay_arrival(m, k).wait_recv()

            forward_push(m, k).start()
        for k in range(nz):
            forward_push(m, k).wait_recv()

    saves = []
    outs = Spare() if fused else r

    def save(src, dst, always=False):
        if fused and not always:
            return
        copy = pltpu.make_async_copy(src, dst, r.v_save_sem.at[next(numbers)])
        copy.start()
        saves.append(copy)

    numbers = iter(range(100))
    lane = lax.broadcasted_iota(jnp.int32, (TD, 128), 1)
    row = lax.broadcasted_iota(jnp.int32, (TD, 128), 0)
    spots = lax.broadcasted_iota(jnp.int32, (1, T), 1)
    tops = jnp.full((1, 128), masked_score, f32)

    slots = kv.shape[0]

    def feed_copies(m):
        pairs = [(out.at[m], r.out_o.at[0, m, 0])]
        if not fused:
            pairs += [
                (first.at[m], outs.first_o.at[m]),
                (hidden.at[m], outs.hidden_o.at[m]),
                (second.at[m], outs.second_o.at[m]),
            ]
        return [
            pltpu.make_async_copy(a, b, r.v_ff_sem.at[m, e]) for e, (a, b) in enumerate(pairs)
        ]

    weight_copies = []
    if not fused:
        pairs = ((attn, outs.attn_o), (up, outs.up_o), (down, outs.down_o))
        weight_copies = [
            pltpu.make_async_copy(a, b, r.v_ff_sem.at[MB, e]) for e, (a, b) in enumerate(pairs)
        ]

    def weights_whole():
        for copy in own_loads[1:]:
            copy.wait()
        for copy in weight_copies:
            copy.start()

    def feed_in(m):
        branch = dot(att[m], attn[3]) + small[1:2, :]
        first[m] = xall[m, mine, :].astype(f32) + branch

    def feed(m):
        hat, _ = norm_parts(first[m])
        normed = hat * small[5:6, :] + small[3:4, :]
        low = normed.astype(bf16)
        second[m] = normed + small[2:3, :]
        for j in range(NCH):
            cols = slice(j * CHUNK, (j + 1) * CHUNK)
            pre = dot(low, up[:, cols]) + small[7 + j : 8 + j, :]
            hidden[m, :, cols] = pre
            second[m] += dot(gelu(pre).astype(bf16), down[cols, :])
        hat, _ = norm_parts(second[m])
        out[m] = (hat * small[6:7, :] + small[4:5, :]).astype(bf16)
        for copy in feed_copies(m):
            copy.start()

    @pl.when(s == 1)
    def _():
        for p in range(8):
            x_arrive(p)
            if p + 2 < 8:
                x_start(p + 2)
            if p and shared[p - 1]:
                z_arrive(p - 1)
        for p in range(8):
            core_arrive(p)
        weights_whole()
        relay_start(0)

    @pl.when(s == 0)
    def _():
        for p in range(3):
            x_arrive(p)
            x_start(p + 2)
        x_start(5)

    for k in range(1, W):
        small_push(k).wait_recv()
    total = small_in[...]
    for k in range(1, W):
        total = total + small_all[k]
    small[...] = total
    save(small, outs.small_o)
    own_loads[0].wait()
    bias_v = small[0:1, :]

    for m in range(MB):
        rows_ready(m)
        if m + 1 < MB:

            @pl.when(s == 1)
            def _():
                relay_start(m + 1)

        if m == 0:

            @pl.when(s == 0)
            def _():
                for p in range(3):
                    core_arrive(p)

        save(xall.at[m], r.xall_o.at[m], True)

        def project(i, _):
            r = pl.ds(pl.multiple_of(i * 256, 256), 256)
            x = xall[m, r, :]
            kv[m % slots, r, 0:D] = dot(x, attn[1]).astype(bf16)
            kv[m % slots, r, D : 2 * D] = (dot(x, attn[2]) + bias_v).astype(bf16)
            return 0

        lax.fori_loop(0, T // 256, project, 0)
        save(kv.at[m % slots], outs.kv_o.at[m])
        kept_kv = saves[-1] if saves else None
        x_own = xall[m, mine, :]
        q[m] = (dot(x_own, attn[0]).astype(bf16).astype(f32) * (HD**-0.5)).astype(bf16)
        save(q.at[m], outs.q_o.at[m])
        length = lens[m]
        live = spots < length
        weights = dot(counts[0, m].astype(bf16), block_lanes(T // BLK, T))
        weights = jnp.where(live, weights, 0.0)
        wide[...] = weights.reshape(PAIRS, 8, T)

        def attend(g, kept):
            lse_c, top_c = kept
            keys = kv[m % slots, :, pair_lanes(g)]
            values = kv[m % slots, :, pl.ds(pl.multiple_of(D + g * 128, 128), 128)]
            scores = dot_t(halves(q[m, :, pair_lanes(g)]), keys)
            count = spread4(wide[g], T)
            scores = jnp.where(count > 0, scores, masked_score)
            largest = jnp.max(scores, 1, keepdims=True)
            powers = jnp.exp(scores - largest) * count
            total = jnp.sum(powers, 1, keepdims=True)
            mixed = dot(powers.astype(bf16), values) / total
            mix[m, :, pair_lanes(g)] = joined(mixed)
            log_total = largest + jnp.log(total)
            for e in range(2):
                lse_c = jnp.where(lane == 2 * g + e, log_total[e * TD : (e + 1) * TD], lse_c)
                top_c = jnp.where(lane == 2 * g + e, largest[e * TD : (e + 1) * TD], top_c)
            return lse_c, top_c

        zeros = jnp.zeros((TD, 128), f32)
        lse_c, top_c = lax.fori_loop(0, PAIRS, attend, (zeros, zeros), unroll=2)
        lse[m] = lse_c
        if slots < MB:
            saves[:] = [x for x in saves if x is not kept_kv]
            kept_kv.wait()
        top_c = jnp.where(c * TD + row < length, top_c, masked_score)
        tops = jnp.maximum(tops, jnp.max(top_c, 0, keepdims=True))
        att[m] = mix[m].astype(bf16)
        save(lse.at[m], outs.lse_o.at[m])
        save(mix.at[m], outs.mix_o.at[m])
        save(att.at[m], outs.att_o.at[m])

        @pl.when(s == 1)
        def _():
            feed_in(m)
            feed(m)

        if m < 2:

            @pl.when(s == 0)
            def _():
                if m == 0:
                    x_arrive(3)
                x_start(6 + m)

    if MB == 1:

        @pl.when(s == 0)
        def _():
            x_start(7)

    top[...] = jnp.broadcast_to(tops, (8, 128))
    save(top, outs.top_o)

    @pl.when(s == 0)
    def _():
        core_arrive(3)
        for m in range(MB):
            feed_in(m)
        x_arrive(4)
        x_arrive(5)
        z_arrive(4)
        x_arrive(6)
        z_arrive(5)
        x_arrive(7)
        z_arrive(6)
        for p in range(4, 8):
            core_arrive(p)
        weights_whole()
        for m in range(MB):
            feed(m)
            if m:
                for k in range(nz):
                    out_push(m - 1, k).wait_send()
            out_relay(m).start()
            out_relay(m).wait_send()
            for k in range(nz):
                out_push(m, k).start()

    def finish():
        for k in range(1, W):
            small_push(k).wait_send()
            for p in range(8):
                weight_push(k, p).wait_send()
                for way in range(3 if shared[p] else 1):
                    weight_forward(k, p, way).wait_send()
        for m in range(MB):
            for k in range(nz):
                forward_push(m, k).wait_send()

            if m == MB - 1:

                @pl.when(s == 0)
                def _():
                    for k in range(nz):
                        out_push(m, k).wait_send()

            @pl.when(s == 1)
            def _():
                for k in range(1, nz):
                    relay_push(m, k).wait_send()

            @pl.when(s == (0 if m == 0 else 1))
            def _():
                for k in range(1, nz):
                    token_push(m, k).wait_send()

        for copy in saves + weight_copies:
            copy.wait()
        for m in range(MB):
            for copy in feed_copies(m):
                copy.wait()

    return finish


def sum_steps(r, nz, W, count, per):
    s, c, w = place()
    z, core = c // 2, lax.rem(c, 2)
    part = D // W
    root = (nz - 1) // 2
    partner = {"ctx": c + 1 - 2 * core}
    xs = [{"wsh": lax.rem(w + k, W)} for k in range(1, W)]
    grads, from_x, chain, sums = r.grads, r.from_x, r.chain, r.sums

    def spot(i, ww):
        at = (i // per) * D + ww * part + lax.rem(i, per) * ROWS
        return pl.ds(pl.multiple_of(at, 16), ROWS)

    def lines(i):
        return pl.ds(pl.multiple_of(i * ROWS, 16), ROWS)

    def x_push(i, k):
        return push(
            grads.at[spot(i, lax.rem(w + k, W))],
            from_x.at[k - 1, lines(i)],
            r.x_send.at[k - 1, i],
            r.x_recv.at[k - 1, i],
            xs[k - 1],
        )

    is_left = z < root
    to_left = {"ctx": jnp.maximum(z - 1, 0) * 2 + core}
    to_right = {"ctx": jnp.minimum(z + 1, nz - 1) * 2 + core}
    far = max(root, nz - 1 - root)
    depth = jnp.where(z == root, far, jnp.where(is_left, z, nz - 1 - z))
    away = jnp.where(is_left, root - z, z - root)

    def chain_push(i, side, peer):
        block = grads.at[spot(i, w)]
        return push(block, chain.at[side, lines(i)], r.ch_send.at[i], r.ch_recv.at[side, i], peer)

    def total_push(i, side, peer, block):
        return push(block, sums.at[core, lines(i)], r.t_send.at[side, i], r.t_recv.at[i], peer)

    def partner_push(i, block):
        return push(block, sums.at[core, lines(i)], r.p_send.at[i], r.p_recv.at[i], partner)

    def partner_arrival(i):
        block = sums.at[1 - core, lines(i)]
        return push(block, block, r.p_send.at[i], r.p_recv.at[i], partner)

    def own_copy(i):
        return pltpu.make_async_copy(grads.at[spot(i, w)], sums.at[core, lines(i)], r.o_sem.at[i])

    def begin():
        for i in range(FLIGHT):
            for k in range(1, W):
                x_push(i, k).start()

    def step(t):
        @pl.when(t + FLIGHT < count)
        def _():
            for k in range(1, W):
                x_push(t, k).wait_send()
                x_push(t + FLIGHT, k).start()

        i = t - LAG * depth

        @pl.when((i >= 0) & (i < count))
        def _():
            acc = grads[spot(i, w), :].astype(f32)
            for k in range(1, W):
                x_push(i, k).wait_recv()
                acc = acc + from_x[k - 1, lines(i), :].astype(f32)
            grads[spot(i, w), :] = acc.astype(bf16)

            @pl.when((z > 0) & (z <= root))
            def _():
                chain_push(i, 0, to_right).wait_recv()
                both = grads[spot(i, w), :].astype(f32) + chain[0, lines(i), :].astype(f32)
                grads[spot(i, w), :] = both.astype(bf16)

            @pl.when((z < nz - 1) & (z >= root))
            def _():
                chain_push(i, 1, to_left).wait_recv()
                both = grads[spot(i, w), :].astype(f32) + chain[1, lines(i), :].astype(f32)
                grads[spot(i, w), :] = both.astype(bf16)

            @pl.when(z < root)
            def _():
                chain_push(i, 0, to_right).start()

            @pl.when(z > root)
            def _():
                chain_push(i, 1, to_left).start()

            @pl.when(z == root)
            def _():
                block = grads.at[spot(i, w)]
                if root > 0:
                    total_push(i, 0, to_left, block).start()
                if root < nz - 1:
                    total_push(i, 1, to_right, block).start()
                partner_push(i, block).start()
                own_copy(i).start()

        b = t - LAG * (far + away)

        @pl.when((b >= 0) & (b < count) & (z != root))
        def _():
            block = sums.at[core, lines(b)]
            total_push(b, 0, to_left, block).wait_recv()

            @pl.when((z < root) & (z > 0))
            def _():
                total_push(b, 0, to_left, block).start()

            @pl.when((z > root) & (z < nz - 1))
            def _():
                total_push(b, 1, to_right, block).start()

            partner_push(b, block).start()

    last = count + LAG * 2 * far

    def drain(begin, end):
        def one(i, _):
            block = sums.at[core, lines(i)]
            partner_arrival(i).wait_recv()
            partner_push(i, block).wait_send()

            @pl.when(i + FLIGHT >= count)
            def _():
                for k in range(1, W):
                    x_push(i, k).wait_send()

            @pl.when(z != root)
            def _():
                chain_push(i, 0, to_right).wait_send()

            @pl.when(z == root)
            def _():
                own_copy(i).wait()

            @pl.when((z <= root) & (z > 0))
            def _():
                total_push(i, 0, to_left, block).wait_send()

            @pl.when((z >= root) & (z < nz - 1))
            def _():
                total_push(i, 1, to_right, block).wait_send()

            return 0

        lax.fori_loop(begin, end, one, 0)

    def tail(now, small):
        settled = jnp.maximum(now, LAG * 2 * far + 4)

        def one(t, _):
            step(t)
            i = t - settled
            drain(jnp.clip(i, 0, count), jnp.clip(i + 1, 0, count))
            return 0

        lax.fori_loop(now, last, one, 0)
        small()
        drain(jnp.clip(last - settled, 0, count), count)

    return begin, step, tail


def small_steps(r, nz, W):
    s, c, w = place()
    z, core = c // 2, lax.rem(c, 2)
    partner = {"ctx": c + 1 - 2 * core}
    xs = [{"wsh": lax.rem(w + k, W)} for k in range(1, W)]
    zs = [{"ctx": lax.rem(z + k, nz) * 2 + core} for k in range(1, nz)]

    def core_push(e):
        return push(r.core_s.at[e], r.core_s.at[e], r.sc_send, r.sc_recv, partner)

    def x_push(k, e):
        return push(
            r.wsh_s.at[e], r.wsh_s.at[e], r.sx_send.at[k - 1], r.sx_recv.at[k - 1], xs[k - 1]
        )

    def z_push(k, e):
        return push(r.z_s.at[e], r.z_s.at[e], r.sz_send.at[k - 1], r.sz_recv.at[k - 1], zs[k - 1])

    def first(value):
        r.core_s[core] = value
        core_push(core).start()

    def second():
        core_push(1 - core).wait_recv()
        r.wsh_s[w] = r.core_s[0] + r.core_s[1]
        for k in range(1, W):
            x_push(k, w).start()

    def third():
        for k in range(1, W):
            x_push(k, lax.rem(w + W - k, W)).wait_recv()
        total = r.wsh_s[0]
        for e in range(1, W):
            total = total + r.wsh_s[e]
        r.z_s[z] = total
        for k in range(1, nz):
            z_push(k, z).start()

    def finish():
        for k in range(1, nz):
            z_push(k, lax.rem(z + nz - k, nz)).wait_recv()
        total = r.z_s[0]
        for e in range(1, nz):
            total = total + r.z_s[e]
        r.small_o[...] = total
        core_push(core).wait_send()
        for k in range(1, W):
            x_push(k, w).wait_send()
        for k in range(1, nz):
            z_push(k, z).wait_send()

    return first, second, third, finish


def clip_weights(r, tops, own, spare):
    factor = jnp.sqrt(clip_limit / jnp.maximum(tops, clip_limit))
    lane = lax.broadcasted_iota(jnp.int32, (128, D), 1)
    head = lax.broadcasted_iota(jnp.int32, (128, D), 0)
    heads = jnp.where(lax.shift_right_logical(lane, 6) == head, 1.0, 0.0).astype(f32)
    wide = jnp.dot(factor, heads, preferred_element_type=f32, precision=exact_dot)[0:1]
    for p in range(2):
        spare[p][...] = (own(p).astype(f32) * wide).astype(bf16)
    copies = [pltpu.make_async_copy(spare[p], r.clip_o.at[0, p], r.clip_sem.at[p]) for p in range(2)]
    for copy in copies:
        copy.start()
    return copies


def down_tiles(r, W):
    part, gate_half = D // W, FF // W // 2
    for e in range(W):
        cols = slice(e * gate_half, (e + 1) * gate_half)
        block = dot_0(r.lg[:, cols], r.rd[...]).astype(bf16)
        for j in range(2):
            at = j * D + e * part
            r.grads[at : at + part] = block[j * part : (j + 1) * part]


def up_tiles(r):
    for j in range(2):
        block = dot_0(r.ln[...], r.rh[:, j * D : (j + 1) * D])
        r.grads[(2 + j) * D : (3 + j) * D] = block.astype(bf16)


def attn_tiles(r):
    for j, (left, right) in enumerate(((r.la, r.ra), (r.lb, r.rb))):
        r.grads[(4 + j) * D : (5 + j) * D] = dot_0(left[...], right[...]).astype(bf16)


def ff_operands(W, cc, gated, down, normed, hidden, r):
    ffp = FF // W
    found = []
    for e in range(W):
        cols = pl.ds(pl.multiple_of(e * ffp + cc * (ffp // 2), 128), ffp // 2)
        found.append((gated.at[:, cols], r.lg, e * (ffp // 2), ffp // 2))
    cols = pl.ds(pl.multiple_of(cc * (FF // 2), 128), FF // 2)
    return found + [(down, r.rd, 0, D), (normed, r.ln, 0, D), (hidden.at[:, cols], r.rh, 0, FF // 2)]


def attn_operands(cc, qkv, att, branch, x, r):
    if cc == 0:
        return [(x, r.la), (qkv.at[:, 0:D], r.ra), (x, r.lb), (qkv.at[:, D : 2 * D], r.rb)]
    return [(x, r.la), (qkv.at[:, 2 * D : 3 * D], r.ra), (att, r.lb), (branch, r.rb)]


def reduce_kernel(nz, W, MB, r):
    s, c, w = place()
    z, core = c // 2, lax.rem(c, 2)
    part = D // W
    per = part // ROWS
    partner = {"ctx": c + 1 - 2 * core}
    xs = [{"wsh": lax.rem(w + k, W)} for k in range(1, W)]
    zs = [{"ctx": lax.rem(z + k, nz) * 2 + core} for k in range(1, nz)]
    greet(xs + zs + [partner])
    begin, step, tail = sum_steps(r, nz, W, 6 * per, per)
    small_first, small_second, small_third, small_finish = small_steps(r, nz, W)
    mine = pl.ds(pl.multiple_of(c * TD, TD), TD)

    def copies(m, cc, far):
        n = W + 3
        found = []
        rows = (r.gated_h.at[m], r.down_h.at[m], r.normed_h.at[m], r.hidden_h.at[m])
        side = (MB + m if far else m) * TD
        for e, (src, dst, at, width) in enumerate(ff_operands(W, cc, *rows, r)):
            spot = dst.at[side : side + TD, at : at + width]
            found.append((src, spot, m * (n + 4) + e))
        rows = (r.qkv_h.at[m], r.att_h.at[m], r.branch_h.at[m], r.x_h.at[m, mine])
        for e, (src, dst) in enumerate(attn_operands(cc, *rows, r)):
            found.append((src, dst.at[side : side + TD], m * (n + 4) + n + e))
        if far:
            return [push(a, b, r.c_send.at[e], r.c_recv.at[e], partner) for a, b, e in found]
        return [pltpu.make_async_copy(a, b, r.load_sem.at[e]) for a, b, e in found]

    own_load = pltpu.make_async_copy(r.attn_w.at[0, 0:2], r.own_w, r.own_sem)
    own_load.start()
    small_first(r.small_g[...])
    for cc in range(2):

        @pl.when(core == cc)
        def _():
            for m in range(MB):
                for copy in copies(m, 1 - cc, True) + copies(m, cc, False):
                    copy.start()
            for m in range(MB):
                for copy in copies(m, cc, False):
                    copy.wait()
                for copy in copies(m, cc, True):
                    copy.wait_recv()

    down_tiles(r, W)
    begin()
    up_tiles(r)
    attn_tiles(r)
    small_second()
    own_load.wait()
    clip_copies = clip_weights(
        r, r.tops[...], lambda p: r.own_w[p], [r.own_w.at[p] for p in range(2)]
    )
    small_third()

    tail(0, small_finish)
    for copy in clip_copies:
        copy.wait()
    for cc in range(2):

        @pl.when(core == cc)
        def _():
            for m in range(MB):
                for copy in copies(m, 1 - cc, True):
                    copy.wait_send()


def backward_part(nz, W, MB, T, fused, r, settle=None):
    lens, cot, counts, top, small = r.lens, r.cot, r.counts, r.top, r.small
    attn, up, down, xall, q, mix, lse = r.attn, r.up, r.down, r.xall, r.q, r.mix, r.lse
    first, second, hidden, dout, gfirst = r.first, r.second, r.hidden, r.dout, r.gfirst
    gbranch, gall, relay, aux = r.gbranch, r.gall, r.relay, r.aux
    wide_q, wide_k, lse_all, del_all, del_c = r.wide_q, r.wide_k, r.lse_all, r.del_all, r.del_c
    gnorm, ghid, gated, gdown = r.gnorm, r.ghid, r.gated, r.gdown
    small_g, top_x = r.small_g, r.top_x
    dqkv = [up.at[m * TD : (m + 1) * TD, 0 : 3 * D] for m in range(MB)]
    gin = [up.at[(MB + m) * TD : (MB + m + 1) * TD, 0:D] for m in range(MB)]
    s, c, w = place()
    z, core = c // 2, lax.rem(c, 2)
    partner = {"ctx": c + 1 - 2 * core}
    xs = [{"wsh": lax.rem(w + k, W)} for k in range(1, W)]
    zs = [{"ctx": lax.rem(z + k, nz) * 2 + core} for k in range(1, nz)]
    across = {"section": 1 - s}
    over = [{"section": 1 - s, "ctx": lax.rem(z + k, nz) * 2 + core} for k in range(1, nz)]
    if not fused:
        greet(xs + zs + over + [across, partner])
    part = D // W
    per = part // ROWS
    if fused:
        begin, step, tail = sum_steps(r, nz, W, 6 * per, per)
        small_first, small_second, small_third, small_finish = small_steps(r, nz, W)

    def rows_of(zz, cc):
        return pl.ds(pl.multiple_of((zz * 2 + cc) * TD, TD), TD)

    mine = rows_of(z, core)
    loads = []

    class Held:
        def wait(self):
            pass

    home = Spare() if fused else r

    def load(src, dst):
        if fused:
            return Held()
        copy = pltpu.make_async_copy(src, dst, r.load_sem.at[len(loads)])
        copy.start()
        loads.append(copy)
        return copy

    saves = []
    numbers = iter(range(100))

    def save(src, dst):
        copy = pltpu.make_async_copy(src, dst, r.save_sem.at[next(numbers)])
        copy.start()
        saves.append(copy)

    def cot_load(m):
        return pltpu.make_async_copy(cot.at[m, 0], dout.at[m], r.y_recv.at[m])

    def grad_push(m):
        return push(gin[m], dout.at[m], r.y_send.at[m], r.y_recv.at[m], across)

    @pl.when(s == 1)
    def _():
        for m in range(MB):
            cot_load(m).start()

    slots = xall.shape[0]
    load_second = [load(home.second_h.at[m], second.at[m]) for m in range(MB)]
    cuts = [slice(j * CHUNK, (j + 1) * CHUNK) for j in range(NCH)]
    load_hidden, load_down, load_up = [[]], [], []
    for cut in cuts:
        load_hidden[0].append(load(home.hidden_h.at[0, :, cut], hidden.at[0, :, cut]))
        load_down.append(load(home.down_h.at[cut], down.at[cut]))
        load_up.append(load(home.up_h.at[:, cut], up.at[:, cut]))
    late = {}

    def load_rest():
        late["first"] = [load(home.first_h.at[m], first.at[m]) for m in range(MB)]
        late["attn"] = load(home.attn_h, attn)
        late["mix"] = [load(home.mix_h.at[m], mix.at[m]) for m in range(MB)]
        late["lse"] = [load(home.lse_h.at[m], lse.at[m]) for m in range(MB)]
        for m in range(1, slots):
            load_hidden.append([load(home.hidden_h.at[m], hidden.at[m])])
        late["x"] = [load(home.xall_h.at[m], xall.at[m]) for m in range(slots)]
        late["kv"] = [load(home.kv_h.at[m, mine], home.kv_own.at[m]) for m in range(MB)]
        late["q"] = [load(home.q_h.at[m], q.at[m]) for m in range(MB)]

    def cut_rows(zz, cc, side):
        return pl.ds(pl.multiple_of((zz * 2 + cc) * TD + side * BLK, BLK), BLK)

    def rows_push(m, k):
        if k == 0:
            block = gall.at[m, mine]
            return push(block, block, r.f_send.at[m, 0], r.f_recv.at[m, 0], partner)
        block = gall.at[m, cut_rows(z, core, 0)]
        return push(block, block, r.b_send.at[m, k], r.b_recv.at[m, k], zs[k - 1])

    def rows_arrival(m, k):
        block = gall.at[m, cut_rows(lax.rem(z + nz - k, nz), core, 0)]
        return push(block, block, r.b_send.at[m, k], r.b_recv.at[m, k], partner)

    def relay_out(m):
        block = gall.at[m, cut_rows(z, core, 1)]
        return push(block, relay.at[m], r.r_send.at[m, 0], r.r_recv.at[m, 0], across)

    def relay_push(m, k):
        block = gall.at[m, cut_rows(z, core, 1)]
        return push(relay.at[m], block, r.r_send.at[m, k], r.r_recv.at[m, k], over[k - 1])

    def relay_arrival(m, k):
        block = gall.at[m, cut_rows(lax.rem(z + nz - k, nz), core, 1)]
        return push(block, block, r.r_send.at[m, k], r.r_recv.at[m, k], partner)

    def rows_forward(m, k):
        block = gall.at[m, rows_of(lax.rem(z + nz - k, nz), core)]
        return push(block, block, r.f_send.at[m, k], r.f_recv.at[m, k], partner)

    def aux_push(m, k):
        block = aux.at[m, c]
        peer = partner if k == 0 else zs[k - 1]
        send, recv = (r.af_send, r.af_recv) if k == 0 else (r.a_send, r.a_recv)
        return push(block, block, send.at[m, k], recv.at[m, k], peer)

    def aux_arrival(m, k):
        block = aux.at[m, lax.rem(z + nz - k, nz) * 2 + core]
        return push(block, block, r.a_send.at[m, k], r.a_recv.at[m, k], partner)

    def aux_forward(m, k):
        block = aux.at[m, lax.rem(z + nz - k, nz) * 2 + core]
        return push(block, block, r.af_send.at[m, k], r.af_recv.at[m, k], partner)

    def top_push(k):
        return push(top_x.at[0], top_x.at[k], r.tp_send.at[k - 1], r.tp_recv.at[k - 1], xs[k - 1])

    def spread_start(m):
        relay_out(m).start()
        for k in range(nz):
            aux_push(m, k).start()
            rows_push(m, k).start()

    def spread_sent(m):
        relay_out(m).wait_send()
        for k in range(1, nz):
            rows_push(m, k).wait_send()

    def relay_one(m):
        relay_out(m).wait_recv()
        for k in range(1, nz):
            relay_push(m, k).start()

    def rows_copies(m, cc, far, late):
        side = (MB + m if far else m) * TD
        found = []
        if late:
            rows = (dqkv[m], r.att.at[m], gbranch.at[m], r.xall_o.at[m, mine])
            for e, (src, dst) in enumerate(attn_operands(cc, *rows, r)):
                found.append((src, dst.at[side : side + TD], m * (W + 7) + W + 3 + e))
        else:
            rows = (gated.at[m], gdown.at[m], gnorm.at[m], ghid.at[m])
            for e, (src, dst, at, width) in enumerate(ff_operands(W, cc, *rows, r)):
                found.append((src, dst.at[side : side + TD, at : at + width], m * (W + 7) + e))
        if far:
            return [push(a, b, r.c_send.at[e], r.c_recv.at[e], partner) for a, b, e in found]
        return [pltpu.make_async_copy(a, b, r.c_load.at[e]) for a, b, e in found]

    def rows_start(m, late):
        for cc in range(2):

            @pl.when(core == cc)
            def _():
                for copy in rows_copies(m, 1 - cc, True, late) + rows_copies(m, cc, False, late):
                    copy.start()

    def rows_here(late, picked):
        for cc in range(2):

            @pl.when(core == cc)
            def _():
                for m in range(MB):
                    for copy in rows_copies(m, cc, False, late)[picked]:
                        copy.wait()
                    for copy in rows_copies(m, cc, True, late)[picked]:
                        copy.wait_recv()

    def ff_gradients():
        rows_here(False, slice(0, W + 1))
        down_tiles(r, W)
        begin()
        rows_here(False, slice(W + 1, None))
        up_tiles(r)

    def rows_sent():
        for cc in range(2):

            @pl.when(core == cc)
            def _():
                for m in range(MB):
                    for late in (False, True):
                        for copy in rows_copies(m, 1 - cc, True, late):
                            copy.wait_send()

    @pl.when(s == 0)
    def _():
        for m in range(MB):
            relay_one(m)

    heads = lax.broadcasted_iota(jnp.int32, (D, 128), 0)
    heads = lax.shift_right_logical(heads, 6) == lax.broadcasted_iota(jnp.int32, (D, 128), 1)
    heads = jnp.where(heads, 1.0, 0.0).astype(f32)
    small_g[...] = jnp.zeros_like(small_g)

    for m in range(MB):
        load_second[m].wait()

        @pl.when(s == 1)
        def _():
            cot_load(m).wait()

        @pl.when(s == 0)
        def _():
            grad_push(m).wait_recv()

        grad_out = dout[m].astype(f32)
        hat, rstd = norm_parts(second[m])
        small_g[1:2, :] += column_sum(grad_out * hat)
        small_g[6:7, :] += column_sum(grad_out)
        grad_second = norm_back(grad_out, hat, rstd, small[6:7, :])
        low_second = grad_second.astype(bf16)
        gdown[m] = low_second
        if not fused:
            save(gdown.at[m], r.rows_down.at[m])
        small_g[4:5, :] += column_sum(low_second.astype(f32))
        if m >= slots:
            load_hidden.append([load(home.hidden_h.at[m], hidden.at[m % slots])])
            for copy in hidden_saves:
                saves[:] = [x for x in saves if x is not copy]
                copy.wait()
        if m:
            load_hidden[m][0].wait()
        gfirst[m] = grad_second
        for j in range(NCH):
            cols = slice(j * CHUNK, (j + 1) * CHUNK)
            if m == 0:
                load_hidden[0][j].wait()
                load_down[j].wait()
                if j == NCH - 1:
                    load_rest()
            value, slope = gelu_both(hidden[m % slots, :, cols])
            gated[m % slots, :, cols] = value.astype(bf16)
            grad_hidden = (slope * dot_t(low_second, down[cols, :])).astype(bf16)
            ghid[m % slots, :, cols] = grad_hidden
            small_g[7 + j : 8 + j, :] += column_sum(grad_hidden.astype(f32))
            if m == 0:
                load_up[j].wait()
            gfirst[m] += dot_t(grad_hidden, up[:, cols])
        if not fused:
            save(gated.at[m % slots], r.rows_gated.at[m])
            save(ghid.at[m % slots], r.rows_hidden.at[m])
            hidden_saves = saves[-2:]
        grad_normed = gfirst[m]
        late["first"][m].wait()
        hat, rstd = norm_parts(first[m])
        gnorm[m] = (hat * small[5:6, :] + small[3:4, :]).astype(bf16)
        if fused:
            rows_start(m, False)
        small_g[0:1, :] += column_sum(grad_normed * hat)
        small_g[5:6, :] += column_sum(grad_normed)
        grad_first = norm_back(grad_normed, hat, rstd, small[5:6, :])
        gfirst[m] = grad_first
        low_first = grad_first.astype(bf16)
        gbranch[m] = low_first
        if not fused:
            save(gnorm.at[m], r.rows_normed.at[m])
            save(gbranch.at[m], r.rows_branch.at[m])
        small_g[3:4, :] += column_sum(low_first.astype(f32))
        late["mix"][m].wait()
        late["lse"][m].wait()
        if m == 0:
            late["attn"].wait()
        grad_att = dot_t(low_first, attn[3]).astype(bf16)
        gall[m, mine, :] = grad_att
        weighed = grad_att.astype(f32) * mix[m]
        delta = jnp.dot(weighed, heads, preferred_element_type=f32, precision=exact_dot)
        del_c[m] = delta
        aux[m, c, 0:16] = lse[m].T[0:16]
        aux[m, c, 16:32] = delta.T[0:16]
        aux[m, c, 32:40] = top[...]
        if m == 0:
            spread_start(0)
        elif m == 1:

            @pl.when(s == 0)
            def _():
                spread_sent(0)
                spread_start(1)

    if fused:
        settle()

        @pl.when(s == 0)
        def _():
            ff_gradients()

    def paced(at):
        if not fused:
            return lambda g: None

        def run(g):
            @pl.when((s == 0) & (lax.rem(g, PACE) == PACE - 1))
            def _():
                step(at * (PAIRS // PACE) + g // PACE)

        return run

    spots = lax.broadcasted_iota(jnp.int32, (1, T), 1)
    here = lax.broadcasted_iota(jnp.int32, (TD, 128), 0)
    def own_pass(m, at):
        if m >= slots:
            late["x"].append(load(home.xall_h.at[m], xall.at[m % slots]))
        for name in ("x", "kv", "q"):
            late[name][m].wait()

        def stream(g):
            if fused:
                return []
            slot = lax.rem(g, 2)
            return [
                pltpu.make_async_copy(
                    r.kv_h.at[m, :, pl.ds(pl.multiple_of(e * D + g * 128, 128), 128)],
                    r.kvp.at[slot, e],
                    r.kvp_sem.at[slot, e],
                )
                for e in range(2)
            ]

        for copy in stream(0):
            copy.start()
        length = lens[m]
        lanes = block_lanes(T // BLK, T)
        counted = jnp.where(spots < length, dot(counts[0, m].astype(bf16), lanes), 0.0)
        counted = jnp.where(counted > 0, jnp.log(jnp.maximum(counted, 1.0)), masked_score)
        wide_q[...] = counted.reshape(PAIRS, 8, T)
        advance = paced(at)

        def own_rows(g, _):
            if not fused:

                @pl.when(g + 1 < PAIRS)
                def _():
                    for copy in stream(g + 1):
                        copy.start()

            for copy in stream(g):
                copy.wait()
            slot = lax.rem(g, 2)
            lse_c = jnp.concatenate([head_column(lse[m], 2 * g + e) for e in range(2)], 0)
            delta = jnp.concatenate([head_column(del_c[m], 2 * g + e) for e in range(2)], 0)
            queries = halves(q[m, :, pair_lanes(g)])
            grads = halves(gall[m, mine, pair_lanes(g)])
            grad_q = jnp.zeros((2 * TD, 2 * HD), f32)
            for t in range(0, T, STEP):
                if fused:
                    keys = r.kv[m, t : t + STEP, pair_lanes(g)]
                    values = r.kv[m, t : t + STEP, value_lanes(g)]
                else:
                    keys = r.kvp[slot, 0, t : t + STEP]
                    values = r.kvp[slot, 1, t : t + STEP]
                shift = wide_q[g, :, t : t + STEP]
                probs = jnp.exp(dot_t(queries, keys) + spread4(shift, STEP) - lse_c)
                grad_probs = dot_t(grads, values)
                grad_scores = (probs * (grad_probs - delta)).astype(bf16)
                grad_q = grad_q + dot(grad_scores, keys)
            dqkv[m][:, pair_lanes(g)] = (joined(grad_q) * (HD**-0.5)).astype(bf16)
            advance(g)
            return 0

        lax.fori_loop(0, PAIRS, own_rows, 0)
        if m + 1 < MB:

            @pl.when((s == 1) | (m > 0))
            def _():
                spread_sent(m)
                spread_start(m + 1)

        def project(i, _):
            rows = pl.ds(pl.multiple_of(i * 256, 256), 256)
            all_q = dot(xall[m % slots, rows, :], attn[0]).astype(bf16).astype(f32)
            xall[m % slots, rows, :] = (all_q * (HD**-0.5)).astype(bf16)
            return 0

        lax.fori_loop(0, T // 256, project, 0)

    def all_pass(m, at):
        lanes = block_lanes(T // BLK, T)
        length = lens[m]
        for k in range(1, nz):
            rows_arrival(m, k).wait_recv()
            relay_arrival(m, k).wait_recv()
            rows_forward(m, k).start()
            aux_arrival(m, k).wait_recv()
            aux_forward(m, k).start()
        for k in range(nz):
            rows_forward(m, k).wait_recv()
            aux_forward(m, k).wait_recv()
        for cc in range(2 * nz):
            lse_all[:, cc * TD : (cc + 1) * TD] = aux[m, cc, 0:16]
            del_all[:, cc * TD : (cc + 1) * TD] = aux[m, cc, 16:32]
        if m == 0:
            most = aux[0, 0, 32:40]
            for cc in range(1, 2 * nz):
                most = jnp.maximum(most, aux[0, cc, 32:40])
            top_x[0] = most
            for k in range(1, W):
                top_push(k).start()
        counted = dot(counts[1, m].astype(bf16), lanes)
        counted = jnp.where(counted > 0, jnp.log(jnp.maximum(counted, 1.0)), masked_score)
        wide_k[...] = counted.reshape(PAIRS, 8, T)
        live = c * TD + here < length
        advance_keys = paced(at)

        def own_keys(g, _):
            own_kv = r.kv.at[m, mine] if fused else r.kv_own.at[m]
            keys = halves(own_kv[:, pair_lanes(g)])
            values = halves(own_kv[:, value_lanes(g)])
            lse_r = [lse_all[pl.ds(2 * g + e, 1), :] for e in range(2)]
            delta = [del_all[pl.ds(2 * g + e, 1), :] for e in range(2)]
            shift = wide_k[g]
            shift = jnp.concatenate([shift[0:2] - lse_r[0], shift[2:4] - lse_r[1]], 0)
            grad_k = jnp.zeros((2 * TD, 2 * HD), f32)
            grad_v = jnp.zeros((2 * TD, 2 * HD), f32)
            for t in range(0, T, STEP):
                queries = xall[m % slots, t : t + STEP, pair_lanes(g)]
                grads = gall[m, t : t + STEP, pair_lanes(g)]
                probs = jnp.exp(dot_t(keys, queries) + spread4(shift[:, t : t + STEP], STEP))
                grad_v = grad_v + dot(probs.astype(bf16), grads)
                centre = jnp.concatenate(
                    [jnp.broadcast_to(d[:, t : t + STEP], (TD, STEP)) for d in delta], 0
                )
                grad_scores = (probs * (dot_t(values, grads) - centre)).astype(bf16)
                grad_k = grad_k + dot(grad_scores, queries)
            grad_k, grad_v = joined(grad_k), joined(grad_v)
            lanes_k = pl.ds(pl.multiple_of(D + g * 128, 128), 128)
            lanes_v = pl.ds(pl.multiple_of(2 * D + g * 128, 128), 128)
            dqkv[m][:, lanes_k] = jnp.where(live, grad_k, 0.0).astype(bf16)
            dqkv[m][:, lanes_v] = jnp.where(live, grad_v, 0.0).astype(bf16)
            advance_keys(g)
            return 0

        lax.fori_loop(0, PAIRS, own_keys, 0, unroll=2)
        if fused:
            rows_start(m, True)
        else:
            save(dqkv[m], r.rows_qkv.at[m])
        small_g[2:3, :] += column_sum(dqkv[m][:, 2 * D : 3 * D].astype(f32))
        total = gfirst[m]
        for p in range(3):
            total = total + dot_t(dqkv[m][:, p * D : (p + 1) * D], attn[p])
        gin[m][...] = total.astype(bf16)

        @pl.when(s == 1)
        def _():
            grad_push(m).start()

        save(gin[m], r.grad_in_o.at[0, m, 0])

    for m in range(MB):
        own_pass(m, 2 * m)
        all_pass(m, 2 * m + 1)

    def loop(t, _):
        step(t)
        return 0

    if fused:
        small_first(small_g[...])
        done_1 = EARLY

        @pl.when(s == 1)
        def _():
            relay_one(0)
            ff_gradients()
            lax.fori_loop(0, EARLY, loop, 0)
            for m in range(1, MB):
                relay_one(m)

        rows_here(True, slice(None))
        attn_tiles(r)
        small_second()
        done_0 = 2 * MB * (PAIRS // PACE)
        now = jnp.where(s == 0, done_0, done_1)
        lax.fori_loop(now, now + 3, loop, 0)
        small_third()
    else:

        @pl.when(s == 1)
        def _():
            for m in range(MB):
                relay_one(m)

        save(small_g, r.small_o)
    for k in range(1, W):
        top_push(k).wait()
    most = top_x[0]
    for k in range(1, W):
        most = jnp.maximum(most, top_x[k])
    if fused:
        for k in range(nz):
            rows_forward(0, k).wait_send()
        saves.extend(
            clip_weights(
                r,
                most,
                lambda p: attn[p, pl.ds(pl.multiple_of(w * part, 16), part), :],
                [gall.at[0, p * part : (p + 1) * part] for p in range(2)],
            )
        )
        tail(now + 3, small_finish)
        rows_sent()
    else:
        r.top_o[...] = most
    for m in range(MB):
        for k in range(nz):
            if m or not fused:
                rows_forward(m, k).wait_send()
            aux_forward(m, k).wait_send()
        for k in range(1, nz):
            aux_push(m, k).wait_send()
            relay_push(m, k).wait_send()
        if m == MB - 1:
            spread_sent(m)

        @pl.when(s == 1)
        def _():
            grad_push(m).wait_send()

    for copy in saves:
        copy.wait()


def finish_kernel(W, r):
    w = lax.axis_index("wsh")
    part, ffp = D // W, FF // W
    span = ffp // D
    straight = [
        [pltpu.make_async_copy(a, b, r.pass_sem.at[0, e]), pltpu.make_async_copy(b, c, r.pass_sem.at[1, e])]
        for e, (a, b, c) in enumerate(
            (
                (r.out, r.out_v, r.out_o),
                (r.grad_in, r.grad_in_v, r.grad_in_o),
                (r.clip, r.clip_v, r.clip_o),
            )
        )
    ]

    def take(t):
        at = ((t // 4) * 2 + t % 2) * part
        source = r.sums.at[(t % 4) // 2, at : at + part]
        return pltpu.make_async_copy(source, r.low.at[t % BUFFERS], r.in_sem.at[t % BUFFERS])

    def give(t):
        if t < 4:
            spot = r.down_o.at[0, t * part : (t + 1) * part]
        elif t < 8:
            spot = r.up_o.at[0, :, (t - 4) * D : (t - 3) * D]
        else:
            spot = r.attn_o.at[0, t - 8]
        return pltpu.make_async_copy(r.wide.at[t % BUFFERS], spot, r.out_sem.at[t % BUFFERS])

    for t in range(BUFFERS):
        take(t).start()
    for come, _ in straight:
        come.start()
    for e in range(W):

        @pl.when(w == e)
        def _():
            cols = slice(e * part, (e + 1) * part)
            r.gains_o[0] = r.small[0:2, cols]
            r.biases_o[0] = r.small[2:7, cols]
            for j in range(span):
                at = 7 + e * span + j
                r.up_b_o[0:1, j * D : (j + 1) * D] = r.small[at : at + 1, :]

    for t in range(12):
        take(t).wait()
        if t >= BUFFERS:
            give(t - BUFFERS).wait()
        r.wide[t % BUFFERS] = r.low[t % BUFFERS].astype(f32)
        give(t).start()
        if t + BUFFERS < 12:
            take(t + BUFFERS).start()
        if t < 3:
            straight[t][0].wait()
            straight[t][1].start()
    for t in range(12 - BUFFERS, 12):
        give(t).wait()
    for _, go in straight:
        go.wait()


VMEM = pl.BlockSpec(memory_space=pltpu.VMEM)
SMEM = pl.BlockSpec(memory_space=pltpu.SMEM)
ANY = pl.BlockSpec(memory_space=pl.ANY)
DMA = pltpu.SemaphoreType.DMA


def slots_of(T, MB):
    return MB if T <= 2048 else 1


def call(kernel, name, number, limit, ins, outs, scratch):
    names = list(ins) + list(outs) + list(scratch)

    def body(*refs):
        kernel(types.SimpleNamespace(**dict(zip(names, refs, strict=True))))

    found = pl.pallas_call(
        body,
        out_shape=[jax.ShapeDtypeStruct(*v[:2]) for v in outs.values()],
        in_specs=[v[1] for v in ins.values()],
        out_specs=[v[2] for v in outs.values()],
        scratch_shapes=list(scratch.values()),
        compiler_params=pltpu.CompilerParams(
            collective_id=number,
            has_side_effects=number is not None,
            vmem_limit_bytes=limit << 20,
        ),
        name=name,
    )(*(v[0] for v in ins.values()))
    return dict(zip(outs, found))


def sum_scratch(nz, W, MB):
    part, R = D // W, MB * TD
    count = 6 * (part // ROWS)
    copies = MB * (W + 7)
    return dict(
        lg=pltpu.VMEM((2 * R, FF // 2), bf16),
        rd=pltpu.VMEM((2 * R, D), bf16),
        ln=pltpu.VMEM((2 * R, D), bf16),
        rh=pltpu.VMEM((2 * R, FF // 2), bf16),
        la=pltpu.VMEM((2 * R, D), bf16),
        ra=pltpu.VMEM((2 * R, D), bf16),
        lb=pltpu.VMEM((2 * R, D), bf16),
        rb=pltpu.VMEM((2 * R, D), bf16),
        from_x=pltpu.VMEM((W - 1, 6 * part, D), bf16),
        chain=pltpu.VMEM((2, 6 * part, D), bf16),
        core_s=pltpu.VMEM((2, 16, D), f32),
        wsh_s=pltpu.VMEM((W, 16, D), f32),
        z_s=pltpu.VMEM((nz, 16, D), f32),
        c_send=DMA((copies,)),
        c_recv=DMA((copies,)),
        c_load=DMA((copies,)),
        x_send=DMA((W - 1, count)),
        x_recv=DMA((W - 1, count)),
        ch_send=DMA((count,)),
        ch_recv=DMA((2, count)),
        t_send=DMA((2, count)),
        t_recv=DMA((count,)),
        p_send=DMA((count,)),
        p_recv=DMA((count,)),
        o_sem=DMA((count,)),
        clip_sem=DMA((2,)),
        sc_send=DMA,
        sc_recv=DMA,
        sx_send=DMA((W - 1,)),
        sx_recv=DMA((W - 1,)),
        sz_send=DMA((nz - 1,)),
        sz_recv=DMA((nz - 1,)),
    )


def sum_outs(W):
    part = D // W
    return dict(
        sums=((2, 6 * part, D), bf16, ANY),
        small_o=((16, D), f32, VMEM),
        clip_o=((1, 2, part, D), bf16, ANY),
    )


def forward_ins(lens, chosen, random, tokens, attn_w, up_w, down_w, bias_w, gain_w, up_b):
    return dict(
        lens=(lens, SMEM),
        chosen=(chosen, SMEM),
        random=(random, VMEM),
        tokens=(tokens, ANY),
        attn_w=(attn_w, ANY),
        up_w=(up_w, ANY),
        down_w=(down_w, ANY),
        bias_w=(bias_w, VMEM),
        gain_w=(gain_w, VMEM),
        up_b=(up_b, VMEM),
    )


def shared_scratch(T, MB, fused):
    slots = slots_of(T, MB)
    return dict(
        attn=pltpu.VMEM((4, D, D), bf16),
        up=pltpu.VMEM((D, FF), bf16),
        down=pltpu.VMEM((FF + 2 * D if fused else FF, D), bf16),
        q=pltpu.VMEM((MB, TD, D), bf16),
        mix=pltpu.VMEM((MB, TD, D), f32),
        lse=pltpu.VMEM((MB, TD, 128), f32),
        first=pltpu.VMEM((MB, TD, D), f32),
        second=pltpu.VMEM((MB, TD, D), f32),
        wide_q=pltpu.VMEM((PAIRS, 8, T), f32),
    )


def forward_scratch(nz, W, MB, T):
    return dict(
        small_in=pltpu.VMEM((16, D), f32),
        small_all=pltpu.VMEM((W, 16, D), f32),
        small=pltpu.VMEM((16, D), f32),
        xall=pltpu.VMEM((MB, T, D), bf16),
        kv=pltpu.VMEM((slots_of(T, MB), T, 2 * D), bf16),
        att=pltpu.VMEM((MB, TD, D), bf16),
        top=pltpu.VMEM((8, 128), f32),
        hidden=pltpu.VMEM((MB, TD, FF), f32),
        out=pltpu.VMEM((MB, TD, D), bf16),
        v_load_sem=DMA((3,)),
        v_w_send=DMA((W - 1, 8)),
        v_w_recv=DMA((W - 1, 8)),
        v_wf_send=DMA((W - 1, 8, 3)),
        v_wf_recv=DMA((W - 1, 8, 3)),
        v_s_send=DMA((W - 1,)),
        v_s_recv=DMA((W - 1,)),
        v_ff_sem=DMA((MB + 1, 4)),
        v_save_sem=DMA((2 + 6 * MB,)),
        **{"v_" + k: DMA((MB, nz)) for k in V_RINGS},
    )


def backward_scratch(nz, W, MB, T):
    slots = slots_of(T, MB)
    return dict(
        dout=pltpu.VMEM((MB, TD, D), bf16),
        gfirst=pltpu.VMEM((MB, TD, D), f32),
        gbranch=pltpu.VMEM((MB, TD, D), bf16),
        gall=pltpu.VMEM((MB, T, D), bf16),
        relay=pltpu.VMEM((MB, BLK, D), bf16),
        aux=pltpu.VMEM((MB, 2 * nz, 40, 128), f32),
        wide_k=pltpu.VMEM((PAIRS, 8, T), f32),
        lse_all=pltpu.VMEM((16, T), f32),
        del_all=pltpu.VMEM((16, T), f32),
        del_c=pltpu.VMEM((MB, TD, 128), f32),
        gnorm=pltpu.VMEM((MB, TD, D), bf16),
        ghid=pltpu.VMEM((slots, TD, FF), bf16),
        gated=pltpu.VMEM((slots, TD, FF), bf16),
        gdown=pltpu.VMEM((MB, TD, D), bf16),
        small_g=pltpu.VMEM((16, D), f32),
        top_x=pltpu.VMEM((W, 8, 128), f32),
        load_sem=DMA((1 + 3 * NCH + 8 * MB,)),
        y_send=DMA((MB,)),
        y_recv=DMA((MB,)),
        tp_send=DMA((W - 1,)),
        tp_recv=DMA((W - 1,)),
        save_sem=DMA((1 + 7 * MB,)),
        **{k: DMA((MB, nz)) for k in RINGS},
    )


def run_layers(nz, W, MB, cot, ins):
    T = 2 * nz * TD
    ins = dict(ins, cot=(cot, ANY))
    outs = dict(
        out_o=((1, MB, 1, TD, D), bf16, ANY),
        xall_o=((MB, T, D), bf16, ANY),
        grad_in_o=((1, MB, 1, TD, D), bf16, ANY),
        **sum_outs(W),
    )
    scratch = shared_scratch(T, MB, True)
    scratch.update(forward_scratch(nz, W, MB, T))
    scratch.update(backward_scratch(nz, W, MB, T))
    scratch.update(sum_scratch(nz, W, MB))
    scratch.update(counts=pltpu.VMEM((2, MB, PAIRS * 8, T // BLK), f32))

    def kernel(r):
        r.grads = r.down
        settle = forward_part(nz, W, MB, T, True, r)
        backward_part(nz, W, MB, T, True, r, settle)

    return call(kernel, "layers", 0, 63, ins, outs, scratch)


def run_forward(nz, W, MB, ins):
    T = 2 * nz * TD
    outs = dict(
        counts=((2, MB, PAIRS * 8, T // BLK), f32, VMEM),
        out_o=((1, MB, 1, TD, D), bf16, ANY),
        xall_o=((MB, T, D), bf16, ANY),
        kv_o=((MB, T, 2 * D), bf16, ANY),
        q_o=((MB, TD, D), bf16, ANY),
        att_o=((MB, TD, D), bf16, ANY),
        mix_o=((MB, TD, D), f32, ANY),
        lse_o=((MB, TD, 128), f32, ANY),
        first_o=((MB, TD, D), f32, ANY),
        second_o=((MB, TD, D), f32, ANY),
        hidden_o=((MB, TD, FF), f32, ANY),
        top_o=((8, 128), f32, ANY),
        attn_o=((4, D, D), bf16, ANY),
        up_o=((D, FF), bf16, ANY),
        down_o=((FF, D), bf16, ANY),
        small_o=((16, D), f32, ANY),
    )
    scratch = shared_scratch(T, MB, False)
    scratch.update(forward_scratch(nz, W, MB, T))

    def kernel(r):
        forward_part(nz, W, MB, T, False, r)()

    return call(kernel, "forward", 0, 60, ins, outs, scratch)


def run_backward(nz, W, MB, lens, cot, saved):
    T = 2 * nz * TD
    slots = slots_of(T, MB)
    ins = dict(
        lens=(lens, SMEM),
        cot=(cot, ANY),
        **{k: (v, VMEM if k in ("top", "small", "counts") else ANY) for k, v in saved.items()},
    )
    outs = dict(
        grad_in_o=((1, MB, 1, TD, D), bf16, ANY),
        rows_qkv=((MB, TD, 3 * D), bf16, ANY),
        rows_branch=((MB, TD, D), bf16, ANY),
        rows_normed=((MB, TD, D), bf16, ANY),
        rows_hidden=((MB, TD, FF), bf16, ANY),
        rows_gated=((MB, TD, FF), bf16, ANY),
        rows_down=((MB, TD, D), bf16, ANY),
        small_o=((16, D), f32, ANY),
        top_o=((8, 128), f32, VMEM),
    )
    scratch = shared_scratch(T, MB, False)
    scratch.update(backward_scratch(nz, W, MB, T))
    scratch.update(
        xall=pltpu.VMEM((slots, T, D), bf16),
        hidden=pltpu.VMEM((slots, TD, FF), f32),
        kv_own=pltpu.VMEM((MB, TD, 2 * D), bf16),
        kvp=pltpu.VMEM((2, 2, T, 2 * HD), bf16),
        kvp_sem=DMA((2, 2)),
    )

    def kernel(r):
        backward_part(nz, W, MB, T, False, r)

    return call(kernel, "backward", 1, 60, ins, outs, scratch)


def run_reduce(nz, W, MB, ins):
    part = D // W
    scratch = sum_scratch(nz, W, MB)
    scratch.update(
        grads=pltpu.VMEM((6 * D, D), bf16),
        own_w=pltpu.VMEM((2, part, D), bf16),
        load_sem=DMA((MB * (W + 7),)),
        own_sem=DMA,
    )
    ins = {k: (v, VMEM if k in ("small_g", "tops") else ANY) for k, v in ins.items()}
    return call(
        functools.partial(reduce_kernel, nz, W, MB), "reduce", 2, 60, ins, sum_outs(W), scratch
    )


def run_finish(W, MB, sums, small, out, grad_in, clip):
    part, ffp = D // W, FF // W
    HBM = pl.BlockSpec(memory_space=pltpu.MemorySpace.HBM)
    ins = dict(
        sums=(sums, HBM),
        small=(small, VMEM),
        out=(out, HBM),
        grad_in=(grad_in, HBM),
        clip=(clip, HBM),
    )
    outs = dict(
        out_o=(out.shape, bf16, HBM),
        grad_in_o=(grad_in.shape, bf16, HBM),
        attn_o=((1, 4, part, D), f32, HBM),
        up_o=((1, part, FF), f32, HBM),
        down_o=((1, ffp, D), f32, HBM),
        gains_o=((1, 2, part), f32, VMEM),
        biases_o=((1, 5, part), f32, VMEM),
        up_b_o=((1, ffp), f32, VMEM),
        clip_o=(clip.shape, bf16, HBM),
    )
    scratch = dict(
        low=pltpu.VMEM((BUFFERS, part, D), bf16),
        wide=pltpu.VMEM((BUFFERS, part, D), f32),
        in_sem=DMA((BUFFERS,)),
        out_sem=DMA((BUFFERS,)),
        pass_sem=DMA((2, 3)),
        out_v=pltpu.VMEM(out.shape, bf16),
        grad_in_v=pltpu.VMEM(grad_in.shape, bf16),
        clip_v=pltpu.VMEM(clip.shape, bf16),
    )
    return call(functools.partial(finish_kernel, W), "finish", None, 62, ins, outs, scratch)


def per_device(
    tokens, out_cotangent, attn_weights, up_weights, down_weights, norm_gains, bias_rows, up_bias,
    seq_lengths, rand_owner, rand_local, global_raw,
):
    n_ctx, W = lax.axis_size("ctx"), lax.axis_size("wsh")
    nz = n_ctx // 2
    MB = tokens.shape[0]
    lens = seq_lengths[:, 0]
    random = (rand_owner * BLK_DEV + rand_local).reshape(MB, BLK_DEV * n_ctx, H * RND)
    ins = forward_ins(
        lens, global_raw, random, tokens, attn_weights, up_weights, down_weights, bias_rows,
        norm_gains, up_bias,
    )
    if W == 2 and n_ctx * TD <= 2048:
        got = run_layers(nz, W, MB, out_cotangent, ins)
        out, grad_in = got["out_o"], got["grad_in_o"]
    else:
        kept = run_forward(nz, W, MB, ins)
        out, att = kept["out_o"], kept["att_o"]
        names = ["xall", "kv", "q", "mix", "lse", "first", "second", "hidden", "attn", "up", "down"]
        saved = {k + "_h": kept[k + "_o"] for k in names}
        saved.update(top=kept["top_o"], small=kept["small_o"], counts=kept["counts"])
        got = run_backward(nz, W, MB, lens, out_cotangent, saved)
        grad_in = got["grad_in_o"]
        names = ("gated", "down", "normed", "hidden", "qkv", "branch")
        rows = {k + "_h": got["rows_" + k] for k in names}
        rows.update(
            att_h=att, x_h=kept["xall_o"], small_g=got["small_o"], tops=got["top_o"],
            attn_w=attn_weights,
        )
        got = run_reduce(nz, W, MB, rows)
    done = run_finish(W, MB, got["sums"], got["small_o"], out, grad_in, got["clip_o"])
    return tuple(done.values())


def solution(mesh):
    placed = (
        P(None, "wsh", "ctx", None),
        P(None, "wsh", "ctx", None),
        P("section", None, "wsh", None),
        P("section", "wsh", None),
        P("section", "wsh", None),
        P("section", None, "wsh"),
        P("section", None, "wsh"),
        P("section", "wsh"),
        P(None, "wsh"),
        P(None, "wsh", None, None, None),
        P(None, "wsh", None, None, None),
        P(None, "wsh", None),
    )
    return jax.shard_map(
        per_device,
        mesh=mesh,
        in_specs=placed,
        out_specs=(
            P("section", None, "wsh", "ctx", None),
            P("section", None, "wsh", "ctx", None),
            P("section", None, "wsh", None),
            P("section", "wsh", None),
            P("section", "wsh", None),
            P("section", None, "wsh"),
            P("section", None, "wsh"),
            P("section", "wsh"),
            P("section", None, "wsh", None),
        ),
        check_vma=False,
    )
```

```python
import functools
import types

import jax
import jax.numpy as jnp
from jax import lax
from jax.experimental import pallas as pl
from jax.experimental.pallas import tpu as pltpu
from jax.sharding import PartitionSpec as P

D = 768
H = 12
HD = 64
FF = 3072
BLK = 64
TD = 128
BLK_DEV = 2
RND = 3
PAIRS = H // 2
CHUNK = 768
NCH = FF // CHUNK
STEP = 1024
ROWS = 48
FLIGHT = 4
LAG = 3
PACE = 1
EARLY = 4
BUFFERS = 4
V_RINGS = [a + b for a in ("b", "f", "r") for b in ("_send", "_recv")] + ["o_send"]
RINGS = [a + b for a in ("b", "f", "a", "af", "r") for b in ("_send", "_recv")]

MESH = pl.DeviceIdType.MESH
norm_eps = 1e-05
clip_limit = 6.0
masked_score = -1e30
exact_dot = lax.Precision.HIGHEST
f32 = jnp.float32
bf16 = jnp.bfloat16


def dot(a, b):
    return jnp.dot(a, b, preferred_element_type=f32)


def dot_t(a, b):
    return lax.dot_general(a, b, (((1,), (1,)), ((), ())), preferred_element_type=f32)


def dot_0(a, b):
    return lax.dot_general(a, b, (((0,), (0,)), ((), ())), preferred_element_type=f32)


def column_sum(v):
    return jnp.sum(v, 0, keepdims=True)


def norm_parts(v):
    center = v - jnp.mean(v, -1, keepdims=True)
    rstd = lax.rsqrt(jnp.mean(center * center, -1, keepdims=True) + norm_eps)
    return center * rstd, rstd


def norm_back(grad, hat, rstd, gain):
    scaled = grad * gain
    return rstd * (
        scaled
        - jnp.mean(scaled, -1, keepdims=True)
        - hat * jnp.mean(scaled * hat, -1, keepdims=True)
    )


def gelu(v):
    return 0.5 * v * (1.0 + lax.erf(v * (0.5**0.5)))


def gelu_both(v):
    phi = 0.5 * (1.0 + lax.erf(v * (0.5**0.5)))
    return v * phi, phi + v * jnp.exp(-0.5 * v * v) * 0.3989422804014327


def place():
    return lax.axis_index("section"), lax.axis_index("ctx"), lax.axis_index("wsh")


def greet(peers):
    barrier = pltpu.get_barrier_semaphore()
    for peer in peers:
        pl.semaphore_signal(barrier, inc=1, device_id=peer, device_id_type=MESH)
    pl.semaphore_wait(barrier, len(peers))


def push(src, dst, send, recv, peer):
    return pltpu.make_async_remote_copy(
        src_ref=src, dst_ref=dst, send_sem=send, recv_sem=recv, device_id=peer, device_id_type=MESH
    )


def halves(rows):
    low = lax.broadcasted_iota(jnp.int32, rows.shape, 1) < HD
    zero = jnp.zeros_like(rows)
    return jnp.concatenate([jnp.where(low, rows, zero), jnp.where(low, zero, rows)], 0)


def joined(rows):
    low = lax.broadcasted_iota(jnp.int32, (TD, 2 * HD), 1) < HD
    return jnp.where(low, rows[:TD], rows[TD:])


def spread4(rows, width):
    return jnp.concatenate(
        [jnp.broadcast_to(rows[r : r + 1], (BLK, width)) for r in range(4)], 0
    )


def block_lanes(blocks, width):
    lane = lax.broadcasted_iota(jnp.int32, (blocks, width), 1)
    row = lax.broadcasted_iota(jnp.int32, (blocks, width), 0)
    return jnp.where(lax.shift_right_logical(lane, 6) == row, 1.0, 0.0).astype(bf16)


def value_lanes(g):
    return pl.ds(pl.multiple_of(D + g * (2 * HD), 2 * HD), 2 * HD)


def head_column(columns, head):
    lane = lax.broadcasted_iota(jnp.int32, columns.shape, 1)
    return jnp.sum(jnp.where(lane == head, columns, 0.0), 1, keepdims=True)


def pair_lanes(g):
    return pl.ds(pl.multiple_of(g * (2 * HD), 2 * HD), 2 * HD)


def count_tables(m, lens, chosen, random, c, blocks):
    rows, names = PAIRS * 8, H * RND
    valid = (lens[m] + BLK - 1) // BLK
    picked = [lax.rem(chosen[m, 0, k], valid) for k in range(2)]
    table = random[m]
    row = lax.broadcasted_iota(jnp.int32, (rows, blocks), 0)
    lane = lax.broadcasted_iota(jnp.int32, (rows, blocks), 1)
    here = c * BLK_DEV + lax.rem(row, BLK_DEV)
    near = jnp.where(jnp.abs(lane - here) <= 1, 1.0, 0.0)

    def is_picked(ids):
        return [jnp.where(ids == p, 1.0, 0.0) for p in picked]

    kind = lax.broadcasted_iota(jnp.int32, (rows, names), 0)
    name = lax.broadcasted_iota(jnp.int32, (rows, names), 1)
    owner = (kind // 8) * 2 + lax.rem(kind, 8) // BLK_DEV
    same = (lax.rem(kind, 8) < 4) & (name // RND == owner)
    diagonal = jnp.where(
        lax.broadcasted_iota(jnp.int32, (names, names), 0)
        == lax.broadcasted_iota(jnp.int32, (names, names), 1),
        1.0,
        0.0,
    )
    lanes = lax.broadcasted_iota(jnp.int32, (names, blocks), 1).astype(f32)
    by_q = near + sum(is_picked(lane))
    by_k = near + sum(is_picked(here))
    for side in range(BLK_DEV):
        pick = jnp.where(same & (lax.rem(kind, BLK_DEV) == side), 1.0, 0.0).astype(bf16)
        own = random[m, pl.ds(c * BLK_DEV + side, 1), :].astype(f32)
        column = dot((diagonal * own).astype(bf16), jnp.ones((names, blocks), bf16))
        by_q += dot(pick, jnp.where(column == lanes, 1.0, 0.0).astype(bf16))
        match = jnp.where(table == c * BLK_DEV + side, 1.0, 0.0).astype(bf16)
        by_k += dot_t(pick, match)
    return (
        jnp.where(sum(is_picked(here)) > 0, 1.0, by_q),
        jnp.where(sum(is_picked(lane)) > 0, 1.0, by_k),
    )


class Spare:
    def __getattr__(self, name):
        return self

    def __getitem__(self, at):
        return self


def forward_part(nz, W, MB, T, fused, r):
    lens, chosen, random, tokens = r.lens, r.chosen, r.random, r.tokens
    attn_w, up_w, down_w, bias_w, gain_w, up_b = (
        r.attn_w, r.up_w, r.down_w, r.bias_w, r.gain_w, r.up_b,
    )
    attn, up, down, small_in, small_all, small = (
        r.attn, r.up, r.down, r.small_in, r.small_all, r.small,
    )
    xall, kv, q, att, mix, lse, top = r.xall, r.kv, r.q, r.att, r.mix, r.lse, r.top
    first, second, hidden, out, wide, counts = (
        r.first, r.second, r.hidden, r.out, r.wide_q, r.counts,
    )
    s, c, w = place()
    z, core = c // 2, lax.rem(c, 2)
    par = lax.rem(z, 2)
    part = D // W
    ffp = FF // W
    partner = {"ctx": c + 1 - 2 * core}
    buddy = {"ctx": (z + 1 - 2 * par) * 2 + core}
    xs = [{"wsh": lax.rem(w + k, W)} for k in range(1, W)]
    zs = [{"ctx": lax.rem(z + k, nz) * 2 + core} for k in range(1, nz)]
    over = [{"section": 1 - s, "ctx": lax.rem(z + k, nz) * 2 + core} for k in range(nz)]
    greet(xs + zs + over + [partner])

    def rows_of(zz, cc):
        return pl.ds(pl.multiple_of((zz * 2 + cc) * TD, TD), TD)

    def direct_rows(zz, cc):
        return pl.ds(pl.multiple_of((zz * 2 + cc) * TD, TD), BLK)

    def relay_rows(zz, cc):
        return pl.ds(pl.multiple_of((zz * 2 + cc) * TD + BLK, BLK), BLK)

    mine = rows_of(z, core)

    def token_push(m, k):
        peer = zs[k - 1] if m == 0 else over[k]
        return push(tokens.at[m, 0], xall.at[m, mine], r.v_b_send.at[m, k], r.v_b_recv.at[m, k], peer)

    def token_arrival(m, k):
        block = xall.at[m, rows_of(lax.rem(z + nz - k, nz), core)]
        return push(block, block, r.v_b_send.at[m, k], r.v_b_recv.at[m, k], partner)

    def own_tokens(m):
        return pltpu.make_async_copy(tokens.at[m, 0], xall.at[m, mine], r.v_b_recv.at[m, 0])

    def out_push(m, k):
        return push(
            out.at[m, 0:BLK],
            xall.at[m, direct_rows(z, core)],
            r.v_o_send.at[m, k],
            r.v_b_recv.at[m, k],
            over[k],
        )

    def out_arrival(m, k):
        block = xall.at[m, direct_rows(lax.rem(z + nz - k, nz), core)]
        return push(block, block, r.v_o_send.at[m, k], r.v_b_recv.at[m, k], partner)

    def out_relay(m):
        return push(
            out.at[m, BLK:TD],
            xall.at[m, relay_rows(z, core)],
            r.v_r_send.at[m, 0],
            r.v_r_recv.at[m, 0],
            over[0],
        )

    def relay_push(m, k):
        block = xall.at[m, relay_rows(z, core)]
        return push(block, block, r.v_r_send.at[m, k], r.v_r_recv.at[m, k], zs[k - 1])

    def relay_arrival(m, k):
        block = xall.at[m, relay_rows(lax.rem(z + nz - k, nz), core)]
        return push(block, block, r.v_r_send.at[m, k], r.v_r_recv.at[m, k], partner)

    def forward_push(m, k):
        zz = lax.rem(z + nz - k, nz)
        block = xall.at[m, rows_of(zz, core)]
        return push(block, block, r.v_f_send.at[m, k], r.v_f_recv.at[m, k], partner)

    def cut(base, ww, stride, rows, cc, zp, shared):
        share = rows // 4 if shared else rows // 2
        at = base + ww * stride + ((cc * 2 + zp) if shared else cc) * share
        return pl.ds(pl.multiple_of(at, 16), share)

    def piece(p, ww, cc, zp, local):
        stride = 0 if local else 1
        if p < 4:
            r = cut(0, ww, part * stride, part, cc, zp, False)
            matrix = (1, 2, 0, 3)[p]
            return attn_w.at[0, matrix, r] if local else attn.at[matrix, r]
        if p < 6:
            r = cut(0, ww, part * stride, part, cc, zp, True)
            cols = pl.ds((p - 4) * (FF // 2), FF // 2)
            return up_w.at[0, r, cols] if local else up.at[r, cols]
        base = (p - 6) * (ffp // 2)
        r = cut(base, ww, ffp * stride, ffp // 2, cc, zp, p == 6)
        return down_w.at[0, r] if local else down.at[r]

    shared = [p in (4, 5, 6) for p in range(8)]

    def weight_push(k, p):
        return push(
            piece(p, w, core, par, True),
            piece(p, w, core, par, False),
            r.v_w_send.at[k - 1, p],
            r.v_w_recv.at[k - 1, p],
            xs[k - 1],
        )

    def weight_forward(k, p, way):
        zp = 1 - par if way == 2 else par
        spot = piece(p, lax.rem(w + W - k, W), core, zp, False)
        peer = buddy if way == 1 else partner
        return push(spot, spot, r.v_wf_send.at[k - 1, p, way], r.v_wf_recv.at[k - 1, p, way], peer)

    def x_start(p):
        for k in range(1, W):
            weight_push(k, p).start()

    def x_arrive(p):
        for k in range(1, W):
            weight_push(k, p).wait_recv()
            weight_forward(k, p, 0).start()
            if shared[p]:
                weight_forward(k, p, 1).start()

    def z_arrive(p):
        for k in range(1, W):
            weight_forward(k, p, 1).wait_recv()
            weight_forward(k, p, 2).start()

    def core_arrive(p):
        for k in range(1, W):
            weight_forward(k, p, 0).wait_recv()
            if shared[p]:
                weight_forward(k, p, 2).wait_recv()

    def small_push(k):
        return push(small_in, small_all.at[k], r.v_s_send.at[k - 1], r.v_s_recv.at[k - 1], xs[k - 1])

    own_r = pl.ds(pl.multiple_of(w * part, 16), part)
    own_f = pl.ds(pl.multiple_of(w * ffp, 16), ffp)
    own_loads = [
        pltpu.make_async_copy(attn_w.at[0], attn.at[:, own_r], r.v_load_sem.at[0]),
        pltpu.make_async_copy(up_w.at[0], up.at[own_r], r.v_load_sem.at[1]),
        pltpu.make_async_copy(down_w.at[0], down.at[own_f], r.v_load_sem.at[2]),
    ]

    @pl.when(s == 0)
    def _():
        for k in range(1, nz):
            token_push(0, k).start()
        for m in range(MB):
            own_tokens(m).start()

    @pl.when(s == 1)
    def _():
        for m in range(1, MB):
            for k in range(1, nz):
                token_push(m, k).start()

    x_start(0)
    x_start(1)
    for copy in own_loads:
        copy.start()
    small_in[...] = jnp.zeros_like(small_in)
    span = ffp // D
    for e in range(W):

        @pl.when(w == e)
        def _():
            cols = slice(e * part, (e + 1) * part)
            small_in[0:5, cols] = bias_w[0].astype(f32)
            small_in[5:7, cols] = gain_w[0].astype(f32)
            for j in range(span):
                at = 7 + e * span + j
                small_in[at : at + 1, :] = up_b[0:1, j * D : (j + 1) * D].astype(f32)

    for k in range(1, W):
        small_push(k).start()
    for m in range(MB):
        counts[0, m], counts[1, m] = count_tables(m, lens, chosen, random, c, T // BLK)

    def relay_start(m):
        out_relay(m).wait_recv()
        for k in range(1, nz):
            relay_push(m, k).start()

    def rows_ready(m):
        @pl.when(s == 0)
        def _():
            own_tokens(m).wait()

        @pl.when(s == 1)
        def _():
            out_arrival(m, 0).wait_recv()

        forward_push(m, 0).start()
        for k in range(1, nz):

            @pl.when(s == 0)
            def _():
                token_arrival(m, k).wait_recv()

            @pl.when(s == 1)
            def _():
                out_arrival(m, k).wait_recv()
                relay_arrival(m, k).wait_recv()

            forward_push(m, k).start()
        for k in range(nz):
            forward_push(m, k).wait_recv()

    saves = []
    outs = Spare() if fused else r

    def save(src, dst, always=False):
        if fused and not always:
            return
        copy = pltpu.make_async_copy(src, dst, r.v_save_sem.at[next(numbers)])
        copy.start()
        saves.append(copy)

    numbers = iter(range(100))
    lane = lax.broadcasted_iota(jnp.int32, (TD, 128), 1)
    row = lax.broadcasted_iota(jnp.int32, (TD, 128), 0)
    spots = lax.broadcasted_iota(jnp.int32, (1, T), 1)
    tops = jnp.full((1, 128), masked_score, f32)

    slots = kv.shape[0]

    def feed_copies(m):
        pairs = [(out.at[m], r.out_o.at[0, m, 0])]
        if not fused:
            pairs += [
                (first.at[m], outs.first_o.at[m]),
                (hidden.at[m], outs.hidden_o.at[m]),
                (second.at[m], outs.second_o.at[m]),
            ]
        return [
            pltpu.make_async_copy(a, b, r.v_ff_sem.at[m, e]) for e, (a, b) in enumerate(pairs)
        ]

    weight_copies = []
    if not fused:
        pairs = ((attn, outs.attn_o), (up, outs.up_o), (down, outs.down_o))
        weight_copies = [
            pltpu.make_async_copy(a, b, r.v_ff_sem.at[MB, e]) for e, (a, b) in enumerate(pairs)
        ]

    def weights_whole():
        for copy in own_loads[1:]:
            copy.wait()
        for copy in weight_copies:
            copy.start()

    def feed_in(m):
        branch = dot(att[m], attn[3]) + small[1:2, :]
        first[m] = xall[m, mine, :].astype(f32) + branch

    def feed(m):
        hat, _ = norm_parts(first[m])
        normed = hat * small[5:6, :] + small[3:4, :]
        low = normed.astype(bf16)
        second[m] = normed + small[2:3, :]
        for j in range(NCH):
            cols = slice(j * CHUNK, (j + 1) * CHUNK)
            pre = dot(low, up[:, cols]) + small[7 + j : 8 + j, :]
            hidden[m, :, cols] = pre
            second[m] += dot(gelu(pre).astype(bf16), down[cols, :])
        hat, _ = norm_parts(second[m])
        out[m] = (hat * small[6:7, :] + small[4:5, :]).astype(bf16)
        for copy in feed_copies(m):
            copy.start()

    @pl.when(s == 1)
    def _():
        for p in range(8):
            x_arrive(p)
            if p + 2 < 8:
                x_start(p + 2)
            if p and shared[p - 1]:
                z_arrive(p - 1)
        for p in range(8):
            core_arrive(p)
        weights_whole()
        relay_start(0)

    @pl.when(s == 0)
    def _():
        for p in range(3):
            x_arrive(p)
            x_start(p + 2)
        x_start(5)

    for k in range(1, W):
        small_push(k).wait_recv()
    total = small_in[...]
    for k in range(1, W):
        total = total + small_all[k]
    small[...] = total
    save(small, outs.small_o)
    own_loads[0].wait()
    bias_v = small[0:1, :]

    for m in range(MB):
        rows_ready(m)
        if m + 1 < MB:

            @pl.when(s == 1)
            def _():
                relay_start(m + 1)

        if m == 0:

            @pl.when(s == 0)
            def _():
                for p in range(3):
                    core_arrive(p)

        save(xall.at[m], r.xall_o.at[m], True)

        def project(i, _):
            r = pl.ds(pl.multiple_of(i * 256, 256), 256)
            x = xall[m, r, :]
            kv[m % slots, r, 0:D] = dot(x, attn[1]).astype(bf16)
            kv[m % slots, r, D : 2 * D] = (dot(x, attn[2]) + bias_v).astype(bf16)
            return 0

        lax.fori_loop(0, T // 256, project, 0)
        save(kv.at[m % slots], outs.kv_o.at[m])
        kept_kv = saves[-1] if saves else None
        x_own = xall[m, mine, :]
        q[m] = (dot(x_own, attn[0]).astype(bf16).astype(f32) * (HD**-0.5)).astype(bf16)
        save(q.at[m], outs.q_o.at[m])
        length = lens[m]
        live = spots < length
        weights = dot(counts[0, m].astype(bf16), block_lanes(T // BLK, T))
        weights = jnp.where(live, weights, 0.0)
        wide[...] = weights.reshape(PAIRS, 8, T)

        def attend(g, kept):
            lse_c, top_c = kept
            keys = kv[m % slots, :, pair_lanes(g)]
            values = kv[m % slots, :, pl.ds(pl.multiple_of(D + g * 128, 128), 128)]
            scores = dot_t(halves(q[m, :, pair_lanes(g)]), keys)
            count = spread4(wide[g], T)
            scores = jnp.where(count > 0, scores, masked_score)
            largest = jnp.max(scores, 1, keepdims=True)
            powers = jnp.exp(scores - largest) * count
            total = jnp.sum(powers, 1, keepdims=True)
            mixed = dot(powers.astype(bf16), values) / total
            mix[m, :, pair_lanes(g)] = joined(mixed)
            log_total = largest + jnp.log(total)
            for e in range(2):
                lse_c = jnp.where(lane == 2 * g + e, log_total[e * TD : (e + 1) * TD], lse_c)
                top_c = jnp.where(lane == 2 * g + e, largest[e * TD : (e + 1) * TD], top_c)
            return lse_c, top_c

        zeros = jnp.zeros((TD, 128), f32)
        lse_c, top_c = lax.fori_loop(0, PAIRS, attend, (zeros, zeros), unroll=2)
        lse[m] = lse_c
        if slots < MB:
            saves[:] = [x for x in saves if x is not kept_kv]
            kept_kv.wait()
        top_c = jnp.where(c * TD + row < length, top_c, masked_score)
        tops = jnp.maximum(tops, jnp.max(top_c, 0, keepdims=True))
        att[m] = mix[m].astype(bf16)
        save(lse.at[m], outs.lse_o.at[m])
        save(mix.at[m], outs.mix_o.at[m])
        save(att.at[m], outs.att_o.at[m])

        @pl.when(s == 1)
        def _():
            feed_in(m)
            feed(m)

        if m < 2:

            @pl.when(s == 0)
            def _():
                if m == 0:
                    x_arrive(3)
                x_start(6 + m)

    if MB == 1:

        @pl.when(s == 0)
        def _():
            x_start(7)

    top[...] = jnp.broadcast_to(tops, (8, 128))
    save(top, outs.top_o)

    @pl.when(s == 0)
    def _():
        core_arrive(3)
        for m in range(MB):
            feed_in(m)
        x_arrive(4)
        x_arrive(5)
        z_arrive(4)
        x_arrive(6)
        z_arrive(5)
        x_arrive(7)
        z_arrive(6)
        for p in range(4, 8):
            core_arrive(p)
        weights_whole()
        for m in range(MB):
            feed(m)
            if m:
                for k in range(nz):
                    out_push(m - 1, k).wait_send()
            out_relay(m).start()
            out_relay(m).wait_send()
            for k in range(nz):
                out_push(m, k).start()

    def finish():
        for k in range(1, W):
            small_push(k).wait_send()
            for p in range(8):
                weight_push(k, p).wait_send()
                for way in range(3 if shared[p] else 1):
                    weight_forward(k, p, way).wait_send()
        for m in range(MB):
            for k in range(nz):
                forward_push(m, k).wait_send()

            if m == MB - 1:

                @pl.when(s == 0)
                def _():
                    for k in range(nz):
                        out_push(m, k).wait_send()

            @pl.when(s == 1)
            def _():
                for k in range(1, nz):
                    relay_push(m, k).wait_send()

            @pl.when(s == (0 if m == 0 else 1))
            def _():
                for k in range(1, nz):
                    token_push(m, k).wait_send()

        for copy in saves + weight_copies:
            copy.wait()
        for m in range(MB):
            for copy in feed_copies(m):
                copy.wait()

    return finish


def sum_steps(r, nz, W, count, per):
    s, c, w = place()
    z, core = c // 2, lax.rem(c, 2)
    part = D // W
    root = (nz - 1) // 2
    partner = {"ctx": c + 1 - 2 * core}
    xs = [{"wsh": lax.rem(w + k, W)} for k in range(1, W)]
    grads, from_x, chain, sums = r.grads, r.from_x, r.chain, r.sums

    def spot(i, ww):
        at = (i // per) * D + ww * part + lax.rem(i, per) * ROWS
        return pl.ds(pl.multiple_of(at, 16), ROWS)

    def lines(i):
        return pl.ds(pl.multiple_of(i * ROWS, 16), ROWS)

    def x_push(i, k):
        return push(
            grads.at[spot(i, lax.rem(w + k, W))],
            from_x.at[k - 1, lines(i)],
            r.x_send.at[k - 1, i],
            r.x_recv.at[k - 1, i],
            xs[k - 1],
        )

    is_left = z < root
    to_left = {"ctx": jnp.maximum(z - 1, 0) * 2 + core}
    to_right = {"ctx": jnp.minimum(z + 1, nz - 1) * 2 + core}
    far = max(root, nz - 1 - root)
    depth = jnp.where(z == root, far, jnp.where(is_left, z, nz - 1 - z))
    away = jnp.where(is_left, root - z, z - root)

    def chain_push(i, side, peer):
        block = grads.at[spot(i, w)]
        return push(block, chain.at[side, lines(i)], r.ch_send.at[i], r.ch_recv.at[side, i], peer)

    def total_push(i, side, peer, block):
        return push(block, sums.at[core, lines(i)], r.t_send.at[side, i], r.t_recv.at[i], peer)

    def partner_push(i, block):
        return push(block, sums.at[core, lines(i)], r.p_send.at[i], r.p_recv.at[i], partner)

    def partner_arrival(i):
        block = sums.at[1 - core, lines(i)]
        return push(block, block, r.p_send.at[i], r.p_recv.at[i], partner)

    def own_copy(i):
        return pltpu.make_async_copy(grads.at[spot(i, w)], sums.at[core, lines(i)], r.o_sem.at[i])

    def begin():
        for i in range(FLIGHT):
            for k in range(1, W):
                x_push(i, k).start()

    def step(t):
        @pl.when(t + FLIGHT < count)
        def _():
            for k in range(1, W):
                x_push(t, k).wait_send()
                x_push(t + FLIGHT, k).start()

        i = t - LAG * depth

        @pl.when((i >= 0) & (i < count))
        def _():
            acc = grads[spot(i, w), :].astype(f32)
            for k in range(1, W):
                x_push(i, k).wait_recv()
                acc = acc + from_x[k - 1, lines(i), :].astype(f32)
            grads[spot(i, w), :] = acc.astype(bf16)

            @pl.when((z > 0) & (z <= root))
            def _():
                chain_push(i, 0, to_right).wait_recv()
                both = grads[spot(i, w), :].astype(f32) + chain[0, lines(i), :].astype(f32)
                grads[spot(i, w), :] = both.astype(bf16)

            @pl.when((z < nz - 1) & (z >= root))
            def _():
                chain_push(i, 1, to_left).wait_recv()
                both = grads[spot(i, w), :].astype(f32) + chain[1, lines(i), :].astype(f32)
                grads[spot(i, w), :] = both.astype(bf16)

            @pl.when(z < root)
            def _():
                chain_push(i, 0, to_right).start()

            @pl.when(z > root)
            def _():
                chain_push(i, 1, to_left).start()

            @pl.when(z == root)
            def _():
                block = grads.at[spot(i, w)]
                if root > 0:
                    total_push(i, 0, to_left, block).start()
                if root < nz - 1:
                    total_push(i, 1, to_right, block).start()
                partner_push(i, block).start()
                own_copy(i).start()

        b = t - LAG * (far + away)

        @pl.when((b >= 0) & (b < count) & (z != root))
        def _():
            block = sums.at[core, lines(b)]
            total_push(b, 0, to_left, block).wait_recv()

            @pl.when((z < root) & (z > 0))
            def _():
                total_push(b, 0, to_left, block).start()

            @pl.when((z > root) & (z < nz - 1))
            def _():
                total_push(b, 1, to_right, block).start()

            partner_push(b, block).start()

    last = count + LAG * 2 * far

    def drain(begin, end):
        def one(i, _):
            block = sums.at[core, lines(i)]
            partner_arrival(i).wait_recv()
            partner_push(i, block).wait_send()

            @pl.when(i + FLIGHT >= count)
            def _():
                for k in range(1, W):
                    x_push(i, k).wait_send()

            @pl.when(z != root)
            def _():
                chain_push(i, 0, to_right).wait_send()

            @pl.when(z == root)
            def _():
                own_copy(i).wait()

            @pl.when((z <= root) & (z > 0))
            def _():
                total_push(i, 0, to_left, block).wait_send()

            @pl.when((z >= root) & (z < nz - 1))
            def _():
                total_push(i, 1, to_right, block).wait_send()

            return 0

        lax.fori_loop(begin, end, one, 0)

    def tail(now, small):
        settled = jnp.maximum(now, LAG * 2 * far + 4)

        def one(t, _):
            step(t)
            i = t - settled
            drain(jnp.clip(i, 0, count), jnp.clip(i + 1, 0, count))
            return 0

        lax.fori_loop(now, last, one, 0)
        small()
        drain(jnp.clip(last - settled, 0, count), count)

    return begin, step, tail


def small_steps(r, nz, W):
    s, c, w = place()
    z, core = c // 2, lax.rem(c, 2)
    partner = {"ctx": c + 1 - 2 * core}
    xs = [{"wsh": lax.rem(w + k, W)} for k in range(1, W)]
    zs = [{"ctx": lax.rem(z + k, nz) * 2 + core} for k in range(1, nz)]

    def core_push(e):
        return push(r.core_s.at[e], r.core_s.at[e], r.sc_send, r.sc_recv, partner)

    def x_push(k, e):
        return push(
            r.wsh_s.at[e], r.wsh_s.at[e], r.sx_send.at[k - 1], r.sx_recv.at[k - 1], xs[k - 1]
        )

    def z_push(k, e):
        return push(r.z_s.at[e], r.z_s.at[e], r.sz_send.at[k - 1], r.sz_recv.at[k - 1], zs[k - 1])

    def first(value):
        r.core_s[core] = value
        core_push(core).start()

    def second():
        core_push(1 - core).wait_recv()
        r.wsh_s[w] = r.core_s[0] + r.core_s[1]
        for k in range(1, W):
            x_push(k, w).start()

    def third():
        for k in range(1, W):
            x_push(k, lax.rem(w + W - k, W)).wait_recv()
        total = r.wsh_s[0]
        for e in range(1, W):
            total = total + r.wsh_s[e]
        r.z_s[z] = total
        for k in range(1, nz):
            z_push(k, z).start()

    def finish():
        for k in range(1, nz):
            z_push(k, lax.rem(z + nz - k, nz)).wait_recv()
        total = r.z_s[0]
        for e in range(1, nz):
            total = total + r.z_s[e]
        r.small_o[...] = total
        core_push(core).wait_send()
        for k in range(1, W):
            x_push(k, w).wait_send()
        for k in range(1, nz):
            z_push(k, z).wait_send()

    return first, second, third, finish


def clip_weights(r, tops, own, spare):
    factor = jnp.sqrt(clip_limit / jnp.maximum(tops, clip_limit))
    lane = lax.broadcasted_iota(jnp.int32, (128, D), 1)
    head = lax.broadcasted_iota(jnp.int32, (128, D), 0)
    heads = jnp.where(lax.shift_right_logical(lane, 6) == head, 1.0, 0.0).astype(f32)
    wide = jnp.dot(factor, heads, preferred_element_type=f32, precision=exact_dot)[0:1]
    for p in range(2):
        spare[p][...] = (own(p).astype(f32) * wide).astype(bf16)
    copies = [pltpu.make_async_copy(spare[p], r.clip_o.at[0, p], r.clip_sem.at[p]) for p in range(2)]
    for copy in copies:
        copy.start()
    return copies


def down_tiles(r, W):
    part, gate_half = D // W, FF // W // 2
    for e in range(W):
        cols = slice(e * gate_half, (e + 1) * gate_half)
        block = dot_0(r.lg[:, cols], r.rd[...]).astype(bf16)
        for j in range(2):
            at = j * D + e * part
            r.grads[at : at + part] = block[j * part : (j + 1) * part]


def up_tiles(r):
    for j in range(2):
        block = dot_0(r.ln[...], r.rh[:, j * D : (j + 1) * D])
        r.grads[(2 + j) * D : (3 + j) * D] = block.astype(bf16)


def attn_tiles(r):
    for j, (left, right) in enumerate(((r.la, r.ra), (r.lb, r.rb))):
        r.grads[(4 + j) * D : (5 + j) * D] = dot_0(left[...], right[...]).astype(bf16)


def ff_operands(W, cc, gated, down, normed, hidden, r):
    ffp = FF // W
    found = []
    for e in range(W):
        cols = pl.ds(pl.multiple_of(e * ffp + cc * (ffp // 2), 128), ffp // 2)
        found.append((gated.at[:, cols], r.lg, e * (ffp // 2), ffp // 2))
    cols = pl.ds(pl.multiple_of(cc * (FF // 2), 128), FF // 2)
    return found + [(down, r.rd, 0, D), (normed, r.ln, 0, D), (hidden.at[:, cols], r.rh, 0, FF // 2)]


def attn_operands(cc, qkv, att, branch, x, r):
    if cc == 0:
        return [(x, r.la), (qkv.at[:, 0:D], r.ra), (x, r.lb), (qkv.at[:, D : 2 * D], r.rb)]
    return [(x, r.la), (qkv.at[:, 2 * D : 3 * D], r.ra), (att, r.lb), (branch, r.rb)]


def reduce_kernel(nz, W, MB, r):
    s, c, w = place()
    z, core = c // 2, lax.rem(c, 2)
    part = D // W
    per = part // ROWS
    partner = {"ctx": c + 1 - 2 * core}
    xs = [{"wsh": lax.rem(w + k, W)} for k in range(1, W)]
    zs = [{"ctx": lax.rem(z + k, nz) * 2 + core} for k in range(1, nz)]
    greet(xs + zs + [partner])
    begin, step, tail = sum_steps(r, nz, W, 6 * per, per)
    small_first, small_second, small_third, small_finish = small_steps(r, nz, W)
    mine = pl.ds(pl.multiple_of(c * TD, TD), TD)

    def copies(m, cc, far):
        n = W + 3
        found = []
        rows = (r.gated_h.at[m], r.down_h.at[m], r.normed_h.at[m], r.hidden_h.at[m])
        side = (MB + m if far else m) * TD
        for e, (src, dst, at, width) in enumerate(ff_operands(W, cc, *rows, r)):
            spot = dst.at[side : side + TD, at : at + width]
            found.append((src, spot, m * (n + 4) + e))
        rows = (r.qkv_h.at[m], r.att_h.at[m], r.branch_h.at[m], r.x_h.at[m, mine])
        for e, (src, dst) in enumerate(attn_operands(cc, *rows, r)):
            found.append((src, dst.at[side : side + TD], m * (n + 4) + n + e))
        if far:
            return [push(a, b, r.c_send.at[e], r.c_recv.at[e], partner) for a, b, e in found]
        return [pltpu.make_async_copy(a, b, r.load_sem.at[e]) for a, b, e in found]

    own_load = pltpu.make_async_copy(r.attn_w.at[0, 0:2], r.own_w, r.own_sem)
    own_load.start()
    small_first(r.small_g[...])
    for cc in range(2):

        @pl.when(core == cc)
        def _():
            for m in range(MB):
                for copy in copies(m, 1 - cc, True) + copies(m, cc, False):
                    copy.start()
            for m in range(MB):
                for copy in copies(m, cc, False):
                    copy.wait()
                for copy in copies(m, cc, True):
                    copy.wait_recv()

    down_tiles(r, W)
    begin()
    up_tiles(r)
    attn_tiles(r)
    small_second()
    own_load.wait()
    clip_copies = clip_weights(
        r, r.tops[...], lambda p: r.own_w[p], [r.own_w.at[p] for p in range(2)]
    )
    small_third()

    tail(0, small_finish)
    for copy in clip_copies:
        copy.wait()
    for cc in range(2):

        @pl.when(core == cc)
        def _():
            for m in range(MB):
                for copy in copies(m, 1 - cc, True):
                    copy.wait_send()


def backward_part(nz, W, MB, T, fused, r, settle=None):
    lens, cot, counts, top, small = r.lens, r.cot, r.counts, r.top, r.small
    attn, up, down, xall, q, mix, lse = r.attn, r.up, r.down, r.xall, r.q, r.mix, r.lse
    first, second, hidden, dout, gfirst = r.first, r.second, r.hidden, r.dout, r.gfirst
    gbranch, gall, relay, aux = r.gbranch, r.gall, r.relay, r.aux
    wide_q, wide_k, lse_all, del_all, del_c = r.wide_q, r.wide_k, r.lse_all, r.del_all, r.del_c
    gnorm, ghid, gated, gdown = r.gnorm, r.ghid, r.gated, r.gdown
    small_g, top_x = r.small_g, r.top_x
    dqkv = [up.at[m * TD : (m + 1) * TD, 0 : 3 * D] for m in range(MB)]
    gin = [up.at[(MB + m) * TD : (MB + m + 1) * TD, 0:D] for m in range(MB)]
    s, c, w = place()
    z, core = c // 2, lax.rem(c, 2)
    partner = {"ctx": c + 1 - 2 * core}
    xs = [{"wsh": lax.rem(w + k, W)} for k in range(1, W)]
    zs = [{"ctx": lax.rem(z + k, nz) * 2 + core} for k in range(1, nz)]
    across = {"section": 1 - s}
    over = [{"section": 1 - s, "ctx": lax.rem(z + k, nz) * 2 + core} for k in range(1, nz)]
    if not fused:
        greet(xs + zs + over + [across, partner])
    part = D // W
    per = part // ROWS
    if fused:
        begin, step, tail = sum_steps(r, nz, W, 6 * per, per)
        small_first, small_second, small_third, small_finish = small_steps(r, nz, W)

    def rows_of(zz, cc):
        return pl.ds(pl.multiple_of((zz * 2 + cc) * TD, TD), TD)

    mine = rows_of(z, core)
    loads = []

    class Held:
        def wait(self):
            pass

    home = Spare() if fused else r

    def load(src, dst):
        if fused:
            return Held()
        copy = pltpu.make_async_copy(src, dst, r.load_sem.at[len(loads)])
        copy.start()
        loads.append(copy)
        return copy

    saves = []
    numbers = iter(range(100))

    def save(src, dst):
        copy = pltpu.make_async_copy(src, dst, r.save_sem.at[next(numbers)])
        copy.start()
        saves.append(copy)

    def cot_load(m):
        return pltpu.make_async_copy(cot.at[m, 0], dout.at[m], r.y_recv.at[m])

    def grad_push(m):
        return push(gin[m], dout.at[m], r.y_send.at[m], r.y_recv.at[m], across)

    @pl.when(s == 1)
    def _():
        for m in range(MB):
            cot_load(m).start()

    slots = xall.shape[0]
    load_second = [load(home.second_h.at[m], second.at[m]) for m in range(MB)]
    cuts = [slice(j * CHUNK, (j + 1) * CHUNK) for j in range(NCH)]
    load_hidden, load_down, load_up = [[]], [], []
    for cut in cuts:
        load_hidden[0].append(load(home.hidden_h.at[0, :, cut], hidden.at[0, :, cut]))
        load_down.append(load(home.down_h.at[cut], down.at[cut]))
        load_up.append(load(home.up_h.at[:, cut], up.at[:, cut]))
    late = {}

    def load_rest():
        late["first"] = [load(home.first_h.at[m], first.at[m]) for m in range(MB)]
        late["attn"] = load(home.attn_h, attn)
        late["mix"] = [load(home.mix_h.at[m], mix.at[m]) for m in range(MB)]
        late["lse"] = [load(home.lse_h.at[m], lse.at[m]) for m in range(MB)]
        for m in range(1, slots):
            load_hidden.append([load(home.hidden_h.at[m], hidden.at[m])])
        late["x"] = [load(home.xall_h.at[m], xall.at[m]) for m in range(slots)]
        late["kv"] = [load(home.kv_h.at[m, mine], home.kv_own.at[m]) for m in range(MB)]
        late["q"] = [load(home.q_h.at[m], q.at[m]) for m in range(MB)]

    def cut_rows(zz, cc, side):
        return pl.ds(pl.multiple_of((zz * 2 + cc) * TD + side * BLK, BLK), BLK)

    def rows_push(m, k):
        if k == 0:
            block = gall.at[m, mine]
            return push(block, block, r.f_send.at[m, 0], r.f_recv.at[m, 0], partner)
        block = gall.at[m, cut_rows(z, core, 0)]
        return push(block, block, r.b_send.at[m, k], r.b_recv.at[m, k], zs[k - 1])

    def rows_arrival(m, k):
        block = gall.at[m, cut_rows(lax.rem(z + nz - k, nz), core, 0)]
        return push(block, block, r.b_send.at[m, k], r.b_recv.at[m, k], partner)

    def relay_out(m):
        block = gall.at[m, cut_rows(z, core, 1)]
        return push(block, relay.at[m], r.r_send.at[m, 0], r.r_recv.at[m, 0], across)

    def relay_push(m, k):
        block = gall.at[m, cut_rows(z, core, 1)]
        return push(relay.at[m], block, r.r_send.at[m, k], r.r_recv.at[m, k], over[k - 1])

    def relay_arrival(m, k):
        block = gall.at[m, cut_rows(lax.rem(z + nz - k, nz), core, 1)]
        return push(block, block, r.r_send.at[m, k], r.r_recv.at[m, k], partner)

    def rows_forward(m, k):
        block = gall.at[m, rows_of(lax.rem(z + nz - k, nz), core)]
        return push(block, block, r.f_send.at[m, k], r.f_recv.at[m, k], partner)

    def aux_push(m, k):
        block = aux.at[m, c]
        peer = partner if k == 0 else zs[k - 1]
        send, recv = (r.af_send, r.af_recv) if k == 0 else (r.a_send, r.a_recv)
        return push(block, block, send.at[m, k], recv.at[m, k], peer)

    def aux_arrival(m, k):
        block = aux.at[m, lax.rem(z + nz - k, nz) * 2 + core]
        return push(block, block, r.a_send.at[m, k], r.a_recv.at[m, k], partner)

    def aux_forward(m, k):
        block = aux.at[m, lax.rem(z + nz - k, nz) * 2 + core]
        return push(block, block, r.af_send.at[m, k], r.af_recv.at[m, k], partner)

    def top_push(k):
        return push(top_x.at[0], top_x.at[k], r.tp_send.at[k - 1], r.tp_recv.at[k - 1], xs[k - 1])

    def spread_start(m):
        relay_out(m).start()
        for k in range(nz):
            aux_push(m, k).start()
            rows_push(m, k).start()

    def spread_sent(m):
        relay_out(m).wait_send()
        for k in range(1, nz):
            rows_push(m, k).wait_send()

    def relay_one(m):
        relay_out(m).wait_recv()
        for k in range(1, nz):
            relay_push(m, k).start()

    def rows_copies(m, cc, far, late):
        side = (MB + m if far else m) * TD
        found = []
        if late:
            rows = (dqkv[m], r.att.at[m], gbranch.at[m], r.xall_o.at[m, mine])
            for e, (src, dst) in enumerate(attn_operands(cc, *rows, r)):
                found.append((src, dst.at[side : side + TD], m * (W + 7) + W + 3 + e))
        else:
            rows = (gated.at[m], gdown.at[m], gnorm.at[m], ghid.at[m])
            for e, (src, dst, at, width) in enumerate(ff_operands(W, cc, *rows, r)):
                found.append((src, dst.at[side : side + TD, at : at + width], m * (W + 7) + e))
        if far:
            return [push(a, b, r.c_send.at[e], r.c_recv.at[e], partner) for a, b, e in found]
        return [pltpu.make_async_copy(a, b, r.c_load.at[e]) for a, b, e in found]

    def rows_start(m, late):
        for cc in range(2):

            @pl.when(core == cc)
            def _():
                for copy in rows_copies(m, 1 - cc, True, late) + rows_copies(m, cc, False, late):
                    copy.start()

    def rows_here(late, picked):
        for cc in range(2):

            @pl.when(core == cc)
            def _():
                for m in range(MB):
                    for copy in rows_copies(m, cc, False, late)[picked]:
                        copy.wait()
                    for copy in rows_copies(m, cc, True, late)[picked]:
                        copy.wait_recv()

    def ff_gradients():
        rows_here(False, slice(0, W + 1))
        down_tiles(r, W)
        begin()
        rows_here(False, slice(W + 1, None))
        up_tiles(r)

    def rows_sent():
        for cc in range(2):

            @pl.when(core == cc)
            def _():
                for m in range(MB):
                    for late in (False, True):
                        for copy in rows_copies(m, 1 - cc, True, late):
                            copy.wait_send()

    @pl.when(s == 0)
    def _():
        for m in range(MB):
            relay_one(m)

    heads = lax.broadcasted_iota(jnp.int32, (D, 128), 0)
    heads = lax.shift_right_logical(heads, 6) == lax.broadcasted_iota(jnp.int32, (D, 128), 1)
    heads = jnp.where(heads, 1.0, 0.0).astype(f32)
    small_g[...] = jnp.zeros_like(small_g)

    for m in range(MB):
        load_second[m].wait()

        @pl.when(s == 1)
        def _():
            cot_load(m).wait()

        @pl.when(s == 0)
        def _():
            grad_push(m).wait_recv()

        grad_out = dout[m].astype(f32)
        hat, rstd = norm_parts(second[m])
        small_g[1:2, :] += column_sum(grad_out * hat)
        small_g[6:7, :] += column_sum(grad_out)
        grad_second = norm_back(grad_out, hat, rstd, small[6:7, :])
        low_second = grad_second.astype(bf16)
        gdown[m] = low_second
        if not fused:
            save(gdown.at[m], r.rows_down.at[m])
        small_g[4:5, :] += column_sum(low_second.astype(f32))
        if m >= slots:
            load_hidden.append([load(home.hidden_h.at[m], hidden.at[m % slots])])
            for copy in hidden_saves:
                saves[:] = [x for x in saves if x is not copy]
                copy.wait()
        if m:
            load_hidden[m][0].wait()
        gfirst[m] = grad_second
        for j in range(NCH):
            cols = slice(j * CHUNK, (j + 1) * CHUNK)
            if m == 0:
                load_hidden[0][j].wait()
                load_down[j].wait()
                if j == NCH - 1:
                    load_rest()
            value, slope = gelu_both(hidden[m % slots, :, cols])
            gated[m % slots, :, cols] = value.astype(bf16)
            grad_hidden = (slope * dot_t(low_second, down[cols, :])).astype(bf16)
            ghid[m % slots, :, cols] = grad_hidden
            small_g[7 + j : 8 + j, :] += column_sum(grad_hidden.astype(f32))
            if m == 0:
                load_up[j].wait()
            gfirst[m] += dot_t(grad_hidden, up[:, cols])
        if not fused:
            save(gated.at[m % slots], r.rows_gated.at[m])
            save(ghid.at[m % slots], r.rows_hidden.at[m])
            hidden_saves = saves[-2:]
        grad_normed = gfirst[m]
        late["first"][m].wait()
        hat, rstd = norm_parts(first[m])
        gnorm[m] = (hat * small[5:6, :] + small[3:4, :]).astype(bf16)
        if fused:
            rows_start(m, False)
        small_g[0:1, :] += column_sum(grad_normed * hat)
        small_g[5:6, :] += column_sum(grad_normed)
        grad_first = norm_back(grad_normed, hat, rstd, small[5:6, :])
        gfirst[m] = grad_first
        low_first = grad_first.astype(bf16)
        gbranch[m] = low_first
        if not fused:
            save(gnorm.at[m], r.rows_normed.at[m])
            save(gbranch.at[m], r.rows_branch.at[m])
        small_g[3:4, :] += column_sum(low_first.astype(f32))
        late["mix"][m].wait()
        late["lse"][m].wait()
        if m == 0:
            late["attn"].wait()
        grad_att = dot_t(low_first, attn[3]).astype(bf16)
        gall[m, mine, :] = grad_att
        weighed = grad_att.astype(f32) * mix[m]
        delta = jnp.dot(weighed, heads, preferred_element_type=f32, precision=exact_dot)
        del_c[m] = delta
        aux[m, c, 0:16] = lse[m].T[0:16]
        aux[m, c, 16:32] = delta.T[0:16]
        aux[m, c, 32:40] = top[...]
        if m == 0:
            spread_start(0)
        elif m == 1:

            @pl.when(s == 0)
            def _():
                spread_sent(0)
                spread_start(1)

    if fused:
        settle()

        @pl.when(s == 0)
        def _():
            ff_gradients()

    row_steps = PAIRS // PACE
    mid_steps = 2
    per_pass = 2 * row_steps + mid_steps

    def paced(base, period):
        if not fused:
            return lambda g: None

        def run(g):
            @pl.when((s == 0) & (lax.rem(g, period) == period - 1))
            def _():
                step(base + g // period)

        return run

    spots = lax.broadcasted_iota(jnp.int32, (1, T), 1)
    here = lax.broadcasted_iota(jnp.int32, (TD, 128), 0)
    def own_pass(m):
        if m >= slots:
            late["x"].append(load(home.xall_h.at[m], xall.at[m % slots]))
        for name in ("x", "kv", "q"):
            late[name][m].wait()

        def stream(g):
            if fused:
                return []
            slot = lax.rem(g, 2)
            return [
                pltpu.make_async_copy(
                    r.kv_h.at[m, :, pl.ds(pl.multiple_of(e * D + g * 128, 128), 128)],
                    r.kvp.at[slot, e],
                    r.kvp_sem.at[slot, e],
                )
                for e in range(2)
            ]

        for copy in stream(0):
            copy.start()
        length = lens[m]
        lanes = block_lanes(T // BLK, T)
        counted = jnp.where(spots < length, dot(counts[0, m].astype(bf16), lanes), 0.0)
        counted = jnp.where(counted > 0, jnp.log(jnp.maximum(counted, 1.0)), masked_score)
        wide_q[...] = counted.reshape(PAIRS, 8, T)
        advance = paced(m * per_pass, PACE)
        advance_mid = paced(m * per_pass + row_steps, max(1, T // 256 // mid_steps))

        def own_rows(g, _):
            if not fused:

                @pl.when(g + 1 < PAIRS)
                def _():
                    for copy in stream(g + 1):
                        copy.start()

            for copy in stream(g):
                copy.wait()
            slot = lax.rem(g, 2)
            lse_c = jnp.concatenate([head_column(lse[m], 2 * g + e) for e in range(2)], 0)
            delta = jnp.concatenate([head_column(del_c[m], 2 * g + e) for e in range(2)], 0)
            queries = halves(q[m, :, pair_lanes(g)])
            grads = halves(gall[m, mine, pair_lanes(g)])
            grad_q = jnp.zeros((2 * TD, 2 * HD), f32)
            for t in range(0, T, STEP):
                if fused:
                    keys = r.kv[m, t : t + STEP, pair_lanes(g)]
                    values = r.kv[m, t : t + STEP, value_lanes(g)]
                else:
                    keys = r.kvp[slot, 0, t : t + STEP]
                    values = r.kvp[slot, 1, t : t + STEP]
                shift = wide_q[g, :, t : t + STEP]
                probs = jnp.exp(dot_t(queries, keys) + spread4(shift, STEP) - lse_c)
                grad_probs = dot_t(grads, values)
                grad_scores = (probs * (grad_probs - delta)).astype(bf16)
                grad_q = grad_q + dot(grad_scores, keys)
            dqkv[m][:, pair_lanes(g)] = (joined(grad_q) * (HD**-0.5)).astype(bf16)
            advance(g)
            return 0

        lax.fori_loop(0, PAIRS, own_rows, 0, unroll=2)
        if m + 1 < MB:

            @pl.when((s == 1) | (m > 0))
            def _():
                spread_sent(m)
                spread_start(m + 1)

        def project(i, _):
            rows = pl.ds(pl.multiple_of(i * 256, 256), 256)
            all_q = dot(xall[m % slots, rows, :], attn[0]).astype(bf16).astype(f32)
            xall[m % slots, rows, :] = (all_q * (HD**-0.5)).astype(bf16)
            advance_mid(i)
            return 0

        lax.fori_loop(0, T // 256, project, 0)

    def all_pass(m):
        lanes = block_lanes(T // BLK, T)
        length = lens[m]
        for k in range(1, nz):
            rows_arrival(m, k).wait_recv()
            relay_arrival(m, k).wait_recv()
            rows_forward(m, k).start()
            aux_arrival(m, k).wait_recv()
            aux_forward(m, k).start()
        for k in range(nz):
            rows_forward(m, k).wait_recv()
            aux_forward(m, k).wait_recv()
        for cc in range(2 * nz):
            lse_all[:, cc * TD : (cc + 1) * TD] = aux[m, cc, 0:16]
            del_all[:, cc * TD : (cc + 1) * TD] = aux[m, cc, 16:32]
        if m == 0:
            most = aux[0, 0, 32:40]
            for cc in range(1, 2 * nz):
                most = jnp.maximum(most, aux[0, cc, 32:40])
            top_x[0] = most
            for k in range(1, W):
                top_push(k).start()
        counted = dot(counts[1, m].astype(bf16), lanes)
        counted = jnp.where(counted > 0, jnp.log(jnp.maximum(counted, 1.0)), masked_score)
        wide_k[...] = counted.reshape(PAIRS, 8, T)
        live = c * TD + here < length
        advance_keys = paced(m * per_pass + row_steps + mid_steps, PACE)

        def own_keys(g, _):
            own_kv = r.kv.at[m, mine] if fused else r.kv_own.at[m]
            keys = halves(own_kv[:, pair_lanes(g)])
            values = halves(own_kv[:, value_lanes(g)])
            lse_r = [lse_all[pl.ds(2 * g + e, 1), :] for e in range(2)]
            delta = [del_all[pl.ds(2 * g + e, 1), :] for e in range(2)]
            shift = wide_k[g]
            shift = jnp.concatenate([shift[0:2] - lse_r[0], shift[2:4] - lse_r[1]], 0)
            grad_k = jnp.zeros((2 * TD, 2 * HD), f32)
            grad_v = jnp.zeros((2 * TD, 2 * HD), f32)
            for t in range(0, T, STEP):
                queries = xall[m % slots, t : t + STEP, pair_lanes(g)]
                grads = gall[m, t : t + STEP, pair_lanes(g)]
                probs = jnp.exp(dot_t(keys, queries) + spread4(shift[:, t : t + STEP], STEP))
                grad_v = grad_v + dot(probs.astype(bf16), grads)
                centre = jnp.concatenate(
                    [jnp.broadcast_to(d[:, t : t + STEP], (TD, STEP)) for d in delta], 0
                )
                grad_scores = (probs * (dot_t(values, grads) - centre)).astype(bf16)
                grad_k = grad_k + dot(grad_scores, queries)
            grad_k, grad_v = joined(grad_k), joined(grad_v)
            lanes_k = pl.ds(pl.multiple_of(D + g * 128, 128), 128)
            lanes_v = pl.ds(pl.multiple_of(2 * D + g * 128, 128), 128)
            dqkv[m][:, lanes_k] = jnp.where(live, grad_k, 0.0).astype(bf16)
            dqkv[m][:, lanes_v] = jnp.where(live, grad_v, 0.0).astype(bf16)
            advance_keys(g)
            return 0

        lax.fori_loop(0, PAIRS, own_keys, 0, unroll=2)
        if fused:
            rows_start(m, True)
        else:
            save(dqkv[m], r.rows_qkv.at[m])
        small_g[2:3, :] += column_sum(dqkv[m][:, 2 * D : 3 * D].astype(f32))
        total = gfirst[m]
        for p in range(3):
            total = total + dot_t(dqkv[m][:, p * D : (p + 1) * D], attn[p])
        gin[m][...] = total.astype(bf16)

        @pl.when(s == 1)
        def _():
            grad_push(m).start()

        save(gin[m], r.grad_in_o.at[0, m, 0])

    for m in range(MB):
        own_pass(m)
        all_pass(m)

    def loop(t, _):
        step(t)
        return 0

    if fused:
        small_first(small_g[...])
        done_1 = EARLY

        @pl.when(s == 1)
        def _():
            relay_one(0)
            ff_gradients()
            lax.fori_loop(0, EARLY, loop, 0)
            for m in range(1, MB):
                relay_one(m)

        rows_here(True, slice(None))
        attn_tiles(r)
        small_second()
        done_0 = MB * per_pass
        now = jnp.where(s == 0, done_0, done_1)
        lax.fori_loop(now, now + 3, loop, 0)
        small_third()
    else:

        @pl.when(s == 1)
        def _():
            for m in range(MB):
                relay_one(m)

        save(small_g, r.small_o)
    for k in range(1, W):
        top_push(k).wait()
    most = top_x[0]
    for k in range(1, W):
        most = jnp.maximum(most, top_x[k])
    if fused:
        for k in range(nz):
            rows_forward(0, k).wait_send()
        saves.extend(
            clip_weights(
                r,
                most,
                lambda p: attn[p, pl.ds(pl.multiple_of(w * part, 16), part), :],
                [gall.at[0, p * part : (p + 1) * part] for p in range(2)],
            )
        )
        tail(now + 3, small_finish)
        rows_sent()
    else:
        r.top_o[...] = most
    for m in range(MB):
        for k in range(nz):
            if m or not fused:
                rows_forward(m, k).wait_send()
            aux_forward(m, k).wait_send()
        for k in range(1, nz):
            aux_push(m, k).wait_send()
            relay_push(m, k).wait_send()
        if m == MB - 1:
            spread_sent(m)

        @pl.when(s == 1)
        def _():
            grad_push(m).wait_send()

    for copy in saves:
        copy.wait()


def finish_kernel(W, r):
    w = lax.axis_index("wsh")
    part, ffp = D // W, FF // W
    span = ffp // D
    straight = [
        [pltpu.make_async_copy(a, b, r.pass_sem.at[0, e]), pltpu.make_async_copy(b, c, r.pass_sem.at[1, e])]
        for e, (a, b, c) in enumerate(
            (
                (r.out, r.out_v, r.out_o),
                (r.grad_in, r.grad_in_v, r.grad_in_o),
                (r.clip, r.clip_v, r.clip_o),
            )
        )
    ]

    def take(t):
        at = ((t // 4) * 2 + t % 2) * part
        source = r.sums.at[(t % 4) // 2, at : at + part]
        return pltpu.make_async_copy(source, r.low.at[t % BUFFERS], r.in_sem.at[t % BUFFERS])

    def give(t):
        if t < 4:
            spot = r.down_o.at[0, t * part : (t + 1) * part]
        elif t < 8:
            spot = r.up_o.at[0, :, (t - 4) * D : (t - 3) * D]
        else:
            spot = r.attn_o.at[0, t - 8]
        return pltpu.make_async_copy(r.wide.at[t % BUFFERS], spot, r.out_sem.at[t % BUFFERS])

    for t in range(BUFFERS):
        take(t).start()
    for come, _ in straight:
        come.start()
    for e in range(W):

        @pl.when(w == e)
        def _():
            cols = slice(e * part, (e + 1) * part)
            r.gains_o[0] = r.small[0:2, cols]
            for j in range(5):
                r.biases_o[j] = r.small[2 + j : 3 + j, cols]
            for j in range(span):
                at = 7 + e * span + j
                r.up_b_o[0:1, j * D : (j + 1) * D] = r.small[at : at + 1, :]

    for t in range(12):
        take(t).wait()
        if t >= BUFFERS:
            give(t - BUFFERS).wait()
        r.wide[t % BUFFERS] = r.low[t % BUFFERS].astype(f32)
        give(t).start()
        if t + BUFFERS < 12:
            take(t + BUFFERS).start()
        if t < 3:
            straight[t][0].wait()
            straight[t][1].start()
    for t in range(12 - BUFFERS, 12):
        give(t).wait()
    for _, go in straight:
        go.wait()


VMEM = pl.BlockSpec(memory_space=pltpu.VMEM)
SMEM = pl.BlockSpec(memory_space=pltpu.SMEM)
ANY = pl.BlockSpec(memory_space=pl.ANY)
DMA = pltpu.SemaphoreType.DMA


def slots_of(T, MB):
    return MB if T <= 2048 else 1


def call(kernel, name, number, limit, ins, outs, scratch):
    names = list(ins) + list(outs) + list(scratch)

    def body(*refs):
        kernel(types.SimpleNamespace(**dict(zip(names, refs, strict=True))))

    found = pl.pallas_call(
        body,
        out_shape=[jax.ShapeDtypeStruct(*v[:2]) for v in outs.values()],
        in_specs=[v[1] for v in ins.values()],
        out_specs=[v[2] for v in outs.values()],
        scratch_shapes=list(scratch.values()),
        compiler_params=pltpu.CompilerParams(
            collective_id=number,
            has_side_effects=number is not None,
            vmem_limit_bytes=limit << 20,
        ),
        name=name,
    )(*(v[0] for v in ins.values()))
    return dict(zip(outs, found))


def sum_scratch(nz, W, MB):
    part, R = D // W, MB * TD
    count = 6 * (part // ROWS)
    copies = MB * (W + 7)
    return dict(
        lg=pltpu.VMEM((2 * R, FF // 2), bf16),
        rd=pltpu.VMEM((2 * R, D), bf16),
        ln=pltpu.VMEM((2 * R, D), bf16),
        rh=pltpu.VMEM((2 * R, FF // 2), bf16),
        la=pltpu.VMEM((2 * R, D), bf16),
        ra=pltpu.VMEM((2 * R, D), bf16),
        lb=pltpu.VMEM((2 * R, D), bf16),
        rb=pltpu.VMEM((2 * R, D), bf16),
        from_x=pltpu.VMEM((W - 1, 6 * part, D), bf16),
        chain=pltpu.VMEM((2, 6 * part, D), bf16),
        core_s=pltpu.VMEM((2, 16, D), f32),
        wsh_s=pltpu.VMEM((W, 16, D), f32),
        z_s=pltpu.VMEM((nz, 16, D), f32),
        c_send=DMA((copies,)),
        c_recv=DMA((copies,)),
        c_load=DMA((copies,)),
        x_send=DMA((W - 1, count)),
        x_recv=DMA((W - 1, count)),
        ch_send=DMA((count,)),
        ch_recv=DMA((2, count)),
        t_send=DMA((2, count)),
        t_recv=DMA((count,)),
        p_send=DMA((count,)),
        p_recv=DMA((count,)),
        o_sem=DMA((count,)),
        clip_sem=DMA((2,)),
        sc_send=DMA,
        sc_recv=DMA,
        sx_send=DMA((W - 1,)),
        sx_recv=DMA((W - 1,)),
        sz_send=DMA((nz - 1,)),
        sz_recv=DMA((nz - 1,)),
    )


def sum_outs(W):
    part = D // W
    return dict(
        sums=((2, 6 * part, D), bf16, ANY),
        small_o=((16, D), f32, VMEM),
        clip_o=((1, 2, part, D), bf16, ANY),
    )


def forward_ins(lens, chosen, random, tokens, attn_w, up_w, down_w, bias_w, gain_w, up_b):
    return dict(
        lens=(lens, SMEM),
        chosen=(chosen, SMEM),
        random=(random, VMEM),
        tokens=(tokens, ANY),
        attn_w=(attn_w, ANY),
        up_w=(up_w, ANY),
        down_w=(down_w, ANY),
        bias_w=(bias_w, VMEM),
        gain_w=(gain_w, VMEM),
        up_b=(up_b, VMEM),
    )


def shared_scratch(T, MB, fused):
    slots = slots_of(T, MB)
    return dict(
        attn=pltpu.VMEM((4, D, D), bf16),
        up=pltpu.VMEM((D, FF), bf16),
        down=pltpu.VMEM((FF + 2 * D if fused else FF, D), bf16),
        q=pltpu.VMEM((MB, TD, D), bf16),
        mix=pltpu.VMEM((MB, TD, D), f32),
        lse=pltpu.VMEM((MB, TD, 128), f32),
        first=pltpu.VMEM((MB, TD, D), f32),
        second=pltpu.VMEM((MB, TD, D), f32),
        wide_q=pltpu.VMEM((PAIRS, 8, T), f32),
    )


def forward_scratch(nz, W, MB, T):
    return dict(
        small_in=pltpu.VMEM((16, D), f32),
        small_all=pltpu.VMEM((W, 16, D), f32),
        small=pltpu.VMEM((16, D), f32),
        xall=pltpu.VMEM((MB, T, D), bf16),
        kv=pltpu.VMEM((slots_of(T, MB), T, 2 * D), bf16),
        att=pltpu.VMEM((MB, TD, D), bf16),
        top=pltpu.VMEM((8, 128), f32),
        hidden=pltpu.VMEM((MB, TD, FF), f32),
        out=pltpu.VMEM((MB, TD, D), bf16),
        v_load_sem=DMA((3,)),
        v_w_send=DMA((W - 1, 8)),
        v_w_recv=DMA((W - 1, 8)),
        v_wf_send=DMA((W - 1, 8, 3)),
        v_wf_recv=DMA((W - 1, 8, 3)),
        v_s_send=DMA((W - 1,)),
        v_s_recv=DMA((W - 1,)),
        v_ff_sem=DMA((MB + 1, 4)),
        v_save_sem=DMA((2 + 6 * MB,)),
        **{"v_" + k: DMA((MB, nz)) for k in V_RINGS},
    )


def backward_scratch(nz, W, MB, T):
    slots = slots_of(T, MB)
    return dict(
        dout=pltpu.VMEM((MB, TD, D), bf16),
        gfirst=pltpu.VMEM((MB, TD, D), f32),
        gbranch=pltpu.VMEM((MB, TD, D), bf16),
        gall=pltpu.VMEM((MB, T, D), bf16),
        relay=pltpu.VMEM((MB, BLK, D), bf16),
        aux=pltpu.VMEM((MB, 2 * nz, 40, 128), f32),
        wide_k=pltpu.VMEM((PAIRS, 8, T), f32),
        lse_all=pltpu.VMEM((16, T), f32),
        del_all=pltpu.VMEM((16, T), f32),
        del_c=pltpu.VMEM((MB, TD, 128), f32),
        gnorm=pltpu.VMEM((MB, TD, D), bf16),
        ghid=pltpu.VMEM((slots, TD, FF), bf16),
        gated=pltpu.VMEM((slots, TD, FF), bf16),
        gdown=pltpu.VMEM((MB, TD, D), bf16),
        small_g=pltpu.VMEM((16, D), f32),
        top_x=pltpu.VMEM((W, 8, 128), f32),
        load_sem=DMA((1 + 3 * NCH + 8 * MB,)),
        y_send=DMA((MB,)),
        y_recv=DMA((MB,)),
        tp_send=DMA((W - 1,)),
        tp_recv=DMA((W - 1,)),
        save_sem=DMA((1 + 7 * MB,)),
        **{k: DMA((MB, nz)) for k in RINGS},
    )


def run_layers(nz, W, MB, cot, ins):
    T = 2 * nz * TD
    ins = dict(ins, cot=(cot, ANY))
    outs = dict(
        out_o=((1, MB, 1, TD, D), bf16, ANY),
        xall_o=((MB, T, D), bf16, ANY),
        grad_in_o=((1, MB, 1, TD, D), bf16, ANY),
        **sum_outs(W),
    )
    scratch = shared_scratch(T, MB, True)
    scratch.update(forward_scratch(nz, W, MB, T))
    scratch.update(backward_scratch(nz, W, MB, T))
    scratch.update(sum_scratch(nz, W, MB))
    scratch.update(counts=pltpu.VMEM((2, MB, PAIRS * 8, T // BLK), f32))

    def kernel(r):
        r.grads = r.down
        settle = forward_part(nz, W, MB, T, True, r)
        backward_part(nz, W, MB, T, True, r, settle)

    return call(kernel, "layers", 0, 63, ins, outs, scratch)


def run_forward(nz, W, MB, ins):
    T = 2 * nz * TD
    outs = dict(
        counts=((2, MB, PAIRS * 8, T // BLK), f32, VMEM),
        out_o=((1, MB, 1, TD, D), bf16, ANY),
        xall_o=((MB, T, D), bf16, ANY),
        kv_o=((MB, T, 2 * D), bf16, ANY),
        q_o=((MB, TD, D), bf16, ANY),
        att_o=((MB, TD, D), bf16, ANY),
        mix_o=((MB, TD, D), f32, ANY),
        lse_o=((MB, TD, 128), f32, ANY),
        first_o=((MB, TD, D), f32, ANY),
        second_o=((MB, TD, D), f32, ANY),
        hidden_o=((MB, TD, FF), f32, ANY),
        top_o=((8, 128), f32, ANY),
        attn_o=((4, D, D), bf16, ANY),
        up_o=((D, FF), bf16, ANY),
        down_o=((FF, D), bf16, ANY),
        small_o=((16, D), f32, ANY),
    )
    scratch = shared_scratch(T, MB, False)
    scratch.update(forward_scratch(nz, W, MB, T))

    def kernel(r):
        forward_part(nz, W, MB, T, False, r)()

    return call(kernel, "forward", 0, 60, ins, outs, scratch)


def run_backward(nz, W, MB, lens, cot, saved):
    T = 2 * nz * TD
    slots = slots_of(T, MB)
    ins = dict(
        lens=(lens, SMEM),
        cot=(cot, ANY),
        **{k: (v, VMEM if k in ("top", "small", "counts") else ANY) for k, v in saved.items()},
    )
    outs = dict(
        grad_in_o=((1, MB, 1, TD, D), bf16, ANY),
        rows_qkv=((MB, TD, 3 * D), bf16, ANY),
        rows_branch=((MB, TD, D), bf16, ANY),
        rows_normed=((MB, TD, D), bf16, ANY),
        rows_hidden=((MB, TD, FF), bf16, ANY),
        rows_gated=((MB, TD, FF), bf16, ANY),
        rows_down=((MB, TD, D), bf16, ANY),
        small_o=((16, D), f32, ANY),
        top_o=((8, 128), f32, VMEM),
    )
    scratch = shared_scratch(T, MB, False)
    scratch.update(backward_scratch(nz, W, MB, T))
    scratch.update(
        xall=pltpu.VMEM((slots, T, D), bf16),
        hidden=pltpu.VMEM((slots, TD, FF), f32),
        kv_own=pltpu.VMEM((MB, TD, 2 * D), bf16),
        kvp=pltpu.VMEM((2, 2, T, 2 * HD), bf16),
        kvp_sem=DMA((2, 2)),
    )

    def kernel(r):
        backward_part(nz, W, MB, T, False, r)

    return call(kernel, "backward", 1, 60, ins, outs, scratch)


def run_reduce(nz, W, MB, ins):
    part = D // W
    scratch = sum_scratch(nz, W, MB)
    scratch.update(
        grads=pltpu.VMEM((6 * D, D), bf16),
        own_w=pltpu.VMEM((2, part, D), bf16),
        load_sem=DMA((MB * (W + 7),)),
        own_sem=DMA,
    )
    ins = {k: (v, VMEM if k in ("small_g", "tops") else ANY) for k, v in ins.items()}
    return call(
        functools.partial(reduce_kernel, nz, W, MB), "reduce", 2, 60, ins, sum_outs(W), scratch
    )


def run_finish(W, MB, sums, small, out, grad_in, clip):
    part, ffp = D // W, FF // W
    HBM = pl.BlockSpec(memory_space=pltpu.MemorySpace.HBM)
    ins = dict(
        sums=(sums, HBM),
        small=(small, VMEM),
        out=(out, HBM),
        grad_in=(grad_in, HBM),
        clip=(clip, HBM),
    )
    outs = dict(
        out_o=(out.shape, bf16, HBM),
        grad_in_o=(grad_in.shape, bf16, HBM),
        attn_o=((1, 4, part, D), f32, HBM),
        up_o=((1, part, FF), f32, HBM),
        down_o=((1, ffp, D), f32, HBM),
        gains_o=((1, 2, part), f32, VMEM),
        biases_o=((5, 1, part), f32, VMEM),
        up_b_o=((1, ffp), f32, VMEM),
        clip_o=(clip.shape, bf16, HBM),
    )
    scratch = dict(
        low=pltpu.VMEM((BUFFERS, part, D), bf16),
        wide=pltpu.VMEM((BUFFERS, part, D), f32),
        in_sem=DMA((BUFFERS,)),
        out_sem=DMA((BUFFERS,)),
        pass_sem=DMA((2, 3)),
        out_v=pltpu.VMEM(out.shape, bf16),
        grad_in_v=pltpu.VMEM(grad_in.shape, bf16),
        clip_v=pltpu.VMEM(clip.shape, bf16),
    )
    return call(functools.partial(finish_kernel, W), "finish", None, 62, ins, outs, scratch)


def per_device(
    tokens, out_cotangent, attn_weights, up_weights, down_weights, norm_gains, bias_rows, up_bias,
    seq_lengths, rand_owner, rand_local, global_raw,
):
    n_ctx, W = lax.axis_size("ctx"), lax.axis_size("wsh")
    nz = n_ctx // 2
    MB = tokens.shape[0]
    lens = seq_lengths[:, 0]
    random = (rand_owner * BLK_DEV + rand_local).reshape(MB, BLK_DEV * n_ctx, H * RND)
    ins = forward_ins(
        lens, global_raw, random, tokens, attn_weights, up_weights, down_weights, bias_rows,
        norm_gains, up_bias,
    )
    if W == 2 and n_ctx * TD <= 2048:
        got = run_layers(nz, W, MB, out_cotangent, ins)
        out, grad_in = got["out_o"], got["grad_in_o"]
    else:
        kept = run_forward(nz, W, MB, ins)
        out, att = kept["out_o"], kept["att_o"]
        names = ["xall", "kv", "q", "mix", "lse", "first", "second", "hidden", "attn", "up", "down"]
        saved = {k + "_h": kept[k + "_o"] for k in names}
        saved.update(top=kept["top_o"], small=kept["small_o"], counts=kept["counts"])
        got = run_backward(nz, W, MB, lens, out_cotangent, saved)
        grad_in = got["grad_in_o"]
        names = ("gated", "down", "normed", "hidden", "qkv", "branch")
        rows = {k + "_h": got["rows_" + k] for k in names}
        rows.update(
            att_h=att, x_h=kept["xall_o"], small_g=got["small_o"], tops=got["top_o"],
            attn_w=attn_weights,
        )
        got = run_reduce(nz, W, MB, rows)
    done = run_finish(W, MB, got["sums"], got["small_o"], out, grad_in, got["clip_o"])
    done["biases_o"] = done["biases_o"].transpose(1, 0, 2)
    return tuple(done.values())


def solution(mesh):
    placed = (
        P(None, "wsh", "ctx", None),
        P(None, "wsh", "ctx", None),
        P("section", None, "wsh", None),
        P("section", "wsh", None),
        P("section", "wsh", None),
        P("section", None, "wsh"),
        P("section", None, "wsh"),
        P("section", "wsh"),
        P(None, "wsh"),
        P(None, "wsh", None, None, None),
        P(None, "wsh", None, None, None),
        P(None, "wsh", None),
    )
    return jax.shard_map(
        per_device,
        mesh=mesh,
        in_specs=placed,
        out_specs=(
            P("section", None, "wsh", "ctx", None),
            P("section", None, "wsh", "ctx", None),
            P("section", None, "wsh", None),
            P("section", "wsh", None),
            P("section", "wsh", None),
            P("section", None, "wsh"),
            P("section", None, "wsh"),
            P("section", "wsh"),
            P("section", None, "wsh", None),
        ),
        check_vma=False,
    )
```

```python
import functools
import types

import jax
import jax.numpy as jnp
from jax import lax
from jax.experimental import pallas as pl
from jax.experimental.pallas import tpu as pltpu
from jax.sharding import PartitionSpec as P

D = 768
H = 12
HD = 64
FF = 3072
BLK = 64
TD = 128
BLK_DEV = 2
RND = 3
PAIRS = H // 2
CHUNK = 768
NCH = FF // CHUNK
STEP = 1024
ROWS = 48
FLIGHT = 4
LAG = 3
PACE = 1
EARLY = 4
BUFFERS = 4
V_RINGS = [a + b for a in ("b", "f", "r") for b in ("_send", "_recv")] + ["o_send"]
RINGS = [a + b for a in ("b", "f", "a", "af", "r") for b in ("_send", "_recv")]

MESH = pl.DeviceIdType.MESH
norm_eps = 1e-05
clip_limit = 6.0
masked_score = -1e30
exact_dot = lax.Precision.HIGHEST
f32 = jnp.float32
bf16 = jnp.bfloat16


def dot(a, b):
    return jnp.dot(a, b, preferred_element_type=f32)


def dot_t(a, b):
    return lax.dot_general(a, b, (((1,), (1,)), ((), ())), preferred_element_type=f32)


def dot_0(a, b):
    return lax.dot_general(a, b, (((0,), (0,)), ((), ())), preferred_element_type=f32)


def column_sum(v):
    return jnp.sum(v, 0, keepdims=True)


def norm_parts(v):
    center = v - jnp.mean(v, -1, keepdims=True)
    rstd = lax.rsqrt(jnp.mean(center * center, -1, keepdims=True) + norm_eps)
    return center * rstd, rstd


def norm_back(grad, hat, rstd, gain):
    scaled = grad * gain
    return rstd * (
        scaled
        - jnp.mean(scaled, -1, keepdims=True)
        - hat * jnp.mean(scaled * hat, -1, keepdims=True)
    )


def gelu(v):
    return 0.5 * v * (1.0 + lax.erf(v * (0.5**0.5)))


def gelu_both(v):
    phi = 0.5 * (1.0 + lax.erf(v * (0.5**0.5)))
    return v * phi, phi + v * jnp.exp(-0.5 * v * v) * 0.3989422804014327


def place():
    return lax.axis_index("section"), lax.axis_index("ctx"), lax.axis_index("wsh")


def greet(peers):
    barrier = pltpu.get_barrier_semaphore()
    for peer in peers:
        pl.semaphore_signal(barrier, inc=1, device_id=peer, device_id_type=MESH)
    pl.semaphore_wait(barrier, len(peers))


def push(src, dst, send, recv, peer):
    return pltpu.make_async_remote_copy(
        src_ref=src, dst_ref=dst, send_sem=send, recv_sem=recv, device_id=peer, device_id_type=MESH
    )


def halves(rows):
    low = lax.broadcasted_iota(jnp.int32, rows.shape, 1) < HD
    zero = jnp.zeros_like(rows)
    return jnp.concatenate([jnp.where(low, rows, zero), jnp.where(low, zero, rows)], 0)


def joined(rows):
    low = lax.broadcasted_iota(jnp.int32, (TD, 2 * HD), 1) < HD
    return jnp.where(low, rows[:TD], rows[TD:])


def spread4(rows, width):
    return jnp.concatenate(
        [jnp.broadcast_to(rows[r : r + 1], (BLK, width)) for r in range(4)], 0
    )


def block_lanes(blocks, width):
    lane = lax.broadcasted_iota(jnp.int32, (blocks, width), 1)
    row = lax.broadcasted_iota(jnp.int32, (blocks, width), 0)
    return jnp.where(lax.shift_right_logical(lane, 6) == row, 1.0, 0.0).astype(bf16)


def value_lanes(g):
    return pl.ds(pl.multiple_of(D + g * (2 * HD), 2 * HD), 2 * HD)


def head_column(columns, head):
    lane = lax.broadcasted_iota(jnp.int32, columns.shape, 1)
    return jnp.sum(jnp.where(lane == head, columns, 0.0), 1, keepdims=True)


def pair_lanes(g):
    return pl.ds(pl.multiple_of(g * (2 * HD), 2 * HD), 2 * HD)


def count_tables(m, lens, chosen, random, c, blocks):
    rows, names = PAIRS * 8, H * RND
    valid = (lens[m] + BLK - 1) // BLK
    picked = [lax.rem(chosen[m, 0, k], valid) for k in range(2)]
    table = random[m]
    row = lax.broadcasted_iota(jnp.int32, (rows, blocks), 0)
    lane = lax.broadcasted_iota(jnp.int32, (rows, blocks), 1)
    here = c * BLK_DEV + lax.rem(row, BLK_DEV)
    near = jnp.where(jnp.abs(lane - here) <= 1, 1.0, 0.0)

    def is_picked(ids):
        return [jnp.where(ids == p, 1.0, 0.0) for p in picked]

    kind = lax.broadcasted_iota(jnp.int32, (rows, names), 0)
    name = lax.broadcasted_iota(jnp.int32, (rows, names), 1)
    owner = (kind // 8) * 2 + lax.rem(kind, 8) // BLK_DEV
    same = (lax.rem(kind, 8) < 4) & (name // RND == owner)
    diagonal = jnp.where(
        lax.broadcasted_iota(jnp.int32, (names, names), 0)
        == lax.broadcasted_iota(jnp.int32, (names, names), 1),
        1.0,
        0.0,
    )
    lanes = lax.broadcasted_iota(jnp.int32, (names, blocks), 1).astype(f32)
    by_q = near + sum(is_picked(lane))
    by_k = near + sum(is_picked(here))
    for side in range(BLK_DEV):
        pick = jnp.where(same & (lax.rem(kind, BLK_DEV) == side), 1.0, 0.0).astype(bf16)
        own = random[m, pl.ds(c * BLK_DEV + side, 1), :].astype(f32)
        column = dot((diagonal * own).astype(bf16), jnp.ones((names, blocks), bf16))
        by_q += dot(pick, jnp.where(column == lanes, 1.0, 0.0).astype(bf16))
        match = jnp.where(table == c * BLK_DEV + side, 1.0, 0.0).astype(bf16)
        by_k += dot_t(pick, match)
    return (
        jnp.where(sum(is_picked(here)) > 0, 1.0, by_q),
        jnp.where(sum(is_picked(lane)) > 0, 1.0, by_k),
    )


class Spare:
    def __getattr__(self, name):
        return self

    def __getitem__(self, at):
        return self


def forward_part(nz, W, MB, T, fused, r):
    lens, chosen, random, tokens = r.lens, r.chosen, r.random, r.tokens
    attn_w, up_w, down_w, bias_w, gain_w, up_b = (
        r.attn_w, r.up_w, r.down_w, r.bias_w, r.gain_w, r.up_b,
    )
    attn, up, down, small_in, small_all, small = (
        r.attn, r.up, r.down, r.small_in, r.small_all, r.small,
    )
    xall, kv, q, att, mix, lse, top = r.xall, r.kv, r.q, r.att, r.mix, r.lse, r.top
    first, second, hidden, out, wide, counts = (
        r.first, r.second, r.hidden, r.out, r.wide_q, r.counts,
    )
    s, c, w = place()
    z, core = c // 2, lax.rem(c, 2)
    par = lax.rem(z, 2)
    part = D // W
    ffp = FF // W
    partner = {"ctx": c + 1 - 2 * core}
    buddy = {"ctx": (z + 1 - 2 * par) * 2 + core}
    xs = [{"wsh": lax.rem(w + k, W)} for k in range(1, W)]
    zs = [{"ctx": lax.rem(z + k, nz) * 2 + core} for k in range(1, nz)]
    over = [{"section": 1 - s, "ctx": lax.rem(z + k, nz) * 2 + core} for k in range(nz)]
    greet(xs + zs + over + [partner])

    def rows_of(zz, cc):
        return pl.ds(pl.multiple_of((zz * 2 + cc) * TD, TD), TD)

    def direct_rows(zz, cc):
        return pl.ds(pl.multiple_of((zz * 2 + cc) * TD, TD), BLK)

    def relay_rows(zz, cc):
        return pl.ds(pl.multiple_of((zz * 2 + cc) * TD + BLK, BLK), BLK)

    mine = rows_of(z, core)

    def token_push(m, k):
        peer = zs[k - 1] if m == 0 else over[k]
        return push(tokens.at[m, 0], xall.at[m, mine], r.v_b_send.at[m, k], r.v_b_recv.at[m, k], peer)

    def token_arrival(m, k):
        block = xall.at[m, rows_of(lax.rem(z + nz - k, nz), core)]
        return push(block, block, r.v_b_send.at[m, k], r.v_b_recv.at[m, k], partner)

    def own_tokens(m):
        return pltpu.make_async_copy(tokens.at[m, 0], xall.at[m, mine], r.v_b_recv.at[m, 0])

    def out_push(m, k):
        return push(
            out.at[m, 0:BLK],
            xall.at[m, direct_rows(z, core)],
            r.v_o_send.at[m, k],
            r.v_b_recv.at[m, k],
            over[k],
        )

    def out_arrival(m, k):
        block = xall.at[m, direct_rows(lax.rem(z + nz - k, nz), core)]
        return push(block, block, r.v_o_send.at[m, k], r.v_b_recv.at[m, k], partner)

    def out_relay(m):
        return push(
            out.at[m, BLK:TD],
            xall.at[m, relay_rows(z, core)],
            r.v_r_send.at[m, 0],
            r.v_r_recv.at[m, 0],
            over[0],
        )

    def relay_push(m, k):
        block = xall.at[m, relay_rows(z, core)]
        return push(block, block, r.v_r_send.at[m, k], r.v_r_recv.at[m, k], zs[k - 1])

    def relay_arrival(m, k):
        block = xall.at[m, relay_rows(lax.rem(z + nz - k, nz), core)]
        return push(block, block, r.v_r_send.at[m, k], r.v_r_recv.at[m, k], partner)

    def forward_push(m, k):
        zz = lax.rem(z + nz - k, nz)
        block = xall.at[m, rows_of(zz, core)]
        return push(block, block, r.v_f_send.at[m, k], r.v_f_recv.at[m, k], partner)

    def cut(base, ww, stride, rows, cc, zp, shared):
        share = rows // 4 if shared else rows // 2
        at = base + ww * stride + ((cc * 2 + zp) if shared else cc) * share
        return pl.ds(pl.multiple_of(at, 16), share)

    def piece(p, ww, cc, zp, local):
        stride = 0 if local else 1
        if p < 4:
            r = cut(0, ww, part * stride, part, cc, zp, False)
            matrix = (1, 2, 0, 3)[p]
            return attn_w.at[0, matrix, r] if local else attn.at[matrix, r]
        if p < 6:
            r = cut(0, ww, part * stride, part, cc, zp, True)
            cols = pl.ds((p - 4) * (FF // 2), FF // 2)
            return up_w.at[0, r, cols] if local else up.at[r, cols]
        base = (p - 6) * (ffp // 2)
        r = cut(base, ww, ffp * stride, ffp // 2, cc, zp, p == 6)
        return down_w.at[0, r] if local else down.at[r]

    shared = [p in (4, 5, 6) for p in range(8)]

    def weight_push(k, p):
        return push(
            piece(p, w, core, par, True),
            piece(p, w, core, par, False),
            r.v_w_send.at[k - 1, p],
            r.v_w_recv.at[k - 1, p],
            xs[k - 1],
        )

    def weight_forward(k, p, way):
        zp = 1 - par if way == 2 else par
        spot = piece(p, lax.rem(w + W - k, W), core, zp, False)
        peer = buddy if way == 1 else partner
        return push(spot, spot, r.v_wf_send.at[k - 1, p, way], r.v_wf_recv.at[k - 1, p, way], peer)

    def x_start(p):
        for k in range(1, W):
            weight_push(k, p).start()

    def x_arrive(p):
        for k in range(1, W):
            weight_push(k, p).wait_recv()
            weight_forward(k, p, 0).start()
            if shared[p]:
                weight_forward(k, p, 1).start()

    def z_arrive(p):
        for k in range(1, W):
            weight_forward(k, p, 1).wait_recv()
            weight_forward(k, p, 2).start()

    def core_arrive(p):
        for k in range(1, W):
            weight_forward(k, p, 0).wait_recv()
            if shared[p]:
                weight_forward(k, p, 2).wait_recv()

    def small_push(k):
        return push(small_in, small_all.at[k], r.v_s_send.at[k - 1], r.v_s_recv.at[k - 1], xs[k - 1])

    own_r = pl.ds(pl.multiple_of(w * part, 16), part)
    own_f = pl.ds(pl.multiple_of(w * ffp, 16), ffp)
    own_loads = [
        pltpu.make_async_copy(attn_w.at[0], attn.at[:, own_r], r.v_load_sem.at[0]),
        pltpu.make_async_copy(up_w.at[0], up.at[own_r], r.v_load_sem.at[1]),
        pltpu.make_async_copy(down_w.at[0], down.at[own_f], r.v_load_sem.at[2]),
    ]

    @pl.when(s == 0)
    def _():
        for k in range(1, nz):
            token_push(0, k).start()
        for m in range(MB):
            own_tokens(m).start()

    @pl.when(s == 1)
    def _():
        for m in range(1, MB):
            for k in range(1, nz):
                token_push(m, k).start()

    x_start(0)
    x_start(1)
    for copy in own_loads:
        copy.start()
    small_in[...] = jnp.zeros_like(small_in)
    span = ffp // D
    for e in range(W):

        @pl.when(w == e)
        def _():
            cols = slice(e * part, (e + 1) * part)
            small_in[0:5, cols] = bias_w[0].astype(f32)
            small_in[5:7, cols] = gain_w[0].astype(f32)
            for j in range(span):
                at = 7 + e * span + j
                small_in[at : at + 1, :] = up_b[0:1, j * D : (j + 1) * D].astype(f32)

    for k in range(1, W):
        small_push(k).start()
    for m in range(MB):
        counts[0, m], counts[1, m] = count_tables(m, lens, chosen, random, c, T // BLK)

    def relay_start(m):
        out_relay(m).wait_recv()
        for k in range(1, nz):
            relay_push(m, k).start()

    def rows_ready(m):
        @pl.when(s == 0)
        def _():
            own_tokens(m).wait()

        @pl.when(s == 1)
        def _():
            out_arrival(m, 0).wait_recv()

        forward_push(m, 0).start()
        for k in range(1, nz):

            @pl.when(s == 0)
            def _():
                token_arrival(m, k).wait_recv()

            @pl.when(s == 1)
            def _():
                out_arrival(m, k).wait_recv()
                relay_arrival(m, k).wait_recv()

            forward_push(m, k).start()
        for k in range(nz):
            forward_push(m, k).wait_recv()

    saves = []
    outs = Spare() if fused else r

    def save(src, dst, always=False):
        if fused and not always:
            return
        copy = pltpu.make_async_copy(src, dst, r.v_save_sem.at[next(numbers)])
        copy.start()
        saves.append(copy)

    numbers = iter(range(100))
    lane = lax.broadcasted_iota(jnp.int32, (TD, 128), 1)
    row = lax.broadcasted_iota(jnp.int32, (TD, 128), 0)
    spots = lax.broadcasted_iota(jnp.int32, (1, T), 1)
    tops = jnp.full((1, 128), masked_score, f32)

    slots = kv.shape[0]

    def feed_copies(m):
        pairs = [(out.at[m], r.out_o.at[0, m, 0])]
        if not fused:
            pairs += [
                (first.at[m], outs.first_o.at[m]),
                (hidden.at[m], outs.hidden_o.at[m]),
                (second.at[m], outs.second_o.at[m]),
            ]
        return [
            pltpu.make_async_copy(a, b, r.v_ff_sem.at[m, e]) for e, (a, b) in enumerate(pairs)
        ]

    weight_copies = []
    if not fused:
        pairs = ((attn, outs.attn_o), (up, outs.up_o), (down, outs.down_o))
        weight_copies = [
            pltpu.make_async_copy(a, b, r.v_ff_sem.at[MB, e]) for e, (a, b) in enumerate(pairs)
        ]

    def weights_whole():
        for copy in own_loads[1:]:
            copy.wait()
        for copy in weight_copies:
            copy.start()

    def feed_in(m):
        branch = dot(att[m], attn[3]) + small[1:2, :]
        first[m] = xall[m, mine, :].astype(f32) + branch

    def feed(m):
        hat, _ = norm_parts(first[m])
        normed = hat * small[5:6, :] + small[3:4, :]
        low = normed.astype(bf16)
        second[m] = normed + small[2:3, :]
        for j in range(NCH):
            cols = slice(j * CHUNK, (j + 1) * CHUNK)
            pre = dot(low, up[:, cols]) + small[7 + j : 8 + j, :]
            hidden[m, :, cols] = pre
            second[m] += dot(gelu(pre).astype(bf16), down[cols, :])
        hat, _ = norm_parts(second[m])
        out[m] = (hat * small[6:7, :] + small[4:5, :]).astype(bf16)
        for copy in feed_copies(m):
            copy.start()

    @pl.when(s == 1)
    def _():
        for p in range(8):
            x_arrive(p)
            if p + 2 < 8:
                x_start(p + 2)
            if p and shared[p - 1]:
                z_arrive(p - 1)
        for p in range(8):
            core_arrive(p)
        weights_whole()
        relay_start(0)

    @pl.when(s == 0)
    def _():
        for p in range(3):
            x_arrive(p)
            x_start(p + 2)
        x_start(5)

    for k in range(1, W):
        small_push(k).wait_recv()
    total = small_in[...]
    for k in range(1, W):
        total = total + small_all[k]
    small[...] = total
    save(small, outs.small_o)
    own_loads[0].wait()
    bias_v = small[0:1, :]

    for m in range(MB):
        rows_ready(m)
        if m + 1 < MB:

            @pl.when(s == 1)
            def _():
                relay_start(m + 1)

        if m == 0:

            @pl.when(s == 0)
            def _():
                for p in range(3):
                    core_arrive(p)

        save(xall.at[m], r.xall_o.at[m], True)

        def project(i, _):
            r = pl.ds(pl.multiple_of(i * 256, 256), 256)
            x = xall[m, r, :]
            kv[m % slots, r, 0:D] = dot(x, attn[1]).astype(bf16)
            kv[m % slots, r, D : 2 * D] = (dot(x, attn[2]) + bias_v).astype(bf16)
            return 0

        lax.fori_loop(0, T // 256, project, 0)
        save(kv.at[m % slots], outs.kv_o.at[m])
        kept_kv = saves[-1] if saves else None
        x_own = xall[m, mine, :]
        q[m] = (dot(x_own, attn[0]).astype(bf16).astype(f32) * (HD**-0.5)).astype(bf16)
        save(q.at[m], outs.q_o.at[m])
        length = lens[m]
        live = spots < length
        weights = dot(counts[0, m].astype(bf16), block_lanes(T // BLK, T))
        weights = jnp.where(live, weights, 0.0)
        wide[...] = weights.reshape(PAIRS, 8, T)

        def attend(g, kept):
            lse_c, top_c = kept
            keys = kv[m % slots, :, pair_lanes(g)]
            values = kv[m % slots, :, pl.ds(pl.multiple_of(D + g * 128, 128), 128)]
            scores = dot_t(halves(q[m, :, pair_lanes(g)]), keys)
            count = spread4(wide[g], T)
            scores = jnp.where(count > 0, scores, masked_score)
            largest = jnp.max(scores, 1, keepdims=True)
            powers = jnp.exp(scores - largest) * count
            total = jnp.sum(powers, 1, keepdims=True)
            mixed = dot(powers.astype(bf16), values) / total
            mix[m, :, pair_lanes(g)] = joined(mixed)
            log_total = largest + jnp.log(total)
            for e in range(2):
                lse_c = jnp.where(lane == 2 * g + e, log_total[e * TD : (e + 1) * TD], lse_c)
                top_c = jnp.where(lane == 2 * g + e, largest[e * TD : (e + 1) * TD], top_c)
            return lse_c, top_c

        zeros = jnp.zeros((TD, 128), f32)
        lse_c, top_c = lax.fori_loop(0, PAIRS, attend, (zeros, zeros), unroll=2)
        lse[m] = lse_c
        if slots < MB:
            saves[:] = [x for x in saves if x is not kept_kv]
            kept_kv.wait()
        top_c = jnp.where(c * TD + row < length, top_c, masked_score)
        tops = jnp.maximum(tops, jnp.max(top_c, 0, keepdims=True))
        att[m] = mix[m].astype(bf16)
        save(lse.at[m], outs.lse_o.at[m])
        save(mix.at[m], outs.mix_o.at[m])
        save(att.at[m], outs.att_o.at[m])

        @pl.when(s == 1)
        def _():
            feed_in(m)
            feed(m)

        if m < 2:

            @pl.when(s == 0)
            def _():
                if m == 0:
                    x_arrive(3)
                x_start(6 + m)

    if MB == 1:

        @pl.when(s == 0)
        def _():
            x_start(7)

    top[...] = jnp.broadcast_to(tops, (8, 128))
    save(top, outs.top_o)

    @pl.when(s == 0)
    def _():
        core_arrive(3)
        for m in range(MB):
            feed_in(m)
        x_arrive(4)
        x_arrive(5)
        z_arrive(4)
        x_arrive(6)
        z_arrive(5)
        x_arrive(7)
        z_arrive(6)
        for p in range(4, 8):
            core_arrive(p)
        weights_whole()
        for m in range(MB):
            feed(m)
            if m:
                for k in range(nz):
                    out_push(m - 1, k).wait_send()
            out_relay(m).start()
            out_relay(m).wait_send()
            for k in range(nz):
                out_push(m, k).start()

    def finish():
        for k in range(1, W):
            small_push(k).wait_send()
            for p in range(8):
                weight_push(k, p).wait_send()
                for way in range(3 if shared[p] else 1):
                    weight_forward(k, p, way).wait_send()
        for m in range(MB):
            for k in range(nz):
                forward_push(m, k).wait_send()

            if m == MB - 1:

                @pl.when(s == 0)
                def _():
                    for k in range(nz):
                        out_push(m, k).wait_send()

            @pl.when(s == 1)
            def _():
                for k in range(1, nz):
                    relay_push(m, k).wait_send()

            @pl.when(s == (0 if m == 0 else 1))
            def _():
                for k in range(1, nz):
                    token_push(m, k).wait_send()

        for copy in saves + weight_copies:
            copy.wait()
        for m in range(MB):
            for copy in feed_copies(m):
                copy.wait()

    return finish


def sum_steps(r, nz, W, count, per):
    s, c, w = place()
    z, core = c // 2, lax.rem(c, 2)
    part = D // W
    root = (nz - 1) // 2
    partner = {"ctx": c + 1 - 2 * core}
    xs = [{"wsh": lax.rem(w + k, W)} for k in range(1, W)]
    grads, from_x, chain, sums = r.grads, r.from_x, r.chain, r.sums

    def spot(i, ww):
        at = (i // per) * D + ww * part + lax.rem(i, per) * ROWS
        return pl.ds(pl.multiple_of(at, 16), ROWS)

    def lines(i):
        return pl.ds(pl.multiple_of(i * ROWS, 16), ROWS)

    def x_push(i, k):
        return push(
            grads.at[spot(i, lax.rem(w + k, W))],
            from_x.at[k - 1, lines(i)],
            r.x_send.at[k - 1, i],
            r.x_recv.at[k - 1, i],
            xs[k - 1],
        )

    is_left = z < root
    to_left = {"ctx": jnp.maximum(z - 1, 0) * 2 + core}
    to_right = {"ctx": jnp.minimum(z + 1, nz - 1) * 2 + core}
    far = max(root, nz - 1 - root)
    depth = jnp.where(z == root, far, jnp.where(is_left, z, nz - 1 - z))
    away = jnp.where(is_left, root - z, z - root)

    def chain_push(i, side, peer):
        block = grads.at[spot(i, w)]
        return push(block, chain.at[side, lines(i)], r.ch_send.at[i], r.ch_recv.at[side, i], peer)

    def total_push(i, side, peer, block):
        return push(block, sums.at[core, lines(i)], r.t_send.at[side, i], r.t_recv.at[i], peer)

    def partner_push(i, block):
        return push(block, sums.at[core, lines(i)], r.p_send.at[i], r.p_recv.at[i], partner)

    def partner_arrival(i):
        block = sums.at[1 - core, lines(i)]
        return push(block, block, r.p_send.at[i], r.p_recv.at[i], partner)

    def own_copy(i):
        return pltpu.make_async_copy(grads.at[spot(i, w)], sums.at[core, lines(i)], r.o_sem.at[i])

    def begin():
        for i in range(FLIGHT):
            for k in range(1, W):
                x_push(i, k).start()

    def step(t):
        @pl.when(t + FLIGHT < count)
        def _():
            for k in range(1, W):
                x_push(t, k).wait_send()
                x_push(t + FLIGHT, k).start()

        i = t - LAG * depth

        @pl.when((i >= 0) & (i < count))
        def _():
            acc = grads[spot(i, w), :].astype(f32)
            for k in range(1, W):
                x_push(i, k).wait_recv()
                acc = acc + from_x[k - 1, lines(i), :].astype(f32)
            grads[spot(i, w), :] = acc.astype(bf16)

            @pl.when((z > 0) & (z <= root))
            def _():
                chain_push(i, 0, to_right).wait_recv()
                both = grads[spot(i, w), :].astype(f32) + chain[0, lines(i), :].astype(f32)
                grads[spot(i, w), :] = both.astype(bf16)

            @pl.when((z < nz - 1) & (z >= root))
            def _():
                chain_push(i, 1, to_left).wait_recv()
                both = grads[spot(i, w), :].astype(f32) + chain[1, lines(i), :].astype(f32)
                grads[spot(i, w), :] = both.astype(bf16)

            @pl.when(z < root)
            def _():
                chain_push(i, 0, to_right).start()

            @pl.when(z > root)
            def _():
                chain_push(i, 1, to_left).start()

            @pl.when(z == root)
            def _():
                block = grads.at[spot(i, w)]
                if root > 0:
                    total_push(i, 0, to_left, block).start()
                if root < nz - 1:
                    total_push(i, 1, to_right, block).start()
                partner_push(i, block).start()
                own_copy(i).start()

        b = t - LAG * far - 2 * away

        @pl.when((b >= 0) & (b < count) & (z != root))
        def _():
            block = sums.at[core, lines(b)]
            total_push(b, 0, to_left, block).wait_recv()

            @pl.when((z < root) & (z > 0))
            def _():
                total_push(b, 0, to_left, block).start()

            @pl.when((z > root) & (z < nz - 1))
            def _():
                total_push(b, 1, to_right, block).start()

            partner_push(b, block).start()

    last = count + LAG * 2 * far

    def drain(begin, end):
        def one(i, _):
            block = sums.at[core, lines(i)]
            partner_arrival(i).wait_recv()
            partner_push(i, block).wait_send()

            @pl.when(i + FLIGHT >= count)
            def _():
                for k in range(1, W):
                    x_push(i, k).wait_send()

            @pl.when(z != root)
            def _():
                chain_push(i, 0, to_right).wait_send()

            @pl.when(z == root)
            def _():
                own_copy(i).wait()

            @pl.when((z <= root) & (z > 0))
            def _():
                total_push(i, 0, to_left, block).wait_send()

            @pl.when((z >= root) & (z < nz - 1))
            def _():
                total_push(i, 1, to_right, block).wait_send()

            return 0

        lax.fori_loop(begin, end, one, 0)

    def tail(now, small):
        settled = jnp.maximum(now, LAG * 2 * far + 4)

        def one(t, _):
            step(t)
            i = t - settled
            drain(jnp.clip(i, 0, count), jnp.clip(i + 1, 0, count))
            return 0

        lax.fori_loop(now, last, one, 0)
        small()
        drain(jnp.clip(last - settled, 0, count), count)

    return begin, step, tail


def small_steps(r, nz, W):
    s, c, w = place()
    z, core = c // 2, lax.rem(c, 2)
    partner = {"ctx": c + 1 - 2 * core}
    xs = [{"wsh": lax.rem(w + k, W)} for k in range(1, W)]
    zs = [{"ctx": lax.rem(z + k, nz) * 2 + core} for k in range(1, nz)]

    def core_push(e):
        return push(r.core_s.at[e], r.core_s.at[e], r.sc_send, r.sc_recv, partner)

    def x_push(k, e):
        return push(
            r.wsh_s.at[e], r.wsh_s.at[e], r.sx_send.at[k - 1], r.sx_recv.at[k - 1], xs[k - 1]
        )

    def z_push(k, e):
        return push(r.z_s.at[e], r.z_s.at[e], r.sz_send.at[k - 1], r.sz_recv.at[k - 1], zs[k - 1])

    def first(value):
        r.core_s[core] = value
        core_push(core).start()

    def second():
        core_push(1 - core).wait_recv()
        r.wsh_s[w] = r.core_s[0] + r.core_s[1]
        for k in range(1, W):
            x_push(k, w).start()

    def third():
        for k in range(1, W):
            x_push(k, lax.rem(w + W - k, W)).wait_recv()
        total = r.wsh_s[0]
        for e in range(1, W):
            total = total + r.wsh_s[e]
        r.z_s[z] = total
        for k in range(1, nz):
            z_push(k, z).start()

    def finish():
        for k in range(1, nz):
            z_push(k, lax.rem(z + nz - k, nz)).wait_recv()
        total = r.z_s[0]
        for e in range(1, nz):
            total = total + r.z_s[e]
        r.small_o[...] = total
        core_push(core).wait_send()
        for k in range(1, W):
            x_push(k, w).wait_send()
        for k in range(1, nz):
            z_push(k, z).wait_send()

    return first, second, third, finish


def clip_weights(r, tops, own, spare):
    factor = jnp.sqrt(clip_limit / jnp.maximum(tops, clip_limit))
    lane = lax.broadcasted_iota(jnp.int32, (128, D), 1)
    head = lax.broadcasted_iota(jnp.int32, (128, D), 0)
    heads = jnp.where(lax.shift_right_logical(lane, 6) == head, 1.0, 0.0).astype(f32)
    wide = jnp.dot(factor, heads, preferred_element_type=f32, precision=exact_dot)[0:1]
    for p in range(2):
        spare[p][...] = (own(p).astype(f32) * wide).astype(bf16)
    copies = [pltpu.make_async_copy(spare[p], r.clip_o.at[0, p], r.clip_sem.at[p]) for p in range(2)]
    for copy in copies:
        copy.start()
    return copies


def down_tiles(r, W):
    part, gate_half = D // W, FF // W // 2
    for e in range(W):
        cols = slice(e * gate_half, (e + 1) * gate_half)
        block = dot_0(r.lg[:, cols], r.rd[...]).astype(bf16)
        for j in range(2):
            at = j * D + e * part
            r.grads[at : at + part] = block[j * part : (j + 1) * part]


def up_tiles(r):
    for j in range(2):
        block = dot_0(r.ln[...], r.rh[:, j * D : (j + 1) * D])
        r.grads[(2 + j) * D : (3 + j) * D] = block.astype(bf16)


def attn_tiles(r):
    for j, (left, right) in enumerate(((r.la, r.ra), (r.lb, r.rb))):
        r.grads[(4 + j) * D : (5 + j) * D] = dot_0(left[...], right[...]).astype(bf16)


def ff_operands(W, cc, gated, down, normed, hidden, r):
    ffp = FF // W
    found = []
    for e in range(W):
        cols = pl.ds(pl.multiple_of(e * ffp + cc * (ffp // 2), 128), ffp // 2)
        found.append((gated.at[:, cols], r.lg, e * (ffp // 2), ffp // 2))
    cols = pl.ds(pl.multiple_of(cc * (FF // 2), 128), FF // 2)
    return found + [(down, r.rd, 0, D), (normed, r.ln, 0, D), (hidden.at[:, cols], r.rh, 0, FF // 2)]


def attn_operands(cc, qkv, att, branch, x, r):
    if cc == 0:
        return [(x, r.la), (qkv.at[:, 0:D], r.ra), (x, r.lb), (qkv.at[:, D : 2 * D], r.rb)]
    return [(x, r.la), (qkv.at[:, 2 * D : 3 * D], r.ra), (att, r.lb), (branch, r.rb)]


def reduce_kernel(nz, W, MB, r):
    s, c, w = place()
    z, core = c // 2, lax.rem(c, 2)
    part = D // W
    per = part // ROWS
    partner = {"ctx": c + 1 - 2 * core}
    xs = [{"wsh": lax.rem(w + k, W)} for k in range(1, W)]
    zs = [{"ctx": lax.rem(z + k, nz) * 2 + core} for k in range(1, nz)]
    greet(xs + zs + [partner])
    begin, step, tail = sum_steps(r, nz, W, 6 * per, per)
    small_first, small_second, small_third, small_finish = small_steps(r, nz, W)
    mine = pl.ds(pl.multiple_of(c * TD, TD), TD)

    def copies(m, cc, far):
        n = W + 3
        found = []
        rows = (r.gated_h.at[m], r.down_h.at[m], r.normed_h.at[m], r.hidden_h.at[m])
        side = (MB + m if far else m) * TD
        for e, (src, dst, at, width) in enumerate(ff_operands(W, cc, *rows, r)):
            spot = dst.at[side : side + TD, at : at + width]
            found.append((src, spot, m * (n + 4) + e))
        rows = (r.qkv_h.at[m], r.att_h.at[m], r.branch_h.at[m], r.x_h.at[m, mine])
        for e, (src, dst) in enumerate(attn_operands(cc, *rows, r)):
            found.append((src, dst.at[side : side + TD], m * (n + 4) + n + e))
        if far:
            return [push(a, b, r.c_send.at[e], r.c_recv.at[e], partner) for a, b, e in found]
        return [pltpu.make_async_copy(a, b, r.load_sem.at[e]) for a, b, e in found]

    own_load = pltpu.make_async_copy(r.attn_w.at[0, 0:2], r.own_w, r.own_sem)
    own_load.start()
    small_first(r.small_g[...])
    for cc in range(2):

        @pl.when(core == cc)
        def _():
            for m in range(MB):
                for copy in copies(m, 1 - cc, True) + copies(m, cc, False):
                    copy.start()
            for m in range(MB):
                for copy in copies(m, cc, False):
                    copy.wait()
                for copy in copies(m, cc, True):
                    copy.wait_recv()

    down_tiles(r, W)
    begin()
    up_tiles(r)
    attn_tiles(r)
    small_second()
    own_load.wait()
    clip_copies = clip_weights(
        r, r.tops[...], lambda p: r.own_w[p], [r.own_w.at[p] for p in range(2)]
    )
    small_third()

    tail(0, small_finish)
    for copy in clip_copies:
        copy.wait()
    for cc in range(2):

        @pl.when(core == cc)
        def _():
            for m in range(MB):
                for copy in copies(m, 1 - cc, True):
                    copy.wait_send()


def backward_part(nz, W, MB, T, fused, r, settle=None):
    lens, cot, counts, top, small = r.lens, r.cot, r.counts, r.top, r.small
    attn, up, down, xall, q, mix, lse = r.attn, r.up, r.down, r.xall, r.q, r.mix, r.lse
    first, second, hidden, dout, gfirst = r.first, r.second, r.hidden, r.dout, r.gfirst
    gbranch, gall, relay, aux = r.gbranch, r.gall, r.relay, r.aux
    wide_q, wide_k, lse_all, del_all, del_c = r.wide_q, r.wide_k, r.lse_all, r.del_all, r.del_c
    gnorm, ghid, gated, gdown = r.gnorm, r.ghid, r.gated, r.gdown
    small_g, top_x = r.small_g, r.top_x
    dqkv = [up.at[m * TD : (m + 1) * TD, 0 : 3 * D] for m in range(MB)]
    gin = [up.at[(MB + m) * TD : (MB + m + 1) * TD, 0:D] for m in range(MB)]
    s, c, w = place()
    z, core = c // 2, lax.rem(c, 2)
    partner = {"ctx": c + 1 - 2 * core}
    xs = [{"wsh": lax.rem(w + k, W)} for k in range(1, W)]
    zs = [{"ctx": lax.rem(z + k, nz) * 2 + core} for k in range(1, nz)]
    across = {"section": 1 - s}
    over = [{"section": 1 - s, "ctx": lax.rem(z + k, nz) * 2 + core} for k in range(1, nz)]
    if not fused:
        greet(xs + zs + over + [across, partner])
    part = D // W
    per = part // ROWS
    if fused:
        begin, step, tail = sum_steps(r, nz, W, 6 * per, per)
        small_first, small_second, small_third, small_finish = small_steps(r, nz, W)

    def rows_of(zz, cc):
        return pl.ds(pl.multiple_of((zz * 2 + cc) * TD, TD), TD)

    mine = rows_of(z, core)
    loads = []

    class Held:
        def wait(self):
            pass

    home = Spare() if fused else r

    def load(src, dst):
        if fused:
            return Held()
        copy = pltpu.make_async_copy(src, dst, r.load_sem.at[len(loads)])
        copy.start()
        loads.append(copy)
        return copy

    saves = []
    numbers = iter(range(100))

    def save(src, dst):
        copy = pltpu.make_async_copy(src, dst, r.save_sem.at[next(numbers)])
        copy.start()
        saves.append(copy)

    def cot_load(m):
        return pltpu.make_async_copy(cot.at[m, 0], dout.at[m], r.y_recv.at[m])

    def grad_push(m):
        return push(gin[m], dout.at[m], r.y_send.at[m], r.y_recv.at[m], across)

    @pl.when(s == 1)
    def _():
        for m in range(MB):
            cot_load(m).start()

    slots = xall.shape[0]
    load_second = [load(home.second_h.at[m], second.at[m]) for m in range(MB)]
    cuts = [slice(j * CHUNK, (j + 1) * CHUNK) for j in range(NCH)]
    load_hidden, load_down, load_up = [[]], [], []
    for cut in cuts:
        load_hidden[0].append(load(home.hidden_h.at[0, :, cut], hidden.at[0, :, cut]))
        load_down.append(load(home.down_h.at[cut], down.at[cut]))
        load_up.append(load(home.up_h.at[:, cut], up.at[:, cut]))
    late = {}

    def load_rest():
        late["first"] = [load(home.first_h.at[m], first.at[m]) for m in range(MB)]
        late["attn"] = load(home.attn_h, attn)
        late["mix"] = [load(home.mix_h.at[m], mix.at[m]) for m in range(MB)]
        late["lse"] = [load(home.lse_h.at[m], lse.at[m]) for m in range(MB)]
        for m in range(1, slots):
            load_hidden.append([load(home.hidden_h.at[m], hidden.at[m])])
        late["x"] = [load(home.xall_h.at[m], xall.at[m]) for m in range(slots)]
        late["kv"] = [load(home.kv_h.at[m, mine], home.kv_own.at[m]) for m in range(MB)]
        late["q"] = [load(home.q_h.at[m], q.at[m]) for m in range(MB)]

    def cut_rows(zz, cc, side):
        return pl.ds(pl.multiple_of((zz * 2 + cc) * TD + side * BLK, BLK), BLK)

    def rows_push(m, k):
        if k == 0:
            block = gall.at[m, mine]
            return push(block, block, r.f_send.at[m, 0], r.f_recv.at[m, 0], partner)
        block = gall.at[m, cut_rows(z, core, 0)]
        return push(block, block, r.b_send.at[m, k], r.b_recv.at[m, k], zs[k - 1])

    def rows_arrival(m, k):
        block = gall.at[m, cut_rows(lax.rem(z + nz - k, nz), core, 0)]
        return push(block, block, r.b_send.at[m, k], r.b_recv.at[m, k], partner)

    def relay_out(m):
        block = gall.at[m, cut_rows(z, core, 1)]
        return push(block, relay.at[m], r.r_send.at[m, 0], r.r_recv.at[m, 0], across)

    def relay_push(m, k):
        block = gall.at[m, cut_rows(z, core, 1)]
        return push(relay.at[m], block, r.r_send.at[m, k], r.r_recv.at[m, k], over[k - 1])

    def relay_arrival(m, k):
        block = gall.at[m, cut_rows(lax.rem(z + nz - k, nz), core, 1)]
        return push(block, block, r.r_send.at[m, k], r.r_recv.at[m, k], partner)

    def rows_forward(m, k):
        block = gall.at[m, rows_of(lax.rem(z + nz - k, nz), core)]
        return push(block, block, r.f_send.at[m, k], r.f_recv.at[m, k], partner)

    def aux_push(m, k):
        block = aux.at[m, c]
        peer = partner if k == 0 else zs[k - 1]
        send, recv = (r.af_send, r.af_recv) if k == 0 else (r.a_send, r.a_recv)
        return push(block, block, send.at[m, k], recv.at[m, k], peer)

    def aux_arrival(m, k):
        block = aux.at[m, lax.rem(z + nz - k, nz) * 2 + core]
        return push(block, block, r.a_send.at[m, k], r.a_recv.at[m, k], partner)

    def aux_forward(m, k):
        block = aux.at[m, lax.rem(z + nz - k, nz) * 2 + core]
        return push(block, block, r.af_send.at[m, k], r.af_recv.at[m, k], partner)

    def top_push(k):
        return push(top_x.at[0], top_x.at[k], r.tp_send.at[k - 1], r.tp_recv.at[k - 1], xs[k - 1])

    def spread_start(m):
        relay_out(m).start()
        for k in range(nz):
            aux_push(m, k).start()
            rows_push(m, k).start()

    def spread_sent(m):
        relay_out(m).wait_send()
        for k in range(1, nz):
            rows_push(m, k).wait_send()

    def relay_one(m):
        relay_out(m).wait_recv()
        for k in range(1, nz):
            relay_push(m, k).start()

    def rows_copies(m, cc, far, late):
        side = (MB + m if far else m) * TD
        found = []
        if late:
            rows = (dqkv[m], r.att.at[m], gbranch.at[m], r.xall_o.at[m, mine])
            for e, (src, dst) in enumerate(attn_operands(cc, *rows, r)):
                found.append((src, dst.at[side : side + TD], m * (W + 7) + W + 3 + e))
        else:
            rows = (gated.at[m], gdown.at[m], gnorm.at[m], ghid.at[m])
            for e, (src, dst, at, width) in enumerate(ff_operands(W, cc, *rows, r)):
                found.append((src, dst.at[side : side + TD, at : at + width], m * (W + 7) + e))
        if far:
            return [push(a, b, r.c_send.at[e], r.c_recv.at[e], partner) for a, b, e in found]
        return [pltpu.make_async_copy(a, b, r.c_load.at[e]) for a, b, e in found]

    def rows_start(m, late):
        for cc in range(2):

            @pl.when(core == cc)
            def _():
                for copy in rows_copies(m, 1 - cc, True, late) + rows_copies(m, cc, False, late):
                    copy.start()

    def rows_here(late, picked):
        for cc in range(2):

            @pl.when(core == cc)
            def _():
                for m in range(MB):
                    for copy in rows_copies(m, cc, False, late)[picked]:
                        copy.wait()
                    for copy in rows_copies(m, cc, True, late)[picked]:
                        copy.wait_recv()

    def ff_gradients():
        rows_here(False, slice(0, W + 1))
        down_tiles(r, W)
        begin()
        rows_here(False, slice(W + 1, None))
        up_tiles(r)

    def rows_sent():
        for cc in range(2):

            @pl.when(core == cc)
            def _():
                for m in range(MB):
                    for late in (False, True):
                        for copy in rows_copies(m, 1 - cc, True, late):
                            copy.wait_send()

    @pl.when(s == 0)
    def _():
        for m in range(MB):
            relay_one(m)

    heads = lax.broadcasted_iota(jnp.int32, (D, 128), 0)
    heads = lax.shift_right_logical(heads, 6) == lax.broadcasted_iota(jnp.int32, (D, 128), 1)
    heads = jnp.where(heads, 1.0, 0.0).astype(f32)
    small_g[...] = jnp.zeros_like(small_g)

    for m in range(MB):
        load_second[m].wait()

        @pl.when(s == 1)
        def _():
            cot_load(m).wait()

        @pl.when(s == 0)
        def _():
            grad_push(m).wait_recv()

        grad_out = dout[m].astype(f32)
        hat, rstd = norm_parts(second[m])
        small_g[1:2, :] += column_sum(grad_out * hat)
        small_g[6:7, :] += column_sum(grad_out)
        grad_second = norm_back(grad_out, hat, rstd, small[6:7, :])
        low_second = grad_second.astype(bf16)
        gdown[m] = low_second
        if not fused:
            save(gdown.at[m], r.rows_down.at[m])
        small_g[4:5, :] += column_sum(low_second.astype(f32))
        if m >= slots:
            load_hidden.append([load(home.hidden_h.at[m], hidden.at[m % slots])])
            for copy in hidden_saves:
                saves[:] = [x for x in saves if x is not copy]
                copy.wait()
        if m:
            load_hidden[m][0].wait()
        gfirst[m] = grad_second
        for j in range(NCH):
            cols = slice(j * CHUNK, (j + 1) * CHUNK)
            if m == 0:
                load_hidden[0][j].wait()
                load_down[j].wait()
                if j == NCH - 1:
                    load_rest()
            value, slope = gelu_both(hidden[m % slots, :, cols])
            gated[m % slots, :, cols] = value.astype(bf16)
            grad_hidden = (slope * dot_t(low_second, down[cols, :])).astype(bf16)
            ghid[m % slots, :, cols] = grad_hidden
            small_g[7 + j : 8 + j, :] += column_sum(grad_hidden.astype(f32))
            if m == 0:
                load_up[j].wait()
            gfirst[m] += dot_t(grad_hidden, up[:, cols])
        if not fused:
            save(gated.at[m % slots], r.rows_gated.at[m])
            save(ghid.at[m % slots], r.rows_hidden.at[m])
            hidden_saves = saves[-2:]
        grad_normed = gfirst[m]
        late["first"][m].wait()
        hat, rstd = norm_parts(first[m])
        gnorm[m] = (hat * small[5:6, :] + small[3:4, :]).astype(bf16)
        if fused:
            rows_start(m, False)
        small_g[0:1, :] += column_sum(grad_normed * hat)
        small_g[5:6, :] += column_sum(grad_normed)
        grad_first = norm_back(grad_normed, hat, rstd, small[5:6, :])
        gfirst[m] = grad_first
        low_first = grad_first.astype(bf16)
        gbranch[m] = low_first
        if not fused:
            save(gnorm.at[m], r.rows_normed.at[m])
            save(gbranch.at[m], r.rows_branch.at[m])
        small_g[3:4, :] += column_sum(low_first.astype(f32))
        late["mix"][m].wait()
        late["lse"][m].wait()
        if m == 0:
            late["attn"].wait()
        grad_att = dot_t(low_first, attn[3]).astype(bf16)
        gall[m, mine, :] = grad_att
        weighed = grad_att.astype(f32) * mix[m]
        delta = jnp.dot(weighed, heads, preferred_element_type=f32, precision=exact_dot)
        del_c[m] = delta
        aux[m, c, 0:16] = lse[m].T[0:16]
        aux[m, c, 16:32] = delta.T[0:16]
        aux[m, c, 32:40] = top[...]
        if m == 0:
            spread_start(0)
        elif m == 1:

            @pl.when(s == 0)
            def _():
                spread_sent(0)
                spread_start(1)

    if fused:
        settle()

        @pl.when(s == 0)
        def _():
            ff_gradients()

    row_steps = PAIRS // PACE
    mid_steps = 2
    per_pass = 2 * row_steps + mid_steps

    def paced(base, period):
        if not fused:
            return lambda g: None

        def run(g):
            @pl.when((s == 0) & (lax.rem(g, period) == period - 1))
            def _():
                step(base + g // period)

        return run

    spots = lax.broadcasted_iota(jnp.int32, (1, T), 1)
    here = lax.broadcasted_iota(jnp.int32, (TD, 128), 0)
    def own_pass(m):
        if m >= slots:
            late["x"].append(load(home.xall_h.at[m], xall.at[m % slots]))
        for name in ("x", "kv", "q"):
            late[name][m].wait()

        def stream(g):
            if fused:
                return []
            slot = lax.rem(g, 2)
            return [
                pltpu.make_async_copy(
                    r.kv_h.at[m, :, pl.ds(pl.multiple_of(e * D + g * 128, 128), 128)],
                    r.kvp.at[slot, e],
                    r.kvp_sem.at[slot, e],
                )
                for e in range(2)
            ]

        for copy in stream(0):
            copy.start()
        length = lens[m]
        lanes = block_lanes(T // BLK, T)
        counted = jnp.where(spots < length, dot(counts[0, m].astype(bf16), lanes), 0.0)
        counted = jnp.where(counted > 0, jnp.log(jnp.maximum(counted, 1.0)), masked_score)
        wide_q[...] = counted.reshape(PAIRS, 8, T)
        advance = paced(m * per_pass, PACE)
        advance_mid = paced(m * per_pass + row_steps, max(1, T // 256 // mid_steps))

        def own_rows(g, _):
            if not fused:

                @pl.when(g + 1 < PAIRS)
                def _():
                    for copy in stream(g + 1):
                        copy.start()

            for copy in stream(g):
                copy.wait()
            slot = lax.rem(g, 2)
            lse_c = jnp.concatenate([head_column(lse[m], 2 * g + e) for e in range(2)], 0)
            delta = jnp.concatenate([head_column(del_c[m], 2 * g + e) for e in range(2)], 0)
            queries = halves(q[m, :, pair_lanes(g)])
            grads = halves(gall[m, mine, pair_lanes(g)])
            grad_q = jnp.zeros((2 * TD, 2 * HD), f32)
            for t in range(0, T, STEP):
                if fused:
                    keys = r.kv[m, t : t + STEP, pair_lanes(g)]
                    values = r.kv[m, t : t + STEP, value_lanes(g)]
                else:
                    keys = r.kvp[slot, 0, t : t + STEP]
                    values = r.kvp[slot, 1, t : t + STEP]
                shift = wide_q[g, :, t : t + STEP]
                probs = jnp.exp(dot_t(queries, keys) + spread4(shift, STEP) - lse_c)
                grad_probs = dot_t(grads, values)
                grad_scores = (probs * (grad_probs - delta)).astype(bf16)
                grad_q = grad_q + dot(grad_scores, keys)
            dqkv[m][:, pair_lanes(g)] = (joined(grad_q) * (HD**-0.5)).astype(bf16)
            advance(g)
            return 0

        lax.fori_loop(0, PAIRS, own_rows, 0, unroll=2)
        if m + 1 < MB:

            @pl.when((s == 1) | (m > 0))
            def _():
                spread_sent(m)
                spread_start(m + 1)

        def project(i, _):
            rows = pl.ds(pl.multiple_of(i * 256, 256), 256)
            all_q = dot(xall[m % slots, rows, :], attn[0]).astype(bf16).astype(f32)
            xall[m % slots, rows, :] = (all_q * (HD**-0.5)).astype(bf16)
            advance_mid(i)
            return 0

        lax.fori_loop(0, T // 256, project, 0)

    def all_pass(m):
        lanes = block_lanes(T // BLK, T)
        length = lens[m]
        for k in range(1, nz):
            rows_arrival(m, k).wait_recv()
            relay_arrival(m, k).wait_recv()
            rows_forward(m, k).start()
            aux_arrival(m, k).wait_recv()
            aux_forward(m, k).start()
        for k in range(nz):
            rows_forward(m, k).wait_recv()
            aux_forward(m, k).wait_recv()
        for cc in range(2 * nz):
            lse_all[:, cc * TD : (cc + 1) * TD] = aux[m, cc, 0:16]
            del_all[:, cc * TD : (cc + 1) * TD] = aux[m, cc, 16:32]
        if m == 0:
            most = aux[0, 0, 32:40]
            for cc in range(1, 2 * nz):
                most = jnp.maximum(most, aux[0, cc, 32:40])
            top_x[0] = most
            for k in range(1, W):
                top_push(k).start()
        counted = dot(counts[1, m].astype(bf16), lanes)
        counted = jnp.where(counted > 0, jnp.log(jnp.maximum(counted, 1.0)), masked_score)
        wide_k[...] = counted.reshape(PAIRS, 8, T)
        live = c * TD + here < length
        advance_keys = paced(m * per_pass + row_steps + mid_steps, PACE)

        def own_keys(g, _):
            own_kv = r.kv.at[m, mine] if fused else r.kv_own.at[m]
            keys = halves(own_kv[:, pair_lanes(g)])
            values = halves(own_kv[:, value_lanes(g)])
            lse_r = [lse_all[pl.ds(2 * g + e, 1), :] for e in range(2)]
            delta = [del_all[pl.ds(2 * g + e, 1), :] for e in range(2)]
            shift = wide_k[g]
            shift = jnp.concatenate([shift[0:2] - lse_r[0], shift[2:4] - lse_r[1]], 0)
            grad_k = jnp.zeros((2 * TD, 2 * HD), f32)
            grad_v = jnp.zeros((2 * TD, 2 * HD), f32)
            for t in range(0, T, STEP):
                queries = xall[m % slots, t : t + STEP, pair_lanes(g)]
                grads = gall[m, t : t + STEP, pair_lanes(g)]
                probs = jnp.exp(dot_t(keys, queries) + spread4(shift[:, t : t + STEP], STEP))
                grad_v = grad_v + dot(probs.astype(bf16), grads)
                centre = jnp.concatenate(
                    [jnp.broadcast_to(d[:, t : t + STEP], (TD, STEP)) for d in delta], 0
                )
                grad_scores = (probs * (dot_t(values, grads) - centre)).astype(bf16)
                grad_k = grad_k + dot(grad_scores, queries)
            grad_k, grad_v = joined(grad_k), joined(grad_v)
            lanes_k = pl.ds(pl.multiple_of(D + g * 128, 128), 128)
            lanes_v = pl.ds(pl.multiple_of(2 * D + g * 128, 128), 128)
            dqkv[m][:, lanes_k] = jnp.where(live, grad_k, 0.0).astype(bf16)
            dqkv[m][:, lanes_v] = jnp.where(live, grad_v, 0.0).astype(bf16)
            advance_keys(g)
            return 0

        lax.fori_loop(0, PAIRS, own_keys, 0, unroll=2)
        if fused:
            rows_start(m, True)
        else:
            save(dqkv[m], r.rows_qkv.at[m])
        small_g[2:3, :] += column_sum(dqkv[m][:, 2 * D : 3 * D].astype(f32))
        total = gfirst[m]
        for p in range(3):
            total = total + dot_t(dqkv[m][:, p * D : (p + 1) * D], attn[p])
        gin[m][...] = total.astype(bf16)

        @pl.when(s == 1)
        def _():
            grad_push(m).start()

        save(gin[m], r.grad_in_o.at[0, m, 0])

    for m in range(MB):
        own_pass(m)
        all_pass(m)

    def loop(t, _):
        step(t)
        return 0

    if fused:
        small_first(small_g[...])
        done_1 = EARLY

        @pl.when(s == 1)
        def _():
            relay_one(0)
            ff_gradients()
            lax.fori_loop(0, EARLY, loop, 0)
            for m in range(1, MB):
                relay_one(m)

        rows_here(True, slice(None))
        attn_tiles(r)
        small_second()
        done_0 = MB * per_pass
        now = jnp.where(s == 0, done_0, done_1)
        lax.fori_loop(now, now + 3, loop, 0)
        small_third()
    else:

        @pl.when(s == 1)
        def _():
            for m in range(MB):
                relay_one(m)

        save(small_g, r.small_o)
    for k in range(1, W):
        top_push(k).wait()
    most = top_x[0]
    for k in range(1, W):
        most = jnp.maximum(most, top_x[k])
    if fused:
        for k in range(nz):
            rows_forward(0, k).wait_send()
        saves.extend(
            clip_weights(
                r,
                most,
                lambda p: attn[p, pl.ds(pl.multiple_of(w * part, 16), part), :],
                [gall.at[0, p * part : (p + 1) * part] for p in range(2)],
            )
        )
        tail(now + 3, small_finish)
        rows_sent()
    else:
        r.top_o[...] = most
    for m in range(MB):
        for k in range(nz):
            if m or not fused:
                rows_forward(m, k).wait_send()
            aux_forward(m, k).wait_send()
        for k in range(1, nz):
            aux_push(m, k).wait_send()
            relay_push(m, k).wait_send()
        if m == MB - 1:
            spread_sent(m)

        @pl.when(s == 1)
        def _():
            grad_push(m).wait_send()

    for copy in saves:
        copy.wait()


def finish_kernel(W, r):
    w = lax.axis_index("wsh")
    part, ffp = D // W, FF // W
    span = ffp // D
    straight = [
        [pltpu.make_async_copy(a, b, r.pass_sem.at[0, e]), pltpu.make_async_copy(b, c, r.pass_sem.at[1, e])]
        for e, (a, b, c) in enumerate(
            (
                (r.out, r.out_v, r.out_o),
                (r.grad_in, r.grad_in_v, r.grad_in_o),
                (r.clip, r.clip_v, r.clip_o),
            )
        )
    ]

    def take(t):
        at = ((t // 4) * 2 + t % 2) * part
        source = r.sums.at[(t % 4) // 2, at : at + part]
        return pltpu.make_async_copy(source, r.low.at[t % BUFFERS], r.in_sem.at[t % BUFFERS])

    def give(t):
        if t < 4:
            spot = r.down_o.at[0, t * part : (t + 1) * part]
        elif t < 8:
            spot = r.up_o.at[0, :, (t - 4) * D : (t - 3) * D]
        else:
            spot = r.attn_o.at[0, t - 8]
        return pltpu.make_async_copy(r.wide.at[t % BUFFERS], spot, r.out_sem.at[t % BUFFERS])

    for t in range(BUFFERS):
        take(t).start()
    for come, _ in straight:
        come.start()
    for e in range(W):

        @pl.when(w == e)
        def _():
            cols = slice(e * part, (e + 1) * part)
            r.gains_o[0] = r.small[0:2, cols]
            for j in range(5):
                r.biases_o[j] = r.small[2 + j : 3 + j, cols]
            for j in range(span):
                at = 7 + e * span + j
                r.up_b_o[0:1, j * D : (j + 1) * D] = r.small[at : at + 1, :]

    for t in range(12):
        take(t).wait()
        if t >= BUFFERS:
            give(t - BUFFERS).wait()
        r.wide[t % BUFFERS] = r.low[t % BUFFERS].astype(f32)
        give(t).start()
        if t + BUFFERS < 12:
            take(t + BUFFERS).start()
        if t < 3:
            straight[t][0].wait()
            straight[t][1].start()
    for t in range(12 - BUFFERS, 12):
        give(t).wait()
    for _, go in straight:
        go.wait()


VMEM = pl.BlockSpec(memory_space=pltpu.VMEM)
SMEM = pl.BlockSpec(memory_space=pltpu.SMEM)
ANY = pl.BlockSpec(memory_space=pl.ANY)
DMA = pltpu.SemaphoreType.DMA


def slots_of(T, MB):
    return MB if T <= 2048 else 1


def call(kernel, name, number, limit, ins, outs, scratch):
    names = list(ins) + list(outs) + list(scratch)

    def body(*refs):
        kernel(types.SimpleNamespace(**dict(zip(names, refs, strict=True))))

    found = pl.pallas_call(
        body,
        out_shape=[jax.ShapeDtypeStruct(*v[:2]) for v in outs.values()],
        in_specs=[v[1] for v in ins.values()],
        out_specs=[v[2] for v in outs.values()],
        scratch_shapes=list(scratch.values()),
        compiler_params=pltpu.CompilerParams(
            collective_id=number,
            has_side_effects=number is not None,
            vmem_limit_bytes=limit << 20,
        ),
        name=name,
    )(*(v[0] for v in ins.values()))
    return dict(zip(outs, found))


def sum_scratch(nz, W, MB):
    part, R = D // W, MB * TD
    count = 6 * (part // ROWS)
    copies = MB * (W + 7)
    return dict(
        lg=pltpu.VMEM((2 * R, FF // 2), bf16),
        rd=pltpu.VMEM((2 * R, D), bf16),
        ln=pltpu.VMEM((2 * R, D), bf16),
        rh=pltpu.VMEM((2 * R, FF // 2), bf16),
        la=pltpu.VMEM((2 * R, D), bf16),
        ra=pltpu.VMEM((2 * R, D), bf16),
        lb=pltpu.VMEM((2 * R, D), bf16),
        rb=pltpu.VMEM((2 * R, D), bf16),
        from_x=pltpu.VMEM((W - 1, 6 * part, D), bf16),
        chain=pltpu.VMEM((2, 6 * part, D), bf16),
        core_s=pltpu.VMEM((2, 16, D), f32),
        wsh_s=pltpu.VMEM((W, 16, D), f32),
        z_s=pltpu.VMEM((nz, 16, D), f32),
        c_send=DMA((copies,)),
        c_recv=DMA((copies,)),
        c_load=DMA((copies,)),
        x_send=DMA((W - 1, count)),
        x_recv=DMA((W - 1, count)),
        ch_send=DMA((count,)),
        ch_recv=DMA((2, count)),
        t_send=DMA((2, count)),
        t_recv=DMA((count,)),
        p_send=DMA((count,)),
        p_recv=DMA((count,)),
        o_sem=DMA((count,)),
        clip_sem=DMA((2,)),
        sc_send=DMA,
        sc_recv=DMA,
        sx_send=DMA((W - 1,)),
        sx_recv=DMA((W - 1,)),
        sz_send=DMA((nz - 1,)),
        sz_recv=DMA((nz - 1,)),
    )


def sum_outs(W):
    part = D // W
    return dict(
        sums=((2, 6 * part, D), bf16, ANY),
        small_o=((16, D), f32, VMEM),
        clip_o=((1, 2, part, D), bf16, ANY),
    )


def forward_ins(lens, chosen, random, tokens, attn_w, up_w, down_w, bias_w, gain_w, up_b):
    return dict(
        lens=(lens, SMEM),
        chosen=(chosen, SMEM),
        random=(random, VMEM),
        tokens=(tokens, ANY),
        attn_w=(attn_w, ANY),
        up_w=(up_w, ANY),
        down_w=(down_w, ANY),
        bias_w=(bias_w, VMEM),
        gain_w=(gain_w, VMEM),
        up_b=(up_b, VMEM),
    )


def shared_scratch(T, MB, fused):
    slots = slots_of(T, MB)
    return dict(
        attn=pltpu.VMEM((4, D, D), bf16),
        up=pltpu.VMEM((D, FF), bf16),
        down=pltpu.VMEM((FF + 2 * D if fused else FF, D), bf16),
        q=pltpu.VMEM((MB, TD, D), bf16),
        mix=pltpu.VMEM((MB, TD, D), f32),
        lse=pltpu.VMEM((MB, TD, 128), f32),
        first=pltpu.VMEM((MB, TD, D), f32),
        second=pltpu.VMEM((MB, TD, D), f32),
        wide_q=pltpu.VMEM((PAIRS, 8, T), f32),
    )


def forward_scratch(nz, W, MB, T):
    return dict(
        small_in=pltpu.VMEM((16, D), f32),
        small_all=pltpu.VMEM((W, 16, D), f32),
        small=pltpu.VMEM((16, D), f32),
        xall=pltpu.VMEM((MB, T, D), bf16),
        kv=pltpu.VMEM((slots_of(T, MB), T, 2 * D), bf16),
        att=pltpu.VMEM((MB, TD, D), bf16),
        top=pltpu.VMEM((8, 128), f32),
        hidden=pltpu.VMEM((MB, TD, FF), f32),
        out=pltpu.VMEM((MB, TD, D), bf16),
        v_load_sem=DMA((3,)),
        v_w_send=DMA((W - 1, 8)),
        v_w_recv=DMA((W - 1, 8)),
        v_wf_send=DMA((W - 1, 8, 3)),
        v_wf_recv=DMA((W - 1, 8, 3)),
        v_s_send=DMA((W - 1,)),
        v_s_recv=DMA((W - 1,)),
        v_ff_sem=DMA((MB + 1, 4)),
        v_save_sem=DMA((2 + 6 * MB,)),
        **{"v_" + k: DMA((MB, nz)) for k in V_RINGS},
    )


def backward_scratch(nz, W, MB, T):
    slots = slots_of(T, MB)
    return dict(
        dout=pltpu.VMEM((MB, TD, D), bf16),
        gfirst=pltpu.VMEM((MB, TD, D), f32),
        gbranch=pltpu.VMEM((MB, TD, D), bf16),
        gall=pltpu.VMEM((MB, T, D), bf16),
        relay=pltpu.VMEM((MB, BLK, D), bf16),
        aux=pltpu.VMEM((MB, 2 * nz, 40, 128), f32),
        wide_k=pltpu.VMEM((PAIRS, 8, T), f32),
        lse_all=pltpu.VMEM((16, T), f32),
        del_all=pltpu.VMEM((16, T), f32),
        del_c=pltpu.VMEM((MB, TD, 128), f32),
        gnorm=pltpu.VMEM((MB, TD, D), bf16),
        ghid=pltpu.VMEM((slots, TD, FF), bf16),
        gated=pltpu.VMEM((slots, TD, FF), bf16),
        gdown=pltpu.VMEM((MB, TD, D), bf16),
        small_g=pltpu.VMEM((16, D), f32),
        top_x=pltpu.VMEM((W, 8, 128), f32),
        load_sem=DMA((1 + 3 * NCH + 8 * MB,)),
        y_send=DMA((MB,)),
        y_recv=DMA((MB,)),
        tp_send=DMA((W - 1,)),
        tp_recv=DMA((W - 1,)),
        save_sem=DMA((1 + 7 * MB,)),
        **{k: DMA((MB, nz)) for k in RINGS},
    )


def run_layers(nz, W, MB, cot, ins):
    T = 2 * nz * TD
    ins = dict(ins, cot=(cot, ANY))
    outs = dict(
        out_o=((1, MB, 1, TD, D), bf16, ANY),
        xall_o=((MB, T, D), bf16, ANY),
        grad_in_o=((1, MB, 1, TD, D), bf16, ANY),
        **sum_outs(W),
    )
    scratch = shared_scratch(T, MB, True)
    scratch.update(forward_scratch(nz, W, MB, T))
    scratch.update(backward_scratch(nz, W, MB, T))
    scratch.update(sum_scratch(nz, W, MB))
    scratch.update(counts=pltpu.VMEM((2, MB, PAIRS * 8, T // BLK), f32))

    def kernel(r):
        r.grads = r.down
        settle = forward_part(nz, W, MB, T, True, r)
        backward_part(nz, W, MB, T, True, r, settle)

    return call(kernel, "layers", 0, 63, ins, outs, scratch)


def run_forward(nz, W, MB, ins):
    T = 2 * nz * TD
    outs = dict(
        counts=((2, MB, PAIRS * 8, T // BLK), f32, VMEM),
        out_o=((1, MB, 1, TD, D), bf16, ANY),
        xall_o=((MB, T, D), bf16, ANY),
        kv_o=((MB, T, 2 * D), bf16, ANY),
        q_o=((MB, TD, D), bf16, ANY),
        att_o=((MB, TD, D), bf16, ANY),
        mix_o=((MB, TD, D), f32, ANY),
        lse_o=((MB, TD, 128), f32, ANY),
        first_o=((MB, TD, D), f32, ANY),
        second_o=((MB, TD, D), f32, ANY),
        hidden_o=((MB, TD, FF), f32, ANY),
        top_o=((8, 128), f32, ANY),
        attn_o=((4, D, D), bf16, ANY),
        up_o=((D, FF), bf16, ANY),
        down_o=((FF, D), bf16, ANY),
        small_o=((16, D), f32, ANY),
    )
    scratch = shared_scratch(T, MB, False)
    scratch.update(forward_scratch(nz, W, MB, T))

    def kernel(r):
        forward_part(nz, W, MB, T, False, r)()

    return call(kernel, "forward", 0, 60, ins, outs, scratch)


def run_backward(nz, W, MB, lens, cot, saved):
    T = 2 * nz * TD
    slots = slots_of(T, MB)
    ins = dict(
        lens=(lens, SMEM),
        cot=(cot, ANY),
        **{k: (v, VMEM if k in ("top", "small", "counts") else ANY) for k, v in saved.items()},
    )
    outs = dict(
        grad_in_o=((1, MB, 1, TD, D), bf16, ANY),
        rows_qkv=((MB, TD, 3 * D), bf16, ANY),
        rows_branch=((MB, TD, D), bf16, ANY),
        rows_normed=((MB, TD, D), bf16, ANY),
        rows_hidden=((MB, TD, FF), bf16, ANY),
        rows_gated=((MB, TD, FF), bf16, ANY),
        rows_down=((MB, TD, D), bf16, ANY),
        small_o=((16, D), f32, ANY),
        top_o=((8, 128), f32, VMEM),
    )
    scratch = shared_scratch(T, MB, False)
    scratch.update(backward_scratch(nz, W, MB, T))
    scratch.update(
        xall=pltpu.VMEM((slots, T, D), bf16),
        hidden=pltpu.VMEM((slots, TD, FF), f32),
        kv_own=pltpu.VMEM((MB, TD, 2 * D), bf16),
        kvp=pltpu.VMEM((2, 2, T, 2 * HD), bf16),
        kvp_sem=DMA((2, 2)),
    )

    def kernel(r):
        backward_part(nz, W, MB, T, False, r)

    return call(kernel, "backward", 1, 60, ins, outs, scratch)


def run_reduce(nz, W, MB, ins):
    part = D // W
    scratch = sum_scratch(nz, W, MB)
    scratch.update(
        grads=pltpu.VMEM((6 * D, D), bf16),
        own_w=pltpu.VMEM((2, part, D), bf16),
        load_sem=DMA((MB * (W + 7),)),
        own_sem=DMA,
    )
    ins = {k: (v, VMEM if k in ("small_g", "tops") else ANY) for k, v in ins.items()}
    return call(
        functools.partial(reduce_kernel, nz, W, MB), "reduce", 2, 60, ins, sum_outs(W), scratch
    )


def run_finish(W, MB, sums, small, out, grad_in, clip):
    part, ffp = D // W, FF // W
    HBM = pl.BlockSpec(memory_space=pltpu.MemorySpace.HBM)
    ins = dict(
        sums=(sums, HBM),
        small=(small, VMEM),
        out=(out, HBM),
        grad_in=(grad_in, HBM),
        clip=(clip, HBM),
    )
    outs = dict(
        out_o=(out.shape, bf16, HBM),
        grad_in_o=(grad_in.shape, bf16, HBM),
        attn_o=((1, 4, part, D), f32, HBM),
        up_o=((1, part, FF), f32, HBM),
        down_o=((1, ffp, D), f32, HBM),
        gains_o=((1, 2, part), f32, VMEM),
        biases_o=((5, 1, part), f32, VMEM),
        up_b_o=((1, ffp), f32, VMEM),
        clip_o=(clip.shape, bf16, HBM),
    )
    scratch = dict(
        low=pltpu.VMEM((BUFFERS, part, D), bf16),
        wide=pltpu.VMEM((BUFFERS, part, D), f32),
        in_sem=DMA((BUFFERS,)),
        out_sem=DMA((BUFFERS,)),
        pass_sem=DMA((2, 3)),
        out_v=pltpu.VMEM(out.shape, bf16),
        grad_in_v=pltpu.VMEM(grad_in.shape, bf16),
        clip_v=pltpu.VMEM(clip.shape, bf16),
    )
    return call(functools.partial(finish_kernel, W), "finish", None, 62, ins, outs, scratch)


def per_device(
    tokens, out_cotangent, attn_weights, up_weights, down_weights, norm_gains, bias_rows, up_bias,
    seq_lengths, rand_owner, rand_local, global_raw,
):
    n_ctx, W = lax.axis_size("ctx"), lax.axis_size("wsh")
    nz = n_ctx // 2
    MB = tokens.shape[0]
    lens = seq_lengths[:, 0]
    random = (rand_owner * BLK_DEV + rand_local).reshape(MB, BLK_DEV * n_ctx, H * RND)
    ins = forward_ins(
        lens, global_raw, random, tokens, attn_weights, up_weights, down_weights, bias_rows,
        norm_gains, up_bias,
    )
    if W == 2 and n_ctx * TD <= 2048:
        got = run_layers(nz, W, MB, out_cotangent, ins)
        out, grad_in = got["out_o"], got["grad_in_o"]
    else:
        kept = run_forward(nz, W, MB, ins)
        out, att = kept["out_o"], kept["att_o"]
        names = ["xall", "kv", "q", "mix", "lse", "first", "second", "hidden", "attn", "up", "down"]
        saved = {k + "_h": kept[k + "_o"] for k in names}
        saved.update(top=kept["top_o"], small=kept["small_o"], counts=kept["counts"])
        got = run_backward(nz, W, MB, lens, out_cotangent, saved)
        grad_in = got["grad_in_o"]
        names = ("gated", "down", "normed", "hidden", "qkv", "branch")
        rows = {k + "_h": got["rows_" + k] for k in names}
        rows.update(
            att_h=att, x_h=kept["xall_o"], small_g=got["small_o"], tops=got["top_o"],
            attn_w=attn_weights,
        )
        got = run_reduce(nz, W, MB, rows)
    done = run_finish(W, MB, got["sums"], got["small_o"], out, grad_in, got["clip_o"])
    done["biases_o"] = done["biases_o"].transpose(1, 0, 2)
    return tuple(done.values())


def solution(mesh):
    placed = (
        P(None, "wsh", "ctx", None),
        P(None, "wsh", "ctx", None),
        P("section", None, "wsh", None),
        P("section", "wsh", None),
        P("section", "wsh", None),
        P("section", None, "wsh"),
        P("section", None, "wsh"),
        P("section", "wsh"),
        P(None, "wsh"),
        P(None, "wsh", None, None, None),
        P(None, "wsh", None, None, None),
        P(None, "wsh", None),
    )
    return jax.shard_map(
        per_device,
        mesh=mesh,
        in_specs=placed,
        out_specs=(
            P("section", None, "wsh", "ctx", None),
            P("section", None, "wsh", "ctx", None),
            P("section", None, "wsh", None),
            P("section", "wsh", None),
            P("section", "wsh", None),
            P("section", None, "wsh"),
            P("section", None, "wsh"),
            P("section", "wsh"),
            P("section", None, "wsh", None),
        ),
        check_vma=False,
    )
```
